32 devices in a mesh: lvl: 2 (over y), row: 16 (over z, x, core).
Axes of the slice: x: 2, y: 2, z: 4, core: 2. Of those that a mesh axis runs over, the one named last changes fastest.
Arguments:
- node_latent: float32 [8192, 512], P('row'), may hold values from -6 to 6
- edge_latent: float32 [81920, 512], P(('lvl', 'row')), may hold values from -6 to 6
- senders: int32 [81920], P(('lvl', 'row')), may hold values from 0 to 8191, as said below
- receivers: int32 [81920], P(('lvl', 'row')), may hold values from 0 to 8191, as said below
- live_edges: int32 [32], P(('lvl', 'row')), may hold values from 640 to 2560, as said below
- edge_w1: bfloat16 [2, 1536, 512], replicated, may hold values from -0.15625 to 0.15625
- edge_b1: float32 [2, 512], replicated, may hold values from -3 to 3
- edge_w2: bfloat16 [2, 512, 512], replicated, may hold values from -0.25 to 0.25
- edge_b2: float32 [2, 512], replicated, may hold values from -3 to 3
- edge_gain: float32 [2, 512], replicated, may hold values from 0.5 to 1.5
- edge_shift: float32 [2, 512], replicated, may hold values from -2 to 2
- node_w1: bfloat16 [2, 1024, 512], replicated, may hold values from -0.1875 to 0.1875
- node_b1: float32 [2, 512], replicated, may hold values from -3 to 3
- node_w2: bfloat16 [2, 512, 512], replicated, may hold values from -0.25 to 0.25
- node_b2: float32 [2, 512], replicated, may hold values from -3 to 3
- node_gain: float32 [2, 512], replicated, may hold values from 0.5 to 1.5
- node_shift: float32 [2, 512], replicated, may hold values from -2 to 2
- node_cotangent: float32 [8192, 512], P('row'), may hold values from -6 to 6
- edge_cotangent: float32 [81920, 512], P(('lvl', 'row')), may hold values from -6 to 6
Outputs:
- node_out: float32 [8192, 512], P('row')
- edge_out: float32 [81920, 512], P(('lvl', 'row'))
- node_grad: float32 [8192, 512], P('row')
- edge_grad: float32 [81920, 512], P(('lvl', 'row'))
- grad_edge_w1: float32 [2, 1536, 512], replicated
- grad_edge_b1: float32 [2, 512], replicated
- grad_edge_w2: float32 [2, 512, 512], replicated
- grad_edge_b2: float32 [2, 512], replicated
- grad_edge_gain: float32 [2, 512], replicated
- grad_edge_shift: float32 [2, 512], replicated
- grad_node_w1: float32 [2, 1024, 512], replicated
- grad_node_b1: float32 [2, 512], replicated
- grad_node_w2: float32 [2, 512, 512], replicated
- grad_node_b2: float32 [2, 512], replicated
- grad_node_gain: float32 [2, 512], replicated
- grad_node_shift: float32 [2, 512], replicated
- stream_rms: float32 [2, 4], replicated
The draws below stay inside these ranges and needn't reach their ends.
Inputs may be any that keep to these rules, and one draw needn't show every extreme that they name: Edge block b (slots b * 2560 to (b + 1) * 2560 - 1) has receivers in node rows (b mod 16) * 512 to (b mod 16 + 1) * 512 - 1, never falling within the block, its first slot at the first of these rows and its last slot at the last; padded slots also carry such receivers. In each edge block, for each r, exactly 160 slots have senders in node rows r * 512 to (r + 1) * 512 - 1. `live_edges`: some edge block has all 2560 slots live in every draw.
All inputs are finite; a program needn't handle non-finite values.
Results may differ from the reference program's by a relative error of at most 0.02.
Values may be sent and summed in bfloat16 or wider, within the bound.
A program may use at most 320 MiB of HBM per device.

```python
import jax
import jax.numpy as jnp
from jax import lax

D = 512
LAYERS = 2
NODE_DEV = 512
E_DEV = 2560
NODE_BLOCKS = 16
EDGE_BLOCKS = 32
NODES = 8192
EDGES = 81920


def draw_senders(key, part):
    key = jax.random.fold_in(key, 5)
    order_key, row_key = jax.random.split(key)
    block_keys = jax.random.split(order_key, EDGE_BLOCKS)

    def shuffle_one(one_key):
        return jax.random.permutation(one_key, E_DEV)
    spread = jax.vmap(shuffle_one)(block_keys)
    owners = (spread % NODE_BLOCKS).astype(jnp.int32)
    local_rows = jax.random.randint(row_key, (EDGE_BLOCKS, E_DEV), 0, NODE_DEV)
    return (owners * NODE_DEV + local_rows).reshape(EDGES).astype(jnp.int32)


def draw_receivers(key, part):
    key = jax.random.fold_in(key, 11)
    local_rows = jnp.sort(jax.random.randint(key, (EDGE_BLOCKS, E_DEV), 0, NODE_DEV), axis=1)
    local_rows = local_rows.at[:, 0].set(0).at[:, E_DEV - 1].set(NODE_DEV - 1)
    owners = jnp.arange(EDGE_BLOCKS, dtype=jnp.int32) % NODE_BLOCKS
    return (local_rows + owners[:, None] * NODE_DEV).reshape(EDGES).astype(jnp.int32)


def draw_live_edges(key, part):
    key = jax.random.fold_in(key, 23)
    first_key, second_key = jax.random.split(key)
    counts = jax.random.randint(first_key, (EDGE_BLOCKS,), E_DEV // 4, E_DEV + 1)
    busiest = jax.random.randint(second_key, (), 0, EDGE_BLOCKS)
    return jnp.where(jnp.arange(EDGE_BLOCKS) == busiest, E_DEV, counts).astype(jnp.int32)


def steps_of(rng, shape, shards, smallest, high):
    def one(dim, shards_of):
        heights = jax.random.uniform(jax.random.fold_in(jax.random.fold_in(rng, 6), dim), (shards_of,), jnp.float32, smallest / len(shards), high / len(shards))
        return jnp.repeat(jnp.exp(heights), shape[dim] // shards_of).reshape((-1,) + (1,) * (len(shape) - dim - 1))

    factor_of = one(*shards[0])
    for cut in shards[1:]:
        factor_of = factor_of * one(*cut)
    return factor_of


def normal_values(key, extent, scale, most, shards=(), held_as=jnp.bfloat16):
    array = scale * jax.random.normal(key, extent, jnp.float32)
    if shards:
        array = array * steps_of(key, extent, shards, -0.22, 0.18)
    return jnp.clip(array, -most, most).astype(held_as)


def setup_inputs(seed: int = 0) -> dict:
    key_of = jax.random.split(jax.random.key(seed), 20)
    return {
        "node_latent": normal_values(key_of[0], (NODES, D), 1.0, 6.0, ((0, 16),), jnp.float32),
        "edge_latent": normal_values(key_of[1], (EDGES, D), 1.0, 6.0, ((0, 32),), jnp.float32),
        "senders": draw_senders(jax.random.fold_in(key_of[19], 71), 0),
        "receivers": draw_receivers(jax.random.fold_in(key_of[19], 71), 0),
        "live_edges": draw_live_edges(jax.random.fold_in(key_of[19], 71), 0),
        "edge_w1": normal_values(key_of[5], (LAYERS, 3 * D, D), (3 * D) ** -0.5, 0.15625),
        "edge_b1": normal_values(key_of[6], (LAYERS, D), 0.5, 3.0, (), jnp.float32),
        "edge_w2": normal_values(key_of[7], (LAYERS, D, D), D ** -0.5, 0.25),
        "edge_b2": normal_values(key_of[8], (LAYERS, D), 0.5, 3.0, (), jnp.float32),
        "edge_gain": jnp.clip(1.0 + 0.1 * jax.random.normal(key_of[9], (LAYERS, D), jnp.float32), 0.5, 1.5),
        "edge_shift": normal_values(key_of[10], (LAYERS, D), 0.3, 2.0, (), jnp.float32),
        "node_w1": normal_values(key_of[11], (LAYERS, 2 * D, D), (2 * D) ** -0.5, 0.1875),
        "node_b1": normal_values(key_of[12], (LAYERS, D), 0.5, 3.0, (), jnp.float32),
        "node_w2": normal_values(key_of[13], (LAYERS, D, D), D ** -0.5, 0.25),
        "node_b2": normal_values(key_of[14], (LAYERS, D), 0.5, 3.0, (), jnp.float32),
        "node_gain": jnp.clip(1.0 + 0.1 * jax.random.normal(key_of[15], (LAYERS, D), jnp.float32), 0.5, 1.5),
        "node_shift": normal_values(key_of[16], (LAYERS, D), 0.3, 2.0, (), jnp.float32),
        "node_cotangent": normal_values(key_of[17], (NODES, D), 1.0, 6.0, ((0, 16),), jnp.float32),
        "edge_cotangent": normal_values(key_of[18], (EDGES, D), 1.0, 6.0, ((0, 32),), jnp.float32),
    }


NORM_EPS = 1e-05
HIGH = lax.Precision.HIGHEST

@jax.custom_vjp
def low(v):
    return lax.optimization_barrier(v.astype(jnp.bfloat16)).astype(jnp.float32)

@jax.custom_vjp
def low_back(v):
    return v

def low_keep(v):
    return (low(v), None)

def low_pass(kept, grad):
    return (grad,)

def back_keep(v):
    return (v, None)

def back_low(kept, grad):
    return (low(grad),)
low.defvjp(low_keep, low_pass)
low_back.defvjp(back_keep, back_low)

def layer_norm(values, norm_gain, norm_shift):
    average = lax.optimization_barrier(jnp.mean(values, axis=-1, keepdims=True))
    centered = values - average
    variance = lax.optimization_barrier(jnp.mean(centered * centered, axis=-1, keepdims=True))
    return centered * lax.rsqrt(variance + NORM_EPS) * norm_gain + norm_shift

def perceptron(joined, first_w, first_b, second_w, second_b, norm_gain, norm_shift):
    pre_one = low_back(jnp.dot(joined, first_w, precision=HIGH) + first_b)
    active = low(jax.nn.silu(pre_one))
    pre_two = low_back(jnp.dot(active, second_w, precision=HIGH) + second_b)
    return layer_norm(pre_two, norm_gain, norm_shift)

def root_mean(values):
    return jnp.sqrt(jnp.mean(values * values))

def forward(node_state, edge_state, weights, senders, receivers, live_mask):
    blocks = EDGES // E_DEV
    stats = []
    for layer_idx in range(LAYERS):
        picked = [weight[layer_idx] for weight in weights]
        edge_params = picked[:6]
        node_params = picked[6:]
        low_node = low(node_state)
        low_edge = low(edge_state)

        def edge_block(block_items):
            edge_rows, send_ids, recv_ids, mask_rows = block_items
            joined = jnp.concatenate([edge_rows, jnp.take(low_node, send_ids, axis=0), jnp.take(low_node, recv_ids, axis=0)], axis=1)
            return perceptron(joined, *edge_params) * mask_rows[:, None]
        update = lax.map(jax.checkpoint(edge_block), (low_edge.reshape(blocks, E_DEV, D), senders.reshape(blocks, E_DEV), receivers.reshape(blocks, E_DEV), live_mask.reshape(blocks, E_DEV))).reshape(EDGES, D)
        edge_state = edge_state + update
        received = jax.ops.segment_sum(low(update), receivers, num_segments=NODES)
        joined_node = jnp.concatenate([low_node, low(received)], axis=1)
        node_update = perceptron(joined_node, *node_params)
        node_state = node_state + node_update
        stats.append(jnp.stack([root_mean(node_state), root_mean(edge_state), root_mean(update), root_mean(node_update)]))
    return ((node_state, edge_state), jnp.stack(stats))

def reference(node_latent, edge_latent, senders, receivers, live_edges, edge_w1, edge_b1, edge_w2, edge_b2, edge_gain, edge_shift, node_w1, node_b1, node_w2, node_b2, node_gain, node_shift, node_cotangent, edge_cotangent):
    slot_ids = jnp.arange(EDGES, dtype=jnp.int32) % E_DEV
    live_mask = (slot_ids < jnp.repeat(live_edges, E_DEV)).astype(jnp.float32)
    weights = tuple((weight.astype(jnp.float32) for weight in (edge_w1, edge_b1, edge_w2, edge_b2, edge_gain, edge_shift, node_w1, node_b1, node_w2, node_b2, node_gain, node_shift)))

    def run_layers(node_state, edge_state, params):
        return forward(node_state, edge_state, params, senders, receivers, live_mask)
    (node_out, edge_out), pullback, stream_rms = jax.vjp(run_layers, node_latent, edge_latent, weights, has_aux=True)
    node_grad, edge_grad, wgrads = pullback((node_cotangent, edge_cotangent))
    return (node_out, edge_out, node_grad, edge_grad, wgrads[0], wgrads[1], wgrads[2], wgrads[3], wgrads[4], wgrads[5], wgrads[6], wgrads[7], wgrads[8], wgrads[9], wgrads[10], wgrads[11], stream_rms)
```

```python
import functools

import jax
import jax.numpy as jnp
from jax import lax
from jax.experimental import pallas as pl
from jax.experimental.pallas import tpu as pltpu
from jax.sharding import PartitionSpec as P

MESH = pl.DeviceIdType.MESH
NORM_EPS = 1e-05
F32 = jnp.float32
BF16 = jnp.bfloat16
VMEM_BYTES = 61 * 2**20


NEAREST = ((0, 1, 2, 3), (1, 0, 2, 3), (2, 3, 1, 0), (3, 2, 1, 0))


class Grid:
    def __init__(self, levels, rows):
        self.L, self.R = levels, rows
        self.Z = 4
        self.X = rows // (2 * self.Z)
        self.l = lax.axis_index("lvl")
        row = lax.axis_index("row")
        self.row = row
        self.core = lax.rem(row, 2)
        self.x = lax.rem(row // 2, self.X)
        self.z = row // (2 * self.X)
        self.up = self.z < self.Z - 1
        self.down = self.z > 0

    def block(self, z, x, core):
        return (z * self.X + x) * 2 + core

    def mate(self):
        return (self.l, self.block(self.z, self.x, 1 - self.core))

    def at_z(self, z):
        return (self.l, self.block(jnp.clip(z, 0, self.Z - 1), self.x, self.core))

    def x_other(self, i):
        x = lax.rem(self.x + i, self.X)
        return x, (self.l, self.block(self.z, x, self.core))

    def l_other(self, i):
        l = lax.rem(self.l + i, self.L)
        return l, (l, self.row)

    def nth(self, k, z=None):
        z_here = self.z if z is None else z
        order = NEAREST
        out = jnp.int32(0)
        for z in range(4):
            for j in range(4):
                if order[z][j]:
                    out = jnp.where((z_here == z) & (k == j), order[z][j], out)
        return out

    def local(self, zk, z=None):
        return (zk // 2) == lax.rem(self.z if z is None else z, 2)

    def corner_z(self, q):
        side = lax.rem(lax.rem(self.z, 2) + q // 2, 2)
        return side * 2 + lax.rem(q, 2)

    def pair_z(self):
        return self.z + 1 - 2 * lax.rem(self.z, 2)

    def greet(self):
        barrier = pltpu.get_barrier_semaphore()

        def hello(who):
            pl.semaphore_signal(barrier, inc=1, device_id=who, device_id_type=MESH)

        hello(self.mate())
        for i in range(1, self.X):
            hello(self.x_other(i)[1])
        for i in range(1, self.L):
            hello(self.l_other(i)[1])
        pl.when(self.up)(lambda: hello(self.at_z(self.z + 1)))
        pl.when(self.down)(lambda: hello(self.at_z(self.z - 1)))
        pl.semaphore_wait(barrier, self.X + self.L - 1 + self.up.astype(jnp.int32) + self.down.astype(jnp.int32))


def only(when, act):
    if when is None:
        act()
    else:
        pl.when(when)(act)


def cuts(h):
    first = -(-h // 32) * 16
    return ((0, first), (first, h - first)) if h > first else ((0, h),)


class Gather:
    def __init__(self, grid, table, h, send_sem, recv_sem):
        self.g, self.table, self.h = grid, table, h
        self.cuts = cuts(h)
        self.send_sem, self.recv_sem = send_sem, recv_sem
        X, L = grid.X, grid.L
        self.per_column = X + L + 1
        self.per_sides = 2 * (X - 1) * (L - 1) + X - 1 + L - 1
        self.at_sides = 4 * self.per_column
        self.at_corners = self.at_sides + 4 * self.per_sides
        self.drain = False

    @staticmethod
    def sends(levels, rows):
        X, L = rows // 8, levels
        return 2 * (4 * (X + L + 1) + 4 * (2 * (X - 1) * (L - 1) + X + L - 2) + 8 * (X - 1) * (L - 1))

    def slot(self, block, l, s=None):
        start, size = (0, self.h) if s is None else self.cuts[s]
        return self.table.at[pl.ds(pl.multiple_of((block * self.g.L + l) * self.h + start, 16), size)]

    def push(self, at, block, l, s, who, when=None):
        place = self.slot(block, l, s)
        copy = pltpu.make_async_remote_copy(
            place, place, self.send_sem.at[2 * at + s], self.recv_sem.at[(block * self.g.L + l) * 2 + s], device_id=who, device_id_type=MESH
        )
        only(when, copy.wait_send if self.drain else copy.start)

    def arrived(self, block, l, s):
        if self.drain:
            return
        place = self.slot(block, l, s)
        pltpu.make_async_remote_copy(
            place, place, self.send_sem.at[0], self.recv_sem.at[(block * self.g.L + l) * 2 + s], device_id=self.g.mate(), device_id_type=MESH
        ).wait_recv()

    def column(self, k, s, own=False):
        g = self.g
        zk = g.nth(k)
        block = g.block(zk, g.x, g.core)
        at = k * self.per_column
        if not own:
            self.arrived(block, g.l, s)
        self.push(at, block, g.l, s, g.at_z(g.z + 1), g.up & (zk <= g.z))
        self.push(at + 1, block, g.l, s, g.at_z(g.z - 1), g.down & (zk >= g.z))
        for i in range(1, g.X):
            self.push(at + 1 + i, block, g.l, s, g.x_other(i)[1])
        for j in range(1, g.L):
            self.push(at + g.X + j, block, g.l, s, g.l_other(j)[1])
        self.push(at + g.X + g.L, block, g.l, s, g.mate())

    def sides(self, k, s):
        g = self.g
        zk = g.nth(k)
        even = lax.rem(zk, 2) == 0
        at = self.at_sides + k * self.per_sides
        for i in range(1, g.X):
            block = g.block(zk, g.x_other(i)[0], g.core)
            self.arrived(block, g.l, s)
            for j in range(1, g.L):
                self.push(at, block, g.l, s, g.l_other(j)[1], g.local(zk) & even)
                at = at + 1
            self.push(at, block, g.l, s, g.mate())
            at = at + 1
        for j in range(1, g.L):
            block = g.block(zk, g.x, g.core)
            l = g.l_other(j)[0]
            self.arrived(block, l, s)
            for i in range(1, g.X):
                self.push(at, block, l, s, g.x_other(i)[1], g.local(zk) & jnp.logical_not(even))
                at = at + 1
            self.push(at, block, l, s, g.mate())
            at = at + 1

    def corners(self, z, s, local):
        g = self.g
        q = lax.rem(z, 2) + (0 if local else 2)
        for i in range(1, g.X):
            block = g.block(z, lax.rem(g.x + i, g.X), g.core)
            for j in range(1, g.L):
                l = g.l_other(j)[0]
                at = self.at_corners + ((q * (g.X - 1) + i - 1) * (g.L - 1) + j - 1) * 2
                self.arrived(block, l, s)
                if local:
                    self.push(at, block, l, s, g.at_z(g.pair_z()))
                self.push(at + 1, block, l, s, g.mate())

    def mates(self, z, x):
        for l in range(self.g.L):
            for s in range(len(self.cuts)):
                self.arrived(self.g.block(z, x, 1 - self.g.core), l, s)

    def begin(self):
        for s in range(len(self.cuts)):
            self.column(0, s, own=True)

    def wave(self, k, s):
        g = self.g
        pl.when(k < 3)(lambda: self.column(k + 1, s))
        pl.when(k < 4)(lambda: self.sides(k, s))
        if g.L == 1:
            return
        two = len(self.cuts) == 2
        late = 1 - s if two else s
        back = 2 - s if two else 1
        for local, lag in ((True, back), (False, back + 1)):
            who = None if local else g.pair_z()
            kk = k - lag
            z = g.nth(jnp.clip(kk, 0, 3), who)
            pl.when((kk >= 0) & (kk < 4) & g.local(z, who))(lambda z=z, local=local: self.corners(z, late, local))

    def due(self, k, c):
        g = self.g
        own = c == 0
        far = c > g.X - 1
        off = jnp.where(own, 0, lax.rem(c - 1, max(g.X - 1, 1)) + 1)
        kk = jnp.where(own, k - 1, jnp.where(far, k - 3, k - 2))
        who = jnp.where(far, g.pair_z(), g.z)
        z = g.nth(jnp.clip(kk, 0, 3), who)
        there = (kk >= 0) & (kk < 4) & (own | g.local(z, who))
        return z, lax.rem(g.x + off, g.X), there

    def run(self, work=None):
        g = self.g
        parts = 2 * g.X - 1
        self.begin()

        def one(i, done):
            k, c = i // parts, lax.rem(i, parts)
            for s in range(len(self.cuts)):
                pl.when(c == s)(lambda s=s: self.wave(k, s))
            z, x, there = self.due(k, c)

            def ready():
                self.mates(z, x)
                if work is not None:
                    work(z, x, done)

            pl.when(there)(ready)
            return done + there.astype(jnp.int32)

        lax.fori_loop(0, 7 * parts, one, jnp.int32(0))

    def finish(self):
        self.drain = True
        self.begin()

        def one(k, carry):
            for s in range(len(self.cuts)):
                self.wave(k, s)
            return carry

        lax.fori_loop(0, 7, one, 0)


class Scatter:
    def __init__(self, grid, stage, inbox, h, send_sem, recv_sem):
        self.g, self.stage, self.inbox, self.h = grid, stage, inbox, h
        self.cuts = cuts(h)
        self.send_sem, self.recv_sem = send_sem, recv_sem
        X, L = grid.X, grid.L
        at = 0
        self.base = {}
        for name, count in self.parts(X, L):
            self.base[name] = at
            at += count
        at = 0
        self.out = {}
        for name, count in self.out_parts(X, L):
            self.out[name] = at
            at += count
        self.drain = False
        self.prepare()

    @staticmethod
    def parts(X, L):
        side = (X - 1) * (L - 1)
        return (("mate", 4 * X * L), ("pair", 2 * side), ("l2", side), ("x2", side), ("xc", 4 * (X - 1)), ("lc", 4 * (L - 1)), ("z", 5))

    @staticmethod
    def out_parts(X, L):
        side = (X - 1) * (L - 1)
        return (("mate", 4 * X * L), ("corner", 8 * side), ("xc", 4 * (X - 1)), ("lc", 4 * (L - 1)), ("z", 4))

    @staticmethod
    def receives(levels, rows):
        return sum(count for _, count in Scatter.parts(rows // 8, levels))

    @staticmethod
    def sends(levels, rows):
        return 2 * sum(count for _, count in Scatter.out_parts(rows // 8, levels))

    def slot(self, block, l, s=None):
        start, size = (0, self.h) if s is None else self.cuts[s]
        return self.stage.at[pl.ds(pl.multiple_of((block * self.g.L + l) * self.h + start, 16), size)]

    def push(self, out, block, l, s, at, who, when=None):
        start, size = self.cuts[s]
        copy = pltpu.make_async_remote_copy(
            self.slot(block, l, s),
            self.inbox.at[at, pl.ds(start, size)],
            self.send_sem.at[2 * out + s],
            self.recv_sem.at[2 * at + s],
            device_id=who,
            device_id_type=MESH,
        )
        only(when, copy.wait_send if self.drain else copy.start)

    def arrived(self, at, s):
        start, size = self.cuts[s]
        place = self.inbox.at[at, pl.ds(start, size)]
        pltpu.make_async_remote_copy(
            place, place, self.send_sem.at[0], self.recv_sem.at[2 * at + s], device_id=self.g.mate(), device_id_type=MESH
        ).wait_recv()

    def total(self, block, l, s, ats):
        start, size = self.cuts[s]
        for at in ats:
            self.arrived(at, s)
        out = self.slot(block, l, s)[...].astype(F32)
        for at in ats:
            out = out + self.inbox[at, start : start + size].astype(F32)
        return out

    def add(self, block, l, s, ats, when=None):
        if self.drain:
            return

        def act():
            self.slot(block, l, s)[...] = self.total(block, l, s, ats).astype(BF16)

        only(when, act)

    def each(self):
        return range(len(self.cuts))

    def to_mate(self, z, x):
        g = self.g
        for l in range(g.L):
            at = (z * g.X + x) * g.L + l
            for s in self.each():
                self.push(self.out["mate"] + at, g.block(z, x, 1 - g.core), l, s, self.base["mate"] + at, g.mate())

    def from_mate(self, z, x):
        g = self.g
        for l in range(g.L):
            for s in self.each():
                self.add(g.block(z, x, g.core), l, s, [self.base["mate"] + (z * g.X + x) * g.L + l])

    def corner_far(self, z, i):
        g = self.g
        block = g.block(z, lax.rem(g.x + i, g.X), g.core)
        for j in range(1, g.L):
            l = g.l_other(j)[0]
            spot = (lax.rem(z, 2) * (g.X - 1) + i - 1) * (g.L - 1) + j - 1
            for s in self.each():
                self.push(self.out["corner"] + spot, block, l, s, self.base["pair"] + spot, g.at_z(g.pair_z()))

    def corner_near(self, z, i):
        g = self.g
        x, x_dev = g.x_other(i)
        block = g.block(z, x, g.core)
        even = lax.rem(z, 2) == 0
        side = (g.X - 1) * (g.L - 1)
        for j in range(1, g.L):
            l, l_dev = g.l_other(j)
            spot = (lax.rem(z, 2) * (g.X - 1) + i - 1) * (g.L - 1) + j - 1
            out = self.out["corner"] + 2 * side + spot
            for s in self.each():
                self.add(block, l, s, [self.base["pair"] + spot])
                self.push(out, block, l, s, self.base["l2"] + (i - 1) * (g.L - 1) + g.L - j - 1, l_dev, even)
                self.push(out, block, l, s, self.base["x2"] + (g.X - i - 1) * (g.L - 1) + j - 1, x_dev, jnp.logical_not(even))

    def side_x(self, zk, i, waits):
        g = self.g
        x, x_dev = g.x_other(i)
        block = g.block(zk, x, g.core)
        ats = [self.base["l2"] + (i - 1) * (g.L - 1) + j - 1 for j in range(1, g.L)]
        for s in self.each():
            if ats and waits:
                self.add(block, g.l, s, ats)
            self.push(self.out["xc"] + zk * (g.X - 1) + i - 1, block, g.l, s, self.base["xc"] + zk * (g.X - 1) + g.X - i - 1, x_dev)

    def side_l(self, zk, waits):
        g = self.g
        block = g.block(zk, g.x, g.core)
        for j in range(1, g.L):
            l, l_dev = g.l_other(j)
            ats = [self.base["x2"] + (i - 1) * (g.L - 1) + j - 1 for i in range(1, g.X)]
            for s in self.each():
                if waits:
                    self.add(block, l, s, ats)
                self.push(self.out["lc"] + zk * (g.L - 1) + j - 1, block, l, s, self.base["lc"] + zk * (g.L - 1) + g.L - j - 1, l_dev)

    def around(self, zk):
        g = self.g
        ats = [self.base["xc"] + zk * (g.X - 1) + i - 1 for i in range(1, g.X)]
        return ats + [self.base["lc"] + zk * (g.L - 1) + j - 1 for j in range(1, g.L)]

    def column(self, zk):
        g = self.g
        block = g.block(zk, g.x, g.core)
        behind = jnp.where(zk > g.z, g.down, g.up)
        near = jnp.abs(zk - g.z) == 1
        spot = jnp.where(near & (zk < g.z), 4, zk)
        for s in self.each():
            self.add(block, g.l, s, self.around(zk))
            self.add(block, g.l, s, [self.base["z"] + zk], behind)
            self.push(self.out["z"] + zk, block, g.l, s, self.base["z"] + spot, g.at_z(jnp.where(zk > g.z, g.z + 1, g.z - 1)))

    def last(self, out):
        g = self.g
        for s in self.each():
            start, size = self.cuts[s]
            out[start : start + size, :] = self.total(g.row, g.l, s, self.around(g.z))
            for at, there in ((self.base["z"] + g.z, g.down), (self.base["z"] + 4, g.up)):

                def take(at=at, s=s, start=start, size=size):
                    self.arrived(at, s)
                    out[start : start + size, :] += self.inbox[at, start : start + size].astype(F32)

                pl.when(there)(take)

    @staticmethod
    def plan(X, hop=2):
        orders, spots = [], []
        for z in range(4):
            corners = (3, 2, 1, 0) if z < 2 else (0, 1, 2, 3)
            own = tuple(reversed(NEAREST[z]))
            order = []
            for j in range(4):
                order += [(corners[j], off) for off in range(1, X)] + [(own[j], 0)]
            orders.append(order)
            spots.append(({zk: max(m for m, (a, off) in enumerate(order) if a == zk and off) for zk in range(4)},
                          {zk: order.index((zk, 0)) for zk in range(4)}))
        names = ("far", "sx", "sl", "near", "sx_late", "sl_late", "column")
        due = [{name: {} for name in names} for _ in range(4)]

        def put(z, name, zk, step):
            while step in due[z][name]:
                step += 1
            due[z][name][step] = zk
            return step

        sides = [{}, {}, {}, {}]
        for z in range(4):
            pair = z + 1 - 2 * (z % 2)
            for zk in sorted(range(4), key=lambda a: spots[z][0][a]):
                near = zk // 2 == z % 2
                corner, own = spots[z][0][zk] + 1, spots[z][1][zk] + 1
                ready = put(z, "near", zk, max(corner, spots[pair][0][zk] + 1 + hop)) if near else put(z, "far", zk, corner)
                sx = put(z, "sx_late", zk, ready + hop) if near and zk % 2 == 0 else put(z, "sx", zk, corner)
                sl = put(z, "sl_late", zk, max(ready + hop, own)) if near and zk % 2 else put(z, "sl", zk, own)
                sides[z][zk] = max(sx, sl)
        for zk in range(4):
            for chain in (range(0, zk), range(3, zk, -1)):
                before = 0
                for z in chain:
                    before = put(z, "column", zk, max(sides[z][zk], before) + hop)
        steps = 1 + max(step for z in range(4) for name in names for step in due[z][name])
        return orders, due, steps

    def prepare(self):
        self.orders, self.due, self.steps = self.plan(self.g.X)
        self.blocks = 4 * self.g.X

    def pick(self, tables, m):
        out = jnp.int32(-1)
        for z in range(4):
            for at, value in tables[z].items():
                out = jnp.where((self.g.z == z) & (m == at), value, out)
        return out

    def place(self, m):
        g = self.g
        code = self.pick([{at: zk * g.X + off for at, (zk, off) in enumerate(order)} for order in self.orders], m)
        return code // g.X, lax.rem(g.x + lax.rem(code, g.X), g.X)

    def step(self, m):
        g = self.g

        def first():
            self.to_mate(*self.place(m))

        def second():
            self.from_mate(*self.place(m - 1))

        pl.when(m < self.blocks)(first)
        pl.when((m >= 1) & (m <= self.blocks))(second)

        def send(name, act, over_x):
            zk = self.pick([due[name] for due in self.due], m)

            def go():
                if over_x:
                    for i in range(1, g.X):
                        act(zk, i)
                else:
                    act(zk)

            pl.when(zk >= 0)(go)

        send("column", self.column, False)
        send("sl_late", lambda zk: self.side_l(zk, True), False)
        send("sx_late", lambda zk, i: self.side_x(zk, i, True), True)
        if g.L > 1:
            send("near", self.corner_near, True)
            send("far", self.corner_far, True)
        send("sl", lambda zk: self.side_l(zk, False), False)
        send("sx", lambda zk, i: self.side_x(zk, i, False), True)

    def run(self, work=None, ahead=4):
        def one(m, carry):
            if work is not None:
                work(m)
            self.step(m)

            def wait():
                self.drain = True
                self.step(m - ahead)
                self.drain = False

            pl.when(m >= ahead)(wait)
            return carry

        lax.fori_loop(0, self.steps, one, 0)
        self.ahead = ahead

    def finish(self):
        self.drain = True

        def one(m, carry):
            self.step(m)
            return carry

        lax.fori_loop(self.steps - self.ahead, self.steps, one, 0)


def dot(left, right):
    return jnp.dot(left, right, preferred_element_type=F32)


def dot_nt(left, right):
    return lax.dot_general(left, right, (((1,), (1,)), ((), ())), preferred_element_type=F32)


def dot_tn(left, right):
    return lax.dot_general(left, right, (((0,), (0,)), ((), ())), preferred_element_type=F32)


def fold(values):
    rows, width = values.shape
    return jnp.sum(values.reshape(rows // 8, 8, width), axis=0)


def norm_parts(values):
    average = jnp.mean(values, axis=-1, keepdims=True)
    centered = values - average
    scale = lax.rsqrt(jnp.mean(centered * centered, axis=-1, keepdims=True) + NORM_EPS)
    return centered * scale, scale


def norm_back(normed, scale, d_normed):
    mean_d = jnp.mean(d_normed, axis=-1, keepdims=True)
    mean_dn = jnp.mean(d_normed * normed, axis=-1, keepdims=True)
    return scale * (d_normed - mean_d - normed * mean_dn)


def silu_back(pre, d_active):
    gate = lax.logistic(pre)
    return d_active * (gate * (1.0 + pre * (1.0 - gate)))


def order_kernel(row_total, node_count, senders, receivers, live, edges, cot, cols_out, rows_out, edges_out, cot_out, place, side, joined):
    tiles = senders.shape[0]
    count = tiles * 128
    group = count // row_total
    width = edges.shape[1]
    first = lax.axis_index("row") * node_count
    lane = lax.broadcasted_iota(jnp.int32, (128, 128), 1)
    sub = lax.broadcasted_iota(jnp.int32, (128, 128), 0)
    before = (sub < lane).astype(BF16)
    owner_ids = lax.broadcasted_iota(jnp.int32, (row_total, 128), 0)
    carry = owner_ids[:, :1].astype(F32) * group
    for tile in range(tiles):
        send = senders[tile : tile + 1, :]
        recv = receivers[tile : tile + 1, :] - first
        owner = lax.div(send, node_count)
        local = send - owner * node_count
        mine = owner_ids == owner
        ranks = dot(mine.astype(BF16), before) + carry
        spot = jnp.sum(jnp.where(mine, ranks, 0.0), axis=0, keepdims=True)
        carry = carry + jnp.sum(mine.astype(F32), axis=1, keepdims=True)
        place[tile : tile + 1, :] = spot.astype(jnp.int32)
        alive = (lane[:1] + tile * 128 < live[0, 0]).astype(jnp.int32)
        facts = jnp.where(sub == 0, lax.div(local, 16), 0)
        facts = jnp.where(sub == 1, lax.rem(local, 16), facts)
        facts = jnp.where(sub == 2, lax.div(recv, 16), facts)
        facts = jnp.where(sub == 3, lax.rem(recv, 16), facts)
        facts = jnp.where(sub == 4, alive, facts).astype(F32)
        side[:, pl.ds(tile * 128, 128)] = facts[:16].astype(BF16)
        joined[pl.ds(tile * 128, 128), pl.ds(2 * width, 128)] = facts.T.astype(BF16)
        joined[pl.ds(tile * 128, 128), pl.ds(0, width)] = edges[pl.ds(tile * 128, 128), :].astype(BF16)
        joined[pl.ds(tile * 128, 128), pl.ds(width, width)] = cot[pl.ds(tile * 128, 128), :].astype(BF16)

    def one(pair, carry):
        start = pl.multiple_of(pair * 2 * group, 2 * group)
        ids = lax.broadcasted_iota(jnp.int32, (2 * group, 128), 0) + start
        pick = jnp.concatenate([(ids == place[tile : tile + 1, :]).astype(BF16) for tile in range(tiles)], axis=1)
        moved = dot(pick, joined[...])
        edges_out[pl.ds(start, 2 * group), :] = moved[:, :width].astype(BF16)
        cot_out[pl.ds(start, 2 * group), :] = moved[:, width : 2 * width].astype(BF16)
        cols = moved[:, 2 * width :]
        lanes = lax.broadcasted_iota(jnp.int32, cols.shape, 1)
        sent = cols[:, 0:1] * 16.0 + cols[:, 1:2]
        got = cols[:, 2:3] * 16.0 + cols[:, 3:4]
        cols_out[pl.ds(start, 2 * group), :] = jnp.where(lanes == 0, sent, jnp.where(lanes == 1, got, jnp.where(lanes == 2, cols[:, 4:5], 0.0)))
        for half in range(2):
            rows = dot_nt(side[...], pick[half * group : (half + 1) * group])
            rows_out[pair * 2 + half] = jnp.concatenate(
                [rows[0:1] * 16.0 + rows[1:2], rows[2:3] * 16.0 + rows[3:4], rows[4:10]], axis=0
            )
        return carry

    lax.fori_loop(0, row_total // 2, one, 0)


def order_edges(node_count, senders, receivers, live, edges, cot):
    row_total = lax.axis_size("row")
    count, width = edges.shape
    tiles = count // 128
    vmem = pl.BlockSpec(memory_space=pltpu.VMEM)
    return pl.pallas_call(
        functools.partial(order_kernel, row_total, node_count),
        out_shape=(
            jax.ShapeDtypeStruct((count, 128), F32),
            jax.ShapeDtypeStruct((row_total, 8, count // row_total), F32),
            jax.ShapeDtypeStruct((count, width), BF16),
            jax.ShapeDtypeStruct((count, width), BF16),
            jax.ShapeDtypeStruct((tiles, 128), jnp.int32),
        ),
        in_specs=[vmem, vmem, pl.BlockSpec(memory_space=pltpu.SMEM), vmem, vmem],
        out_specs=(vmem,) * 5,
        scratch_shapes=[pltpu.VMEM((16, count), BF16), pltpu.VMEM((count, 2 * width + 128), BF16)],
        compiler_params=pltpu.CompilerParams(vmem_limit_bytes=VMEM_BYTES),
        name="order_edges",
    )(senders.reshape(tiles, 128), receivers.reshape(tiles, 128), live.reshape(1, 1), edges, cot)


def restore_kernel(place, update, d_edge, edges, cot, edge_out, cot_out):
    tiles = place.shape[0]
    count, width = update.shape
    parts = edges.shape[0] // 128
    lane = lax.broadcasted_iota(jnp.int32, (128, 128), 1).astype(F32)
    pick = []
    for part in range(parts):
        spot = jnp.broadcast_to(place[pl.ds(pl.program_id(0) * parts + part, 1), :], (128, 128)).astype(F32).T
        pick.append(jnp.concatenate([(spot == lane + float(128 * j)).astype(BF16) for j in range(tiles)], axis=1))
    pick = jnp.concatenate(pick, axis=0)
    edge_out[...] = edges[...] + dot(pick, update[...])
    cot_out[...] = cot[...] + dot(pick, d_edge[...])


def restore_edges(place, update, d_edge, edges, cot):
    count, width = edges.shape
    whole = lambda shape: pl.BlockSpec(shape, lambda i: (0, 0))
    size = 512 if count % 512 == 0 else 128
    part = pl.BlockSpec((size, width), lambda i: (i, 0))
    return pl.pallas_call(
        restore_kernel,
        grid=(count // size,),
        out_shape=(jax.ShapeDtypeStruct((count, width), F32),) * 2,
        in_specs=[whole(place.shape), whole(update.shape), whole(d_edge.shape), part, part],
        out_specs=(part, part),
        compiler_params=pltpu.CompilerParams(vmem_limit_bytes=VMEM_BYTES),
        name="restore_edges",
    )(place, update, d_edge, edges, cot)


def one_hot_cols(ids, count):
    lanes = lax.broadcasted_iota(jnp.int32, (ids.shape[0], count), 1).astype(F32)
    return (ids == lanes).astype(BF16)


def one_hot_rows(ids, count):
    subs = lax.broadcasted_iota(jnp.int32, (count, ids.shape[1]), 0).astype(F32)
    return (ids == subs).astype(BF16)


def load_all(pairs, sems):
    copies = [pltpu.make_async_copy(src, dst, sems.at[i]) for i, (src, dst) in enumerate(pairs)]
    for copy in copies:
        copy.start()
    return copies


def forward_kernel(
    layer, levels, rows, first_layer,
    node, edges, before, cols, rows_of, b1, b2, gain, shift, nb1, nb2, ngain, nshift, w1_all, w2_all, nw1_all, nw2_all,
    sent_out, pre_out, normed_out, update_out, edges_out, scale_out, block_out, node_out, recv_out, npre_out, nnormed_out, nscale_out, tally,
    table, total, cast, near, far, w1, w2, nw1, nw2, out_buf, scale_buf,
    load_sem, out_sem, send_sem, recv_sem, near_send, near_recv,
):
    g = Grid(levels, rows)
    h = node.shape[0]
    count, width = edges.shape
    group = count // rows
    node_count = h * levels
    loads = load_all(((w1_all.at[layer], w1), (w2_all.at[layer], w2), (nw1_all.at[layer], nw1), (nw2_all.at[layer], nw2)), load_sem)
    ag = Gather(g, table, h, send_sem, recv_sem)
    ag.slot(g.row, g.l)[...] = node[...].astype(BF16)
    tally[...] = jnp.zeros_like(tally)
    total[...] = jnp.zeros_like(total)
    g.greet()
    wide = lambda ref: ref[layer : layer + 1, :]
    outs = (sent_out, pre_out, normed_out, update_out) + ((edges_out,) if first_layer else ())

    def leave(n, place):
        slot = lax.rem(n, 2)
        copies = [pltpu.make_async_copy(out_buf.at[slot, i], ref.at[place], out_sem.at[slot, i]) for i, ref in enumerate(outs)]
        return copies + [pltpu.make_async_copy(scale_buf.at[slot], scale_out.at[place], out_sem.at[slot, 5])]

    def work(z, x, n):
        def own():
            for copy in loads:
                copy.wait()
            here = table[pl.ds(pl.multiple_of(g.row * node_count, 16), node_count), :]
            cast[...] = dot(here, w1[2 * width :, :]).astype(BF16)
            block_out[...] = here

        pl.when(n == 0)(own)
        pair = g.block(z, x, 0)
        place = pl.ds(pl.multiple_of(pair * group, 2 * group), 2 * group)

        def free():
            for copy in leave(n, place):
                copy.wait()

        pl.when(n >= 2)(free)
        slot = lax.rem(n, 2)
        cols_here = cols[place, :]
        send_pick = one_hot_cols(cols_here[:, 0:1], node_count)
        recv_pick = one_hot_cols(cols_here[:, 1:2], node_count)
        start = pl.multiple_of(pair * node_count, 16)
        sent = jnp.concatenate(
            [
                dot(send_pick[:group], table[pl.ds(start, node_count), :]).astype(BF16),
                dot(send_pick[group:], table[pl.ds(start + node_count, node_count), :]).astype(BF16),
            ],
            axis=0,
        )
        out_buf[slot, 0] = sent
        pre = dot(edges[place, :], w1[:width, :]) + dot(sent, w1[width : 2 * width, :]) + dot(recv_pick, cast[...]) + wide(b1)
        out_buf[slot, 1] = pre.astype(BF16)
        active = (pre * lax.logistic(pre)).astype(BF16)
        normed, scale = norm_parts(dot(active, w2[...]) + wide(b2))
        out_buf[slot, 2] = normed.astype(BF16)
        scale_buf[slot] = jnp.broadcast_to(scale, (2 * group, 128))
        update = (normed * wide(gain) + wide(shift)) * cols_here[:, 2:3]
        update_low = update.astype(BF16)
        edge = edges[place, :].astype(F32) + update
        if first_layer:
            out_buf[slot, 3] = update_low
            out_buf[slot, 4] = edge.astype(BF16)
        else:
            out_buf[slot, 3] = (before[place, :].astype(F32) + update).astype(BF16)
        tally[8:16, :] += fold(edge * edge)
        tally[16:24, :] += fold(update * update)
        for half in range(2):
            pick = one_hot_rows(rows_of[pair + half][1:2, :], node_count)
            total[...] += dot(pick, update_low[half * group : (half + 1) * group])
        for copy in leave(n, place):
            copy.start()

    ag.run(work)
    copies = []
    for j in range(1, levels):
        l, l_dev = g.l_other(j)
        near[j - 1] = total[pl.ds(pl.multiple_of(l * h, h), h), :].astype(BF16)
        copy = pltpu.make_async_remote_copy(
            near.at[j - 1], far.at[levels - 1 - j], near_send.at[j - 1], near_recv.at[levels - 1 - j], device_id=l_dev, device_id_type=MESH
        )
        copy.start()
        copies.append(copy)
    received = total[pl.ds(pl.multiple_of(g.l * h, h), h), :]
    npre = dot(node[...].astype(BF16), nw1[:width, :]) + wide(nb1)
    for copy in copies:
        copy.wait()
    for j in range(1, levels):
        received = received + far[j - 1].astype(F32)
    received = received.astype(BF16)
    recv_out[...] = received
    npre = npre + dot(received, nw1[width:, :])
    npre_out[...] = npre
    nnormed, nscale = norm_parts(dot((npre * lax.logistic(npre)).astype(BF16), nw2[...]) + wide(nb2))
    nnormed_out[...] = nnormed
    nscale_out[...] = jnp.broadcast_to(nscale, (h, 128))
    change = nnormed * wide(ngain) + wide(nshift)
    new = node[...] + change
    node_out[...] = new
    tally[0:8, :] = fold(new * new)
    tally[24:32, :] = fold(change * change)
    for n in range(2):
        for copy in leave(n, pl.ds(0, 2 * group)):
            copy.wait()
    ag.finish()


def forward_layer(layer, node, edges, before, cols, rows_of, small, weights):
    levels, rows = lax.axis_size("lvl"), lax.axis_size("row")
    h, width = node.shape
    count = edges.shape[0]
    group = count // rows
    vmem = pl.BlockSpec(memory_space=pltpu.VMEM)
    hbm = pl.BlockSpec(memory_space=pl.ANY)
    first_layer = layer == 0
    shape = jax.ShapeDtypeStruct
    outs = (
        shape((count, width), BF16),
        shape((count, width), BF16),
        shape((count, width), BF16),
        shape((count, width), BF16),
        shape((count, width) if first_layer else (16, 128), BF16),
        shape((count, 128), F32),
        shape((h * levels, width), BF16),
        shape((h, width), F32),
        shape((h, width), BF16),
        shape((h, width), F32),
        shape((h, width), F32),
        shape((h, 128), F32),
        shape((32, width), F32),
    )
    ins = (node, edges, before, cols, rows_of) + small + weights
    others = max(levels - 1, 1)
    return pl.pallas_call(
        functools.partial(forward_kernel, layer, levels, rows, first_layer),
        out_shape=outs,
        in_specs=[vmem] * (len(ins) - 4) + [hbm] * 4,
        out_specs=(hbm,) * 6 + (vmem,) * (len(outs) - 6),
        scratch_shapes=[
            pltpu.VMEM((rows * h * levels, width), BF16),
            pltpu.VMEM((h * levels, width), F32),
            pltpu.VMEM((h * levels, width), BF16),
            pltpu.VMEM((others, h, width), BF16),
            pltpu.VMEM((others, h, width), BF16),
        ]
        + [pltpu.VMEM(weight.shape[1:], BF16) for weight in weights]
        + [
            pltpu.VMEM((2, 5, 2 * group, width), BF16),
            pltpu.VMEM((2, 2 * group, 128), F32),
            pltpu.SemaphoreType.DMA((4,)),
            pltpu.SemaphoreType.DMA((2, 6)),
            pltpu.SemaphoreType.DMA((Gather.sends(levels, rows),)),
            pltpu.SemaphoreType.DMA((2 * rows * levels,)),
            pltpu.SemaphoreType.DMA((others,)),
            pltpu.SemaphoreType.DMA((others,)),
        ],
        compiler_params=pltpu.CompilerParams(collective_id=1 + layer, has_side_effects=True, vmem_limit_bytes=VMEM_BYTES),
        name=f"forward_{layer}",
    )(*ins)


def backward_kernel(
    layer, levels, rows, last_layer,
    d_node, block, recv, npre, nnormed, nscale, cols, rows_of, scale, gain, ngain, d_before, d_edges, pre, normed, edges, sent, w1_all, w2_all, nw1_all, nw2_all,
    d_node_out, d_edges_out, d_change_out, grads, tally,
    stage, inbox, bufs, d_recv, turned, own_sum, out_buf, w1, w2, nw1, nw2,
    load_sem, out_sem, send_sem, recv_sem, near_send, near_recv,
):
    g = Grid(levels, rows)
    h, width = d_node.shape
    count = pre.shape[0]
    group = count // rows
    node_count = h * levels
    loads = load_all(
        ((nw2_all.at[layer], nw2), (nw1_all.at[layer], nw1), (w1_all.at[layer], w1), (w2_all.at[layer], w2))
        + tuple((src, bufs.at[i]) for i, src in enumerate((d_edges, pre, normed, edges, sent))),
        load_sem,
    )
    rs = Scatter(g, stage, inbox, h, send_sem, recv_sem)
    wide = lambda ref: ref[layer : layer + 1, :]
    mine = pl.ds(pl.multiple_of(g.l * h, h), h)
    own_sum[...] = jnp.zeros_like(own_sum)
    tally[...] = jnp.zeros_like(tally)
    for copy in loads[:2]:
        copy.wait()
    tally[48:56, :] = fold(d_node[...] * nnormed[...])
    tally[56:64, :] = fold(d_node[...])
    d_two = norm_back(nnormed[...], nscale[:, 0:1], d_node[...] * wide(ngain)).astype(BF16)
    tally[40:48, :] = fold(d_two.astype(F32))
    d_one = silu_back(npre[...], dot_nt(d_two, nw2[...])).astype(BF16)
    tally[32:40, :] = fold(d_one.astype(F32))
    d_recv[mine, :] = dot_nt(d_one, nw1[width:, :]).astype(BF16)
    g.greet()
    copies = []
    for j in range(1, levels):
        copy = pltpu.make_async_remote_copy(
            d_recv.at[mine], d_recv.at[mine], near_send.at[j - 1], near_recv.at[levels - 1 - j], device_id=g.l_other(j)[1], device_id_type=MESH
        )
        copy.start()
        copies.append(copy)
    d_node_out[...] = d_node[...] + dot_nt(d_one, nw1[:width, :])
    active = (npre[...] * lax.logistic(npre[...])).astype(BF16)
    grads[4 * width + width : 6 * width, :] = dot_tn(recv[...], d_one).astype(BF16)
    grads[4 * width : 5 * width, :] = dot_tn(block[mine, :], d_one).astype(BF16)
    grads[6 * width : 7 * width, :] = dot_tn(active, d_two).astype(BF16)
    for copy in copies:
        copy.wait()
    for copy in loads[2:]:
        copy.wait()

    def work(i):
        z, x = rs.place(i)
        pair = g.block(z, x, 0)
        start = pl.multiple_of(pair * group, 2 * group)
        place = pl.ds(start, 2 * group)
        if not last_layer:
            earlier = pltpu.make_async_copy(d_before.at[place], out_buf.at[lax.rem(i, 2), 0], out_sem.at[lax.rem(i, 2), 0])
            earlier.start()
        cols_here = cols[place, :]
        recv_pick = one_hot_cols(cols_here[:, 1:2], node_count)
        d_edge = bufs[0, place, :].astype(F32)
        d_update = (d_edge + dot(recv_pick, d_recv[...])) * cols_here[:, 2:3]
        norm_here = bufs[2, place, :].astype(F32)
        tally[16:24, :] += fold(d_update * norm_here)
        tally[24:32, :] += fold(d_update)
        d_two = norm_back(norm_here, scale[place, 0:1], d_update * wide(gain)).astype(BF16)
        tally[8:16, :] += fold(d_two.astype(F32))
        pre_here = bufs[1, place, :].astype(F32)
        gate = lax.logistic(pre_here)
        d_one = (dot_nt(d_two, w2[...]) * (gate * (1.0 + pre_here * (1.0 - gate)))).astype(BF16)
        tally[0:8, :] += fold(d_one.astype(F32))
        bufs[0, place, :] = d_one
        bufs[1, place, :] = (pre_here * gate).astype(BF16)
        bufs[2, place, :] = d_two
        d_here = dot_nt(d_one, w1[:width, :])
        slot = lax.rem(i, 2)
        used = [
            pltpu.make_async_copy(out_buf.at[slot, n], ref.at[place], out_sem.at[slot, n])
            for n, ref in enumerate((d_edges_out, d_change_out))
            if n or last_layer
        ]

        def free():
            for copy in used:
                copy.wait()

        pl.when(i >= 2)(free)
        if last_layer:
            out_buf[slot, 0] = (d_edge + d_here).astype(BF16)
            out_buf[slot, 1] = d_here.astype(BF16)
        else:
            earlier.wait()
            out_buf[slot, 1] = (out_buf[slot, 0].astype(F32) + d_here).astype(BF16)
        for copy in used:
            copy.start()
        d_sent = dot_nt(d_one, w1[width : 2 * width, :]).astype(BF16)
        for half in range(2):
            ids = rows_of[pair + half]
            part = slice(half * group, (half + 1) * group)
            own_sum[...] += dot(one_hot_rows(ids[1:2, :], node_count), d_one[part])
            spot = pl.ds(pl.multiple_of((pair + half) * node_count, 16), node_count)
            stage[spot, :] = dot(one_hot_rows(ids[0:1, :], node_count), d_sent[part]).astype(BF16)

        def close():
            low = own_sum[...].astype(BF16)
            spot = pl.ds(pl.multiple_of(g.row * node_count, 16), node_count)
            stage[spot, :] = (stage[spot, :].astype(F32) + dot_nt(low, w1[2 * width :, :])).astype(BF16)
            grads[2 * width : 3 * width, :] = dot_tn(block[...], low).astype(BF16)

        pl.when(i == rs.blocks - 1)(close)

    def step(m):
        pl.when(m < rs.blocks)(lambda: work(m))
        for n, (at, left, right) in enumerate(((0, 3, 0), (1, 4, 0), (3, 1, 2))):

            def grad(at=at, left=left, right=right):
                grads[at * width : (at + 1) * width, :] = dot_tn(bufs[left], bufs[right]).astype(BF16)

            pl.when(m == rs.blocks + n)(grad)

    rs.run(step)
    rs.last(turned)
    d_node_out[...] += turned[...]
    for slot in range(2):
        for n, ref in enumerate((d_edges_out, d_change_out)):
            if n or last_layer:
                pltpu.make_async_copy(out_buf.at[slot, n], ref.at[pl.ds(0, 2 * group)], out_sem.at[slot, n]).wait()
    rs.finish()


def backward_layer(layer, last_layer, d_node, node_saved, cols, rows_of, scale, small, weights, d_edges, edge_saved, d_before):
    levels, rows = lax.axis_size("lvl"), lax.axis_size("row")
    h, width = d_node.shape
    count = d_edges.shape[0]
    group = count // rows
    vmem = pl.BlockSpec(memory_space=pltpu.VMEM)
    hbm = pl.BlockSpec(memory_space=pl.ANY)
    shape = jax.ShapeDtypeStruct
    ins = (d_node,) + node_saved + (cols, rows_of, scale) + small + (d_before, d_edges) + edge_saved + weights
    outs = (
        shape((h, width), F32),
        shape((count, width) if last_layer else (16, 128), BF16),
        shape((count, width), BF16),
        shape((7 * width, width), BF16),
        shape((64, width), F32),
    )
    others = max(levels - 1, 1)
    return pl.pallas_call(
        functools.partial(backward_kernel, layer, levels, rows, last_layer),
        out_shape=outs,
        in_specs=[vmem] * (len(ins) - 10) + [hbm] * 10,
        out_specs=(vmem, hbm, hbm, vmem, vmem),
        scratch_shapes=[
            pltpu.VMEM((rows * h * levels, width), BF16),
            pltpu.VMEM((Scatter.receives(levels, rows), h, width), BF16),
            pltpu.VMEM((5, count, width), BF16),
            pltpu.VMEM((h * levels, width), BF16),
            pltpu.VMEM((h, width), F32),
            pltpu.VMEM((h * levels, width), F32),
            pltpu.VMEM((2, 2, 2 * group, width), BF16),
        ]
        + [pltpu.VMEM(weight.shape[1:], BF16) for weight in weights]
        + [
            pltpu.SemaphoreType.DMA((9,)),
            pltpu.SemaphoreType.DMA((2, 2)),
            pltpu.SemaphoreType.DMA((Scatter.sends(levels, rows),)),
            pltpu.SemaphoreType.DMA((2 * Scatter.receives(levels, rows),)),
            pltpu.SemaphoreType.DMA((others,)),
            pltpu.SemaphoreType.DMA((others,)),
        ],
        compiler_params=pltpu.CompilerParams(collective_id=3 + layer, has_side_effects=True, vmem_limit_bytes=VMEM_BYTES),
        name=f"backward_{layer}",
    )(*ins)


def sum_kernel(levels, rows, h, *refs):
    count = len(refs) - 9
    terms = refs[:count]
    out, stage, inbox, total, scatter_send, scatter_recv, gather_send, gather_recv, load_sem = refs[count:]
    g = Grid(levels, rows)
    pairs = []
    at = 0
    for term in terms:
        pairs.append((term, stage.at[pl.ds(at, term.shape[0])]))
        at += term.shape[0]
    loads = load_all(pairs, load_sem)
    g.greet()
    for copy in loads:
        copy.wait()
    rs = Scatter(g, stage, inbox, h, scatter_send, scatter_recv)
    rs.run(ahead=2)
    rs.last(total)
    ag = Gather(g, out, h, gather_send, gather_recv)
    ag.slot(g.row, g.l)[...] = total[...].astype(BF16)
    ag.run()
    rs.finish()
    ag.finish()


def sum_pieces(terms, call):
    levels, rows = lax.axis_size("lvl"), lax.axis_size("row")
    width = terms[0].shape[1]
    count = sum(term.shape[0] for term in terms)
    h = count // (levels * rows)
    return pl.pallas_call(
        functools.partial(sum_kernel, levels, rows, h),
        out_shape=jax.ShapeDtypeStruct((count, width), BF16),
        in_specs=[pl.BlockSpec(memory_space=pl.ANY)] * len(terms),
        out_specs=pl.BlockSpec(memory_space=pltpu.VMEM),
        scratch_shapes=[
            pltpu.VMEM((count, width), BF16),
            pltpu.VMEM((Scatter.receives(levels, rows), h, width), BF16),
            pltpu.VMEM((h, width), F32),
            pltpu.SemaphoreType.DMA((Scatter.sends(levels, rows),)),
            pltpu.SemaphoreType.DMA((2 * Scatter.receives(levels, rows),)),
            pltpu.SemaphoreType.DMA((Gather.sends(levels, rows),)),
            pltpu.SemaphoreType.DMA((2 * rows * levels,)),
            pltpu.SemaphoreType.DMA((len(terms),)),
        ],
        compiler_params=pltpu.CompilerParams(collective_id=call, has_side_effects=True, vmem_limit_bytes=VMEM_BYTES),
        name=f"sum_{call}",
    )(*terms)


def widen_kernel(parts, sums, *outs):
    i = pl.program_id(0)
    part = lax.rem(i, sum(parts))
    first = 0
    for count, out in zip(parts, outs):

        def write(out=out):
            out[0] = sums[...].astype(F32)

        pl.when((part >= first) & (part < first + count))(write)
        first += count


def widen(sums, layers, parts):
    width = sums.shape[1]
    each = sum(parts)
    specs = []
    first = 0
    for count in parts:

        def index(i, first=first, count=count):
            return i // each, jnp.clip(lax.rem(i, each) - first, 0, count - 1), 0

        specs.append(pl.BlockSpec((1, width, width), index))
        first += count
    return pl.pallas_call(
        functools.partial(widen_kernel, parts),
        grid=(layers * each,),
        out_shape=tuple(jax.ShapeDtypeStruct((layers, count * width, width), F32) for count in parts),
        in_specs=[pl.BlockSpec((width, width), lambda i: (i, 0))],
        out_specs=tuple(specs),
        name="widen",
    )(sums)


def on_device(
    node_latent, edge_latent, senders, receivers, live_edges,
    edge_w1, edge_b1, edge_w2, edge_b2, edge_gain, edge_shift, node_w1, node_b1, node_w2, node_b2, node_gain, node_shift,
    node_cotangent, edge_cotangent,
):
    node_count, width = node_latent.shape
    edge_count = edge_latent.shape[0]
    layers = edge_w1.shape[0]
    row_total, level_total = lax.axis_size("row"), lax.axis_size("lvl")
    half = node_count // level_total
    mine = lambda array: lax.dynamic_slice_in_dim(array, lax.axis_index("lvl") * half, half)
    cols, rows_of, edges, d_edges, place = order_edges(node_count, senders, receivers, live_edges, edge_latent, edge_cotangent)
    node = mine(node_latent)
    update = jnp.zeros((16, 128), BF16)
    saved = []
    tallies = []
    weights = (edge_w1, edge_w2, node_w1, node_w2)
    for layer in range(layers):
        small = (edge_b1, edge_b2, edge_gain, edge_shift, node_b1, node_b2, node_gain, node_shift)
        sent, pre, normed, update, new_edges, scale, block, node, recv, npre, nnormed, nscale, tally = forward_layer(
            layer, node, edges, update, cols, rows_of, small, weights
        )
        saved.append(((block, recv, npre, nnormed, nscale), scale, (pre, normed, edges, sent)))
        tallies.append(tally)
        edges = new_edges
    d_node = mine(node_cotangent)
    d_change = jnp.zeros((16, 128), BF16)
    grads = [None] * layers
    sums = [None] * layers
    for layer in reversed(range(layers)):
        node_saved, scale, edge_saved = saved[layer]
        d_node, d_edges, d_change, grads[layer], sums[layer] = backward_layer(
            layer, layer == layers - 1, d_node, node_saved, cols, rows_of, scale, (edge_gain, node_gain), weights, d_edges, edge_saved, d_change
        )
    small = jnp.concatenate([jnp.sum(part.reshape(8, 8, width), axis=1) for part in sums])
    squares = jnp.stack([jnp.sum(tally.reshape(4, 8 * width), axis=1) for tally in tallies])
    squares = jnp.pad(squares.reshape(1, -1), ((0, 0), (0, width - squares.size)))
    devices = row_total * level_total
    used = layers * 7 * width + small.shape[0] + 1
    share = -(-used // (16 * devices)) * 16
    rest = [small.astype(BF16), squares.astype(BF16), jnp.zeros((share * devices - used, width), BF16)]
    flat = sum_pieces(grads + [jnp.concatenate(rest)], 5)
    big = widen(flat, layers, (3, 1, 2, 1))
    after = layers * 7 * width
    smalls = flat[after : after + 8 * layers].astype(F32).reshape(layers, 8, width)
    squares = flat[after + 8 * layers, : 4 * layers].astype(F32).reshape(layers, 4)
    edge_out, edge_grad = restore_edges(place, update, d_change, edge_latent, edge_cotangent)
    node_entries = float(node_count * row_total * width)
    edge_entries = float(edge_count * row_total * level_total * width)
    entries = jnp.array([node_entries, edge_entries, edge_entries, node_entries], F32)
    both = lax.all_gather(jnp.stack([node, d_node]), "lvl", axis=1, tiled=True)
    return (
        both[0],
        edge_out,
        both[1],
        edge_grad,
        big[0],
        smalls[:, 0],
        big[1],
        smalls[:, 1],
        smalls[:, 2],
        smalls[:, 3],
        big[2],
        smalls[:, 4],
        big[3],
        smalls[:, 5],
        smalls[:, 6],
        smalls[:, 7],
        jnp.sqrt(squares / entries[None, :]),
    )


def solution(mesh):
    rows, both, whole = P("row", None), P(("lvl", "row"), None), P()
    edge = P(("lvl", "row"))
    placed = (rows, both, edge, edge, edge) + (whole,) * 12 + (rows, both)
    outs = (rows, both, rows, both) + (whole,) * 13
    return jax.shard_map(on_device, mesh=mesh, in_specs=placed, out_specs=outs, check_vma=False)
```

```python
import functools

import jax
import jax.numpy as jnp
from jax import lax
from jax.experimental import pallas as pl
from jax.experimental.pallas import tpu as pltpu
from jax.sharding import PartitionSpec as P

MESH = pl.DeviceIdType.MESH
NORM_EPS = 1e-05
F32 = jnp.float32
BF16 = jnp.bfloat16
VMEM_BYTES = 61 * 2**20


NEAREST = ((0, 1, 2, 3), (1, 0, 2, 3), (2, 3, 1, 0), (3, 2, 1, 0))


class Grid:
    def __init__(self, levels, rows):
        self.L, self.R = levels, rows
        self.Z = 4
        self.X = rows // (2 * self.Z)
        self.l = lax.axis_index("lvl")
        row = lax.axis_index("row")
        self.row = row
        self.core = lax.rem(row, 2)
        self.x = lax.rem(row // 2, self.X)
        self.z = row // (2 * self.X)
        self.up = self.z < self.Z - 1
        self.down = self.z > 0

    def block(self, z, x, core):
        return (z * self.X + x) * 2 + core

    def mate(self):
        return (self.l, self.block(self.z, self.x, 1 - self.core))

    def at_z(self, z):
        return (self.l, self.block(jnp.clip(z, 0, self.Z - 1), self.x, self.core))

    def x_other(self, i):
        x = lax.rem(self.x + i, self.X)
        return x, (self.l, self.block(self.z, x, self.core))

    def l_other(self, i):
        l = lax.rem(self.l + i, self.L)
        return l, (l, self.row)

    def nth(self, k, z=None):
        z_here = self.z if z is None else z
        order = NEAREST
        out = jnp.int32(0)
        for z in range(4):
            for j in range(4):
                if order[z][j]:
                    out = jnp.where((z_here == z) & (k == j), order[z][j], out)
        return out

    def local(self, zk, z=None):
        return (zk // 2) == lax.rem(self.z if z is None else z, 2)

    def corner_z(self, q):
        side = lax.rem(lax.rem(self.z, 2) + q // 2, 2)
        return side * 2 + lax.rem(q, 2)

    def pair_z(self):
        return self.z + 1 - 2 * lax.rem(self.z, 2)

    def greet(self):
        barrier = pltpu.get_barrier_semaphore()

        def hello(who):
            pl.semaphore_signal(barrier, inc=1, device_id=who, device_id_type=MESH)

        hello(self.mate())
        for i in range(1, self.X):
            hello(self.x_other(i)[1])
        for i in range(1, self.L):
            hello(self.l_other(i)[1])
        pl.when(self.up)(lambda: hello(self.at_z(self.z + 1)))
        pl.when(self.down)(lambda: hello(self.at_z(self.z - 1)))
        pl.semaphore_wait(barrier, self.X + self.L - 1 + self.up.astype(jnp.int32) + self.down.astype(jnp.int32))


def only(when, act):
    if when is None:
        act()
    else:
        pl.when(when)(act)


def cuts(h):
    first = -(-h // 32) * 16
    return ((0, first), (first, h - first)) if h > first else ((0, h),)


class Gather:
    def __init__(self, grid, table, h, send_sem, recv_sem):
        self.g, self.table, self.h = grid, table, h
        self.cuts = cuts(h)
        self.send_sem, self.recv_sem = send_sem, recv_sem
        X, L = grid.X, grid.L
        self.per_column = X + L + 1
        self.per_sides = 2 * (X - 1) * (L - 1) + X - 1 + L - 1
        self.at_sides = 4 * self.per_column
        self.at_corners = self.at_sides + 4 * self.per_sides
        self.drain = False

    @staticmethod
    def sends(levels, rows):
        X, L = rows // 8, levels
        return 2 * (4 * (X + L + 1) + 4 * (2 * (X - 1) * (L - 1) + X + L - 2) + 8 * (X - 1) * (L - 1))

    def slot(self, block, l, s=None):
        start, size = (0, self.h) if s is None else self.cuts[s]
        return self.table.at[pl.ds(pl.multiple_of((block * self.g.L + l) * self.h + start, 16), size)]

    def push(self, at, block, l, s, who, when=None):
        place = self.slot(block, l, s)
        copy = pltpu.make_async_remote_copy(
            place, place, self.send_sem.at[2 * at + s], self.recv_sem.at[(block * self.g.L + l) * 2 + s], device_id=who, device_id_type=MESH
        )
        only(when, copy.wait_send if self.drain else copy.start)

    def arrived(self, block, l, s):
        if self.drain:
            return
        place = self.slot(block, l, s)
        pltpu.make_async_remote_copy(
            place, place, self.send_sem.at[0], self.recv_sem.at[(block * self.g.L + l) * 2 + s], device_id=self.g.mate(), device_id_type=MESH
        ).wait_recv()

    def column(self, k, s, own=False):
        g = self.g
        zk = g.nth(k)
        block = g.block(zk, g.x, g.core)
        at = k * self.per_column
        if not own:
            self.arrived(block, g.l, s)
        self.push(at, block, g.l, s, g.at_z(g.z + 1), g.up & (zk <= g.z))
        self.push(at + 1, block, g.l, s, g.at_z(g.z - 1), g.down & (zk >= g.z))
        for i in range(1, g.X):
            self.push(at + 1 + i, block, g.l, s, g.x_other(i)[1])
        for j in range(1, g.L):
            self.push(at + g.X + j, block, g.l, s, g.l_other(j)[1])
        self.push(at + g.X + g.L, block, g.l, s, g.mate())

    def sides(self, k, s):
        g = self.g
        zk = g.nth(k)
        even = lax.rem(zk, 2) == 0
        at = self.at_sides + k * self.per_sides
        for i in range(1, g.X):
            block = g.block(zk, g.x_other(i)[0], g.core)
            self.arrived(block, g.l, s)
            for j in range(1, g.L):
                self.push(at, block, g.l, s, g.l_other(j)[1], g.local(zk) & even)
                at = at + 1
            self.push(at, block, g.l, s, g.mate())
            at = at + 1
        for j in range(1, g.L):
            block = g.block(zk, g.x, g.core)
            l = g.l_other(j)[0]
            self.arrived(block, l, s)
            for i in range(1, g.X):
                self.push(at, block, l, s, g.x_other(i)[1], g.local(zk) & jnp.logical_not(even))
                at = at + 1
            self.push(at, block, l, s, g.mate())
            at = at + 1

    def corners(self, z, s, local):
        g = self.g
        q = lax.rem(z, 2) + (0 if local else 2)
        for i in range(1, g.X):
            block = g.block(z, lax.rem(g.x + i, g.X), g.core)
            for j in range(1, g.L):
                l = g.l_other(j)[0]
                at = self.at_corners + ((q * (g.X - 1) + i - 1) * (g.L - 1) + j - 1) * 2
                self.arrived(block, l, s)
                if local:
                    self.push(at, block, l, s, g.at_z(g.pair_z()))
                self.push(at + 1, block, l, s, g.mate())

    def mates(self, z, x):
        for l in range(self.g.L):
            for s in range(len(self.cuts)):
                self.arrived(self.g.block(z, x, 1 - self.g.core), l, s)

    def begin(self):
        for s in range(len(self.cuts)):
            self.column(0, s, own=True)

    def wave(self, k, s):
        g = self.g
        pl.when(k < 3)(lambda: self.column(k + 1, s))
        pl.when(k < 4)(lambda: self.sides(k, s))
        if g.L == 1:
            return
        two = len(self.cuts) == 2
        late = 1 - s if two else s
        back = 2 - s if two else 1
        for local, lag in ((True, back), (False, back + 1)):
            who = None if local else g.pair_z()
            kk = k - lag
            z = g.nth(jnp.clip(kk, 0, 3), who)
            pl.when((kk >= 0) & (kk < 4) & g.local(z, who))(lambda z=z, local=local: self.corners(z, late, local))

    def due(self, k, c):
        g = self.g
        own = c == 0
        far = c > g.X - 1
        off = jnp.where(own, 0, lax.rem(c - 1, max(g.X - 1, 1)) + 1)
        kk = jnp.where(own, k - 1, jnp.where(far, k - 3, k - 2))
        who = jnp.where(far, g.pair_z(), g.z)
        z = g.nth(jnp.clip(kk, 0, 3), who)
        there = (kk >= 0) & (kk < 4) & (own | g.local(z, who))
        return z, lax.rem(g.x + off, g.X), there

    def run(self, work=None, meanwhile=None):
        g = self.g
        parts = 2 * g.X - 1
        self.begin()
        if meanwhile is not None:
            meanwhile()

        def one(i, done):
            k, c = i // parts, lax.rem(i, parts)
            for s in range(len(self.cuts)):
                pl.when(c == s)(lambda s=s: self.wave(k, s))
            z, x, there = self.due(k, c)

            def ready():
                self.mates(z, x)
                if work is not None:
                    work(z, x, done)

            pl.when(there)(ready)
            return done + there.astype(jnp.int32)

        lax.fori_loop(0, 7 * parts, one, jnp.int32(0))

    def finish(self):
        self.drain = True
        self.begin()

        def one(k, carry):
            for s in range(len(self.cuts)):
                self.wave(k, s)
            return carry

        lax.fori_loop(0, 7, one, 0)


class Scatter:
    def __init__(self, grid, stage, inbox, h, send_sem, recv_sem):
        self.g, self.stage, self.inbox, self.h = grid, stage, inbox, h
        self.cuts = cuts(h)
        self.send_sem, self.recv_sem = send_sem, recv_sem
        X, L = grid.X, grid.L
        at = 0
        self.base = {}
        for name, count in self.parts(X, L):
            self.base[name] = at
            at += count
        at = 0
        self.out = {}
        for name, count in self.out_parts(X, L):
            self.out[name] = at
            at += count
        self.drain = False
        self.prepare()

    @staticmethod
    def parts(X, L):
        side = (X - 1) * (L - 1)
        return (("mate", 4 * X * L), ("pair", 2 * side), ("l2", side), ("x2", side), ("xc", 4 * (X - 1)), ("lc", 4 * (L - 1)), ("z", 5))

    @staticmethod
    def out_parts(X, L):
        side = (X - 1) * (L - 1)
        return (("mate", 4 * X * L), ("corner", 8 * side), ("xc", 4 * (X - 1)), ("lc", 4 * (L - 1)), ("z", 4))

    @staticmethod
    def receives(levels, rows):
        return sum(count for _, count in Scatter.parts(rows // 8, levels))

    @staticmethod
    def sends(levels, rows):
        return 2 * sum(count for _, count in Scatter.out_parts(rows // 8, levels))

    def slot(self, block, l, s=None):
        start, size = (0, self.h) if s is None else self.cuts[s]
        return self.stage.at[pl.ds(pl.multiple_of((block * self.g.L + l) * self.h + start, 16), size)]

    def push(self, out, block, l, s, at, who, when=None):
        start, size = self.cuts[s]
        copy = pltpu.make_async_remote_copy(
            self.slot(block, l, s),
            self.inbox.at[at, pl.ds(start, size)],
            self.send_sem.at[2 * out + s],
            self.recv_sem.at[2 * at + s],
            device_id=who,
            device_id_type=MESH,
        )
        only(when, copy.wait_send if self.drain else copy.start)

    def arrived(self, at, s):
        start, size = self.cuts[s]
        place = self.inbox.at[at, pl.ds(start, size)]
        pltpu.make_async_remote_copy(
            place, place, self.send_sem.at[0], self.recv_sem.at[2 * at + s], device_id=self.g.mate(), device_id_type=MESH
        ).wait_recv()

    def total(self, block, l, s, ats):
        start, size = self.cuts[s]
        for at in ats:
            self.arrived(at, s)
        out = self.slot(block, l, s)[...].astype(F32)
        for at in ats:
            out = out + self.inbox[at, start : start + size].astype(F32)
        return out

    def add(self, block, l, s, ats, when=None):
        if self.drain:
            return

        def act():
            self.slot(block, l, s)[...] = self.total(block, l, s, ats).astype(BF16)

        only(when, act)

    def each(self):
        return range(len(self.cuts))

    def to_mate(self, z, x):
        g = self.g
        for l in range(g.L):
            at = (z * g.X + x) * g.L + l
            for s in self.each():
                self.push(self.out["mate"] + at, g.block(z, x, 1 - g.core), l, s, self.base["mate"] + at, g.mate())

    def from_mate(self, z, x):
        g = self.g
        for l in range(g.L):
            for s in self.each():
                self.add(g.block(z, x, g.core), l, s, [self.base["mate"] + (z * g.X + x) * g.L + l])

    def corner_far(self, z, i):
        g = self.g
        block = g.block(z, lax.rem(g.x + i, g.X), g.core)
        for j in range(1, g.L):
            l = g.l_other(j)[0]
            spot = (lax.rem(z, 2) * (g.X - 1) + i - 1) * (g.L - 1) + j - 1
            for s in self.each():
                self.push(self.out["corner"] + spot, block, l, s, self.base["pair"] + spot, g.at_z(g.pair_z()))

    def corner_near(self, z, i):
        g = self.g
        x, x_dev = g.x_other(i)
        block = g.block(z, x, g.core)
        even = lax.rem(z, 2) == 0
        side = (g.X - 1) * (g.L - 1)
        for j in range(1, g.L):
            l, l_dev = g.l_other(j)
            spot = (lax.rem(z, 2) * (g.X - 1) + i - 1) * (g.L - 1) + j - 1
            out = self.out["corner"] + 2 * side + spot
            for s in self.each():
                self.add(block, l, s, [self.base["pair"] + spot])
                self.push(out, block, l, s, self.base["l2"] + (i - 1) * (g.L - 1) + g.L - j - 1, l_dev, even)
                self.push(out, block, l, s, self.base["x2"] + (g.X - i - 1) * (g.L - 1) + j - 1, x_dev, jnp.logical_not(even))

    def side_x(self, zk, i, waits):
        g = self.g
        x, x_dev = g.x_other(i)
        block = g.block(zk, x, g.core)
        ats = [self.base["l2"] + (i - 1) * (g.L - 1) + j - 1 for j in range(1, g.L)]
        for s in self.each():
            if ats and waits:
                self.add(block, g.l, s, ats)
            self.push(self.out["xc"] + zk * (g.X - 1) + i - 1, block, g.l, s, self.base["xc"] + zk * (g.X - 1) + g.X - i - 1, x_dev)

    def side_l(self, zk, waits):
        g = self.g
        block = g.block(zk, g.x, g.core)
        for j in range(1, g.L):
            l, l_dev = g.l_other(j)
            ats = [self.base["x2"] + (i - 1) * (g.L - 1) + j - 1 for i in range(1, g.X)]
            for s in self.each():
                if waits:
                    self.add(block, l, s, ats)
                self.push(self.out["lc"] + zk * (g.L - 1) + j - 1, block, l, s, self.base["lc"] + zk * (g.L - 1) + g.L - j - 1, l_dev)

    def around(self, zk):
        g = self.g
        ats = [self.base["xc"] + zk * (g.X - 1) + i - 1 for i in range(1, g.X)]
        return ats + [self.base["lc"] + zk * (g.L - 1) + j - 1 for j in range(1, g.L)]

    def column(self, zk):
        g = self.g
        block = g.block(zk, g.x, g.core)
        behind = jnp.where(zk > g.z, g.down, g.up)
        near = jnp.abs(zk - g.z) == 1
        spot = jnp.where(near & (zk < g.z), 4, zk)
        for s in self.each():
            self.add(block, g.l, s, self.around(zk))
            self.add(block, g.l, s, [self.base["z"] + zk], behind)
            self.push(self.out["z"] + zk, block, g.l, s, self.base["z"] + spot, g.at_z(jnp.where(zk > g.z, g.z + 1, g.z - 1)))

    def last(self, out):
        g = self.g
        for s in self.each():
            start, size = self.cuts[s]
            out[start : start + size, :] = self.total(g.row, g.l, s, self.around(g.z))
            for at, there in ((self.base["z"] + g.z, g.down), (self.base["z"] + 4, g.up)):

                def take(at=at, s=s, start=start, size=size):
                    self.arrived(at, s)
                    out[start : start + size, :] += self.inbox[at, start : start + size].astype(F32)

                pl.when(there)(take)

    @staticmethod
    def plan(X, hop=2):
        orders, spots = [], []
        for z in range(4):
            corners = (3, 2, 1, 0) if z < 2 else (0, 1, 2, 3)
            own = tuple(reversed(NEAREST[z]))
            order = []
            for j in range(4):
                order += [(corners[j], off) for off in range(1, X)] + [(own[j], 0)]
            orders.append(order)
            spots.append(({zk: max(m for m, (a, off) in enumerate(order) if a == zk and off) for zk in range(4)},
                          {zk: order.index((zk, 0)) for zk in range(4)}))
        names = ("far", "sx", "sl", "near", "sx_late", "sl_late", "column")
        due = [{name: {} for name in names} for _ in range(4)]

        def put(z, name, zk, step):
            while step in due[z][name]:
                step += 1
            due[z][name][step] = zk
            return step

        sides = [{}, {}, {}, {}]
        for z in range(4):
            pair = z + 1 - 2 * (z % 2)
            for zk in sorted(range(4), key=lambda a: spots[z][0][a]):
                near = zk // 2 == z % 2
                corner, own = spots[z][0][zk] + 1, spots[z][1][zk] + 1
                ready = put(z, "near", zk, max(corner, spots[pair][0][zk] + 1 + hop)) if near else put(z, "far", zk, corner)
                sx = put(z, "sx_late", zk, ready + hop) if near and zk % 2 == 0 else put(z, "sx", zk, corner)
                sl = put(z, "sl_late", zk, max(ready + hop, own)) if near and zk % 2 else put(z, "sl", zk, own)
                sides[z][zk] = max(sx, sl)
        for zk in range(4):
            for chain in (range(0, zk), range(3, zk, -1)):
                before = 0
                for z in chain:
                    before = put(z, "column", zk, max(sides[z][zk], before) + hop)
        steps = 1 + max(step for z in range(4) for name in names for step in due[z][name])
        return orders, due, steps

    def prepare(self):
        self.orders, self.due, self.steps = self.plan(self.g.X)
        self.blocks = 4 * self.g.X

    def pick(self, tables, m):
        out = jnp.int32(-1)
        for z in range(4):
            for at, value in tables[z].items():
                out = jnp.where((self.g.z == z) & (m == at), value, out)
        return out

    def place(self, m):
        g = self.g
        code = self.pick([{at: zk * g.X + off for at, (zk, off) in enumerate(order)} for order in self.orders], m)
        return code // g.X, lax.rem(g.x + lax.rem(code, g.X), g.X)

    def step(self, m):
        g = self.g

        def first():
            self.to_mate(*self.place(m))

        def second():
            self.from_mate(*self.place(m - 1))

        pl.when(m < self.blocks)(first)
        pl.when((m >= 1) & (m <= self.blocks))(second)

        def send(name, act, over_x):
            zk = self.pick([due[name] for due in self.due], m)

            def go():
                if over_x:
                    for i in range(1, g.X):
                        act(zk, i)
                else:
                    act(zk)

            pl.when(zk >= 0)(go)

        send("column", self.column, False)
        send("sl_late", lambda zk: self.side_l(zk, True), False)
        send("sx_late", lambda zk, i: self.side_x(zk, i, True), True)
        if g.L > 1:
            send("near", self.corner_near, True)
            send("far", self.corner_far, True)
        send("sl", lambda zk: self.side_l(zk, False), False)
        send("sx", lambda zk, i: self.side_x(zk, i, False), True)

    def run(self, work=None, ahead=4):
        def one(m, carry):
            if work is not None:
                work(m)
            self.step(m)

            def wait():
                self.drain = True
                self.step(m - ahead)
                self.drain = False

            pl.when(m >= ahead)(wait)
            return carry

        lax.fori_loop(0, self.steps, one, 0)
        self.ahead = ahead

    def finish(self):
        self.drain = True

        def one(m, carry):
            self.step(m)
            return carry

        lax.fori_loop(self.steps - self.ahead, self.steps, one, 0)


def dot(left, right):
    return jnp.dot(left, right, preferred_element_type=F32)


def dot_nt(left, right):
    return lax.dot_general(left, right, (((1,), (1,)), ((), ())), preferred_element_type=F32)


def dot_tn(left, right):
    return lax.dot_general(left, right, (((0,), (0,)), ((), ())), preferred_element_type=F32)


def fold(values):
    rows, width = values.shape
    return jnp.sum(values.reshape(rows // 8, 8, width), axis=0)


def norm_parts(values):
    average = jnp.mean(values, axis=-1, keepdims=True)
    centered = values - average
    scale = lax.rsqrt(jnp.mean(centered * centered, axis=-1, keepdims=True) + NORM_EPS)
    return centered * scale, scale


def norm_back(normed, scale, d_normed):
    mean_d = jnp.mean(d_normed, axis=-1, keepdims=True)
    mean_dn = jnp.mean(d_normed * normed, axis=-1, keepdims=True)
    return scale * (d_normed - mean_d - normed * mean_dn)


def silu_back(pre, d_active):
    gate = lax.logistic(pre)
    return d_active * (gate * (1.0 + pre * (1.0 - gate)))


def find_places(row_total, node_count, senders, receivers, live, place, side, facts_out):
    tiles = senders.shape[0]
    group = tiles * 128 // row_total
    first = lax.axis_index("row") * node_count
    lane = lax.broadcasted_iota(jnp.int32, (128, 128), 1)
    sub = lax.broadcasted_iota(jnp.int32, (128, 128), 0)
    before = (sub < lane).astype(BF16)
    owner_ids = lax.broadcasted_iota(jnp.int32, (row_total, 128), 0)
    carry = owner_ids[:, :1].astype(F32) * group
    for tile in range(tiles):
        send = senders[tile : tile + 1, :]
        recv = receivers[tile : tile + 1, :] - first
        owner = lax.div(send, node_count)
        local = send - owner * node_count
        mine = owner_ids == owner
        ranks = dot(mine.astype(BF16), before) + carry
        spot = jnp.sum(jnp.where(mine, ranks, 0.0), axis=0, keepdims=True)
        carry = carry + jnp.sum(mine.astype(F32), axis=1, keepdims=True)
        place[tile : tile + 1, :] = spot.astype(jnp.int32)
        alive = (lane[:1] + tile * 128 < live[0, 0]).astype(jnp.int32)
        facts = jnp.where(sub == 0, lax.div(local, 16), 0)
        facts = jnp.where(sub == 1, lax.rem(local, 16), facts)
        facts = jnp.where(sub == 2, lax.div(recv, 16), facts)
        facts = jnp.where(sub == 3, lax.rem(recv, 16), facts)
        facts = jnp.where(sub == 4, alive, facts).astype(F32)
        side[:, pl.ds(tile * 128, 128)] = facts[:16].astype(BF16)
        facts_out[pl.ds(tile * 128, 128), :] = facts.T.astype(BF16)


def picker(place, start, size):
    ids = lax.broadcasted_iota(jnp.int32, (size, 128), 0) + start
    return jnp.concatenate([(ids == place[tile : tile + 1, :]).astype(BF16) for tile in range(place.shape[0])], axis=1)


def one_hot_cols(ids, count):
    lanes = lax.broadcasted_iota(jnp.int32, (ids.shape[0], count), 1).astype(F32)
    return (ids == lanes).astype(BF16)


def one_hot_rows(ids, count):
    subs = lax.broadcasted_iota(jnp.int32, (count, ids.shape[1]), 0).astype(F32)
    return (ids == subs).astype(BF16)


def load_all(pairs, sems):
    copies = [pltpu.make_async_copy(src, dst, sems.at[i]) for i, (src, dst) in enumerate(pairs)]
    for copy in copies:
        copy.start()
    return copies


def forward_kernel(
    layer, levels, rows, first_layer, *refs
):
    (node, b1, b2, gain, shift, nb1, nb2, ngain, nshift, w1_all, w2_all, nw1_all, nw2_all, plain_all) = refs[:14]
    refs = refs[14:]
    if first_layer:
        senders, receivers, live = refs[:3]
        refs = refs[3:]
    else:
        place, rows_of, cols_all, edges_all, before_all = refs[:5]
        refs = refs[5:]
    sent_out, pre_out, normed_out, update_out, moved_out = refs[:5]
    refs = refs[5:]
    if first_layer:
        edges_out, place, rows_of, cols = refs[:4]
        refs = refs[4:]
    scale_out, block_out, node_out, recv_out, npre_out, nnormed_out, nscale_out, tally = refs[:8]
    (
        table, total, cast, near, far, w1, w2, nw1, nw2, plain, joined, out_buf, scale_buf,
        load_sem, out_sem, send_sem, recv_sem, near_send, near_recv,
    ) = refs[8:27]
    if first_layer:
        side = refs[27]
    else:
        cols, edges, before = refs[27:]
    g = Grid(levels, rows)
    h, width = node.shape
    count = plain.shape[0]
    group = count // rows
    node_count = h * levels
    pairs = ((plain_all, plain), (w1_all.at[layer], w1), (w2_all.at[layer], w2), (nw1_all.at[layer], nw1), (nw2_all.at[layer], nw2))
    if not first_layer:
        pairs += ((cols_all, cols), (edges_all, edges), (before_all, before))
    loads = load_all(pairs, load_sem)
    ag = Gather(g, table, h, send_sem, recv_sem)
    ag.slot(g.row, g.l)[...] = node[...].astype(BF16)
    tally[...] = jnp.zeros_like(tally)
    total[...] = jnp.zeros_like(total)
    g.greet()
    wide = lambda ref: ref[layer : layer + 1, :]
    outs = (sent_out, pre_out, normed_out, update_out, moved_out) + ((edges_out,) if first_layer else ())

    def meanwhile():
        if first_layer:
            find_places(rows, node_count, senders, receivers, live, place, side, joined.at[:, pl.ds(width, 128)])
        for copy in loads:
            copy.wait()

        def cast_rows(i, carry):
            part = pl.ds(pl.multiple_of(i * 2 * group, 2 * group), 2 * group)
            joined[part, 0:width] = plain[part, :].astype(BF16)
            return carry

        lax.fori_loop(0, rows // 2, cast_rows, 0)

    def leave(n, part):
        slot = lax.rem(n, 2)
        copies = [pltpu.make_async_copy(out_buf.at[slot, i], ref.at[part], out_sem.at[slot, i]) for i, ref in enumerate(outs)]
        return copies + [pltpu.make_async_copy(scale_buf.at[slot], scale_out.at[part], out_sem.at[slot, 6])]

    def work(z, x, n):
        def own():
            here = table[pl.ds(pl.multiple_of(g.row * node_count, 16), node_count), :]
            cast[...] = dot(here, w1[2 * width :, :]).astype(BF16)
            block_out[...] = here

        pl.when(n == 0)(own)
        pair = g.block(z, x, 0)
        first = pl.multiple_of(pair * group, 2 * group)
        part = pl.ds(first, 2 * group)

        def free():
            for copy in leave(n, part):
                copy.wait()

        pl.when(n >= 2)(free)
        slot = lax.rem(n, 2)
        pick = picker(place, first, 2 * group)
        moved = dot(pick, joined[...])
        if first_layer:
            low = moved[:, :width].astype(BF16)
            digits = moved[:, width:]
            lanes = lax.broadcasted_iota(jnp.int32, digits.shape, 1)
            ids = digits[:, 0:1] * 16.0 + digits[:, 1:2]
            got = digits[:, 2:3] * 16.0 + digits[:, 3:4]
            cols_here = jnp.where(lanes == 0, ids, jnp.where(lanes == 1, got, jnp.where(lanes == 2, digits[:, 4:5], 0.0)))
            cols[part, :] = cols_here
            for half in range(2):
                digits = dot_nt(side[...], pick[half * group : (half + 1) * group])
                rows_of[pair + half] = jnp.concatenate(
                    [digits[0:1] * 16.0 + digits[1:2], digits[2:3] * 16.0 + digits[3:4], digits[4:10]], axis=0
                )
        else:
            low = edges[part, :]
            cols_here = cols[part, :]
        out_buf[slot, 4] = moved[:, :width].astype(BF16)
        send_pick = one_hot_cols(cols_here[:, 0:1], node_count)
        recv_pick = one_hot_cols(cols_here[:, 1:2], node_count)
        start = pl.multiple_of(pair * node_count, 16)
        sent = jnp.concatenate(
            [
                dot(send_pick[:group], table[pl.ds(start, node_count), :]).astype(BF16),
                dot(send_pick[group:], table[pl.ds(start + node_count, node_count), :]).astype(BF16),
            ],
            axis=0,
        )
        out_buf[slot, 0] = sent
        pre = dot(low, w1[:width, :]) + dot(sent, w1[width : 2 * width, :]) + dot(recv_pick, cast[...]) + wide(b1)
        out_buf[slot, 1] = pre.astype(BF16)
        active = (pre * lax.logistic(pre)).astype(BF16)
        normed, scale = norm_parts(dot(active, w2[...]) + wide(b2))
        out_buf[slot, 2] = normed.astype(BF16)
        scale_buf[slot] = jnp.broadcast_to(scale, (2 * group, 128))
        update = (normed * wide(gain) + wide(shift)) * cols_here[:, 2:3]
        update_low = update.astype(BF16)
        edge = low.astype(F32) + update
        if first_layer:
            out_buf[slot, 3] = update_low
            out_buf[slot, 5] = edge.astype(BF16)
        else:
            out_buf[slot, 3] = (before[part, :].astype(F32) + update).astype(BF16)
        tally[8:16, :] += fold(edge * edge)
        tally[16:24, :] += fold(update * update)
        for half in range(2):
            pick = one_hot_rows(rows_of[pair + half][1:2, :], node_count)
            total[...] += dot(pick, update_low[half * group : (half + 1) * group])
        for copy in leave(n, part):
            copy.start()

    ag.run(work, meanwhile)
    copies = []
    for j in range(1, levels):
        l, l_dev = g.l_other(j)
        near[j - 1] = total[pl.ds(pl.multiple_of(l * h, h), h), :].astype(BF16)
        copy = pltpu.make_async_remote_copy(
            near.at[j - 1], far.at[levels - 1 - j], near_send.at[j - 1], near_recv.at[levels - 1 - j], device_id=l_dev, device_id_type=MESH
        )
        copy.start()
        copies.append(copy)
    received = total[pl.ds(pl.multiple_of(g.l * h, h), h), :]
    npre = dot(node[...].astype(BF16), nw1[:width, :]) + wide(nb1)
    for copy in copies:
        copy.wait()
    for j in range(1, levels):
        received = received + far[j - 1].astype(F32)
    received = received.astype(BF16)
    recv_out[...] = received
    npre = npre + dot(received, nw1[width:, :])
    npre_out[...] = npre
    nnormed, nscale = norm_parts(dot((npre * lax.logistic(npre)).astype(BF16), nw2[...]) + wide(nb2))
    nnormed_out[...] = nnormed
    nscale_out[...] = jnp.broadcast_to(nscale, (h, 128))
    change = nnormed * wide(ngain) + wide(nshift)
    new = node[...] + change
    node_out[...] = new
    tally[0:8, :] = fold(new * new)
    tally[24:32, :] = fold(change * change)
    for n in range(2):
        for copy in leave(n, pl.ds(0, 2 * group)):
            copy.wait()
    ag.finish()


def forward_layer(layer, node, small, weights, plain, index, edges=None, before=None):
    levels, rows = lax.axis_size("lvl"), lax.axis_size("row")
    h, width = node.shape
    count = plain.shape[0]
    group = count // rows
    vmem = pl.BlockSpec(memory_space=pltpu.VMEM)
    hbm = pl.BlockSpec(memory_space=pl.ANY)
    first_layer = layer == 0
    shape = jax.ShapeDtypeStruct
    wide = shape((count, width), BF16)
    ins = (node,) + small + weights + (plain,) + index
    in_specs = [vmem] * 9 + [hbm] * 5
    outs = [wide] * 5
    out_specs = [hbm] * 5
    scratch = []
    if first_layer:
        in_specs += [vmem, vmem, pl.BlockSpec(memory_space=pltpu.SMEM)]
        outs += [wide, shape(index[0].shape, jnp.int32), shape((rows, 8, group), F32), shape((count, 128), F32)]
        out_specs += [hbm, vmem, vmem, vmem]
        scratch = [pltpu.VMEM((16, count), BF16)]
    else:
        ins += (edges, before)
        in_specs += [vmem, vmem, hbm, hbm, hbm]
        scratch = [pltpu.VMEM((count, 128), F32), pltpu.VMEM((count, width), BF16), pltpu.VMEM((count, width), BF16)]
    outs += [
        shape((count, 128), F32),
        shape((h * levels, width), BF16),
        shape((h, width), F32),
        shape((h, width), BF16),
        shape((h, width), F32),
        shape((h, width), F32),
        shape((h, 128), F32),
        shape((32, width), F32),
    ]
    out_specs += [hbm] + [vmem] * 7
    others = max(levels - 1, 1)
    return pl.pallas_call(
        functools.partial(forward_kernel, layer, levels, rows, first_layer),
        out_shape=outs,
        in_specs=in_specs,
        out_specs=out_specs,
        scratch_shapes=[
            pltpu.VMEM((rows * h * levels, width), BF16),
            pltpu.VMEM((h * levels, width), F32),
            pltpu.VMEM((h * levels, width), BF16),
            pltpu.VMEM((others, h, width), BF16),
            pltpu.VMEM((others, h, width), BF16),
        ]
        + [pltpu.VMEM(weight.shape[1:], BF16) for weight in weights]
        + [
            pltpu.VMEM((count, width), F32),
            pltpu.VMEM((count, width + (128 if first_layer else 0)), BF16),
            pltpu.VMEM((2, 6, 2 * group, width), BF16),
            pltpu.VMEM((2, 2 * group, 128), F32),
            pltpu.SemaphoreType.DMA((8,)),
            pltpu.SemaphoreType.DMA((2, 7)),
            pltpu.SemaphoreType.DMA((Gather.sends(levels, rows),)),
            pltpu.SemaphoreType.DMA((2 * rows * levels,)),
            pltpu.SemaphoreType.DMA((others,)),
            pltpu.SemaphoreType.DMA((others,)),
        ]
        + scratch,
        compiler_params=pltpu.CompilerParams(collective_id=1 + layer, has_side_effects=True, vmem_limit_bytes=VMEM_BYTES),
        name=f"forward_{layer}",
    )(*ins)


def backward_kernel(
    layer, levels, rows, last_layer,
    d_node, block, recv, npre, nnormed, nscale, rows_of, gain, ngain, node, d_before, cols_all, scale_all, d_edges, pre, normed, edges, sent,
    w1_all, w2_all, nw1_all, nw2_all,
    d_node_out, d_edges_out, d_change_out, grads, tally, node_all,
    stage, inbox, bufs, d_recv, turned, own_sum, out_buf, cols, scale, w1, w2, nw1, nw2,
    load_sem, out_sem, send_sem, recv_sem, near_send, near_recv,
):
    g = Grid(levels, rows)
    h, width = d_node.shape
    count = pre.shape[0]
    group = count // rows
    node_count = h * levels
    loads = load_all(
        ((nw2_all.at[layer], nw2), (nw1_all.at[layer], nw1), (w1_all.at[layer], w1), (w2_all.at[layer], w2))
        + tuple((src, bufs.at[i]) for i, src in enumerate((d_edges, pre, normed, edges, sent)))
        + ((cols_all, cols), (scale_all, scale)),
        load_sem,
    )
    rs = Scatter(g, stage, inbox, h, send_sem, recv_sem)
    wide = lambda ref: ref[layer : layer + 1, :]
    mine = pl.ds(pl.multiple_of(g.l * h, h), h)
    own_sum[...] = jnp.zeros_like(own_sum)
    tally[...] = jnp.zeros_like(tally)
    for copy in loads[:2]:
        copy.wait()
    tally[48:56, :] = fold(d_node[...] * nnormed[...])
    tally[56:64, :] = fold(d_node[...])
    d_two = norm_back(nnormed[...], nscale[:, 0:1], d_node[...] * wide(ngain)).astype(BF16)
    tally[40:48, :] = fold(d_two.astype(F32))
    d_one = silu_back(npre[...], dot_nt(d_two, nw2[...])).astype(BF16)
    tally[32:40, :] = fold(d_one.astype(F32))
    d_recv[mine, :] = dot_nt(d_one, nw1[width:, :]).astype(BF16)
    g.greet()
    copies = []
    for j in range(1, levels):
        copy = pltpu.make_async_remote_copy(
            d_recv.at[mine], d_recv.at[mine], near_send.at[j - 1], near_recv.at[levels - 1 - j], device_id=g.l_other(j)[1], device_id_type=MESH
        )
        copy.start()
        copies.append(copy)
    d_node_out[...] = d_node[...] + dot_nt(d_one, nw1[:width, :])
    active = (npre[...] * lax.logistic(npre[...])).astype(BF16)
    grads[4 * width + width : 6 * width, :] = dot_tn(recv[...], d_one).astype(BF16)
    grads[4 * width : 5 * width, :] = dot_tn(block[mine, :], d_one).astype(BF16)
    grads[6 * width : 7 * width, :] = dot_tn(active, d_two).astype(BF16)
    if last_layer:
        node_all[mine, :] = node[...].astype(BF16)
    for copy in copies:
        copy.wait()
    copies = []
    for j in range(1, levels if last_layer else 1):
        copy = pltpu.make_async_remote_copy(
            node_all.at[mine],
            node_all.at[mine],
            near_send.at[levels + j - 2],
            near_recv.at[2 * levels - 2 - j],
            device_id=g.l_other(j)[1],
            device_id_type=MESH,
        )
        copy.start()
        copies.append(copy)
    for copy in loads[2:]:
        copy.wait()

    def work(i):
        z, x = rs.place(i)
        pair = g.block(z, x, 0)
        start = pl.multiple_of(pair * group, 2 * group)
        place = pl.ds(start, 2 * group)
        if not last_layer:
            earlier = pltpu.make_async_copy(d_before.at[place], out_buf.at[lax.rem(i, 2), 0], out_sem.at[lax.rem(i, 2), 0])
            earlier.start()
        cols_here = cols[place, :]
        recv_pick = one_hot_cols(cols_here[:, 1:2], node_count)
        d_edge = bufs[0, place, :].astype(F32)
        d_update = (d_edge + dot(recv_pick, d_recv[...])) * cols_here[:, 2:3]
        norm_here = bufs[2, place, :].astype(F32)
        tally[16:24, :] += fold(d_update * norm_here)
        tally[24:32, :] += fold(d_update)
        d_two = norm_back(norm_here, scale[place, 0:1], d_update * wide(gain)).astype(BF16)
        tally[8:16, :] += fold(d_two.astype(F32))
        pre_here = bufs[1, place, :].astype(F32)
        gate = lax.logistic(pre_here)
        d_one = (dot_nt(d_two, w2[...]) * (gate * (1.0 + pre_here * (1.0 - gate)))).astype(BF16)
        tally[0:8, :] += fold(d_one.astype(F32))
        bufs[0, place, :] = d_one
        bufs[1, place, :] = (pre_here * gate).astype(BF16)
        bufs[2, place, :] = d_two
        d_here = dot_nt(d_one, w1[:width, :])
        slot = lax.rem(i, 2)
        used = [
            pltpu.make_async_copy(out_buf.at[slot, n], ref.at[place], out_sem.at[slot, n])
            for n, ref in enumerate((d_edges_out, d_change_out))
            if n or last_layer
        ]

        def free():
            for copy in used:
                copy.wait()

        pl.when(i >= 2)(free)
        if last_layer:
            out_buf[slot, 0] = (d_edge + d_here).astype(BF16)
            out_buf[slot, 1] = d_here.astype(BF16)
        else:
            earlier.wait()
            out_buf[slot, 1] = (out_buf[slot, 0].astype(F32) + d_here).astype(BF16)
        for copy in used:
            copy.start()
        d_sent = dot_nt(d_one, w1[width : 2 * width, :]).astype(BF16)
        for half in range(2):
            ids = rows_of[pair + half]
            part = slice(half * group, (half + 1) * group)
            own_sum[...] += dot(one_hot_rows(ids[1:2, :], node_count), d_one[part])
            spot = pl.ds(pl.multiple_of((pair + half) * node_count, 16), node_count)
            stage[spot, :] = dot(one_hot_rows(ids[0:1, :], node_count), d_sent[part]).astype(BF16)

        def close():
            low = own_sum[...].astype(BF16)
            spot = pl.ds(pl.multiple_of(g.row * node_count, 16), node_count)
            stage[spot, :] = (stage[spot, :].astype(F32) + dot_nt(low, w1[2 * width :, :])).astype(BF16)
            grads[2 * width : 3 * width, :] = dot_tn(block[...], low).astype(BF16)

        pl.when(i == rs.blocks - 1)(close)

    def step(m):
        pl.when(m < rs.blocks)(lambda: work(m))
        for n, (at, left, right) in enumerate(((0, 3, 0), (1, 4, 0), (3, 1, 2))):

            def grad(at=at, left=left, right=right):
                grads[at * width : (at + 1) * width, :] = dot_tn(bufs[left], bufs[right]).astype(BF16)

            pl.when(m == rs.blocks + n)(grad)

    rs.run(step)
    rs.last(turned)
    for copy in copies:
        copy.wait()
    d_node_out[...] += turned[...]
    for slot in range(2):
        for n, ref in enumerate((d_edges_out, d_change_out)):
            if n or last_layer:
                pltpu.make_async_copy(out_buf.at[slot, n], ref.at[pl.ds(0, 2 * group)], out_sem.at[slot, n]).wait()
    rs.finish()


def backward_layer(layer, last_layer, d_node, node_saved, cols, rows_of, scale, small, weights, d_edges, edge_saved, node, d_before):
    levels, rows = lax.axis_size("lvl"), lax.axis_size("row")
    h, width = d_node.shape
    count = d_edges.shape[0]
    group = count // rows
    vmem = pl.BlockSpec(memory_space=pltpu.VMEM)
    hbm = pl.BlockSpec(memory_space=pl.ANY)
    shape = jax.ShapeDtypeStruct
    ins = (d_node,) + node_saved + (rows_of,) + small + (node, d_before, cols, scale, d_edges) + edge_saved + weights
    outs = (
        shape((h, width), F32),
        shape((count, width) if last_layer else (16, 128), BF16),
        shape((count, width), BF16),
        shape((7 * width, width), BF16),
        shape((64, width), F32),
        shape((h * levels, width) if last_layer else (16, 128), BF16),
    )
    others = max(levels - 1, 1)
    return pl.pallas_call(
        functools.partial(backward_kernel, layer, levels, rows, last_layer),
        out_shape=outs,
        in_specs=[vmem] * (len(ins) - 12) + [hbm] * 12,
        out_specs=(vmem, hbm, hbm, vmem, vmem, vmem),
        scratch_shapes=[
            pltpu.VMEM((rows * h * levels, width), BF16),
            pltpu.VMEM((Scatter.receives(levels, rows), h, width), BF16),
            pltpu.VMEM((5, count, width), BF16),
            pltpu.VMEM((h * levels, width), BF16),
            pltpu.VMEM((h, width), F32),
            pltpu.VMEM((h * levels, width), F32),
            pltpu.VMEM((2, 2, 2 * group, width), BF16),
            pltpu.VMEM((count, 128), F32),
            pltpu.VMEM((count, 128), F32),
        ]
        + [pltpu.VMEM(weight.shape[1:], BF16) for weight in weights]
        + [
            pltpu.SemaphoreType.DMA((11,)),
            pltpu.SemaphoreType.DMA((2, 2)),
            pltpu.SemaphoreType.DMA((Scatter.sends(levels, rows),)),
            pltpu.SemaphoreType.DMA((2 * Scatter.receives(levels, rows),)),
            pltpu.SemaphoreType.DMA((2 * others,)),
            pltpu.SemaphoreType.DMA((2 * others,)),
        ],
        compiler_params=pltpu.CompilerParams(collective_id=3 + layer, has_side_effects=True, vmem_limit_bytes=VMEM_BYTES),
        name=f"backward_{layer}",
    )(*ins)


def sum_kernel(levels, rows, h, *refs):
    count = len(refs) - 13
    d_node, terms = refs[0], refs[1 : count + 1]
    out, d_node_all, stage, inbox, total, scatter_send, scatter_recv, gather_send, gather_recv, load_sem, near_send, near_recv = refs[count + 1 :]
    g = Grid(levels, rows)
    mine = pl.ds(pl.multiple_of(g.l * d_node.shape[0], d_node.shape[0]), d_node.shape[0])
    d_node_all[mine, :] = d_node[...].astype(BF16)
    pairs = []
    at = 0
    for term in terms:
        pairs.append((term, stage.at[pl.ds(at, term.shape[0])]))
        at += term.shape[0]
    loads = load_all(pairs, load_sem)
    g.greet()
    for copy in loads:
        copy.wait()
    copies = []
    for j in range(1, levels):
        copy = pltpu.make_async_remote_copy(
            d_node_all.at[mine], d_node_all.at[mine], near_send.at[j - 1], near_recv.at[levels - 1 - j], device_id=g.l_other(j)[1], device_id_type=MESH
        )
        copy.start()
        copies.append(copy)
    rs = Scatter(g, stage, inbox, h, scatter_send, scatter_recv)
    rs.run(ahead=2)
    rs.last(total)
    ag = Gather(g, out, h, gather_send, gather_recv)
    ag.slot(g.row, g.l)[...] = total[...].astype(BF16)
    ag.run()
    for copy in copies:
        copy.wait()
    rs.finish()
    ag.finish()


def sum_pieces(d_node, terms, call):
    levels, rows = lax.axis_size("lvl"), lax.axis_size("row")
    width = terms[0].shape[1]
    count = sum(term.shape[0] for term in terms)
    h = count // (levels * rows)
    return pl.pallas_call(
        functools.partial(sum_kernel, levels, rows, h),
        out_shape=(jax.ShapeDtypeStruct((count, width), BF16), jax.ShapeDtypeStruct((d_node.shape[0] * levels, width), BF16)),
        in_specs=[pl.BlockSpec(memory_space=pltpu.VMEM)] + [pl.BlockSpec(memory_space=pl.ANY)] * len(terms),
        out_specs=(pl.BlockSpec(memory_space=pltpu.VMEM),) * 2,
        scratch_shapes=[
            pltpu.VMEM((count, width), BF16),
            pltpu.VMEM((Scatter.receives(levels, rows), h, width), BF16),
            pltpu.VMEM((h, width), F32),
            pltpu.SemaphoreType.DMA((Scatter.sends(levels, rows),)),
            pltpu.SemaphoreType.DMA((2 * Scatter.receives(levels, rows),)),
            pltpu.SemaphoreType.DMA((Gather.sends(levels, rows),)),
            pltpu.SemaphoreType.DMA((2 * rows * levels,)),
            pltpu.SemaphoreType.DMA((len(terms),)),
            pltpu.SemaphoreType.DMA((max(levels - 1, 1),)),
            pltpu.SemaphoreType.DMA((max(levels - 1, 1),)),
        ],
        compiler_params=pltpu.CompilerParams(collective_id=call, has_side_effects=True, vmem_limit_bytes=VMEM_BYTES),
        name=f"sum_{call}",
    )(d_node, *terms)


def finish_kernel(
    parts, place, update, d_change, first_sums, last_sums, edges, cot, edge_out, cot_out, *refs
):
    wide_outs, (sums, ins, outs, wide, sums_sem, in_sem, out_sem, wide_sem) = refs[: len(parts)], refs[len(parts) :]
    tiles = place.shape[0]
    size, width = ins.shape[2:]
    steps = tiles * 128 // size
    targets = [(n, i) for n, count in enumerate(parts) for i in range(count)]
    loads = load_all([(ref.at[pl.ds(0, sums.shape[1])], sums.at[layer]) for layer, ref in enumerate((first_sums, last_sums))], sums_sem)
    lane = lax.broadcasted_iota(jnp.int32, (128, 128), 1).astype(F32)

    def load(step):
        here = pl.ds(step * size, size)
        return [pltpu.make_async_copy(ref.at[here], ins.at[step % 2, n], in_sem.at[step % 2, n]) for n, ref in enumerate((edges, cot))]

    def leave(step):
        here = pl.ds(step * size, size)
        return [pltpu.make_async_copy(outs.at[step % 2, n], ref.at[here], out_sem.at[step % 2, n]) for n, ref in enumerate((edge_out, cot_out))]

    def widen(at):
        n, i = targets[at % len(targets)]
        ref = wide_outs[n].at[at // len(targets), pl.ds(i * width, width)]
        return pltpu.make_async_copy(wide.at[at % 4], ref, wide_sem.at[at % 4])

    total = 2 * len(targets)
    done = 0
    for copy in load(0):
        copy.start()
    for step in range(steps):
        if step + 1 < steps:
            for copy in load(step + 1):
                copy.start()
        pick = []
        for part in range(size // 128):
            row = step * (size // 128) + part
            spot = jnp.broadcast_to(place[row : row + 1, :], (128, 128)).astype(F32).T
            pick.append(jnp.concatenate([(spot == lane + float(128 * j)).astype(BF16) for j in range(tiles)], axis=1))
        pick = jnp.concatenate(pick, axis=0)
        for copy in load(step):
            copy.wait()
        if step >= 2:
            for copy in leave(step - 2):
                copy.wait()
        outs[step % 2, 0] = ins[step % 2, 0] + dot(pick, update[...])
        outs[step % 2, 1] = ins[step % 2, 1] + dot(pick, d_change[...])
        for copy in leave(step):
            copy.start()
        if step == 0:
            for copy in loads:
                copy.wait()
        while done < total * (step + 1) // steps:
            if done >= 4:
                widen(done - 4).wait()
            layer, at = done // len(targets), done % len(targets)
            wide[done % 4] = sums[layer, at * width : (at + 1) * width, :].astype(F32)
            widen(done).start()
            done += 1
    for step in range(max(steps - 2, 0), steps):
        for copy in leave(step):
            copy.wait()
    for at in range(total - 4, total):
        widen(at).wait()


def finish_edges(place, update, d_change, first_sums, last_sums, edges, cot, parts):
    count, width = edges.shape
    size = 512 if count % 512 == 0 else 128
    vmem = pl.BlockSpec(memory_space=pltpu.VMEM)
    hbm = pl.BlockSpec(memory_space=pl.ANY)
    shape = jax.ShapeDtypeStruct
    outs = (shape((count, width), F32),) * 2 + tuple(shape((2, part * width, width), F32) for part in parts)
    return pl.pallas_call(
        functools.partial(finish_kernel, parts),
        out_shape=outs,
        in_specs=[vmem] * 3 + [hbm] * 4,
        out_specs=(hbm,) * len(outs),
        scratch_shapes=[
            pltpu.VMEM((2, sum(parts) * width, width), BF16),
            pltpu.VMEM((2, 2, size, width), F32),
            pltpu.VMEM((2, 2, size, width), F32),
            pltpu.VMEM((4, width, width), F32),
            pltpu.SemaphoreType.DMA((2,)),
            pltpu.SemaphoreType.DMA((2, 2)),
            pltpu.SemaphoreType.DMA((2, 2)),
            pltpu.SemaphoreType.DMA((4,)),
        ],
        compiler_params=pltpu.CompilerParams(vmem_limit_bytes=VMEM_BYTES),
        name="finish_edges",
    )(place, update, d_change, first_sums, last_sums, edges, cot)


def on_device(
    node_latent, edge_latent, senders, receivers, live_edges,
    edge_w1, edge_b1, edge_w2, edge_b2, edge_gain, edge_shift, node_w1, node_b1, node_w2, node_b2, node_gain, node_shift,
    node_cotangent, edge_cotangent,
):
    node_count, width = node_latent.shape
    edge_count = edge_latent.shape[0]
    layers = edge_w1.shape[0]
    row_total, level_total = lax.axis_size("row"), lax.axis_size("lvl")
    half = node_count // level_total
    mine = lambda array: lax.dynamic_slice_in_dim(array, lax.axis_index("lvl") * half, half)
    node = mine(node_latent)
    weights = (edge_w1, edge_w2, node_w1, node_w2)
    small = (edge_b1, edge_b2, edge_gain, edge_shift, node_b1, node_b2, node_gain, node_shift)
    tiles = edge_count // 128
    index = (senders.reshape(tiles, 128), receivers.reshape(tiles, 128), live_edges.reshape(1, 1))
    sent, pre, normed, update, edges, edges_next, place, rows_of, cols, scale, block, node, recv, npre, nnormed, nscale, tally = forward_layer(
        0, node, small, weights, edge_latent, index
    )
    first = ((block, recv, npre, nnormed, nscale), scale, (pre, normed, edges, sent))
    sent, pre, normed, update, d_edges, scale, block, node, recv, npre, nnormed, nscale, tally_last = forward_layer(
        1, node, small, weights, edge_cotangent, (place, rows_of, cols), edges_next, update
    )
    last = ((block, recv, npre, nnormed, nscale), scale, (pre, normed, edges_next, sent))
    tallies = [tally, tally_last]
    d_node = mine(node_cotangent)
    gains = (edge_gain, node_gain)
    d_node, d_edges, d_change, last_grads, last_sums, node_all = backward_layer(
        1, True, d_node, last[0], cols, rows_of, last[1], gains, weights, d_edges, last[2], node, d_edges
    )
    last_grads = lax.psum(last_grads, ("lvl", "row"))
    d_node, _, d_change, first_grads, first_sums, _ = backward_layer(
        0, False, d_node, first[0], cols, rows_of, first[1], gains, weights, d_edges, first[2], node, d_change
    )
    sums = [first_sums, last_sums]
    small = jnp.concatenate([jnp.sum(part.reshape(8, 8, width), axis=1) for part in sums])
    squares = jnp.stack([jnp.sum(tally.reshape(4, 8 * width), axis=1) for tally in tallies])
    squares = jnp.pad(squares.reshape(1, -1), ((0, 0), (0, width - squares.size)))
    devices = row_total * level_total
    used = 7 * width + small.shape[0] + 1
    share = -(-used // (16 * devices)) * 16
    rest = [small.astype(BF16), squares.astype(BF16), jnp.zeros((share * devices - used, width), BF16)]
    flat, d_node_all = sum_pieces(d_node, [first_grads, jnp.concatenate(rest)], 5)
    after = 7 * width
    smalls = flat[after : after + 8 * layers].astype(F32).reshape(layers, 8, width)
    squares = flat[after + 8 * layers, : 4 * layers].astype(F32).reshape(layers, 4)
    edge_out, edge_grad, *big = finish_edges(place, update, d_change, flat, last_grads, edge_latent, edge_cotangent, (3, 1, 2, 1))
    node_entries = float(node_count * row_total * width)
    edge_entries = float(edge_count * row_total * level_total * width)
    entries = jnp.array([node_entries, edge_entries, edge_entries, node_entries], F32)
    return (
        node_all.astype(F32),
        edge_out,
        d_node_all.astype(F32),
        edge_grad,
        big[0],
        smalls[:, 0],
        big[1],
        smalls[:, 1],
        smalls[:, 2],
        smalls[:, 3],
        big[2],
        smalls[:, 4],
        big[3],
        smalls[:, 5],
        smalls[:, 6],
        smalls[:, 7],
        jnp.sqrt(squares / entries[None, :]),
    )


def solution(mesh):
    rows, both, whole = P("row", None), P(("lvl", "row"), None), P()
    edge = P(("lvl", "row"))
    placed = (rows, both, edge, edge, edge) + (whole,) * 12 + (rows, both)
    outs = (rows, both, rows, both) + (whole,) * 13
    return jax.shard_map(on_device, mesh=mesh, in_specs=placed, out_specs=outs, check_vma=False)
```

```python
import functools

import jax
import jax.numpy as jnp
from jax import lax
from jax.experimental import pallas as pl
from jax.experimental.pallas import tpu as pltpu
from jax.sharding import PartitionSpec as P

MESH = pl.DeviceIdType.MESH
NORM_EPS = 1e-05
F32 = jnp.float32
BF16 = jnp.bfloat16
VMEM_BYTES = 61 * 2**20


WORK_ORDER = (
    (
        1089728, 289296, 536069, 551556, 141360, 612561, 159764, 1528408, 356492, 400397,
        858841, 422440, 750249, 990892, 1707549, 1799737, 2097129,
    ),
    (
        1089728, 1392676, 131237, 197853, 1464864, 215760, 1448028, 272952, 399521, 881172,
        290876, 745128, 724581, 482457, 1774801, 1717985, 2097129,
    ),
)
ORDER = (
    (
        266400, 82449, 788882, 135431, 104611, 150052, 820491, 853654, 609459, 445454,
        201638, 755629, 347034, 923038, 693433, 481974, 464424, 513978, 908990, 974399,
    ),
    (
        4616, 168577, 183049, 854950, 200706, 541080, 645773, 661524, 559118, 804778,
        281910, 940344, 414866, 774588, 1006515, 495253, 1018298, 1036204, 744878, 445995,
    ),
)
PLAIN_ORDER = (
    (
        524816, 133680, 394788, 465448, 990252,
    ),
    (
        328704, 526372, 658444, 464948, 990252,
    ),
)


NEAREST = ((0, 1, 2, 3), (1, 0, 2, 3), (2, 3, 1, 0), (3, 2, 1, 0))


class Grid:
    def __init__(self, levels, rows):
        self.L, self.R = levels, rows
        self.Z = 4
        self.X = rows // (2 * self.Z)
        self.l = lax.axis_index("lvl")
        row = lax.axis_index("row")
        self.row = row
        self.core = lax.rem(row, 2)
        self.x = lax.rem(row // 2, self.X)
        self.z = row // (2 * self.X)
        self.up = self.z < self.Z - 1
        self.down = self.z > 0

    def block(self, z, x, core):
        return (z * self.X + x) * 2 + core

    def mate(self):
        return (self.l, self.block(self.z, self.x, 1 - self.core))

    def at_z(self, z):
        return (self.l, self.block(jnp.clip(z, 0, self.Z - 1), self.x, self.core))

    def x_other(self, i):
        x = lax.rem(self.x + i, self.X)
        return x, (self.l, self.block(self.z, x, self.core))

    def l_other(self, i):
        l = lax.rem(self.l + i, self.L)
        return l, (l, self.row)

    def nth(self, k, z=None):
        z_here = self.z if z is None else z
        order = NEAREST
        out = jnp.int32(0)
        for z in range(4):
            for j in range(4):
                if order[z][j]:
                    out = jnp.where((z_here == z) & (k == j), order[z][j], out)
        return out

    def local(self, zk, z=None):
        return (zk // 2) == lax.rem(self.z if z is None else z, 2)

    def corner_z(self, q):
        side = lax.rem(lax.rem(self.z, 2) + q // 2, 2)
        return side * 2 + lax.rem(q, 2)

    def pair_z(self):
        return self.z + 1 - 2 * lax.rem(self.z, 2)

    def greet(self):
        barrier = pltpu.get_barrier_semaphore()

        def hello(who):
            pl.semaphore_signal(barrier, inc=1, device_id=who, device_id_type=MESH)

        hello(self.mate())
        for i in range(1, self.X):
            hello(self.x_other(i)[1])
        for i in range(1, self.L):
            hello(self.l_other(i)[1])
        pl.when(self.up)(lambda: hello(self.at_z(self.z + 1)))
        pl.when(self.down)(lambda: hello(self.at_z(self.z - 1)))
        pl.semaphore_wait(barrier, self.X + self.L - 1 + self.up.astype(jnp.int32) + self.down.astype(jnp.int32))


def only(when, act):
    if when is None:
        act()
    else:
        pl.when(when)(act)


def cuts(h):
    first = -(-h // 32) * 16
    return ((0, first), (first, h - first)) if h > first else ((0, h),)


class Gather:
    def __init__(self, grid, table, h, send_sem, recv_sem):
        self.g, self.table, self.h = grid, table, h
        self.cuts = cuts(h)
        self.send_sem, self.recv_sem = send_sem, recv_sem
        X, L = grid.X, grid.L
        self.per_column = X + L + 1
        self.per_sides = 2 * (X - 1) * (L - 1) + X - 1 + L - 1
        self.at_sides = 4 * self.per_column
        self.at_corners = self.at_sides + 4 * self.per_sides
        self.drain = False

    @staticmethod
    def sends(levels, rows):
        X, L = rows // 8, levels
        return 2 * (4 * (X + L + 1) + 4 * (2 * (X - 1) * (L - 1) + X + L - 2) + 8 * (X - 1) * (L - 1))

    def slot(self, block, l, s=None):
        start, size = (0, self.h) if s is None else self.cuts[s]
        return self.table.at[pl.ds(pl.multiple_of((block * self.g.L + l) * self.h + start, 16), size)]

    def push(self, at, block, l, s, who, when=None):
        place = self.slot(block, l, s)
        copy = pltpu.make_async_remote_copy(
            place, place, self.send_sem.at[2 * at + s], self.recv_sem.at[(block * self.g.L + l) * 2 + s], device_id=who, device_id_type=MESH
        )
        only(when, copy.wait_send if self.drain else copy.start)

    def arrived(self, block, l, s):
        if self.drain:
            return
        place = self.slot(block, l, s)
        pltpu.make_async_remote_copy(
            place, place, self.send_sem.at[0], self.recv_sem.at[(block * self.g.L + l) * 2 + s], device_id=self.g.mate(), device_id_type=MESH
        ).wait_recv()

    def column(self, k, s, own=False):
        g = self.g
        zk = g.nth(k)
        block = g.block(zk, g.x, g.core)
        at = k * self.per_column
        if not own:
            self.arrived(block, g.l, s)
        self.push(at, block, g.l, s, g.at_z(g.z + 1), g.up & (zk <= g.z))
        self.push(at + 1, block, g.l, s, g.at_z(g.z - 1), g.down & (zk >= g.z))
        for i in range(1, g.X):
            self.push(at + 1 + i, block, g.l, s, g.x_other(i)[1])
        for j in range(1, g.L):
            self.push(at + g.X + j, block, g.l, s, g.l_other(j)[1])
        self.push(at + g.X + g.L, block, g.l, s, g.mate())

    def sides(self, k, s):
        g = self.g
        zk = g.nth(k)
        even = lax.rem(zk, 2) == 0
        at = self.at_sides + k * self.per_sides
        for i in range(1, g.X):
            block = g.block(zk, g.x_other(i)[0], g.core)
            self.arrived(block, g.l, s)
            for j in range(1, g.L):
                self.push(at, block, g.l, s, g.l_other(j)[1], g.local(zk) & even)
                at = at + 1
            self.push(at, block, g.l, s, g.mate())
            at = at + 1
        for j in range(1, g.L):
            block = g.block(zk, g.x, g.core)
            l = g.l_other(j)[0]
            self.arrived(block, l, s)
            for i in range(1, g.X):
                self.push(at, block, l, s, g.x_other(i)[1], g.local(zk) & jnp.logical_not(even))
                at = at + 1
            self.push(at, block, l, s, g.mate())
            at = at + 1

    def corners(self, z, s, local):
        g = self.g
        q = lax.rem(z, 2) + (0 if local else 2)
        for i in range(1, g.X):
            block = g.block(z, lax.rem(g.x + i, g.X), g.core)
            for j in range(1, g.L):
                l = g.l_other(j)[0]
                at = self.at_corners + ((q * (g.X - 1) + i - 1) * (g.L - 1) + j - 1) * 2
                self.arrived(block, l, s)
                if local:
                    self.push(at, block, l, s, g.at_z(g.pair_z()))
                self.push(at + 1, block, l, s, g.mate())

    def mates(self, z, x):
        for l in range(self.g.L):
            for s in range(len(self.cuts)):
                self.arrived(self.g.block(z, x, 1 - self.g.core), l, s)

    def begin(self):
        for s in range(len(self.cuts)):
            self.column(0, s, own=True)

    def wave(self, k, s):
        g = self.g
        pl.when(k < 3)(lambda: self.column(k + 1, s))
        pl.when(k < 4)(lambda: self.sides(k, s))
        if g.L == 1:
            return
        two = len(self.cuts) == 2
        late = 1 - s if two else s
        back = 2 - s if two else 1
        for local, lag in ((True, back), (False, back + 1)):
            who = None if local else g.pair_z()
            kk = k - lag
            z = g.nth(jnp.clip(kk, 0, 3), who)
            pl.when((kk >= 0) & (kk < 4) & g.local(z, who))(lambda z=z, local=local: self.corners(z, late, local))

    def due(self, k, c):
        g = self.g
        own = c == 0
        far = c > g.X - 1
        off = jnp.where(own, 0, lax.rem(c - 1, max(g.X - 1, 1)) + 1)
        kk = jnp.where(own, k - 1, jnp.where(far, k - 3, k - 2))
        who = jnp.where(far, g.pair_z(), g.z)
        z = g.nth(jnp.clip(kk, 0, 3), who)
        there = (kk >= 0) & (kk < 4) & (own | g.local(z, who))
        return z, lax.rem(g.x + off, g.X), there

    def run(self, work=None, meanwhile=None):
        g = self.g
        parts = 2 * g.X - 1
        self.begin()

        def one(i, done):
            k, c = i // parts, lax.rem(i, parts)
            for s in range(len(self.cuts)):
                pl.when(c == s)(lambda s=s: self.wave(k, s))
            if meanwhile is not None:
                for at in range(3):
                    pl.when(i == at)(lambda at=at: meanwhile(at))
            z, x, there = self.due(k, c)

            def ready():
                self.mates(z, x)
                if work is not None:
                    work(z, x, done)

            pl.when(there)(ready)
            return done + there.astype(jnp.int32)

        lax.fori_loop(0, 7 * parts, one, jnp.int32(0))

    def finish(self):
        self.drain = True
        self.begin()

        def one(k, carry):
            for s in range(len(self.cuts)):
                self.wave(k, s)
            return carry

        lax.fori_loop(0, 7, one, 0)


class Courier:
    def __init__(self, grid, table, h, cuts, send_sem, recv_sem):
        self.g, self.table, self.h = grid, table, h
        self.cuts = cuts
        self.size = h // self.cuts
        self.send_sem, self.recv_sem = send_sem, recv_sem
        self.drain = False

    @staticmethod
    def kinds(levels, rows):
        X, L = rows // 8, levels
        return (X + L + 1, (X - 1) * L, (L - 1) * X, 3 * (X - 1) * (L - 1))

    @staticmethod
    def sends(levels, rows, cuts):
        return 4 * sum(Courier.kinds(levels, rows)) * cuts

    @staticmethod
    def receives(levels, rows, cuts):
        return levels * rows * cuts

    def at(self, kind, zk, n, s):
        counts = self.kinds(self.g.L, self.g.R)
        return (4 * sum(counts[:kind]) + zk * counts[kind] + n) * self.cuts + s

    def slot(self, block, l, s=0, size=None):
        start = (block * self.g.L + l) * self.h + s * self.size
        return self.table.at[pl.ds(pl.multiple_of(start, 16), size or self.size)]

    def own(self):
        return self.slot(self.g.row, self.g.l, 0, self.h)

    def push(self, at, block, l, s, who, when=None):
        place = self.slot(block, l, s)
        copy = pltpu.make_async_remote_copy(
            place,
            place,
            self.send_sem.at[at],
            self.recv_sem.at[(block * self.g.L + l) * self.cuts + s],
            device_id=who,
            device_id_type=MESH,
        )
        only(when, copy.wait_send if self.drain else copy.start)

    def arrived(self, block, l, s):
        if self.drain:
            return
        place = self.slot(block, l, s)
        pltpu.make_async_remote_copy(
            place,
            place,
            self.send_sem.at[0],
            self.recv_sem.at[(block * self.g.L + l) * self.cuts + s],
            device_id=self.g.mate(),
            device_id_type=MESH,
        ).wait_recv()

    def near(self, zk):
        z = self.g.z
        return (zk == z) | ((z == 0) & (zk == 1)) | ((z == 3) & (zk == 2))

    def even(self, zk):
        return lax.rem(jnp.where(self.g.z < 2, zk, 3 - zk), 2) == 0

    def column(self, zk, s, own=False):
        g = self.g
        block = g.block(zk, g.x, g.core)
        if not own:
            self.arrived(block, g.l, s)
        self.push(self.at(0, zk, 0, s), block, g.l, s, g.at_z(g.z + 1), g.up & (zk <= g.z))
        self.push(self.at(0, zk, 1, s), block, g.l, s, g.at_z(g.z - 1), g.down & (zk >= g.z))
        for i in range(1, g.X):
            self.push(self.at(0, zk, 1 + i, s), block, g.l, s, g.x_other(i)[1])
        for j in range(1, g.L):
            self.push(self.at(0, zk, g.X + j, s), block, g.l, s, g.l_other(j)[1])
        self.push(self.at(0, zk, g.X + g.L, s), block, g.l, s, g.mate())

    def side_x(self, zk, s):
        g = self.g
        n = 0
        for i in range(1, g.X):
            block = g.block(zk, g.x_other(i)[0], g.core)
            self.arrived(block, g.l, s)
            for j in range(1, g.L):
                self.push(self.at(1, zk, n, s), block, g.l, s, g.l_other(j)[1], self.near(zk) & self.even(zk))
                n += 1
            self.push(self.at(1, zk, n, s), block, g.l, s, g.mate())
            n += 1

    def side_l(self, zk, s):
        g = self.g
        block = g.block(zk, g.x, g.core)
        n = 0
        for j in range(1, g.L):
            l = g.l_other(j)[0]
            self.arrived(block, l, s)
            for i in range(1, g.X):
                self.push(self.at(2, zk, n, s), block, l, s, g.x_other(i)[1], self.near(zk) & jnp.logical_not(self.even(zk)))
                n += 1
            self.push(self.at(2, zk, n, s), block, l, s, g.mate())
            n += 1

    def corner(self, zk, s):
        g = self.g
        n = 0
        for i in range(1, g.X):
            block = g.block(zk, g.x_other(i)[0], g.core)
            for j in range(1, g.L):
                l = g.l_other(j)[0]
                self.arrived(block, l, s)
                self.push(self.at(3, zk, n, s), block, l, s, g.at_z(g.z + 1), (zk <= 1) & (g.z >= zk) & g.up)
                self.push(self.at(3, zk, n + 1, s), block, l, s, g.at_z(g.z - 1), (zk >= 2) & (g.z <= zk) & g.down)
                self.push(self.at(3, zk, n + 2, s), block, l, s, g.mate())
                n += 3

    def mates(self, zk, x):
        def one(i, carry):
            self.arrived(self.g.block(zk, x, 1 - self.g.core), i // self.cuts, lax.rem(i, self.cuts))
            return carry

        lax.fori_loop(0, self.g.L * self.cuts, one, 0)

    def run(self, tables, meanwhile=None, prepare=None, work=None):
        g = self.g
        for s in range(self.cuts):
            self.column(g.z, s, own=True)
        low = g.z < 2
        first = (g.z == 0) | (g.z == 3)

        def one(m, done):
            word = jnp.int32(0)
            for at, (a, b) in enumerate(zip(*tables)):
                word = jnp.where(m // 3 == at, jnp.where(first, a, b), word)
            byte = lax.rem(m, 3)
            code = lax.rem(jnp.where(byte == 0, word, jnp.where(byte == 1, word // 128, word // 16384)), 128)
            zk = lax.rem(code // 4, 4)
            zk = jnp.where(low, zk, 3 - zk)
            s = lax.rem(code, 4)
            kind = code // 16
            pl.when(kind == 0)(lambda: self.column(zk, s))
            if g.X > 1:
                pl.when(kind == 1)(lambda: self.side_x(zk, s))
            if g.L > 1:
                pl.when(kind == 2)(lambda: self.side_l(zk, s))
            if g.X > 1 and g.L > 1:
                pl.when(kind == 3)(lambda: self.corner(zk, s))
            if meanwhile is not None:
                for at in range(3):
                    pl.when(code == 64 + at)(lambda at=at: meanwhile(at))
            count = jnp.int32(0)
            if work is not None:
                for off in range(g.X):
                    x = lax.rem(g.x + off, g.X)
                    hit = s == (0 if off == 0 else 1)
                    pl.when((kind == 5) & hit)(lambda x=x: prepare(zk, x))

                    def full(x=x, off=off):
                        self.mates(zk, x)
                        work(zk, x, done + max(off - 1, 0))

                    pl.when((kind == 6) & hit)(full)
                count = jnp.where(kind == 6, jnp.where(s == 0, 1, g.X - 1), 0)
            return done + count

        lax.fori_loop(0, 3 * len(tables[0]), one, jnp.int32(0))
        if work is None:

            def last(i, carry):
                self.mates(i // g.X, lax.rem(i, g.X))
                return carry

            lax.fori_loop(0, 4 * g.X, last, 0)

    def finish(self):
        self.drain = True

        def one(i, carry):
            zk, s = i // self.cuts, lax.rem(i, self.cuts)
            self.column(zk, s)
            self.side_x(zk, s)
            self.side_l(zk, s)
            self.corner(zk, s)
            return carry

        lax.fori_loop(0, 4 * self.cuts, one, 0)


class Scatter:
    def __init__(self, grid, stage, inbox, h, send_sem, recv_sem):
        self.g, self.stage, self.inbox, self.h = grid, stage, inbox, h
        self.cuts = cuts(h)
        self.send_sem, self.recv_sem = send_sem, recv_sem
        X, L = grid.X, grid.L
        at = 0
        self.base = {}
        for name, count in self.parts(X, L):
            self.base[name] = at
            at += count
        at = 0
        self.out = {}
        for name, count in self.out_parts(X, L):
            self.out[name] = at
            at += count
        self.drain = False
        self.prepare()

    @staticmethod
    def parts(X, L):
        side = (X - 1) * (L - 1)
        return (("mate", 4 * X * L), ("pair", 2 * side), ("l2", side), ("x2", side), ("xc", 4 * (X - 1)), ("lc", 4 * (L - 1)), ("z", 5))

    @staticmethod
    def out_parts(X, L):
        side = (X - 1) * (L - 1)
        return (("mate", 4 * X * L), ("corner", 8 * side), ("xc", 4 * (X - 1)), ("lc", 4 * (L - 1)), ("z", 4))

    @staticmethod
    def receives(levels, rows):
        return sum(count for _, count in Scatter.parts(rows // 8, levels))

    @staticmethod
    def sends(levels, rows):
        return 2 * sum(count for _, count in Scatter.out_parts(rows // 8, levels))

    def slot(self, block, l, s=None):
        start, size = (0, self.h) if s is None else self.cuts[s]
        return self.stage.at[pl.ds(pl.multiple_of((block * self.g.L + l) * self.h + start, 16), size)]

    def push(self, out, block, l, s, at, who, when=None):
        start, size = self.cuts[s]
        copy = pltpu.make_async_remote_copy(
            self.slot(block, l, s),
            self.inbox.at[at, pl.ds(start, size)],
            self.send_sem.at[2 * out + s],
            self.recv_sem.at[2 * at + s],
            device_id=who,
            device_id_type=MESH,
        )
        only(when, copy.wait_send if self.drain else copy.start)

    def arrived(self, at, s):
        start, size = self.cuts[s]
        place = self.inbox.at[at, pl.ds(start, size)]
        pltpu.make_async_remote_copy(
            place, place, self.send_sem.at[0], self.recv_sem.at[2 * at + s], device_id=self.g.mate(), device_id_type=MESH
        ).wait_recv()

    def total(self, block, l, s, ats):
        start, size = self.cuts[s]
        for at in ats:
            self.arrived(at, s)
        out = self.slot(block, l, s)[...].astype(F32)
        for at in ats:
            out = out + self.inbox[at, start : start + size].astype(F32)
        return out

    def add(self, block, l, s, ats, when=None):
        if self.drain:
            return

        def act():
            self.slot(block, l, s)[...] = self.total(block, l, s, ats).astype(BF16)

        only(when, act)

    def each(self):
        return range(len(self.cuts))

    def to_mate(self, z, x):
        g = self.g
        for l in range(g.L):
            at = (z * g.X + x) * g.L + l
            for s in self.each():
                self.push(self.out["mate"] + at, g.block(z, x, 1 - g.core), l, s, self.base["mate"] + at, g.mate())

    def from_mate(self, z, x):
        g = self.g
        for l in range(g.L):
            for s in self.each():
                self.add(g.block(z, x, g.core), l, s, [self.base["mate"] + (z * g.X + x) * g.L + l])

    def corner_far(self, z, i):
        g = self.g
        block = g.block(z, lax.rem(g.x + i, g.X), g.core)
        for j in range(1, g.L):
            l = g.l_other(j)[0]
            spot = (lax.rem(z, 2) * (g.X - 1) + i - 1) * (g.L - 1) + j - 1
            for s in self.each():
                self.push(self.out["corner"] + spot, block, l, s, self.base["pair"] + spot, g.at_z(g.pair_z()))

    def corner_near(self, z, i):
        g = self.g
        x, x_dev = g.x_other(i)
        block = g.block(z, x, g.core)
        even = lax.rem(z, 2) == 0
        side = (g.X - 1) * (g.L - 1)
        for j in range(1, g.L):
            l, l_dev = g.l_other(j)
            spot = (lax.rem(z, 2) * (g.X - 1) + i - 1) * (g.L - 1) + j - 1
            out = self.out["corner"] + 2 * side + spot
            for s in self.each():
                self.add(block, l, s, [self.base["pair"] + spot])
                self.push(out, block, l, s, self.base["l2"] + (i - 1) * (g.L - 1) + g.L - j - 1, l_dev, even)
                self.push(out, block, l, s, self.base["x2"] + (g.X - i - 1) * (g.L - 1) + j - 1, x_dev, jnp.logical_not(even))

    def side_x(self, zk, i, waits):
        g = self.g
        x, x_dev = g.x_other(i)
        block = g.block(zk, x, g.core)
        ats = [self.base["l2"] + (i - 1) * (g.L - 1) + j - 1 for j in range(1, g.L)]
        for s in self.each():
            if ats and waits:
                self.add(block, g.l, s, ats)
            self.push(self.out["xc"] + zk * (g.X - 1) + i - 1, block, g.l, s, self.base["xc"] + zk * (g.X - 1) + g.X - i - 1, x_dev)

    def side_l(self, zk, waits):
        g = self.g
        block = g.block(zk, g.x, g.core)
        for j in range(1, g.L):
            l, l_dev = g.l_other(j)
            ats = [self.base["x2"] + (i - 1) * (g.L - 1) + j - 1 for i in range(1, g.X)]
            for s in self.each():
                if waits:
                    self.add(block, l, s, ats)
                self.push(self.out["lc"] + zk * (g.L - 1) + j - 1, block, l, s, self.base["lc"] + zk * (g.L - 1) + g.L - j - 1, l_dev)

    def around(self, zk):
        g = self.g
        ats = [self.base["xc"] + zk * (g.X - 1) + i - 1 for i in range(1, g.X)]
        return ats + [self.base["lc"] + zk * (g.L - 1) + j - 1 for j in range(1, g.L)]

    def column(self, zk):
        g = self.g
        block = g.block(zk, g.x, g.core)
        behind = jnp.where(zk > g.z, g.down, g.up)
        near = jnp.abs(zk - g.z) == 1
        spot = jnp.where(near & (zk < g.z), 4, zk)
        for s in self.each():
            self.add(block, g.l, s, self.around(zk))
            self.add(block, g.l, s, [self.base["z"] + zk], behind)
            self.push(self.out["z"] + zk, block, g.l, s, self.base["z"] + spot, g.at_z(jnp.where(zk > g.z, g.z + 1, g.z - 1)))

    def last(self, out):
        g = self.g
        for s in self.each():
            start, size = self.cuts[s]
            out[start : start + size, :] = self.total(g.row, g.l, s, self.around(g.z))
            for at, there in ((self.base["z"] + g.z, g.down), (self.base["z"] + 4, g.up)):

                def take(at=at, s=s, start=start, size=size):
                    self.arrived(at, s)
                    out[start : start + size, :] += self.inbox[at, start : start + size].astype(F32)

                pl.when(there)(take)

    @staticmethod
    def plan(X, hop=2):
        orders, spots = [], []
        for z in range(4):
            corners = (3, 2, 1, 0) if z < 2 else (0, 1, 2, 3)
            own = tuple(reversed(NEAREST[z]))
            order = []
            for j in range(4):
                order += [(corners[j], off) for off in range(1, X)] + [(own[j], 0)]
            orders.append(order)
            spots.append(({zk: max(m for m, (a, off) in enumerate(order) if a == zk and off) for zk in range(4)},
                          {zk: order.index((zk, 0)) for zk in range(4)}))
        names = ("far", "sx", "sl", "near", "sx_late", "sl_late", "column")
        due = [{name: {} for name in names} for _ in range(4)]

        def put(z, name, zk, step):
            while step in due[z][name]:
                step += 1
            due[z][name][step] = zk
            return step

        sides = [{}, {}, {}, {}]
        for z in range(4):
            pair = z + 1 - 2 * (z % 2)
            for zk in sorted(range(4), key=lambda a: spots[z][0][a]):
                near = zk // 2 == z % 2
                corner, own = spots[z][0][zk] + 1, spots[z][1][zk] + 1
                ready = put(z, "near", zk, max(corner, spots[pair][0][zk] + 1 + hop)) if near else put(z, "far", zk, corner)
                sx = put(z, "sx_late", zk, ready + hop) if near and zk % 2 == 0 else put(z, "sx", zk, corner)
                sl = put(z, "sl_late", zk, max(ready + hop, own)) if near and zk % 2 else put(z, "sl", zk, own)
                sides[z][zk] = max(sx, sl)
        for zk in range(4):
            for chain in (range(0, zk), range(3, zk, -1)):
                before = 0
                for z in chain:
                    before = put(z, "column", zk, max(sides[z][zk], before) + hop)
        steps = 1 + max(step for z in range(4) for name in names for step in due[z][name])
        return orders, due, steps

    def prepare(self):
        self.orders, self.due, self.steps = self.plan(self.g.X)
        self.blocks = 4 * self.g.X

    def pick(self, tables, m):
        out = jnp.int32(-1)
        for z in range(4):
            for at, value in tables[z].items():
                out = jnp.where((self.g.z == z) & (m == at), value, out)
        return out

    def place(self, m):
        g = self.g
        code = self.pick([{at: zk * g.X + off for at, (zk, off) in enumerate(order)} for order in self.orders], m)
        return code // g.X, lax.rem(g.x + lax.rem(code, g.X), g.X)

    def step(self, m):
        g = self.g

        def first():
            self.to_mate(*self.place(m))

        def second():
            self.from_mate(*self.place(m - 1))

        pl.when(m < self.blocks)(first)
        pl.when((m >= 1) & (m <= self.blocks))(second)

        def send(name, act, over_x):
            zk = self.pick([due[name] for due in self.due], m)

            def go():
                if over_x:
                    for i in range(1, g.X):
                        act(zk, i)
                else:
                    act(zk)

            pl.when(zk >= 0)(go)

        send("column", self.column, False)
        send("sl_late", lambda zk: self.side_l(zk, True), False)
        send("sx_late", lambda zk, i: self.side_x(zk, i, True), True)
        if g.L > 1:
            send("near", self.corner_near, True)
            send("far", self.corner_far, True)
        send("sl", lambda zk: self.side_l(zk, False), False)
        send("sx", lambda zk, i: self.side_x(zk, i, False), True)

    def go(self, m, ahead):
        self.step(m)

        def wait():
            self.drain = True
            self.step(m - ahead)
            self.drain = False

        pl.when(m >= ahead)(wait)

    def run(self, work=None, ahead=4, steps=None):
        def one(m, carry):
            if work is not None:
                work(m)
            self.go(m, ahead)
            return carry

        self.steps = steps or self.steps
        self.ahead = ahead
        lax.fori_loop(0, self.steps, one, 0)

    def finish(self):
        self.drain = True

        def one(m, carry):
            self.step(m)
            return carry

        lax.fori_loop(self.steps - self.ahead, self.steps, one, 0)


def dot(left, right):
    return jnp.dot(left, right, preferred_element_type=F32)


def dot_nt(left, right):
    return lax.dot_general(left, right, (((1,), (1,)), ((), ())), preferred_element_type=F32)


def dot_tn(left, right):
    return lax.dot_general(left, right, (((0,), (0,)), ((), ())), preferred_element_type=F32)


def fold(values):
    rows, width = values.shape
    return jnp.sum(values.reshape(rows // 8, 8, width), axis=0)


def norm_parts(values):
    average = jnp.mean(values, axis=-1, keepdims=True)
    centered = values - average
    scale = lax.rsqrt(jnp.mean(centered * centered, axis=-1, keepdims=True) + NORM_EPS)
    return centered * scale, scale


def norm_back(normed, scale, d_normed):
    mean_d = jnp.mean(d_normed, axis=-1, keepdims=True)
    mean_dn = jnp.mean(d_normed * normed, axis=-1, keepdims=True)
    return scale * (d_normed - mean_d - normed * mean_dn)


def silu_back(pre, d_active):
    gate = lax.logistic(pre)
    return d_active * (gate * (1.0 + pre * (1.0 - gate)))


def find_places(row_total, node_count, some, senders, receivers, live, place, side, facts_out, counts):
    tiles = senders.shape[0]
    group = tiles * 128 // row_total
    first = lax.axis_index("row") * node_count
    lane = lax.broadcasted_iota(jnp.int32, (128, 128), 1)
    sub = lax.broadcasted_iota(jnp.int32, (128, 128), 0)
    before = (sub < lane).astype(BF16)
    owner_ids = lax.broadcasted_iota(jnp.int32, (row_total, 128), 0)
    carry = owner_ids[:, :1].astype(F32) * group if some[0] == 0 else counts[:, 0:1]
    for tile in some:
        send = senders[tile : tile + 1, :]
        recv = receivers[tile : tile + 1, :] - first
        owner = lax.div(send, node_count)
        local = send - owner * node_count
        mine = owner_ids == owner
        ranks = dot(mine.astype(BF16), before) + carry
        spot = jnp.sum(jnp.where(mine, ranks, 0.0), axis=0, keepdims=True)
        carry = carry + jnp.sum(mine.astype(F32), axis=1, keepdims=True)
        place[tile : tile + 1, :] = spot.astype(jnp.int32)
        alive = (lane[:1] + tile * 128 < live[0, 0]).astype(jnp.int32)
        facts = jnp.where(sub == 0, lax.div(local, 16), 0)
        facts = jnp.where(sub == 1, lax.rem(local, 16), facts)
        facts = jnp.where(sub == 2, lax.div(recv, 16), facts)
        facts = jnp.where(sub == 3, lax.rem(recv, 16), facts)
        facts = jnp.where(sub == 4, alive, facts).astype(F32)
        side[:, pl.ds(tile * 128, 128)] = facts[:16].astype(BF16)
        facts_out[pl.ds(tile * 128, 128), :] = facts.T.astype(BF16)
    counts[...] = jnp.broadcast_to(carry, counts.shape)


def picker(place, start, size):
    ids = lax.broadcasted_iota(jnp.int32, (size, 128), 0) + start
    return jnp.concatenate([(ids == place[tile : tile + 1, :]).astype(BF16) for tile in range(place.shape[0])], axis=1)


def one_hot_cols(ids, count):
    lanes = lax.broadcasted_iota(jnp.int32, (ids.shape[0], count), 1).astype(F32)
    return (ids == lanes).astype(BF16)


def one_hot_rows(ids, count):
    subs = lax.broadcasted_iota(jnp.int32, (count, ids.shape[1]), 0).astype(F32)
    return (ids == subs).astype(BF16)


def load_all(pairs, sems):
    copies = [pltpu.make_async_copy(src, dst, sems.at[i]) for i, (src, dst) in enumerate(pairs)]
    for copy in copies:
        copy.start()
    return copies


def forward_kernel(
    layer, levels, rows, first_layer, *refs
):
    (node, b1, b2, gain, shift, nb1, nb2, ngain, nshift, w1_all, w2_all, nw1_all, nw2_all, plain_all) = refs[:14]
    refs = refs[14:]
    if first_layer:
        senders, receivers, live = refs[:3]
        refs = refs[3:]
    else:
        place, rows_of, cols_all, edges_all, before_all = refs[:5]
        refs = refs[5:]
    sent_out, pre_out, normed_out, update_out, moved_out = refs[:5]
    refs = refs[5:]
    if first_layer:
        edges_out, place, rows_of, cols = refs[:4]
        refs = refs[4:]
    scale_out, block_out, node_out, recv_out, npre_out, nnormed_out, nscale_out, tally = refs[:8]
    (
        table, total, cast, near, far, w1, w2, nw1, nw2, plain, joined, ordered, out_buf, scale_buf,
        load_sem, out_sem, moved_sem, send_sem, recv_sem, near_send, near_recv,
    ) = refs[8:29]
    if first_layer:
        side, counts = refs[29:]
    else:
        cols, edges, before = refs[29:]
    g = Grid(levels, rows)
    h, width = node_out.shape
    if first_layer:
        node = node.at[pl.ds(pl.multiple_of(g.l * h, h), h)]
    count = plain.shape[0]
    group = count // rows
    node_count = h * levels
    pairs = ((plain_all, plain), (w1_all.at[layer], w1), (w2_all.at[layer], w2), (nw1_all.at[layer], nw1), (nw2_all.at[layer], nw2))
    if not first_layer:
        pairs += ((cols_all, cols), (edges_all, edges), (before_all, before))
    loads = load_all(pairs, load_sem)
    ag = Courier(g, table, h, 2, send_sem, recv_sem)
    ag.own()[...] = node[...].astype(BF16)
    tally[...] = jnp.zeros_like(tally)
    total[...] = jnp.zeros_like(total)
    g.greet()
    wide = lambda ref: ref[layer : layer + 1, :]
    outs = (sent_out, pre_out, normed_out, update_out) + ((edges_out,) if first_layer else ())

    def meanwhile(at):
        if first_layer:
            tiles = place.shape[0]
            some = range(at * tiles // 3, (at + 1) * tiles // 3)
            find_places(rows, node_count, some, senders, receivers, live, place, side, joined.at[:, pl.ds(width, 128)], counts)
        if at == 0:
            for copy in loads:
                copy.wait()

        def cast_rows(i, carry):
            part = pl.ds(pl.multiple_of(i * 2 * group, 2 * group), 2 * group)
            joined[part, 0:width] = plain[part, :].astype(BF16)
            return carry

        lax.fori_loop(at * rows // 6, (at + 1) * rows // 6, cast_rows, 0)

    def leave(n, part):
        slot = lax.rem(n, 2)
        copies = [pltpu.make_async_copy(out_buf.at[slot, i], ref.at[part], out_sem.at[slot, i]) for i, ref in enumerate(outs)]
        return copies + [pltpu.make_async_copy(scale_buf.at[slot], scale_out.at[part], out_sem.at[slot, 5])]

    def spot(z, x):
        pair = g.block(z, x, 0)
        first = pl.multiple_of(pair * group, 2 * group)
        return pair, first, pl.ds(first, 2 * group)

    def moved_copy(z, x):
        part = spot(z, x)[2]
        return pltpu.make_async_copy(ordered.at[part], moved_out.at[part], moved_sem.at[z * g.X + x])

    def prepare(z, x):
        pair, first, part = spot(z, x)
        pick = picker(place, first, 2 * group)
        moved = dot(pick, joined[...])
        ordered[part, :] = moved[:, :width].astype(BF16)
        moved_copy(z, x).start()
        if first_layer:
            digits = moved[:, width:]
            lanes = lax.broadcasted_iota(jnp.int32, digits.shape, 1)
            ids = digits[:, 0:1] * 16.0 + digits[:, 1:2]
            got = digits[:, 2:3] * 16.0 + digits[:, 3:4]
            cols[part, :] = jnp.where(lanes == 0, ids, jnp.where(lanes == 1, got, jnp.where(lanes == 2, digits[:, 4:5], 0.0)))
            for half in range(2):
                digits = dot_nt(side[...], pick[half * group : (half + 1) * group])
                rows_of[pair + half] = jnp.concatenate(
                    [digits[0:1] * 16.0 + digits[1:2], digits[2:3] * 16.0 + digits[3:4], digits[4:10]], axis=0
                )

    def work(z, x, n):
        def own():
            here = table[pl.ds(pl.multiple_of(g.row * node_count, 16), node_count), :]
            cast[...] = dot(here, w1[2 * width :, :]).astype(BF16)
            block_out[...] = here

        pl.when(n == 0)(own)
        pair, first, part = spot(z, x)

        def free():
            for copy in leave(n, part):
                copy.wait()

        pl.when(n >= 2)(free)
        slot = lax.rem(n, 2)
        low = ordered[part, :] if first_layer else edges[part, :]
        cols_here = cols[part, :]
        send_pick = one_hot_cols(cols_here[:, 0:1], node_count)
        recv_pick = one_hot_cols(cols_here[:, 1:2], node_count)
        start = pl.multiple_of(pair * node_count, 16)
        sent = jnp.concatenate(
            [
                dot(send_pick[:group], table[pl.ds(start, node_count), :]).astype(BF16),
                dot(send_pick[group:], table[pl.ds(start + node_count, node_count), :]).astype(BF16),
            ],
            axis=0,
        )
        out_buf[slot, 0] = sent
        pre = dot(low, w1[:width, :]) + dot(sent, w1[width : 2 * width, :]) + dot(recv_pick, cast[...]) + wide(b1)
        out_buf[slot, 1] = pre.astype(BF16)
        active = (pre * lax.logistic(pre)).astype(BF16)
        normed, scale = norm_parts(dot(active, w2[...]) + wide(b2))
        out_buf[slot, 2] = normed.astype(BF16)
        scale_buf[slot] = jnp.broadcast_to(scale, (2 * group, 128))
        update = (normed * wide(gain) + wide(shift)) * cols_here[:, 2:3]
        update_low = update.astype(BF16)
        edge = low.astype(F32) + update
        if first_layer:
            out_buf[slot, 3] = update_low
            out_buf[slot, 4] = edge.astype(BF16)
        else:
            out_buf[slot, 3] = (before[part, :].astype(F32) + update).astype(BF16)
        tally[8:16, :] += fold(edge * edge)
        tally[16:24, :] += fold(update * update)
        for half in range(2):
            pick = one_hot_rows(rows_of[pair + half][1:2, :], node_count)
            total[...] += dot(pick, update_low[half * group : (half + 1) * group])
        for copy in leave(n, part):
            copy.start()

    ag.run(WORK_ORDER, meanwhile, prepare, work)
    copies = []
    for j in range(1, levels):
        l, l_dev = g.l_other(j)
        near[j - 1] = total[pl.ds(pl.multiple_of(l * h, h), h), :].astype(BF16)
        copy = pltpu.make_async_remote_copy(
            near.at[j - 1], far.at[levels - 1 - j], near_send.at[j - 1], near_recv.at[levels - 1 - j], device_id=l_dev, device_id_type=MESH
        )
        copy.start()
        copies.append(copy)
    received = total[pl.ds(pl.multiple_of(g.l * h, h), h), :]
    npre = dot(node[...].astype(BF16), nw1[:width, :]) + wide(nb1)
    for copy in copies:
        copy.wait()
    for j in range(1, levels):
        received = received + far[j - 1].astype(F32)
    received = received.astype(BF16)
    recv_out[...] = received
    npre = npre + dot(received, nw1[width:, :])
    npre_out[...] = npre
    nnormed, nscale = norm_parts(dot((npre * lax.logistic(npre)).astype(BF16), nw2[...]) + wide(nb2))
    nnormed_out[...] = nnormed
    nscale_out[...] = jnp.broadcast_to(nscale, (h, 128))
    change = nnormed * wide(ngain) + wide(nshift)
    new = node[...] + change
    node_out[...] = new
    tally[0:8, :] = fold(new * new)
    tally[24:32, :] = fold(change * change)
    for n in range(2):
        for copy in leave(n, pl.ds(0, 2 * group)):
            copy.wait()
    for n in range(4 * g.X):
        moved_copy(n // g.X, n % g.X).wait()
    ag.finish()


def forward_layer(layer, node, small, weights, plain, index, edges=None, before=None):
    levels, rows = lax.axis_size("lvl"), lax.axis_size("row")
    width = node.shape[1]
    h = node.shape[0] // (levels if layer == 0 else 1)
    count = plain.shape[0]
    group = count // rows
    vmem = pl.BlockSpec(memory_space=pltpu.VMEM)
    hbm = pl.BlockSpec(memory_space=pl.ANY)
    first_layer = layer == 0
    shape = jax.ShapeDtypeStruct
    wide = shape((count, width), BF16)
    ins = (node,) + small + weights + (plain,) + index
    in_specs = [vmem] * 9 + [hbm] * 5
    outs = [wide] * 5
    out_specs = [hbm] * 5
    scratch = []
    if first_layer:
        in_specs += [vmem, vmem, pl.BlockSpec(memory_space=pltpu.SMEM)]
        outs += [wide, shape(index[0].shape, jnp.int32), shape((rows, 8, group), F32), shape((count, 128), F32)]
        out_specs += [hbm, vmem, vmem, vmem]
        scratch = [pltpu.VMEM((16, count), BF16), pltpu.VMEM((rows, 128), F32)]
    else:
        ins += (edges, before)
        in_specs += [vmem, vmem, hbm, hbm, hbm]
        scratch = [pltpu.VMEM((count, 128), F32), pltpu.VMEM((count, width), BF16), pltpu.VMEM((count, width), BF16)]
    outs += [
        shape((count, 128), F32),
        shape((h * levels, width), BF16),
        shape((h, width), F32),
        shape((h, width), BF16),
        shape((h, width), F32),
        shape((h, width), F32),
        shape((h, 128), F32),
        shape((32, width), F32),
    ]
    out_specs += [hbm] + [vmem] * 7
    others = max(levels - 1, 1)
    return pl.pallas_call(
        functools.partial(forward_kernel, layer, levels, rows, first_layer),
        out_shape=outs,
        in_specs=in_specs,
        out_specs=out_specs,
        scratch_shapes=[
            pltpu.VMEM((rows * h * levels, width), BF16),
            pltpu.VMEM((h * levels, width), F32),
            pltpu.VMEM((h * levels, width), BF16),
            pltpu.VMEM((others, h, width), BF16),
            pltpu.VMEM((others, h, width), BF16),
        ]
        + [pltpu.VMEM(weight.shape[1:], BF16) for weight in weights]
        + [
            pltpu.VMEM((count, width), F32),
            pltpu.VMEM((count, width + (128 if first_layer else 0)), BF16),
            pltpu.VMEM((count, width), BF16),
            pltpu.VMEM((2, 5, 2 * group, width), BF16),
            pltpu.VMEM((2, 2 * group, 128), F32),
            pltpu.SemaphoreType.DMA((8,)),
            pltpu.SemaphoreType.DMA((2, 6)),
            pltpu.SemaphoreType.DMA((rows // 2,)),
            pltpu.SemaphoreType.DMA((Courier.sends(levels, rows, 2),)),
            pltpu.SemaphoreType.DMA((Courier.receives(levels, rows, 2),)),
            pltpu.SemaphoreType.DMA((others,)),
            pltpu.SemaphoreType.DMA((others,)),
        ]
        + scratch,
        compiler_params=pltpu.CompilerParams(collective_id=1 + layer, has_side_effects=True, vmem_limit_bytes=VMEM_BYTES),
        name=f"forward_{layer}",
    )(*ins)


def backward_kernel(
    layer, levels, rows, last_layer, share,
    d_node, block, recv, npre, nnormed, nscale, rows_of, gain, ngain, node, d_before, cols_all, scale_all, d_edges, pre, normed, edges, sent,
    w1_all, w2_all, nw1_all, nw2_all, other_grads,
    d_node_out, d_edges_out, d_change_out, grads, tally, node_all, other_out,
    stage, inbox, bufs, d_recv, turned, own_sum, out_buf, cols, scale, w1, w2, nw1, nw2,
    load_sem, out_sem, send_sem, recv_sem, near_send, near_recv, *more,
):
    g = Grid(levels, rows)
    h, width = d_node_out.shape
    if last_layer:
        d_node = d_node.at[pl.ds(pl.multiple_of(g.l * h, h), h)]
    count = pre.shape[0]
    group = count // rows
    node_count = h * levels
    loads = load_all(
        ((nw2_all.at[layer], nw2), (nw1_all.at[layer], nw1), (w1_all.at[layer], w1), (w2_all.at[layer], w2))
        + tuple((src, bufs.at[i]) for i, src in enumerate((d_edges, pre, normed, edges, sent)))
        + ((cols_all, cols), (scale_all, scale)),
        load_sem,
    )
    if share:
        other_stage, other_inbox, other_total, other_send, other_recv, other_sem = more
        other_load = pltpu.make_async_copy(other_grads, other_stage, other_sem)
        other_load.start()
        other = Scatter(g, other_stage, other_inbox, share, other_send, other_recv)
        early = other.steps // 2
    rs = Scatter(g, stage, inbox, h, send_sem, recv_sem)
    wide = lambda ref: ref[layer : layer + 1, :]
    mine = pl.ds(pl.multiple_of(g.l * h, h), h)
    own_sum[...] = jnp.zeros_like(own_sum)
    tally[...] = jnp.zeros_like(tally)
    for copy in loads[:2]:
        copy.wait()
    tally[48:56, :] = fold(d_node[...] * nnormed[...])
    tally[56:64, :] = fold(d_node[...])
    d_two = norm_back(nnormed[...], nscale[:, 0:1], d_node[...] * wide(ngain)).astype(BF16)
    tally[40:48, :] = fold(d_two.astype(F32))
    d_one = silu_back(npre[...], dot_nt(d_two, nw2[...])).astype(BF16)
    tally[32:40, :] = fold(d_one.astype(F32))
    d_recv[mine, :] = dot_nt(d_one, nw1[width:, :]).astype(BF16)
    g.greet()
    copies = []
    for j in range(1, levels):
        copy = pltpu.make_async_remote_copy(
            d_recv.at[mine], d_recv.at[mine], near_send.at[j - 1], near_recv.at[levels - 1 - j], device_id=g.l_other(j)[1], device_id_type=MESH
        )
        copy.start()
        copies.append(copy)
    d_node_out[...] = d_node[...] + dot_nt(d_one, nw1[:width, :])
    active = (npre[...] * lax.logistic(npre[...])).astype(BF16)
    grads[4 * width + width : 6 * width, :] = dot_tn(recv[...], d_one).astype(BF16)
    grads[4 * width : 5 * width, :] = dot_tn(block[mine, :], d_one).astype(BF16)
    grads[6 * width : 7 * width, :] = dot_tn(active, d_two).astype(BF16)
    if last_layer:
        node_all[mine, :] = node[...].astype(BF16)
    if share:
        other_load.wait()

        def first(m, carry):
            other.go(m, 2)
            return carry

        lax.fori_loop(0, early, first, 0)
    for copy in copies:
        copy.wait()
    copies = []
    for j in range(1, levels if last_layer else 1):
        copy = pltpu.make_async_remote_copy(
            node_all.at[mine],
            node_all.at[mine],
            near_send.at[levels + j - 2],
            near_recv.at[2 * levels - 2 - j],
            device_id=g.l_other(j)[1],
            device_id_type=MESH,
        )
        copy.start()
        copies.append(copy)
    for copy in loads[2:]:
        copy.wait()

    def work(i):
        z, x = rs.place(i)
        pair = g.block(z, x, 0)
        start = pl.multiple_of(pair * group, 2 * group)
        place = pl.ds(start, 2 * group)
        if not last_layer:
            earlier = pltpu.make_async_copy(d_before.at[place], out_buf.at[lax.rem(i, 2), 0], out_sem.at[lax.rem(i, 2), 0])
            earlier.start()
        cols_here = cols[place, :]
        recv_pick = one_hot_cols(cols_here[:, 1:2], node_count)
        d_edge = bufs[0, place, :].astype(F32)
        d_update = (d_edge + dot(recv_pick, d_recv[...])) * cols_here[:, 2:3]
        norm_here = bufs[2, place, :].astype(F32)
        tally[16:24, :] += fold(d_update * norm_here)
        tally[24:32, :] += fold(d_update)
        d_two = norm_back(norm_here, scale[place, 0:1], d_update * wide(gain)).astype(BF16)
        tally[8:16, :] += fold(d_two.astype(F32))
        pre_here = bufs[1, place, :].astype(F32)
        gate = lax.logistic(pre_here)
        d_one = (dot_nt(d_two, w2[...]) * (gate * (1.0 + pre_here * (1.0 - gate)))).astype(BF16)
        tally[0:8, :] += fold(d_one.astype(F32))
        bufs[0, place, :] = d_one
        bufs[1, place, :] = (pre_here * gate).astype(BF16)
        bufs[2, place, :] = d_two
        d_here = dot_nt(d_one, w1[:width, :])
        slot = lax.rem(i, 2)
        used = [
            pltpu.make_async_copy(out_buf.at[slot, n], ref.at[place], out_sem.at[slot, n])
            for n, ref in enumerate((d_edges_out, d_change_out))
            if n or last_layer
        ]

        def free():
            for copy in used:
                copy.wait()

        pl.when(i >= 2)(free)
        if last_layer:
            out_buf[slot, 0] = (d_edge + d_here).astype(BF16)
            out_buf[slot, 1] = d_here.astype(BF16)
        else:
            earlier.wait()
            out_buf[slot, 1] = (out_buf[slot, 0].astype(F32) + d_here).astype(BF16)
        for copy in used:
            copy.start()
        d_sent = dot_nt(d_one, w1[width : 2 * width, :]).astype(BF16)
        for half in range(2):
            ids = rows_of[pair + half]
            part = slice(half * group, (half + 1) * group)
            own_sum[...] += dot(one_hot_rows(ids[1:2, :], node_count), d_one[part])
            spot = pl.ds(pl.multiple_of((pair + half) * node_count, 16), node_count)
            stage[spot, :] = dot(one_hot_rows(ids[0:1, :], node_count), d_sent[part]).astype(BF16)

        def close():
            low = own_sum[...].astype(BF16)
            spot = pl.ds(pl.multiple_of(g.row * node_count, 16), node_count)
            stage[spot, :] = (stage[spot, :].astype(F32) + dot_nt(low, w1[2 * width :, :])).astype(BF16)
            grads[2 * width : 3 * width, :] = dot_tn(block[...], low).astype(BF16)

        pl.when(i == rs.blocks - 1)(close)

    def step(m):
        pl.when(m < rs.blocks)(lambda: work(m))
        for n, (at, left, right) in enumerate(((0, 3, 0), (1, 4, 0), (3, 1, 2))):

            def grad(at=at, left=left, right=right):
                grads[at * width : (at + 1) * width, :] = dot_tn(bufs[left], bufs[right]).astype(BF16)

            pl.when(m == rs.blocks + n)(grad)
        if share:
            pl.when(m + early < other.steps)(lambda: other.go(m + early, 2))

    rs.run(step)
    if share:
        other.ahead = 2
        other.last(other_total)
        other_out[...] = other_total[...].astype(BF16)
        other.finish()
    rs.last(turned)
    for copy in copies:
        copy.wait()
    d_node_out[...] += turned[...]
    for slot in range(2):
        for n, ref in enumerate((d_edges_out, d_change_out)):
            if n or last_layer:
                pltpu.make_async_copy(out_buf.at[slot, n], ref.at[pl.ds(0, 2 * group)], out_sem.at[slot, n]).wait()
    rs.finish()


def backward_layer(layer, last_layer, d_node, node_saved, cols, rows_of, scale, small, weights, d_edges, edge_saved, node, d_before, other_grads=None, share=0):
    levels, rows = lax.axis_size("lvl"), lax.axis_size("row")
    width = d_node.shape[1]
    h = d_node.shape[0] // (levels if last_layer else 1)
    count = d_edges.shape[0]
    group = count // rows
    vmem = pl.BlockSpec(memory_space=pltpu.VMEM)
    hbm = pl.BlockSpec(memory_space=pl.ANY)
    shape = jax.ShapeDtypeStruct
    ins = (d_node,) + node_saved + (rows_of,) + small + (node, d_before, cols, scale, d_edges) + edge_saved + weights
    ins += (other_grads if share else d_before,)
    outs = (
        shape((h, width), F32),
        shape((count, width) if last_layer else (16, 128), BF16),
        shape((count, width), BF16),
        shape((7 * width, width), BF16),
        shape((64, width), F32),
        shape((h * levels, width) if last_layer else (16, 128), BF16),
        shape((share, width) if share else (16, 128), BF16),
    )
    others = max(levels - 1, 1)
    return pl.pallas_call(
        functools.partial(backward_kernel, layer, levels, rows, last_layer, share),
        out_shape=outs,
        in_specs=[vmem] * (len(ins) - 13) + [hbm] * 13,
        out_specs=(vmem, hbm, hbm, vmem, vmem, vmem, vmem),
        scratch_shapes=[
            pltpu.VMEM((rows * h * levels, width), BF16),
            pltpu.VMEM((Scatter.receives(levels, rows), h, width), BF16),
            pltpu.VMEM((5, count, width), BF16),
            pltpu.VMEM((h * levels, width), BF16),
            pltpu.VMEM((h, width), F32),
            pltpu.VMEM((h * levels, width), F32),
            pltpu.VMEM((2, 2, 2 * group, width), BF16),
            pltpu.VMEM((count, 128), F32),
            pltpu.VMEM((count, 128), F32),
        ]
        + [pltpu.VMEM(weight.shape[1:], BF16) for weight in weights]
        + [
            pltpu.SemaphoreType.DMA((11,)),
            pltpu.SemaphoreType.DMA((2, 2)),
            pltpu.SemaphoreType.DMA((Scatter.sends(levels, rows),)),
            pltpu.SemaphoreType.DMA((2 * Scatter.receives(levels, rows),)),
            pltpu.SemaphoreType.DMA((2 * others,)),
            pltpu.SemaphoreType.DMA((2 * others,)),
                ]
        + (
            [
                pltpu.VMEM((share * levels * rows, width), BF16),
                pltpu.VMEM((Scatter.receives(levels, rows), share, width), BF16),
                pltpu.VMEM((share, width), F32),
                pltpu.SemaphoreType.DMA((Scatter.sends(levels, rows),)),
                pltpu.SemaphoreType.DMA((2 * Scatter.receives(levels, rows),)),
                pltpu.SemaphoreType.DMA,
            ]
            if share
            else []
        ),
        compiler_params=pltpu.CompilerParams(collective_id=3 + layer, has_side_effects=True, vmem_limit_bytes=VMEM_BYTES),
        name=f"backward_{layer}",
    )(*ins)


def sum_cuts(h):
    return 4 if h % 64 == 0 else 1


def sum_kernel(levels, rows, h, count, share, *refs):
    d_node, place, update, d_change, other_piece = refs[:5]
    terms = refs[5 : count + 5]
    (
        out, d_node_all, update_out, d_change_out, other_out, stage, inbox, total,
        scatter_send, scatter_recv, gather_send, gather_recv, load_sem, near_send, near_recv,
    ) = refs[count + 5 : count + 20]
    g = Grid(levels, rows)
    mine = pl.ds(pl.multiple_of(g.l * d_node.shape[0], d_node.shape[0]), d_node.shape[0])
    d_node_all[mine, :] = d_node[...].astype(BF16)
    pairs = []
    at = 0
    for term in terms:
        pairs.append((term, stage.at[pl.ds(at, term.shape[0])]))
        at += term.shape[0]
    loads = load_all(pairs, load_sem)
    g.greet()
    for copy in loads:
        copy.wait()
    copies = []
    for j in range(1, levels):
        copy = pltpu.make_async_remote_copy(
            d_node_all.at[mine], d_node_all.at[mine], near_send.at[j - 1], near_recv.at[levels - 1 - j], device_id=g.l_other(j)[1], device_id_type=MESH
        )
        copy.start()
        copies.append(copy)
    tiles = place.shape[0]
    size = 256 if tiles % 2 == 0 else 128
    lane = lax.broadcasted_iota(jnp.int32, (128, 128), 1).astype(F32)

    def restore(i):
        pick = []
        for part in range(size // 128):
            spot = jnp.broadcast_to(place[pl.ds(i * (size // 128) + part, 1), :], (128, 128)).astype(F32).T
            pick.append(jnp.concatenate([(spot == lane + float(128 * j)).astype(BF16) for j in range(tiles)], axis=1))
        pick = jnp.concatenate(pick, axis=0)
        here = pl.ds(pl.multiple_of(i * size, size), size)
        update_out[here, :] = dot(pick, update[...]).astype(BF16)
        d_change_out[here, :] = dot(pick, d_change[...]).astype(BF16)

    rs = Scatter(g, stage, inbox, h, scatter_send, scatter_recv)
    after = tiles * 128 // size

    if share:
        other = Gather(g, other_out, share, *refs[count + 20 :])
        other.slot(g.row, g.l)[...] = other_piece[...]
        other.begin()

    def work(m):
        pl.when(m < after)(lambda: restore(jnp.minimum(m, after - 1)))
        if share:
            for s in range(2):
                pl.when((lax.rem(m, 2) == s) & (m < 14))(lambda s=s: other.wave(m // 2, s))

    rs.run(work, ahead=2, steps=max(rs.steps, 14))

    def more(i, carry):
        restore(i)
        return carry

    if after > rs.steps:
        lax.fori_loop(rs.steps, after, more, 0)
    rs.last(total)
    ag = Courier(g, out, h, sum_cuts(h), gather_send, gather_recv)
    ag.own()[...] = total[...].astype(BF16)
    ag.run(ORDER if ag.cuts == 4 else PLAIN_ORDER)
    for copy in copies:
        copy.wait()
    rs.finish()
    if share:

        def last_waits(i, carry):
            other.mates(i // g.X, lax.rem(i, g.X))
            return carry

        lax.fori_loop(0, 4 * g.X, last_waits, 0)
        other.finish()
    ag.finish()


def sum_pieces(d_node, place, update, d_change, other_piece, terms, call, share):
    levels, rows = lax.axis_size("lvl"), lax.axis_size("row")
    width = terms[0].shape[1]
    count = sum(term.shape[0] for term in terms)
    h = count // (levels * rows)
    vmem = pl.BlockSpec(memory_space=pltpu.VMEM)
    shape = jax.ShapeDtypeStruct
    return pl.pallas_call(
        functools.partial(sum_kernel, levels, rows, h, len(terms), share),
        out_shape=(
            shape((count, width), BF16),
            shape((d_node.shape[0] * levels, width), BF16),
            shape(update.shape, BF16),
            shape(update.shape, BF16),
            shape((share * levels * rows, width) if share else (16, 128), BF16),
        ),
        in_specs=[vmem] * 5 + [pl.BlockSpec(memory_space=pl.ANY)] * len(terms),
        out_specs=(vmem,) * 5,
        scratch_shapes=[
            pltpu.VMEM((count, width), BF16),
            pltpu.VMEM((Scatter.receives(levels, rows), h, width), BF16),
            pltpu.VMEM((h, width), F32),
            pltpu.SemaphoreType.DMA((Scatter.sends(levels, rows),)),
            pltpu.SemaphoreType.DMA((2 * Scatter.receives(levels, rows),)),
            pltpu.SemaphoreType.DMA((Courier.sends(levels, rows, sum_cuts(h)),)),
            pltpu.SemaphoreType.DMA((Courier.receives(levels, rows, sum_cuts(h)),)),
            pltpu.SemaphoreType.DMA((len(terms),)),
            pltpu.SemaphoreType.DMA((max(levels - 1, 1),)),
            pltpu.SemaphoreType.DMA((max(levels - 1, 1),)),
        ]
        + ([pltpu.SemaphoreType.DMA((Gather.sends(levels, rows),)), pltpu.SemaphoreType.DMA((2 * rows * levels,))] if share else []),
        compiler_params=pltpu.CompilerParams(collective_id=call, has_side_effects=True, vmem_limit_bytes=VMEM_BYTES),
        name=f"sum_{call}",
    )(d_node, place, update, d_change, other_piece, *terms)


def finish_kernel(parts, smalls, update, d_change, first_sums, last_sums, node, d_node, edges, cot, edge_out, cot_out, *refs):
    count = len(parts) + smalls
    wide_outs, small_outs = refs[: len(parts)], refs[len(parts) : count]
    rms_out, node_out, d_node_out, sums, rest, lows, ins, outs, wide, sums_sem, low_sem, in_sem, out_sem, wide_sem = refs[count:]
    size, width = ins.shape[2:]
    steps = edges.shape[0] // size
    targets = [(n, i) for n, part in enumerate(parts) for i in range(part)]
    big = sums.shape[1]
    loads = load_all([(ref.at[pl.ds(0, big)], sums.at[layer]) for layer, ref in enumerate((first_sums, last_sums))], sums_sem)
    loads.append(pltpu.make_async_copy(first_sums.at[pl.ds(big, rest.shape[0])], rest, low_sem.at[4]))
    loads[-1].start()

    def load(step):
        here = pl.ds(step * size, size)
        pairs = ((edges, ins.at[step % 2, 0], in_sem.at[step % 2, 0]), (cot, ins.at[step % 2, 1], in_sem.at[step % 2, 1]))
        pairs += ((update, lows.at[step % 2, 0], low_sem.at[step % 2 * 2]), (d_change, lows.at[step % 2, 1], low_sem.at[step % 2 * 2 + 1]))
        return [pltpu.make_async_copy(ref.at[here], to, sem) for ref, to, sem in pairs]

    def leave(step):
        here = pl.ds(step * size, size)
        return [pltpu.make_async_copy(outs.at[step % 2, n], ref.at[here], out_sem.at[step % 2, n]) for n, ref in enumerate((edge_out, cot_out))]

    def widen(at):
        n, i = targets[at % len(targets)]
        ref = wide_outs[n].at[at // len(targets), pl.ds(i * width, width)]
        return pltpu.make_async_copy(wide.at[at % 4], ref, wide_sem.at[at % 4])

    total = 2 * len(targets)
    done = 0
    for copy in load(0):
        copy.start()
    for step in range(steps):
        if step + 1 < steps:
            for copy in load(step + 1):
                copy.start()
        for copy in load(step):
            copy.wait()
        if step >= 2:
            for copy in leave(step - 2):
                copy.wait()
        for n in range(2):
            outs[step % 2, n] = ins[step % 2, n] + lows[step % 2, n].astype(F32)
        for copy in leave(step):
            copy.start()
        if step == 0:
            for copy in loads:
                copy.wait()
        while done < total * (step + 1) // steps:
            if done >= 4:
                widen(done - 4).wait()
            layer, at = done // len(targets), done % len(targets)
            wide[done % 4] = sums[layer, at * width : (at + 1) * width, :].astype(F32)
            widen(done).start()
            done += 1
    few = rest[...].astype(F32)
    for n, out in enumerate(small_outs):
        for layer in range(2):
            out[layer : layer + 1, :] = few[layer * smalls + n : layer * smalls + n + 1]
    rms_out[...] = few[2 * smalls : 2 * smalls + 1]
    node_out[...] = node[...].astype(F32)
    d_node_out[...] = d_node[...].astype(F32)
    for step in range(max(steps - 2, 0), steps):
        for copy in leave(step):
            copy.wait()
    for at in range(total - 4, total):
        widen(at).wait()


def finish_all(update, d_change, first_sums, last_sums, node, d_node, edges, cot, parts, smalls):
    count, width = edges.shape
    size = 512 if count % 512 == 0 else 128
    vmem = pl.BlockSpec(memory_space=pltpu.VMEM)
    hbm = pl.BlockSpec(memory_space=pl.ANY)
    shape = jax.ShapeDtypeStruct
    wide = (shape((count, width), F32),) * 2 + tuple(shape((2, part * width, width), F32) for part in parts)
    narrow = (shape((2, width), F32),) * smalls + (shape((1, width), F32), shape(node.shape, F32), shape(node.shape, F32))
    return pl.pallas_call(
        functools.partial(finish_kernel, parts, smalls),
        out_shape=wide + narrow,
        in_specs=[hbm] * 4 + [vmem] * 2 + [hbm] * 2,
        out_specs=(hbm,) * len(wide) + (vmem,) * len(narrow),
        scratch_shapes=[
            pltpu.VMEM((2, sum(parts) * width, width), BF16),
            pltpu.VMEM((32, width), BF16),
            pltpu.VMEM((2, 2, size, width), BF16),
            pltpu.VMEM((2, 2, size, width), F32),
            pltpu.VMEM((2, 2, size, width), F32),
            pltpu.VMEM((4, width, width), F32),
            pltpu.SemaphoreType.DMA((2,)),
            pltpu.SemaphoreType.DMA((5,)),
            pltpu.SemaphoreType.DMA((2, 2)),
            pltpu.SemaphoreType.DMA((2, 2)),
            pltpu.SemaphoreType.DMA((4,)),
        ],
        compiler_params=pltpu.CompilerParams(vmem_limit_bytes=VMEM_BYTES),
        name="finish_all",
    )(update, d_change, first_sums, last_sums, node, d_node, edges, cot)


def on_device(
    node_latent, edge_latent, senders, receivers, live_edges,
    edge_w1, edge_b1, edge_w2, edge_b2, edge_gain, edge_shift, node_w1, node_b1, node_w2, node_b2, node_gain, node_shift,
    node_cotangent, edge_cotangent,
):
    node_count, width = node_latent.shape
    edge_count = edge_latent.shape[0]
    layers = edge_w1.shape[0]
    row_total, level_total = lax.axis_size("row"), lax.axis_size("lvl")
    node = node_latent
    weights = (edge_w1, edge_w2, node_w1, node_w2)
    small = (edge_b1, edge_b2, edge_gain, edge_shift, node_b1, node_b2, node_gain, node_shift)
    tiles = edge_count // 128
    index = (senders.reshape(tiles, 128), receivers.reshape(tiles, 128), live_edges.reshape(1, 1))
    sent, pre, normed, update, edges, edges_next, place, rows_of, cols, scale, block, node, recv, npre, nnormed, nscale, tally = forward_layer(
        0, node, small, weights, edge_latent, index
    )
    first = ((block, recv, npre, nnormed, nscale), scale, (pre, normed, edges, sent))
    sent, pre, normed, update, d_edges, scale, block, node, recv, npre, nnormed, nscale, tally_last = forward_layer(
        1, node, small, weights, edge_cotangent, (place, rows_of, cols), edges_next, update
    )
    last = ((block, recv, npre, nnormed, nscale), scale, (pre, normed, edges_next, sent))
    tallies = [tally, tally_last]
    d_node = node_cotangent
    gains = (edge_gain, node_gain)
    devices = row_total * level_total
    even = 7 * width % (16 * devices) == 0 and devices <= 32
    share = 7 * width // devices if even else 0
    d_node, d_edges, d_change, last_grads, last_sums, node_all, _ = backward_layer(
        1, True, d_node, last[0], cols, rows_of, last[1], gains, weights, d_edges, last[2], node, d_edges
    )
    if not share:
        last_grads = lax.psum(last_grads, ("lvl", "row"))
    d_node, _, d_change, first_grads, first_sums, _, piece = backward_layer(
        0, False, d_node, first[0], cols, rows_of, first[1], gains, weights, d_edges, first[2], node, d_change, last_grads, share
    )
    sums = [first_sums, last_sums]
    small = jnp.concatenate([jnp.sum(part.reshape(8, 8, width), axis=1) for part in sums])
    squares = jnp.stack([jnp.sum(tally.reshape(4, 8 * width), axis=1) for tally in tallies])
    squares = jnp.pad(squares.reshape(1, -1), ((0, 0), (0, width - squares.size)))
    used = 7 * width + small.shape[0] + 1
    each = -(-used // (16 * devices)) * 16
    rest = [small.astype(BF16), squares.astype(BF16), jnp.zeros((each * devices - used, width), BF16)]
    flat, d_node_all, update, d_change, whole = sum_pieces(
        d_node, place, update, d_change, piece, [first_grads, jnp.concatenate(rest)], 5, share
    )
    last_grads = whole if share else last_grads
    edge_out, edge_grad, w1, w2, nw1, nw2, b1, b2, gain, shift, nb1, nb2, ngain, nshift, squares, node, d_node = finish_all(
        update, d_change, flat, last_grads, node_all, d_node_all, edge_latent, edge_cotangent, (3, 1, 2, 1), 8
    )
    node_entries = float(node_count * row_total * width)
    edge_entries = float(edge_count * row_total * level_total * width)
    entries = jnp.array([node_entries, edge_entries, edge_entries, node_entries], F32)
    rms = jnp.sqrt(squares[0, : 4 * layers].reshape(layers, 4) / entries[None, :])
    return node, edge_out, d_node, edge_grad, w1, b1, w2, b2, gain, shift, nw1, nb1, nw2, nb2, ngain, nshift, rms


def solution(mesh):
    rows, both, whole = P("row", None), P(("lvl", "row"), None), P()
    edge = P(("lvl", "row"))
    placed = (rows, both, edge, edge, edge) + (whole,) * 12 + (rows, both)
    outs = (rows, both, rows, both) + (whole,) * 13
    return jax.shard_map(on_device, mesh=mesh, in_specs=placed, out_specs=outs, check_vma=False)
```

```python
import functools

import jax
import jax.numpy as jnp
from jax import lax
from jax.experimental import pallas as pl
from jax.experimental.pallas import tpu as pltpu
from jax.sharding import PartitionSpec as P

MESH = pl.DeviceIdType.MESH
NORM_EPS = 1e-05
F32 = jnp.float32
BF16 = jnp.bfloat16
VMEM_BYTES = 61 * 2**20


WORK_ORDER = (
    (
        1089728, 289296, 536069, 551556, 141360, 612561, 159764, 1528408, 356492, 400397,
        858841, 422440, 750249, 990892, 1707549, 1799737, 2097129,
    ),
    (
        1089728, 1392676, 131237, 197853, 1464864, 215760, 1448028, 272952, 399521, 881172,
        290876, 745128, 724581, 482457, 1774801, 1717985, 2097129,
    ),
)
ORDER = (
    (
        280580, 295586, 590612, 803888, 167948, 151730, 217752, 235036, 693301, 365337,
        855736, 760990, 986429, 740022, 679230,
    ),
    (
        589832, 607380, 32934, 214538, 233524, 808981, 412469, 678712, 548394, 269996,
        657586, 741656, 1023289, 464658, 479002,
    ),
)
PLAIN_ORDER = (
    (
        524816, 133680, 394788, 465448, 990252,
    ),
    (
        328704, 526372, 658444, 464948, 990252,
    ),
)

TERMS_ORDER = (
    (
        246535, 230038, 329348, 54046, 34332, 180388, 147502, 722962, 432138, 820258,
        692248, 2097073,
    ),
    (
        115332, 247427, 184844, 19218, 328838, 233232, 463616, 397320, 431874, 558380,
        825512, 2097072,
    ),
)
SUM_ORDER = (
    (
        82311, 251910, 65686, 820894, 329484, 902566, 809372, 917796, 300826, 1162,
        562704, 525336, 890169, 2087477,
    ),
    (
        792839, 83844, 884894, 803212, 212998, 591254, 296090, 40115, 329752, 135950,
        525623, 871970, 661038, 2087480,
    ),
)


NEAREST = ((0, 1, 2, 3), (1, 0, 2, 3), (2, 3, 1, 0), (3, 2, 1, 0))


class Grid:
    def __init__(self, levels, rows):
        self.L, self.R = levels, rows
        self.Z = 4
        self.X = rows // (2 * self.Z)
        self.l = lax.axis_index("lvl")
        row = lax.axis_index("row")
        self.row = row
        self.core = lax.rem(row, 2)
        self.x = lax.rem(row // 2, self.X)
        self.z = row // (2 * self.X)
        self.up = self.z < self.Z - 1
        self.down = self.z > 0

    def block(self, z, x, core):
        return (z * self.X + x) * 2 + core

    def mate(self):
        return (self.l, self.block(self.z, self.x, 1 - self.core))

    def at_z(self, z):
        return (self.l, self.block(jnp.clip(z, 0, self.Z - 1), self.x, self.core))

    def x_other(self, i):
        x = lax.rem(self.x + i, self.X)
        return x, (self.l, self.block(self.z, x, self.core))

    def l_other(self, i):
        l = lax.rem(self.l + i, self.L)
        return l, (l, self.row)

    def nth(self, k, z=None):
        z_here = self.z if z is None else z
        order = NEAREST
        out = jnp.int32(0)
        for z in range(4):
            for j in range(4):
                if order[z][j]:
                    out = jnp.where((z_here == z) & (k == j), order[z][j], out)
        return out

    def local(self, zk, z=None):
        return (zk // 2) == lax.rem(self.z if z is None else z, 2)

    def corner_z(self, q):
        side = lax.rem(lax.rem(self.z, 2) + q // 2, 2)
        return side * 2 + lax.rem(q, 2)

    def pair_z(self):
        return self.z + 1 - 2 * lax.rem(self.z, 2)

    def greet(self):
        barrier = pltpu.get_barrier_semaphore()

        def hello(who):
            pl.semaphore_signal(barrier, inc=1, device_id=who, device_id_type=MESH)

        hello(self.mate())
        for i in range(1, self.X):
            hello(self.x_other(i)[1])
        for i in range(1, self.L):
            hello(self.l_other(i)[1])
        pl.when(self.up)(lambda: hello(self.at_z(self.z + 1)))
        pl.when(self.down)(lambda: hello(self.at_z(self.z - 1)))
        pl.semaphore_wait(barrier, self.X + self.L - 1 + self.up.astype(jnp.int32) + self.down.astype(jnp.int32))


def only(when, act):
    if when is None:
        act()
    else:
        pl.when(when)(act)


def cuts(h):
    first = -(-h // 32) * 16
    return ((0, first), (first, h - first)) if h > first else ((0, h),)


class Courier:
    def __init__(self, grid, table, h, cuts, send_sem, recv_sem):
        self.g, self.table, self.h = grid, table, h
        self.cuts = cuts
        self.size = h // self.cuts
        self.send_sem, self.recv_sem = send_sem, recv_sem
        self.drain = False

    @staticmethod
    def kinds(levels, rows):
        X, L = rows // 8, levels
        return (X + L + 1, (X - 1) * L, (L - 1) * X, 3 * (X - 1) * (L - 1))

    @staticmethod
    def sends(levels, rows, cuts):
        return 4 * sum(Courier.kinds(levels, rows)) * cuts

    @staticmethod
    def receives(levels, rows, cuts):
        return levels * rows * cuts

    def at(self, kind, zk, n, s):
        counts = self.kinds(self.g.L, self.g.R)
        return (4 * sum(counts[:kind]) + zk * counts[kind] + n) * self.cuts + s

    def slot(self, block, l, s=0, size=None):
        start = (block * self.g.L + l) * self.h + s * self.size
        return self.table.at[pl.ds(pl.multiple_of(start, 16), size or self.size)]

    def own(self):
        return self.slot(self.g.row, self.g.l, 0, self.h)

    def push(self, at, block, l, s, who, when=None):
        place = self.slot(block, l, s)
        copy = pltpu.make_async_remote_copy(
            place,
            place,
            self.send_sem.at[at],
            self.recv_sem.at[(block * self.g.L + l) * self.cuts + s],
            device_id=who,
            device_id_type=MESH,
        )
        only(when, copy.wait_send if self.drain else copy.start)

    def arrived(self, block, l, s):
        if self.drain:
            return
        place = self.slot(block, l, s)
        pltpu.make_async_remote_copy(
            place,
            place,
            self.send_sem.at[0],
            self.recv_sem.at[(block * self.g.L + l) * self.cuts + s],
            device_id=self.g.mate(),
            device_id_type=MESH,
        ).wait_recv()

    def near(self, zk):
        z = self.g.z
        return (zk == z) | ((z == 0) & (zk == 1)) | ((z == 3) & (zk == 2))

    def even(self, zk):
        return lax.rem(jnp.where(self.g.z < 2, zk, 3 - zk), 2) == 0

    def column(self, zk, s, own=False):
        g = self.g
        block = g.block(zk, g.x, g.core)
        if not own:
            self.arrived(block, g.l, s)
        self.push(self.at(0, zk, 0, s), block, g.l, s, g.at_z(g.z + 1), g.up & (zk <= g.z))
        self.push(self.at(0, zk, 1, s), block, g.l, s, g.at_z(g.z - 1), g.down & (zk >= g.z))
        for i in range(1, g.X):
            self.push(self.at(0, zk, 1 + i, s), block, g.l, s, g.x_other(i)[1])
        for j in range(1, g.L):
            self.push(self.at(0, zk, g.X + j, s), block, g.l, s, g.l_other(j)[1])
        self.push(self.at(0, zk, g.X + g.L, s), block, g.l, s, g.mate())

    def side_x(self, zk, s):
        g = self.g
        n = 0
        for i in range(1, g.X):
            block = g.block(zk, g.x_other(i)[0], g.core)
            self.arrived(block, g.l, s)
            for j in range(1, g.L):
                self.push(self.at(1, zk, n, s), block, g.l, s, g.l_other(j)[1], self.near(zk) & self.even(zk))
                n += 1
            self.push(self.at(1, zk, n, s), block, g.l, s, g.mate())
            n += 1

    def side_l(self, zk, s):
        g = self.g
        block = g.block(zk, g.x, g.core)
        n = 0
        for j in range(1, g.L):
            l = g.l_other(j)[0]
            self.arrived(block, l, s)
            for i in range(1, g.X):
                self.push(self.at(2, zk, n, s), block, l, s, g.x_other(i)[1], self.near(zk) & jnp.logical_not(self.even(zk)))
                n += 1
            self.push(self.at(2, zk, n, s), block, l, s, g.mate())
            n += 1

    def corner(self, zk, s):
        g = self.g
        n = 0
        for i in range(1, g.X):
            block = g.block(zk, g.x_other(i)[0], g.core)
            for j in range(1, g.L):
                l = g.l_other(j)[0]
                self.arrived(block, l, s)
                self.push(self.at(3, zk, n, s), block, l, s, g.at_z(g.z + 1), (zk <= 1) & (g.z >= zk) & g.up)
                self.push(self.at(3, zk, n + 1, s), block, l, s, g.at_z(g.z - 1), (zk >= 2) & (g.z <= zk) & g.down)
                self.push(self.at(3, zk, n + 2, s), block, l, s, g.mate())
                n += 3

    def mates(self, zk, x):
        def one(i, carry):
            self.arrived(self.g.block(zk, x, 1 - self.g.core), i // self.cuts, lax.rem(i, self.cuts))
            return carry

        lax.fori_loop(0, self.g.L * self.cuts, one, 0)

    def run(self, tables, meanwhile=None, prepare=None, work=None):
        g = self.g
        for s in range(self.cuts):
            self.column(g.z, s, own=True)
        low = g.z < 2
        first = (g.z == 0) | (g.z == 3)

        def one(m, done):
            word = jnp.int32(0)
            for at, (a, b) in enumerate(zip(*tables)):
                word = jnp.where(m // 3 == at, jnp.where(first, a, b), word)
            byte = lax.rem(m, 3)
            code = lax.rem(jnp.where(byte == 0, word, jnp.where(byte == 1, word // 128, word // 16384)), 128)
            zk = lax.rem(code // 4, 4)
            zk = jnp.where(low, zk, 3 - zk)
            s = lax.rem(code, 4)
            kind = code // 16
            pl.when(kind == 0)(lambda: self.column(zk, s))
            if g.X > 1:
                pl.when(kind == 1)(lambda: self.side_x(zk, s))
            if g.L > 1:
                pl.when(kind == 2)(lambda: self.side_l(zk, s))
            if g.X > 1 and g.L > 1:
                pl.when(kind == 3)(lambda: self.corner(zk, s))
            if meanwhile is not None:
                for at in range(3):
                    pl.when(code == 64 + at)(lambda at=at: meanwhile(at))
            count = jnp.int32(0)
            if work is not None:
                for off in range(g.X):
                    x = lax.rem(g.x + off, g.X)
                    hit = s == (0 if off == 0 else 1)
                    pl.when((kind == 5) & hit)(lambda x=x: prepare(zk, x))

                    def full(x=x, off=off):
                        self.mates(zk, x)
                        work(zk, x, done + max(off - 1, 0))

                    pl.when((kind == 6) & hit)(full)
                count = jnp.where(kind == 6, jnp.where(s == 0, 1, g.X - 1), 0)
            return done + count

        lax.fori_loop(0, 3 * len(tables[0]), one, jnp.int32(0))
        if work is None:

            def last(i, carry):
                self.mates(i // g.X, lax.rem(i, g.X))
                return carry

            lax.fori_loop(0, 4 * g.X, last, 0)

    def finish(self):
        self.drain = True

        def one(i, carry):
            zk, s = i // self.cuts, lax.rem(i, self.cuts)
            self.column(zk, s)
            self.side_x(zk, s)
            self.side_l(zk, s)
            self.corner(zk, s)
            return carry

        lax.fori_loop(0, 4 * self.cuts, one, 0)


class Scatter:
    def __init__(self, grid, stage, inbox, h, send_sem, recv_sem):
        self.g, self.stage, self.inbox, self.h = grid, stage, inbox, h
        self.cuts = cuts(h)
        self.send_sem, self.recv_sem = send_sem, recv_sem
        X, L = grid.X, grid.L
        at = 0
        self.base = {}
        for name, count in self.parts(X, L):
            self.base[name] = at
            at += count
        at = 0
        self.out = {}
        for name, count in self.out_parts(X, L):
            self.out[name] = at
            at += count
        self.drain = False

    @staticmethod
    def parts(X, L):
        side = (X - 1) * (L - 1)
        return (("mate", 4 * X * L), ("pair", 2 * side), ("l2", side), ("x2", side), ("xc", 4 * (X - 1)), ("lc", 4 * (L - 1)), ("z", 5))

    @staticmethod
    def out_parts(X, L):
        side = (X - 1) * (L - 1)
        return (("mate", 4 * X * L), ("corner", 8 * side), ("xc", 4 * (X - 1)), ("lc", 4 * (L - 1)), ("z", 4))

    @staticmethod
    def receives(levels, rows):
        return sum(count for _, count in Scatter.parts(rows // 8, levels))

    @staticmethod
    def sends(levels, rows):
        return 2 * sum(count for _, count in Scatter.out_parts(rows // 8, levels))

    def slot(self, block, l, s=None):
        start, size = (0, self.h) if s is None else self.cuts[s]
        return self.stage.at[pl.ds(pl.multiple_of((block * self.g.L + l) * self.h + start, 16), size)]

    def push(self, out, block, l, s, at, who, when=None):
        start, size = self.cuts[s]
        copy = pltpu.make_async_remote_copy(
            self.slot(block, l, s),
            self.inbox.at[at, pl.ds(start, size)],
            self.send_sem.at[2 * out + s],
            self.recv_sem.at[2 * at + s],
            device_id=who,
            device_id_type=MESH,
        )
        only(when, copy.wait_send if self.drain else copy.start)

    def arrived(self, at, s):
        start, size = self.cuts[s]
        place = self.inbox.at[at, pl.ds(start, size)]
        pltpu.make_async_remote_copy(
            place, place, self.send_sem.at[0], self.recv_sem.at[2 * at + s], device_id=self.g.mate(), device_id_type=MESH
        ).wait_recv()

    def total(self, block, l, s, ats):
        start, size = self.cuts[s]
        for at in ats:
            self.arrived(at, s)
        out = self.slot(block, l, s)[...].astype(F32)
        for at in ats:
            out = out + self.inbox[at, start : start + size].astype(F32)
        return out

    def add(self, block, l, s, ats, when=None):
        if self.drain:
            return

        def act():
            self.slot(block, l, s)[...] = self.total(block, l, s, ats).astype(BF16)

        only(when, act)

    def each(self):
        return range(len(self.cuts))

    def to_mate(self, z, x):
        g = self.g
        for l in range(g.L):
            at = (z * g.X + x) * g.L + l
            for s in self.each():
                self.push(self.out["mate"] + at, g.block(z, x, 1 - g.core), l, s, self.base["mate"] + at, g.mate())

    def from_mate(self, z, x):
        g = self.g
        for l in range(g.L):
            for s in self.each():
                self.add(g.block(z, x, g.core), l, s, [self.base["mate"] + (z * g.X + x) * g.L + l])

    def corner_far(self, z, i):
        g = self.g
        block = g.block(z, lax.rem(g.x + i, g.X), g.core)
        for j in range(1, g.L):
            l = g.l_other(j)[0]
            spot = (lax.rem(z, 2) * (g.X - 1) + i - 1) * (g.L - 1) + j - 1
            for s in self.each():
                self.push(self.out["corner"] + spot, block, l, s, self.base["pair"] + spot, g.at_z(g.pair_z()))

    def corner_near(self, z, i):
        g = self.g
        x, x_dev = g.x_other(i)
        block = g.block(z, x, g.core)
        even = self.even(z)
        side = (g.X - 1) * (g.L - 1)
        for j in range(1, g.L):
            l, l_dev = g.l_other(j)
            spot = (lax.rem(z, 2) * (g.X - 1) + i - 1) * (g.L - 1) + j - 1
            out = self.out["corner"] + 2 * side + spot
            for s in self.each():
                self.add(block, l, s, [self.base["pair"] + spot])
                self.push(out, block, l, s, self.base["l2"] + (i - 1) * (g.L - 1) + g.L - j - 1, l_dev, even)
                self.push(out, block, l, s, self.base["x2"] + (g.X - i - 1) * (g.L - 1) + j - 1, x_dev, jnp.logical_not(even))

    def side_x(self, zk, i, waits):
        g = self.g
        x, x_dev = g.x_other(i)
        block = g.block(zk, x, g.core)
        ats = [self.base["l2"] + (i - 1) * (g.L - 1) + j - 1 for j in range(1, g.L)]
        for s in self.each():
            if ats and waits:
                self.add(block, g.l, s, ats)
            self.push(self.out["xc"] + zk * (g.X - 1) + i - 1, block, g.l, s, self.base["xc"] + zk * (g.X - 1) + g.X - i - 1, x_dev)

    def side_l(self, zk, waits):
        g = self.g
        block = g.block(zk, g.x, g.core)
        for j in range(1, g.L):
            l, l_dev = g.l_other(j)
            ats = [self.base["x2"] + (i - 1) * (g.L - 1) + j - 1 for i in range(1, g.X)]
            for s in self.each():
                if waits:
                    self.add(block, l, s, ats)
                self.push(self.out["lc"] + zk * (g.L - 1) + j - 1, block, l, s, self.base["lc"] + zk * (g.L - 1) + g.L - j - 1, l_dev)

    def around(self, zk):
        g = self.g
        ats = [self.base["xc"] + zk * (g.X - 1) + i - 1 for i in range(1, g.X)]
        return ats + [self.base["lc"] + zk * (g.L - 1) + j - 1 for j in range(1, g.L)]

    def column(self, zk):
        g = self.g
        block = g.block(zk, g.x, g.core)
        behind = jnp.where(zk > g.z, g.down, g.up)
        near = jnp.abs(zk - g.z) == 1
        spot = jnp.where(near & (zk < g.z), 4, zk)
        for s in self.each():
            self.add(block, g.l, s, self.around(zk))
            self.add(block, g.l, s, [self.base["z"] + zk], behind)
            self.push(self.out["z"] + zk, block, g.l, s, self.base["z"] + spot, g.at_z(jnp.where(zk > g.z, g.z + 1, g.z - 1)))

    def last(self, out):
        g = self.g
        for s in self.each():
            start, size = self.cuts[s]
            out[start : start + size, :] = self.total(g.row, g.l, s, self.around(g.z))
            for at, there in ((self.base["z"] + g.z, g.down), (self.base["z"] + 4, g.up)):

                def take(at=at, s=s, start=start, size=size):
                    self.arrived(at, s)
                    out[start : start + size, :] += self.inbox[at, start : start + size].astype(F32)

                pl.when(there)(take)

    def even(self, zk):
        return lax.rem(jnp.where(self.g.z < 2, zk, 3 - zk), 2) == 0

    def decode(self, m):
        g = self.g
        first = (g.z == 0) | (g.z == 3)
        word = jnp.int32(0)
        for at, (a, b) in enumerate(zip(*self.tables)):
            word = jnp.where(m // 3 == at, jnp.where(first, a, b), word)
        byte = lax.rem(m, 3)
        code = lax.rem(jnp.where(byte == 0, word, jnp.where(byte == 1, word // 128, word // 16384)), 128)
        zk = lax.rem(code // 2, 4)
        return code, code // 8, jnp.where(g.z < 2, zk, 3 - zk), lax.rem(code, 2)

    def step(self, m, work=None, extra=None, done=0):
        g = self.g
        code, kind, zk, side = self.decode(m)
        for off in range(g.X):
            x = lax.rem(g.x + off, g.X)
            hit = side == (0 if off == 0 else 1)

            def make(x=x, off=off):
                if work is not None and not self.drain:
                    work(zk, x, done + max(off - 1, 0))
                self.to_mate(zk, x)

            pl.when((kind == 0) & hit)(make)
            if not self.drain:
                pl.when((kind == 1) & hit)(lambda x=x: self.from_mate(zk, x))
        near = g.local(zk)
        for i in range(1, g.X):
            if g.L > 1:
                pl.when((kind == 2) & near)(lambda i=i: self.corner_near(zk, i))
                pl.when((kind == 2) & jnp.logical_not(near))(lambda i=i: self.corner_far(zk, i))
            late = near & self.even(zk)
            pl.when((kind == 3) & late)(lambda i=i: self.side_x(zk, i, True))
            pl.when((kind == 3) & jnp.logical_not(late))(lambda i=i: self.side_x(zk, i, False))
        if g.L > 1:
            late = near & jnp.logical_not(self.even(zk))
            pl.when((kind == 4) & late)(lambda: self.side_l(zk, True))
            pl.when((kind == 4) & jnp.logical_not(late))(lambda: self.side_l(zk, False))
        pl.when(kind == 5)(lambda: self.column(zk))
        if extra is not None and not self.drain:
            pl.when(kind >= 6)(lambda: extra(code - 48))
        return jnp.where(kind == 0, jnp.where(side == 0, 1, g.X - 1), 0)

    def go(self, m, ahead, work=None, extra=None, done=0):
        count = self.step(m, work, extra, done)

        def wait():
            self.drain = True
            self.step(m - ahead)
            self.drain = False

        pl.when(m >= ahead)(wait)
        return count

    def run(self, tables, work=None, extra=None, beside=None, ahead=20):
        self.follow(tables, ahead)

        def one(m, done):
            count = self.go(m, self.ahead, work, extra, done)
            if beside is not None:
                beside(m)
            return done + count

        lax.fori_loop(0, self.steps, one, jnp.int32(0))

    def follow(self, tables, ahead):
        self.tables = tables
        self.steps = 3 * len(tables[0])
        self.ahead = min(ahead, self.steps)

    def finish(self):
        self.drain = True

        def one(m, carry):
            self.step(m)
            return carry

        lax.fori_loop(self.steps - self.ahead, self.steps, one, 0)


def dot(left, right):
    return jnp.dot(left, right, preferred_element_type=F32)


def dot_nt(left, right):
    return lax.dot_general(left, right, (((1,), (1,)), ((), ())), preferred_element_type=F32)


def dot_tn(left, right):
    return lax.dot_general(left, right, (((0,), (0,)), ((), ())), preferred_element_type=F32)


def fold(values):
    rows, width = values.shape
    return jnp.sum(values.reshape(rows // 8, 8, width), axis=0)


def norm_parts(values):
    average = jnp.mean(values, axis=-1, keepdims=True)
    centered = values - average
    scale = lax.rsqrt(jnp.mean(centered * centered, axis=-1, keepdims=True) + NORM_EPS)
    return centered * scale, scale


def norm_back(normed, scale, d_normed):
    mean_d = jnp.mean(d_normed, axis=-1, keepdims=True)
    mean_dn = jnp.mean(d_normed * normed, axis=-1, keepdims=True)
    return scale * (d_normed - mean_d - normed * mean_dn)


def silu_back(pre, d_active):
    gate = lax.logistic(pre)
    return d_active * (gate * (1.0 + pre * (1.0 - gate)))


def find_places(row_total, node_count, some, senders, receivers, live, place, side, facts_out, counts):
    tiles = senders.shape[0]
    group = tiles * 128 // row_total
    first = lax.axis_index("row") * node_count
    lane = lax.broadcasted_iota(jnp.int32, (128, 128), 1)
    sub = lax.broadcasted_iota(jnp.int32, (128, 128), 0)
    before = (sub < lane).astype(BF16)
    owner_ids = lax.broadcasted_iota(jnp.int32, (row_total, 128), 0)
    carry = owner_ids[:, :1].astype(F32) * group if some[0] == 0 else counts[:, 0:1]
    for tile in some:
        send = senders[tile : tile + 1, :]
        recv = receivers[tile : tile + 1, :] - first
        owner = lax.div(send, node_count)
        local = send - owner * node_count
        mine = owner_ids == owner
        ranks = dot(mine.astype(BF16), before) + carry
        spot = jnp.sum(jnp.where(mine, ranks, 0.0), axis=0, keepdims=True)
        carry = carry + jnp.sum(mine.astype(F32), axis=1, keepdims=True)
        place[tile : tile + 1, :] = spot.astype(jnp.int32)
        alive = (lane[:1] + tile * 128 < live[0, 0]).astype(jnp.int32)
        facts = jnp.where(sub == 0, lax.div(local, 16), 0)
        facts = jnp.where(sub == 1, lax.rem(local, 16), facts)
        facts = jnp.where(sub == 2, lax.div(recv, 16), facts)
        facts = jnp.where(sub == 3, lax.rem(recv, 16), facts)
        facts = jnp.where(sub == 4, alive, facts).astype(F32)
        side[:, pl.ds(tile * 128, 128)] = facts[:16].astype(BF16)
        facts_out[pl.ds(tile * 128, 128), :] = facts.T.astype(BF16)
    counts[...] = jnp.broadcast_to(carry, counts.shape)


def picker(place, start, size):
    ids = lax.broadcasted_iota(jnp.int32, (size, 128), 0) + start
    return jnp.concatenate([(ids == place[tile : tile + 1, :]).astype(BF16) for tile in range(place.shape[0])], axis=1)


def one_hot_cols(ids, count):
    lanes = lax.broadcasted_iota(jnp.int32, (ids.shape[0], count), 1).astype(F32)
    return (ids == lanes).astype(BF16)


def one_hot_rows(ids, count):
    subs = lax.broadcasted_iota(jnp.int32, (count, ids.shape[1]), 0).astype(F32)
    return (ids == subs).astype(BF16)


def load_all(pairs, sems):
    copies = [pltpu.make_async_copy(src, dst, sems.at[i]) for i, (src, dst) in enumerate(pairs)]
    for copy in copies:
        copy.start()
    return copies


def forward_kernel(
    layer, levels, rows, first_layer, *refs
):
    (node, b1, b2, gain, shift, nb1, nb2, ngain, nshift, w1_all, w2_all, nw1_all, nw2_all, plain_all) = refs[:14]
    refs = refs[14:]
    if first_layer:
        senders, receivers, live = refs[:3]
        refs = refs[3:]
    else:
        place, rows_of, cols_all, edges_all, before_all = refs[:5]
        refs = refs[5:]
    sent_out, pre_out, normed_out, update_out, moved_out = refs[:5]
    refs = refs[5:]
    if first_layer:
        edges_out, place, rows_of, cols = refs[:4]
        refs = refs[4:]
    scale_out, block_out, node_out, recv_out, npre_out, nnormed_out, nscale_out, tally = refs[:8]
    (
        table, total, cast, near, far, w1, w2, nw1, nw2, plain, joined, ordered, out_buf, scale_buf,
        load_sem, out_sem, moved_sem, send_sem, recv_sem, near_send, near_recv,
    ) = refs[8:29]
    if first_layer:
        side, counts = refs[29:]
    else:
        cols, edges, before = refs[29:]
    g = Grid(levels, rows)
    h, width = node_out.shape
    if first_layer:
        node = node.at[pl.ds(pl.multiple_of(g.l * h, h), h)]
    count = plain.shape[0]
    group = count // rows
    node_count = h * levels
    pairs = ((plain_all, plain), (w1_all.at[layer], w1), (w2_all.at[layer], w2), (nw1_all.at[layer], nw1), (nw2_all.at[layer], nw2))
    if not first_layer:
        pairs += ((cols_all, cols), (edges_all, edges), (before_all, before))
    loads = load_all(pairs, load_sem)
    ag = Courier(g, table, h, 2, send_sem, recv_sem)
    ag.own()[...] = node[...].astype(BF16)
    tally[...] = jnp.zeros_like(tally)
    total[...] = jnp.zeros_like(total)
    g.greet()
    wide = lambda ref: ref[layer : layer + 1, :]
    outs = (sent_out, pre_out, normed_out, update_out) + ((edges_out,) if first_layer else ())

    def meanwhile(at):
        if first_layer:
            tiles = place.shape[0]
            some = range(at * tiles // 3, (at + 1) * tiles // 3)
            find_places(rows, node_count, some, senders, receivers, live, place, side, joined.at[:, pl.ds(width, 128)], counts)
        if at == 0:
            for copy in loads:
                copy.wait()

        def cast_rows(i, carry):
            part = pl.ds(pl.multiple_of(i * 2 * group, 2 * group), 2 * group)
            joined[part, 0:width] = plain[part, :].astype(BF16)
            return carry

        lax.fori_loop(at * rows // 6, (at + 1) * rows // 6, cast_rows, 0)

    def leave(n, part):
        slot = lax.rem(n, 2)
        copies = [pltpu.make_async_copy(out_buf.at[slot, i], ref.at[part], out_sem.at[slot, i]) for i, ref in enumerate(outs)]
        return copies + [pltpu.make_async_copy(scale_buf.at[slot], scale_out.at[part], out_sem.at[slot, 5])]

    def spot(z, x):
        pair = g.block(z, x, 0)
        first = pl.multiple_of(pair * group, 2 * group)
        return pair, first, pl.ds(first, 2 * group)

    def moved_copy(z, x):
        part = spot(z, x)[2]
        return pltpu.make_async_copy(ordered.at[part], moved_out.at[part], moved_sem.at[z * g.X + x])

    def prepare(z, x):
        pair, first, part = spot(z, x)
        pick = picker(place, first, 2 * group)
        moved = dot(pick, joined[...])
        ordered[part, :] = moved[:, :width].astype(BF16)
        moved_copy(z, x).start()
        if first_layer:
            digits = moved[:, width:]
            lanes = lax.broadcasted_iota(jnp.int32, digits.shape, 1)
            ids = digits[:, 0:1] * 16.0 + digits[:, 1:2]
            got = digits[:, 2:3] * 16.0 + digits[:, 3:4]
            cols[part, :] = jnp.where(lanes == 0, ids, jnp.where(lanes == 1, got, jnp.where(lanes == 2, digits[:, 4:5], 0.0)))
            for half in range(2):
                digits = dot_nt(side[...], pick[half * group : (half + 1) * group])
                rows_of[pair + half] = jnp.concatenate(
                    [digits[0:1] * 16.0 + digits[1:2], digits[2:3] * 16.0 + digits[3:4], digits[4:10]], axis=0
                )

    def work(z, x, n):
        def own():
            here = table[pl.ds(pl.multiple_of(g.row * node_count, 16), node_count), :]
            cast[...] = dot(here, w1[2 * width :, :]).astype(BF16)
            block_out[...] = here

        pl.when(n == 0)(own)
        pair, first, part = spot(z, x)

        def free():
            for copy in leave(n, part):
                copy.wait()

        pl.when(n >= 2)(free)
        slot = lax.rem(n, 2)
        low = ordered[part, :] if first_layer else edges[part, :]
        cols_here = cols[part, :]
        send_pick = one_hot_cols(cols_here[:, 0:1], node_count)
        recv_pick = one_hot_cols(cols_here[:, 1:2], node_count)
        start = pl.multiple_of(pair * node_count, 16)
        sent = jnp.concatenate(
            [
                dot(send_pick[:group], table[pl.ds(start, node_count), :]).astype(BF16),
                dot(send_pick[group:], table[pl.ds(start + node_count, node_count), :]).astype(BF16),
            ],
            axis=0,
        )
        out_buf[slot, 0] = sent
        pre = dot(low, w1[:width, :]) + dot(sent, w1[width : 2 * width, :]) + dot(recv_pick, cast[...]) + wide(b1)
        out_buf[slot, 1] = pre.astype(BF16)
        active = (pre * lax.logistic(pre)).astype(BF16)
        normed, scale = norm_parts(dot(active, w2[...]) + wide(b2))
        out_buf[slot, 2] = normed.astype(BF16)
        scale_buf[slot] = jnp.broadcast_to(scale, (2 * group, 128))
        update = (normed * wide(gain) + wide(shift)) * cols_here[:, 2:3]
        update_low = update.astype(BF16)
        edge = low.astype(F32) + update
        if first_layer:
            out_buf[slot, 3] = update_low
            out_buf[slot, 4] = edge.astype(BF16)
        else:
            out_buf[slot, 3] = (before[part, :].astype(F32) + update).astype(BF16)
        tally[8:16, :] += fold(edge * edge)
        tally[16:24, :] += fold(update * update)
        for half in range(2):
            pick = one_hot_rows(rows_of[pair + half][1:2, :], node_count)
            total[...] += dot(pick, update_low[half * group : (half + 1) * group])
        for copy in leave(n, part):
            copy.start()

    ag.run(WORK_ORDER, meanwhile, prepare, work)
    copies = []
    for j in range(1, levels):
        l, l_dev = g.l_other(j)
        near[j - 1] = total[pl.ds(pl.multiple_of(l * h, h), h), :].astype(BF16)
        copy = pltpu.make_async_remote_copy(
            near.at[j - 1], far.at[levels - 1 - j], near_send.at[j - 1], near_recv.at[levels - 1 - j], device_id=l_dev, device_id_type=MESH
        )
        copy.start()
        copies.append(copy)
    received = total[pl.ds(pl.multiple_of(g.l * h, h), h), :]
    npre = dot(node[...].astype(BF16), nw1[:width, :]) + wide(nb1)
    for copy in copies:
        copy.wait()
    for j in range(1, levels):
        received = received + far[j - 1].astype(F32)
    received = received.astype(BF16)
    recv_out[...] = received
    npre = npre + dot(received, nw1[width:, :])
    npre_out[...] = npre
    nnormed, nscale = norm_parts(dot((npre * lax.logistic(npre)).astype(BF16), nw2[...]) + wide(nb2))
    nnormed_out[...] = nnormed
    nscale_out[...] = jnp.broadcast_to(nscale, (h, 128))
    change = nnormed * wide(ngain) + wide(nshift)
    new = node[...] + change
    node_out[...] = new
    tally[0:8, :] = fold(new * new)
    tally[24:32, :] = fold(change * change)
    for n in range(2):
        for copy in leave(n, pl.ds(0, 2 * group)):
            copy.wait()
    for n in range(4 * g.X):
        moved_copy(n // g.X, n % g.X).wait()
    ag.finish()


def forward_layer(layer, node, small, weights, plain, index, edges=None, before=None):
    levels, rows = lax.axis_size("lvl"), lax.axis_size("row")
    width = node.shape[1]
    h = node.shape[0] // (levels if layer == 0 else 1)
    count = plain.shape[0]
    group = count // rows
    vmem = pl.BlockSpec(memory_space=pltpu.VMEM)
    hbm = pl.BlockSpec(memory_space=pl.ANY)
    first_layer = layer == 0
    shape = jax.ShapeDtypeStruct
    wide = shape((count, width), BF16)
    ins = (node,) + small + weights + (plain,) + index
    in_specs = [vmem] * 9 + [hbm] * 5
    outs = [wide] * 5
    out_specs = [hbm] * 5
    scratch = []
    if first_layer:
        in_specs += [vmem, vmem, pl.BlockSpec(memory_space=pltpu.SMEM)]
        outs += [wide, shape(index[0].shape, jnp.int32), shape((rows, 8, group), F32), shape((count, 128), F32)]
        out_specs += [hbm, vmem, vmem, vmem]
        scratch = [pltpu.VMEM((16, count), BF16), pltpu.VMEM((rows, 128), F32)]
    else:
        ins += (edges, before)
        in_specs += [vmem, vmem, hbm, hbm, hbm]
        scratch = [pltpu.VMEM((count, 128), F32), pltpu.VMEM((count, width), BF16), pltpu.VMEM((count, width), BF16)]
    outs += [
        shape((count, 128), F32),
        shape((h * levels, width), BF16),
        shape((h, width), F32),
        shape((h, width), BF16),
        shape((h, width), F32),
        shape((h, width), F32),
        shape((h, 128), F32),
        shape((32, width), F32),
    ]
    out_specs += [hbm] + [vmem] * 7
    others = max(levels - 1, 1)
    return pl.pallas_call(
        functools.partial(forward_kernel, layer, levels, rows, first_layer),
        out_shape=outs,
        in_specs=in_specs,
        out_specs=out_specs,
        scratch_shapes=[
            pltpu.VMEM((rows * h * levels, width), BF16),
            pltpu.VMEM((h * levels, width), F32),
            pltpu.VMEM((h * levels, width), BF16),
            pltpu.VMEM((others, h, width), BF16),
            pltpu.VMEM((others, h, width), BF16),
        ]
        + [pltpu.VMEM(weight.shape[1:], BF16) for weight in weights]
        + [
            pltpu.VMEM((count, width), F32),
            pltpu.VMEM((count, width + (128 if first_layer else 0)), BF16),
            pltpu.VMEM((count, width), BF16),
            pltpu.VMEM((2, 5, 2 * group, width), BF16),
            pltpu.VMEM((2, 2 * group, 128), F32),
            pltpu.SemaphoreType.DMA((8,)),
            pltpu.SemaphoreType.DMA((2, 6)),
            pltpu.SemaphoreType.DMA((rows // 2,)),
            pltpu.SemaphoreType.DMA((Courier.sends(levels, rows, 2),)),
            pltpu.SemaphoreType.DMA((Courier.receives(levels, rows, 2),)),
            pltpu.SemaphoreType.DMA((others,)),
            pltpu.SemaphoreType.DMA((others,)),
        ]
        + scratch,
        compiler_params=pltpu.CompilerParams(collective_id=1 + layer, has_side_effects=True, vmem_limit_bytes=VMEM_BYTES),
        name=f"forward_{layer}",
    )(*ins)


def backward_kernel(
    layer, levels, rows, last_layer,
    d_node, block, recv, npre, nnormed, nscale, rows_of, gain, ngain, node, d_before, cols_all, scale_all, d_edges, pre, normed, edges, sent,
    w1_all, w2_all, nw1_all, nw2_all,
    d_node_out, d_edges_out, d_change_out, grads, tally, node_all,
    stage, inbox, bufs, d_recv, turned, own_sum, out_buf, cols, scale, w1, w2, nw1, nw2,
    load_sem, out_sem, send_sem, recv_sem, near_send, near_recv,
):
    g = Grid(levels, rows)
    h, width = d_node_out.shape
    if last_layer:
        d_node = d_node.at[pl.ds(pl.multiple_of(g.l * h, h), h)]
    count = pre.shape[0]
    group = count // rows
    node_count = h * levels
    loads = load_all(
        ((nw2_all.at[layer], nw2), (nw1_all.at[layer], nw1), (w1_all.at[layer], w1), (w2_all.at[layer], w2))
        + tuple((src, bufs.at[i]) for i, src in enumerate((d_edges, pre, normed, edges, sent)))
        + ((cols_all, cols), (scale_all, scale)),
        load_sem,
    )
    rs = Scatter(g, stage, inbox, h, send_sem, recv_sem)
    wide = lambda ref: ref[layer : layer + 1, :]
    mine = pl.ds(pl.multiple_of(g.l * h, h), h)
    own_sum[...] = jnp.zeros_like(own_sum)
    tally[...] = jnp.zeros_like(tally)
    for copy in loads[:2]:
        copy.wait()
    tally[48:56, :] = fold(d_node[...] * nnormed[...])
    tally[56:64, :] = fold(d_node[...])
    d_two = norm_back(nnormed[...], nscale[:, 0:1], d_node[...] * wide(ngain)).astype(BF16)
    tally[40:48, :] = fold(d_two.astype(F32))
    d_one = silu_back(npre[...], dot_nt(d_two, nw2[...])).astype(BF16)
    tally[32:40, :] = fold(d_one.astype(F32))
    d_recv[mine, :] = dot_nt(d_one, nw1[width:, :]).astype(BF16)
    g.greet()
    copies = []
    for j in range(1, levels):
        copy = pltpu.make_async_remote_copy(
            d_recv.at[mine], d_recv.at[mine], near_send.at[j - 1], near_recv.at[levels - 1 - j], device_id=g.l_other(j)[1], device_id_type=MESH
        )
        copy.start()
        copies.append(copy)
    d_node_out[...] = d_node[...] + dot_nt(d_one, nw1[:width, :])
    active = (npre[...] * lax.logistic(npre[...])).astype(BF16)
    grads[4 * width + width : 6 * width, :] = dot_tn(recv[...], d_one).astype(BF16)
    grads[4 * width : 5 * width, :] = dot_tn(block[mine, :], d_one).astype(BF16)
    grads[6 * width : 7 * width, :] = dot_tn(active, d_two).astype(BF16)
    if last_layer:
        node_all[mine, :] = node[...].astype(BF16)
    for copy in copies:
        copy.wait()
    copies = []
    for j in range(1, levels if last_layer else 1):
        copy = pltpu.make_async_remote_copy(
            node_all.at[mine],
            node_all.at[mine],
            near_send.at[levels + j - 2],
            near_recv.at[2 * levels - 2 - j],
            device_id=g.l_other(j)[1],
            device_id_type=MESH,
        )
        copy.start()
        copies.append(copy)
    for copy in loads[2:]:
        copy.wait()

    def work(z, x, i):
        pair = g.block(z, x, 0)
        start = pl.multiple_of(pair * group, 2 * group)
        place = pl.ds(start, 2 * group)
        if not last_layer:
            earlier = pltpu.make_async_copy(d_before.at[place], out_buf.at[lax.rem(i, 2), 0], out_sem.at[lax.rem(i, 2), 0])
            earlier.start()
        cols_here = cols[place, :]
        recv_pick = one_hot_cols(cols_here[:, 1:2], node_count)
        d_edge = bufs[0, place, :].astype(F32)
        d_update = (d_edge + dot(recv_pick, d_recv[...])) * cols_here[:, 2:3]
        norm_here = bufs[2, place, :].astype(F32)
        tally[16:24, :] += fold(d_update * norm_here)
        tally[24:32, :] += fold(d_update)
        d_two = norm_back(norm_here, scale[place, 0:1], d_update * wide(gain)).astype(BF16)
        tally[8:16, :] += fold(d_two.astype(F32))
        pre_here = bufs[1, place, :].astype(F32)
        gate = lax.logistic(pre_here)
        d_one = (dot_nt(d_two, w2[...]) * (gate * (1.0 + pre_here * (1.0 - gate)))).astype(BF16)
        tally[0:8, :] += fold(d_one.astype(F32))
        bufs[0, place, :] = d_one
        bufs[1, place, :] = (pre_here * gate).astype(BF16)
        bufs[2, place, :] = d_two
        d_here = dot_nt(d_one, w1[:width, :])
        slot = lax.rem(i, 2)
        used = [
            pltpu.make_async_copy(out_buf.at[slot, n], ref.at[place], out_sem.at[slot, n])
            for n, ref in enumerate((d_edges_out, d_change_out))
            if n or last_layer
        ]

        def free():
            for copy in used:
                copy.wait()

        pl.when(i >= 2)(free)
        if last_layer:
            out_buf[slot, 0] = (d_edge + d_here).astype(BF16)
            out_buf[slot, 1] = d_here.astype(BF16)
        else:
            earlier.wait()
            out_buf[slot, 1] = (out_buf[slot, 0].astype(F32) + d_here).astype(BF16)
        for copy in used:
            copy.start()
        d_sent = dot_nt(d_one, w1[width : 2 * width, :]).astype(BF16)
        for half in range(2):
            ids = rows_of[pair + half]
            part = slice(half * group, (half + 1) * group)
            own_sum[...] += dot(one_hot_rows(ids[1:2, :], node_count), d_one[part])
            spot = pl.ds(pl.multiple_of((pair + half) * node_count, 16), node_count)
            stage[spot, :] = dot(one_hot_rows(ids[0:1, :], node_count), d_sent[part]).astype(BF16)

        def close():
            low = own_sum[...].astype(BF16)
            spot = pl.ds(pl.multiple_of(g.row * node_count, 16), node_count)
            stage[spot, :] = (stage[spot, :].astype(F32) + dot_nt(low, w1[2 * width :, :])).astype(BF16)
            grads[2 * width : 3 * width, :] = dot_tn(block[...], low).astype(BF16)

        pl.when((z == g.z) & (x == g.x))(close)

    def extra(n):
        for i, (at, left, right) in enumerate(((0, 3, 0), (1, 4, 0), (3, 1, 2))):

            def grad(at=at, left=left, right=right):
                grads[at * width : (at + 1) * width, :] = dot_tn(bufs[left], bufs[right]).astype(BF16)

            pl.when(n == i)(grad)

    rs.run(TERMS_ORDER, work, extra)
    rs.last(turned)
    for copy in copies:
        copy.wait()
    d_node_out[...] += turned[...]
    for slot in range(2):
        for n, ref in enumerate((d_edges_out, d_change_out)):
            if n or last_layer:
                pltpu.make_async_copy(out_buf.at[slot, n], ref.at[pl.ds(0, 2 * group)], out_sem.at[slot, n]).wait()
    rs.finish()


def backward_layer(layer, last_layer, d_node, node_saved, cols, rows_of, scale, small, weights, d_edges, edge_saved, node, d_before):
    levels, rows = lax.axis_size("lvl"), lax.axis_size("row")
    width = d_node.shape[1]
    h = d_node.shape[0] // (levels if last_layer else 1)
    count = d_edges.shape[0]
    group = count // rows
    vmem = pl.BlockSpec(memory_space=pltpu.VMEM)
    hbm = pl.BlockSpec(memory_space=pl.ANY)
    shape = jax.ShapeDtypeStruct
    ins = (d_node,) + node_saved + (rows_of,) + small + (node, d_before, cols, scale, d_edges) + edge_saved + weights
    outs = (
        shape((h, width), F32),
        shape((count, width) if last_layer else (16, 128), BF16),
        shape((count, width), BF16),
        shape((7 * width, width), BF16),
        shape((64, width), F32),
        shape((h * levels, width) if last_layer else (16, 128), BF16),
    )
    others = max(levels - 1, 1)
    return pl.pallas_call(
        functools.partial(backward_kernel, layer, levels, rows, last_layer),
        out_shape=outs,
        in_specs=[vmem] * (len(ins) - 12) + [hbm] * 12,
        out_specs=(vmem, hbm, hbm, vmem, vmem, vmem),
        scratch_shapes=[
            pltpu.VMEM((rows * h * levels, width), BF16),
            pltpu.VMEM((Scatter.receives(levels, rows), h, width), BF16),
            pltpu.VMEM((5, count, width), BF16),
            pltpu.VMEM((h * levels, width), BF16),
            pltpu.VMEM((h, width), F32),
            pltpu.VMEM((h * levels, width), F32),
            pltpu.VMEM((2, 2, 2 * group, width), BF16),
            pltpu.VMEM((count, 128), F32),
            pltpu.VMEM((count, 128), F32),
        ]
        + [pltpu.VMEM(weight.shape[1:], BF16) for weight in weights]
        + [
            pltpu.SemaphoreType.DMA((11,)),
            pltpu.SemaphoreType.DMA((2, 2)),
            pltpu.SemaphoreType.DMA((Scatter.sends(levels, rows),)),
            pltpu.SemaphoreType.DMA((2 * Scatter.receives(levels, rows),)),
            pltpu.SemaphoreType.DMA((2 * others,)),
            pltpu.SemaphoreType.DMA((2 * others,)),
                ],
        compiler_params=pltpu.CompilerParams(collective_id=3 + layer, has_side_effects=True, vmem_limit_bytes=VMEM_BYTES),
        name=f"backward_{layer}",
    )(*ins)


def sum_cuts(h):
    return 3 if h % 48 == 0 else 1


def sum_kernel(levels, rows, h, count, *refs):
    d_node, place, update, d_change = refs[:4]
    terms = refs[4 : count + 4]
    (
        out, d_node_all, update_out, d_change_out, stage, inbox, total,
        scatter_send, scatter_recv, gather_send, gather_recv, load_sem, near_send, near_recv,
    ) = refs[count + 4 :]
    g = Grid(levels, rows)
    mine = pl.ds(pl.multiple_of(g.l * d_node.shape[0], d_node.shape[0]), d_node.shape[0])
    d_node_all[mine, :] = d_node[...].astype(BF16)
    pairs = []
    at = 0
    for term in terms:
        pairs.append((term, stage.at[pl.ds(at, term.shape[0])]))
        at += term.shape[0]
    loads = load_all(pairs, load_sem)
    g.greet()
    for copy in loads:
        copy.wait()
    copies = []
    for j in range(1, levels):
        copy = pltpu.make_async_remote_copy(
            d_node_all.at[mine], d_node_all.at[mine], near_send.at[j - 1], near_recv.at[levels - 1 - j], device_id=g.l_other(j)[1], device_id_type=MESH
        )
        copy.start()
        copies.append(copy)
    tiles = place.shape[0]
    size = 256 if tiles % 2 == 0 else 128
    lane = lax.broadcasted_iota(jnp.int32, (128, 128), 1).astype(F32)

    def restore(i):
        pick = []
        for part in range(size // 128):
            spot = jnp.broadcast_to(place[pl.ds(i * (size // 128) + part, 1), :], (128, 128)).astype(F32).T
            pick.append(jnp.concatenate([(spot == lane + float(128 * j)).astype(BF16) for j in range(tiles)], axis=1))
        pick = jnp.concatenate(pick, axis=0)
        here = pl.ds(pl.multiple_of(i * size, size), size)
        update_out[here, :] = dot(pick, update[...]).astype(BF16)
        d_change_out[here, :] = dot(pick, d_change[...]).astype(BF16)

    rs = Scatter(g, stage, inbox, h, scatter_send, scatter_recv)
    after = tiles * 128 // size

    def extra(n):
        pl.when(n < after)(lambda: restore(jnp.minimum(n, after - 1)))

    rs.run(SUM_ORDER, None, extra)

    def more(i, carry):
        restore(i)
        return carry

    if after > 10:
        lax.fori_loop(10, after, more, 0)
    rs.last(total)
    ag = Courier(g, out, h, sum_cuts(h), gather_send, gather_recv)
    ag.own()[...] = total[...].astype(BF16)
    ag.run(ORDER if ag.cuts == 3 else PLAIN_ORDER)
    for copy in copies:
        copy.wait()
    rs.finish()
    ag.finish()


def sum_pieces(d_node, place, update, d_change, terms, call):
    levels, rows = lax.axis_size("lvl"), lax.axis_size("row")
    width = terms[0].shape[1]
    count = sum(term.shape[0] for term in terms)
    h = count // (levels * rows)
    vmem = pl.BlockSpec(memory_space=pltpu.VMEM)
    shape = jax.ShapeDtypeStruct
    return pl.pallas_call(
        functools.partial(sum_kernel, levels, rows, h, len(terms)),
        out_shape=(
            shape((count, width), BF16),
            shape((d_node.shape[0] * levels, width), BF16),
            shape(update.shape, BF16),
            shape(update.shape, BF16),
        ),
        in_specs=[vmem] * 4 + [pl.BlockSpec(memory_space=pl.ANY)] * len(terms),
        out_specs=(vmem,) * 4,
        scratch_shapes=[
            pltpu.VMEM((count, width), BF16),
            pltpu.VMEM((Scatter.receives(levels, rows), h, width), BF16),
            pltpu.VMEM((h, width), F32),
            pltpu.SemaphoreType.DMA((Scatter.sends(levels, rows),)),
            pltpu.SemaphoreType.DMA((2 * Scatter.receives(levels, rows),)),
            pltpu.SemaphoreType.DMA((Courier.sends(levels, rows, sum_cuts(h)),)),
            pltpu.SemaphoreType.DMA((Courier.receives(levels, rows, sum_cuts(h)),)),
            pltpu.SemaphoreType.DMA((len(terms),)),
            pltpu.SemaphoreType.DMA((max(levels - 1, 1),)),
            pltpu.SemaphoreType.DMA((max(levels - 1, 1),)),
        ],
        compiler_params=pltpu.CompilerParams(collective_id=call, has_side_effects=True, vmem_limit_bytes=VMEM_BYTES),
        name=f"sum_{call}",
    )(d_node, place, update, d_change, *terms)


def finish_kernel(parts, smalls, update, d_change, all_sums, node, d_node, edges, cot, edge_out, cot_out, *refs):
    count = len(parts) + smalls
    wide_outs, small_outs = refs[: len(parts)], refs[len(parts) : count]
    rms_out, node_out, d_node_out, sums, rest, lows, ins, outs, wide, sums_sem, low_sem, in_sem, out_sem, wide_sem = refs[count:]
    size, width = ins.shape[2:]
    steps = edges.shape[0] // size
    targets = [(n, i) for n, part in enumerate(parts) for i in range(part)]
    big = sums.shape[1]
    loads = load_all([(all_sums.at[pl.ds(layer * big, big)], sums.at[layer]) for layer in range(2)], sums_sem)
    loads.append(pltpu.make_async_copy(all_sums.at[pl.ds(2 * big, rest.shape[0])], rest, low_sem.at[4]))
    loads[-1].start()

    def load(step):
        here = pl.ds(step * size, size)
        pairs = ((edges, ins.at[step % 2, 0], in_sem.at[step % 2, 0]), (cot, ins.at[step % 2, 1], in_sem.at[step % 2, 1]))
        pairs += ((update, lows.at[step % 2, 0], low_sem.at[step % 2 * 2]), (d_change, lows.at[step % 2, 1], low_sem.at[step % 2 * 2 + 1]))
        return [pltpu.make_async_copy(ref.at[here], to, sem) for ref, to, sem in pairs]

    def leave(step):
        here = pl.ds(step * size, size)
        return [pltpu.make_async_copy(outs.at[step % 2, n], ref.at[here], out_sem.at[step % 2, n]) for n, ref in enumerate((edge_out, cot_out))]

    def widen(at):
        n, i = targets[at % len(targets)]
        ref = wide_outs[n].at[at // len(targets), pl.ds(i * width, width)]
        return pltpu.make_async_copy(wide.at[at % 4], ref, wide_sem.at[at % 4])

    total = 2 * len(targets)
    done = 0
    for copy in load(0):
        copy.start()
    for step in range(steps):
        if step + 1 < steps:
            for copy in load(step + 1):
                copy.start()
        for copy in load(step):
            copy.wait()
        if step >= 2:
            for copy in leave(step - 2):
                copy.wait()
        for n in range(2):
            outs[step % 2, n] = ins[step % 2, n] + lows[step % 2, n].astype(F32)
        for copy in leave(step):
            copy.start()
        if step == 0:
            for copy in loads:
                copy.wait()
        while done < total * (step + 1) // steps:
            if done >= 4:
                widen(done - 4).wait()
            layer, at = done // len(targets), done % len(targets)
            wide[done % 4] = sums[layer, at * width : (at + 1) * width, :].astype(F32)
            widen(done).start()
            done += 1
    few = rest[...].astype(F32)
    for n, out in enumerate(small_outs):
        for layer in range(2):
            out[layer : layer + 1, :] = few[layer * smalls + n : layer * smalls + n + 1]
    rms_out[...] = few[2 * smalls : 2 * smalls + 1]
    node_out[...] = node[...].astype(F32)
    d_node_out[...] = d_node[...].astype(F32)
    for step in range(max(steps - 2, 0), steps):
        for copy in leave(step):
            copy.wait()
    for at in range(total - 4, total):
        widen(at).wait()


def finish_all(update, d_change, all_sums, node, d_node, edges, cot, parts, smalls):
    count, width = edges.shape
    size = 512 if count % 512 == 0 else 128
    vmem = pl.BlockSpec(memory_space=pltpu.VMEM)
    hbm = pl.BlockSpec(memory_space=pl.ANY)
    shape = jax.ShapeDtypeStruct
    wide = (shape((count, width), F32),) * 2 + tuple(shape((2, part * width, width), F32) for part in parts)
    narrow = (shape((2, width), F32),) * smalls + (shape((1, width), F32), shape(node.shape, F32), shape(node.shape, F32))
    return pl.pallas_call(
        functools.partial(finish_kernel, parts, smalls),
        out_shape=wide + narrow,
        in_specs=[hbm] * 3 + [vmem] * 2 + [hbm] * 2,
        out_specs=(hbm,) * len(wide) + (vmem,) * len(narrow),
        scratch_shapes=[
            pltpu.VMEM((2, sum(parts) * width, width), BF16),
            pltpu.VMEM((32, width), BF16),
            pltpu.VMEM((2, 2, size, width), BF16),
            pltpu.VMEM((2, 2, size, width), F32),
            pltpu.VMEM((2, 2, size, width), F32),
            pltpu.VMEM((4, width, width), F32),
            pltpu.SemaphoreType.DMA((2,)),
            pltpu.SemaphoreType.DMA((5,)),
            pltpu.SemaphoreType.DMA((2, 2)),
            pltpu.SemaphoreType.DMA((2, 2)),
            pltpu.SemaphoreType.DMA((4,)),
        ],
        compiler_params=pltpu.CompilerParams(vmem_limit_bytes=VMEM_BYTES),
        name="finish_all",
    )(update, d_change, all_sums, node, d_node, edges, cot)


def on_device(
    node_latent, edge_latent, senders, receivers, live_edges,
    edge_w1, edge_b1, edge_w2, edge_b2, edge_gain, edge_shift, node_w1, node_b1, node_w2, node_b2, node_gain, node_shift,
    node_cotangent, edge_cotangent,
):
    node_count, width = node_latent.shape
    edge_count = edge_latent.shape[0]
    layers = edge_w1.shape[0]
    row_total, level_total = lax.axis_size("row"), lax.axis_size("lvl")
    node = node_latent
    weights = (edge_w1, edge_w2, node_w1, node_w2)
    small = (edge_b1, edge_b2, edge_gain, edge_shift, node_b1, node_b2, node_gain, node_shift)
    tiles = edge_count // 128
    index = (senders.reshape(tiles, 128), receivers.reshape(tiles, 128), live_edges.reshape(1, 1))
    sent, pre, normed, update, edges, edges_next, place, rows_of, cols, scale, block, node, recv, npre, nnormed, nscale, tally = forward_layer(
        0, node, small, weights, edge_latent, index
    )
    first = ((block, recv, npre, nnormed, nscale), scale, (pre, normed, edges, sent))
    sent, pre, normed, update, d_edges, scale, block, node, recv, npre, nnormed, nscale, tally_last = forward_layer(
        1, node, small, weights, edge_cotangent, (place, rows_of, cols), edges_next, update
    )
    last = ((block, recv, npre, nnormed, nscale), scale, (pre, normed, edges_next, sent))
    tallies = [tally, tally_last]
    d_node = node_cotangent
    gains = (edge_gain, node_gain)
    d_node, d_edges, d_change, last_grads, last_sums, node_all = backward_layer(
        1, True, d_node, last[0], cols, rows_of, last[1], gains, weights, d_edges, last[2], node, d_edges
    )
    d_node, _, d_change, first_grads, first_sums, _ = backward_layer(
        0, False, d_node, first[0], cols, rows_of, first[1], gains, weights, d_edges, first[2], node, d_change
    )
    sums = [first_sums, last_sums]
    small = jnp.concatenate([jnp.sum(part.reshape(8, 8, width), axis=1) for part in sums])
    squares = jnp.stack([jnp.sum(tally.reshape(4, 8 * width), axis=1) for tally in tallies])
    squares = jnp.pad(squares.reshape(1, -1), ((0, 0), (0, width - squares.size)))
    devices = row_total * level_total
    used = layers * 7 * width + small.shape[0] + 1
    each = -(-used // (16 * devices)) * 16
    rest = [small.astype(BF16), squares.astype(BF16), jnp.zeros((each * devices - used, width), BF16)]
    flat, d_node_all, update, d_change = sum_pieces(
        d_node, place, update, d_change, [first_grads, last_grads, jnp.concatenate(rest)], 5
    )
    edge_out, edge_grad, w1, w2, nw1, nw2, b1, b2, gain, shift, nb1, nb2, ngain, nshift, squares, node, d_node = finish_all(
        update, d_change, flat, node_all, d_node_all, edge_latent, edge_cotangent, (3, 1, 2, 1), 8
    )
    node_entries = float(node_count * row_total * width)
    edge_entries = float(edge_count * row_total * level_total * width)
    entries = jnp.array([node_entries, edge_entries, edge_entries, node_entries], F32)
    rms = jnp.sqrt(squares[0, : 4 * layers].reshape(layers, 4) / entries[None, :])
    return node, edge_out, d_node, edge_grad, w1, b1, w2, b2, gain, shift, nw1, nb1, nw2, nb2, ngain, nshift, rms


def solution(mesh):
    rows, both, whole = P("row", None), P(("lvl", "row"), None), P()
    edge = P(("lvl", "row"))
    placed = (rows, both, edge, edge, edge) + (whole,) * 12 + (rows, both)
    outs = (rows, both, rows, both) + (whole,) * 13
    return jax.shard_map(on_device, mesh=mesh, in_specs=placed, out_specs=outs, check_vma=False)
```

```python
import functools

import jax
import jax.numpy as jnp
from jax import lax
from jax.experimental import pallas as pl
from jax.experimental.pallas import tpu as pltpu
from jax.sharding import PartitionSpec as P

MESH = pl.DeviceIdType.MESH
NORM_EPS = 1e-05
F32 = jnp.float32
BF16 = jnp.bfloat16
VMEM_BYTES = 61 * 2**20


FIRST_ORDER = (
    (
        1089728, 289296, 536069, 551556, 141360, 612561, 159764, 1528408, 356492, 400397,
        858841, 422440, 750249, 990892, 1707549, 1799737, 2097129,
    ),
    (
        1089728, 1392676, 131237, 197853, 1464864, 215760, 1448028, 272952, 399521, 881172,
        290876, 745128, 724581, 482457, 1774801, 1717985, 2097129,
    ),
)
LAST_ORDER = (
    (
        1089728, 526421, 84180, 1507921, 141360, 1530017, 159781, 1462872, 880781, 919081,
        330920, 854680, 745060, 480869, 466664, 1799737, 2097129,
    ),
    (
        1089728, 600797, 338944, 607233, 154201, 214620, 1378337, 920240, 815648, 988240,
        1575989, 1004689, 415277, 937573, 487633, 1734248, 2097133,
    ),
)
ORDER = (
    (
        67728, 295584, 137222, 165041, 594213, 203041, 216120, 630414, 724277, 691860,
        860188, 365736, 744729, 986937, 1022741, 2097070,
    ),
    (
        133632, 152228, 17702, 199298, 856077, 808974, 678584, 985110, 727841, 416061,
        942120, 693914, 563002, 286492, 397085, 2097042,
    ),
)
PLAIN_ORDER = (
    (
        524816, 133680, 204836, 857112, 923164, 2097084,
    ),
    (
        328704, 526372, 401420, 793128, 923164, 2097084,
    ),
)

TERMS_ORDER = (
    (
        246535, 230038, 329348, 54046, 34332, 180388, 147502, 722962, 432138, 820258,
        692248, 2097073,
    ),
    (
        115332, 247427, 184844, 19218, 328838, 233232, 463616, 397320, 431874, 558380,
        825512, 2097072,
    ),
)
SUM_ORDER = (
    (
        66311, 934531, 232207, 21296, 36621, 331276, 591287, 835634, 760841, 267794,
        804122, 399906, 888840, 2087594,
    ),
    (
        786951, 246531, 82078, 181810, 367396, 3346, 214199, 329752, 230402, 529162,
        466099, 563374, 922668, 2087604,
    ),
)


NEAREST = ((0, 1, 2, 3), (1, 0, 2, 3), (2, 3, 1, 0), (3, 2, 1, 0))


class Grid:
    def __init__(self, levels, rows):
        self.L, self.R = levels, rows
        self.Z = 4
        self.X = rows // (2 * self.Z)
        self.l = lax.axis_index("lvl")
        row = lax.axis_index("row")
        self.row = row
        self.core = lax.rem(row, 2)
        self.x = lax.rem(row // 2, self.X)
        self.z = row // (2 * self.X)
        self.up = self.z < self.Z - 1
        self.down = self.z > 0

    def block(self, z, x, core):
        return (z * self.X + x) * 2 + core

    def mate(self):
        return (self.l, self.block(self.z, self.x, 1 - self.core))

    def at_z(self, z):
        return (self.l, self.block(jnp.clip(z, 0, self.Z - 1), self.x, self.core))

    def x_other(self, i):
        x = lax.rem(self.x + i, self.X)
        return x, (self.l, self.block(self.z, x, self.core))

    def l_other(self, i):
        l = lax.rem(self.l + i, self.L)
        return l, (l, self.row)

    def nth(self, k, z=None):
        z_here = self.z if z is None else z
        order = NEAREST
        out = jnp.int32(0)
        for z in range(4):
            for j in range(4):
                if order[z][j]:
                    out = jnp.where((z_here == z) & (k == j), order[z][j], out)
        return out

    def local(self, zk, z=None):
        return (zk // 2) == lax.rem(self.z if z is None else z, 2)

    def corner_z(self, q):
        side = lax.rem(lax.rem(self.z, 2) + q // 2, 2)
        return side * 2 + lax.rem(q, 2)

    def pair_z(self):
        return self.z + 1 - 2 * lax.rem(self.z, 2)

    def greet(self):
        barrier = pltpu.get_barrier_semaphore()

        def hello(who):
            pl.semaphore_signal(barrier, inc=1, device_id=who, device_id_type=MESH)

        hello(self.mate())
        for i in range(1, self.X):
            hello(self.x_other(i)[1])
        for i in range(1, self.L):
            hello(self.l_other(i)[1])
        pl.when(self.up)(lambda: hello(self.at_z(self.z + 1)))
        pl.when(self.down)(lambda: hello(self.at_z(self.z - 1)))
        pl.semaphore_wait(barrier, self.X + self.L - 1 + self.up.astype(jnp.int32) + self.down.astype(jnp.int32))


def only(when, act):
    if when is None:
        act()
    else:
        pl.when(when)(act)


def cuts(h):
    first = -(-h // 32) * 16
    return ((0, first), (first, h - first)) if h > first else ((0, h),)


class Courier:
    def __init__(self, grid, table, h, cuts, send_sem, recv_sem):
        self.g, self.table, self.h = grid, table, h
        self.cuts = cuts
        self.size = h // self.cuts
        self.send_sem, self.recv_sem = send_sem, recv_sem
        self.drain = False

    @staticmethod
    def kinds(levels, rows):
        X, L = rows // 8, levels
        return (X + L + 1, (X - 1) * L, (L - 1) * X, 3 * (X - 1) * (L - 1))

    @staticmethod
    def sends(levels, rows, cuts):
        return 4 * sum(Courier.kinds(levels, rows)) * cuts

    @staticmethod
    def receives(levels, rows, cuts):
        return levels * rows * cuts

    def at(self, kind, zk, n, s):
        counts = self.kinds(self.g.L, self.g.R)
        return (4 * sum(counts[:kind]) + zk * counts[kind] + n) * self.cuts + s

    def slot(self, block, l, s=0, size=None):
        start = (block * self.g.L + l) * self.h + s * self.size
        return self.table.at[pl.ds(pl.multiple_of(start, 16), size or self.size)]

    def own(self):
        return self.slot(self.g.row, self.g.l, 0, self.h)

    def push(self, at, block, l, s, who, when=None):
        place = self.slot(block, l, s)
        copy = pltpu.make_async_remote_copy(
            place,
            place,
            self.send_sem.at[at],
            self.recv_sem.at[(block * self.g.L + l) * self.cuts + s],
            device_id=who,
            device_id_type=MESH,
        )
        only(when, copy.wait_send if self.drain else copy.start)

    def arrived(self, block, l, s):
        if self.drain:
            return
        place = self.slot(block, l, s)
        pltpu.make_async_remote_copy(
            place,
            place,
            self.send_sem.at[0],
            self.recv_sem.at[(block * self.g.L + l) * self.cuts + s],
            device_id=self.g.mate(),
            device_id_type=MESH,
        ).wait_recv()

    def near(self, zk):
        z = self.g.z
        return (zk == z) | ((z == 0) & (zk == 1)) | ((z == 3) & (zk == 2))

    def even(self, zk):
        return lax.rem(jnp.where(self.g.z < 2, zk, 3 - zk), 2) == 0

    def column(self, zk, s, own=False):
        g = self.g
        block = g.block(zk, g.x, g.core)
        if not own:
            self.arrived(block, g.l, s)
        self.push(self.at(0, zk, 0, s), block, g.l, s, g.at_z(g.z + 1), g.up & (zk <= g.z))
        self.push(self.at(0, zk, 1, s), block, g.l, s, g.at_z(g.z - 1), g.down & (zk >= g.z))
        for i in range(1, g.X):
            self.push(self.at(0, zk, 1 + i, s), block, g.l, s, g.x_other(i)[1])
        for j in range(1, g.L):
            self.push(self.at(0, zk, g.X + j, s), block, g.l, s, g.l_other(j)[1])
        self.push(self.at(0, zk, g.X + g.L, s), block, g.l, s, g.mate())

    def side_x(self, zk, s):
        g = self.g
        n = 0
        for i in range(1, g.X):
            block = g.block(zk, g.x_other(i)[0], g.core)
            self.arrived(block, g.l, s)
            for j in range(1, g.L):
                self.push(self.at(1, zk, n, s), block, g.l, s, g.l_other(j)[1], self.near(zk) & self.even(zk))
                n += 1
            self.push(self.at(1, zk, n, s), block, g.l, s, g.mate())
            n += 1

    def side_l(self, zk, s):
        g = self.g
        block = g.block(zk, g.x, g.core)
        n = 0
        for j in range(1, g.L):
            l = g.l_other(j)[0]
            self.arrived(block, l, s)
            for i in range(1, g.X):
                self.push(self.at(2, zk, n, s), block, l, s, g.x_other(i)[1], self.near(zk) & jnp.logical_not(self.even(zk)))
                n += 1
            self.push(self.at(2, zk, n, s), block, l, s, g.mate())
            n += 1

    def corner(self, zk, s):
        g = self.g
        n = 0
        for i in range(1, g.X):
            block = g.block(zk, g.x_other(i)[0], g.core)
            for j in range(1, g.L):
                l = g.l_other(j)[0]
                self.arrived(block, l, s)
                self.push(self.at(3, zk, n, s), block, l, s, g.at_z(g.z + 1), (zk <= 1) & (g.z >= zk) & g.up)
                self.push(self.at(3, zk, n + 1, s), block, l, s, g.at_z(g.z - 1), (zk >= 2) & (g.z <= zk) & g.down)
                self.push(self.at(3, zk, n + 2, s), block, l, s, g.mate())
                n += 3

    def mates(self, zk, x):
        def one(i, carry):
            self.arrived(self.g.block(zk, x, 1 - self.g.core), i // self.cuts, lax.rem(i, self.cuts))
            return carry

        lax.fori_loop(0, self.g.L * self.cuts, one, 0)

    def run(self, tables, meanwhile=None, prepare=None, work=None):
        g = self.g
        for s in range(self.cuts):
            self.column(g.z, s, own=True)
        low = g.z < 2
        first = (g.z == 0) | (g.z == 3)

        def one(m, done):
            word = jnp.int32(0)
            for at, (a, b) in enumerate(zip(*tables)):
                word = jnp.where(m // 3 == at, jnp.where(first, a, b), word)
            byte = lax.rem(m, 3)
            code = lax.rem(jnp.where(byte == 0, word, jnp.where(byte == 1, word // 128, word // 16384)), 128)
            zk = lax.rem(code // 4, 4)
            zk = jnp.where(low, zk, 3 - zk)
            s = lax.rem(code, 4)
            kind = code // 16
            pl.when(kind == 0)(lambda: self.column(zk, s))
            if g.X > 1:
                pl.when(kind == 1)(lambda: self.side_x(zk, s))
            if g.L > 1:
                pl.when(kind == 2)(lambda: self.side_l(zk, s))
            if g.X > 1 and g.L > 1:
                pl.when(kind == 3)(lambda: self.corner(zk, s))
            if meanwhile is not None:
                for at in range(3):
                    pl.when(code == 64 + at)(lambda at=at: meanwhile(at))
            count = jnp.int32(0)
            if work is not None:
                for off in range(g.X):
                    x = lax.rem(g.x + off, g.X)
                    hit = s == (0 if off == 0 else 1)
                    pl.when((kind == 5) & hit)(lambda x=x: prepare(zk, x))

                    def full(x=x, off=off):
                        self.mates(zk, x)
                        work(zk, x, done + max(off - 1, 0))

                    pl.when((kind == 6) & hit)(full)
                count = jnp.where(kind == 6, jnp.where(s == 0, 1, g.X - 1), 0)
            return done + count

        lax.fori_loop(0, 3 * len(tables[0]), one, jnp.int32(0))
        if work is None:

            def last(i, carry):
                self.mates(i // g.X, lax.rem(i, g.X))
                return carry

            lax.fori_loop(0, 4 * g.X, last, 0)

    def finish(self):
        self.drain = True

        def one(i, carry):
            zk, s = i // self.cuts, lax.rem(i, self.cuts)
            self.column(zk, s)
            self.side_x(zk, s)
            self.side_l(zk, s)
            self.corner(zk, s)
            return carry

        lax.fori_loop(0, 4 * self.cuts, one, 0)


class Scatter:
    def __init__(self, grid, stage, inbox, h, send_sem, recv_sem):
        self.g, self.stage, self.inbox, self.h = grid, stage, inbox, h
        self.cuts = cuts(h)
        self.send_sem, self.recv_sem = send_sem, recv_sem
        X, L = grid.X, grid.L
        at = 0
        self.base = {}
        for name, count in self.parts(X, L):
            self.base[name] = at
            at += count
        at = 0
        self.out = {}
        for name, count in self.out_parts(X, L):
            self.out[name] = at
            at += count
        self.drain = False

    @staticmethod
    def parts(X, L):
        side = (X - 1) * (L - 1)
        return (("mate", 4 * X * L), ("pair", 2 * side), ("l2", side), ("x2", side), ("xc", 4 * (X - 1)), ("lc", 4 * (L - 1)), ("z", 5))

    @staticmethod
    def out_parts(X, L):
        side = (X - 1) * (L - 1)
        return (("mate", 4 * X * L), ("corner", 8 * side), ("xc", 4 * (X - 1)), ("lc", 4 * (L - 1)), ("z", 4))

    @staticmethod
    def receives(levels, rows):
        return sum(count for _, count in Scatter.parts(rows // 8, levels))

    @staticmethod
    def sends(levels, rows):
        return 2 * sum(count for _, count in Scatter.out_parts(rows // 8, levels))

    def slot(self, block, l, s=None):
        start, size = (0, self.h) if s is None else self.cuts[s]
        return self.stage.at[pl.ds(pl.multiple_of((block * self.g.L + l) * self.h + start, 16), size)]

    def push(self, out, block, l, s, at, who, when=None):
        start, size = self.cuts[s]
        copy = pltpu.make_async_remote_copy(
            self.slot(block, l, s),
            self.inbox.at[at, pl.ds(start, size)],
            self.send_sem.at[2 * out + s],
            self.recv_sem.at[2 * at + s],
            device_id=who,
            device_id_type=MESH,
        )
        only(when, copy.wait_send if self.drain else copy.start)

    def arrived(self, at, s):
        start, size = self.cuts[s]
        place = self.inbox.at[at, pl.ds(start, size)]
        pltpu.make_async_remote_copy(
            place, place, self.send_sem.at[0], self.recv_sem.at[2 * at + s], device_id=self.g.mate(), device_id_type=MESH
        ).wait_recv()

    def total(self, block, l, s, ats):
        start, size = self.cuts[s]
        for at in ats:
            self.arrived(at, s)
        out = self.slot(block, l, s)[...].astype(F32)
        for at in ats:
            out = out + self.inbox[at, start : start + size].astype(F32)
        return out

    def add(self, block, l, s, ats, when=None):
        if self.drain:
            return

        def act():
            self.slot(block, l, s)[...] = self.total(block, l, s, ats).astype(BF16)

        only(when, act)

    def each(self):
        return range(len(self.cuts))

    def to_mate(self, z, x):
        g = self.g
        for l in range(g.L):
            at = (z * g.X + x) * g.L + l
            for s in self.each():
                self.push(self.out["mate"] + at, g.block(z, x, 1 - g.core), l, s, self.base["mate"] + at, g.mate())

    def from_mate(self, z, x):
        g = self.g
        for l in range(g.L):
            for s in self.each():
                self.add(g.block(z, x, g.core), l, s, [self.base["mate"] + (z * g.X + x) * g.L + l])

    def corner_far(self, z, i):
        g = self.g
        block = g.block(z, lax.rem(g.x + i, g.X), g.core)
        for j in range(1, g.L):
            l = g.l_other(j)[0]
            spot = (lax.rem(z, 2) * (g.X - 1) + i - 1) * (g.L - 1) + j - 1
            for s in self.each():
                self.push(self.out["corner"] + spot, block, l, s, self.base["pair"] + spot, g.at_z(g.pair_z()))

    def corner_near(self, z, i):
        g = self.g
        x, x_dev = g.x_other(i)
        block = g.block(z, x, g.core)
        even = self.even(z)
        side = (g.X - 1) * (g.L - 1)
        for j in range(1, g.L):
            l, l_dev = g.l_other(j)
            spot = (lax.rem(z, 2) * (g.X - 1) + i - 1) * (g.L - 1) + j - 1
            out = self.out["corner"] + 2 * side + spot
            for s in self.each():
                self.add(block, l, s, [self.base["pair"] + spot])
                self.push(out, block, l, s, self.base["l2"] + (i - 1) * (g.L - 1) + g.L - j - 1, l_dev, even)
                self.push(out, block, l, s, self.base["x2"] + (g.X - i - 1) * (g.L - 1) + j - 1, x_dev, jnp.logical_not(even))

    def side_x(self, zk, i, waits):
        g = self.g
        x, x_dev = g.x_other(i)
        block = g.block(zk, x, g.core)
        ats = [self.base["l2"] + (i - 1) * (g.L - 1) + j - 1 for j in range(1, g.L)]
        for s in self.each():
            if ats and waits:
                self.add(block, g.l, s, ats)
            self.push(self.out["xc"] + zk * (g.X - 1) + i - 1, block, g.l, s, self.base["xc"] + zk * (g.X - 1) + g.X - i - 1, x_dev)

    def side_l(self, zk, waits):
        g = self.g
        block = g.block(zk, g.x, g.core)
        for j in range(1, g.L):
            l, l_dev = g.l_other(j)
            ats = [self.base["x2"] + (i - 1) * (g.L - 1) + j - 1 for i in range(1, g.X)]
            for s in self.each():
                if waits:
                    self.add(block, l, s, ats)
                self.push(self.out["lc"] + zk * (g.L - 1) + j - 1, block, l, s, self.base["lc"] + zk * (g.L - 1) + g.L - j - 1, l_dev)

    def around(self, zk):
        g = self.g
        ats = [self.base["xc"] + zk * (g.X - 1) + i - 1 for i in range(1, g.X)]
        return ats + [self.base["lc"] + zk * (g.L - 1) + j - 1 for j in range(1, g.L)]

    def column(self, zk):
        g = self.g
        block = g.block(zk, g.x, g.core)
        behind = jnp.where(zk > g.z, g.down, g.up)
        near = jnp.abs(zk - g.z) == 1
        spot = jnp.where(near & (zk < g.z), 4, zk)
        for s in self.each():
            self.add(block, g.l, s, self.around(zk))
            self.add(block, g.l, s, [self.base["z"] + zk], behind)
            self.push(self.out["z"] + zk, block, g.l, s, self.base["z"] + spot, g.at_z(jnp.where(zk > g.z, g.z + 1, g.z - 1)))

    def last(self, out):
        g = self.g
        for s in self.each():
            start, size = self.cuts[s]
            out[start : start + size, :] = self.total(g.row, g.l, s, self.around(g.z))
            for at, there in ((self.base["z"] + g.z, g.down), (self.base["z"] + 4, g.up)):

                def take(at=at, s=s, start=start, size=size):
                    self.arrived(at, s)
                    out[start : start + size, :] += self.inbox[at, start : start + size].astype(F32)

                pl.when(there)(take)

    def even(self, zk):
        return lax.rem(jnp.where(self.g.z < 2, zk, 3 - zk), 2) == 0

    def decode(self, m):
        g = self.g
        first = (g.z == 0) | (g.z == 3)
        word = jnp.int32(0)
        for at, (a, b) in enumerate(zip(*self.tables)):
            word = jnp.where(m // 3 == at, jnp.where(first, a, b), word)
        byte = lax.rem(m, 3)
        code = lax.rem(jnp.where(byte == 0, word, jnp.where(byte == 1, word // 128, word // 16384)), 128)
        zk = lax.rem(code // 2, 4)
        return code, code // 8, jnp.where(g.z < 2, zk, 3 - zk), lax.rem(code, 2)

    def step(self, m, work=None, extra=None, done=0):
        g = self.g
        code, kind, zk, side = self.decode(m)
        for off in range(g.X):
            x = lax.rem(g.x + off, g.X)
            hit = side == (0 if off == 0 else 1)

            def make(x=x, off=off):
                if work is not None and not self.drain:
                    work(zk, x, done + max(off - 1, 0))
                self.to_mate(zk, x)

            pl.when((kind == 0) & hit)(make)
            if not self.drain:
                pl.when((kind == 1) & hit)(lambda x=x: self.from_mate(zk, x))
        near = g.local(zk)
        for i in range(1, g.X):
            if g.L > 1:
                pl.when((kind == 2) & near)(lambda i=i: self.corner_near(zk, i))
                pl.when((kind == 2) & jnp.logical_not(near))(lambda i=i: self.corner_far(zk, i))
            late = near & self.even(zk)
            pl.when((kind == 3) & late)(lambda i=i: self.side_x(zk, i, True))
            pl.when((kind == 3) & jnp.logical_not(late))(lambda i=i: self.side_x(zk, i, False))
        if g.L > 1:
            late = near & jnp.logical_not(self.even(zk))
            pl.when((kind == 4) & late)(lambda: self.side_l(zk, True))
            pl.when((kind == 4) & jnp.logical_not(late))(lambda: self.side_l(zk, False))
        pl.when(kind == 5)(lambda: self.column(zk))
        if extra is not None and not self.drain:
            pl.when(kind >= 6)(lambda: extra(code - 48))
        return jnp.where(kind == 0, jnp.where(side == 0, 1, g.X - 1), 0)

    def go(self, m, ahead, work=None, extra=None, done=0):
        count = self.step(m, work, extra, done)

        def wait():
            self.drain = True
            self.step(m - ahead)
            self.drain = False

        pl.when(m >= ahead)(wait)
        return count

    def run(self, tables, work=None, extra=None, beside=None, ahead=20):
        self.follow(tables, ahead)

        def one(m, done):
            count = self.go(m, self.ahead, work, extra, done)
            if beside is not None:
                beside(m)
            return done + count

        lax.fori_loop(0, self.steps, one, jnp.int32(0))

    def follow(self, tables, ahead):
        self.tables = tables
        self.steps = 3 * len(tables[0])
        self.ahead = min(ahead, self.steps)

    def finish(self):
        self.drain = True

        def one(m, carry):
            self.step(m)
            return carry

        lax.fori_loop(self.steps - self.ahead, self.steps, one, 0)


def dot(left, right):
    return jnp.dot(left, right, preferred_element_type=F32)


def dot_nt(left, right):
    return lax.dot_general(left, right, (((1,), (1,)), ((), ())), preferred_element_type=F32)


def dot_tn(left, right):
    return lax.dot_general(left, right, (((0,), (0,)), ((), ())), preferred_element_type=F32)


def fold(values):
    rows, width = values.shape
    return jnp.sum(values.reshape(rows // 8, 8, width), axis=0)


def norm_parts(values):
    average = jnp.mean(values, axis=-1, keepdims=True)
    centered = values - average
    scale = lax.rsqrt(jnp.mean(centered * centered, axis=-1, keepdims=True) + NORM_EPS)
    return centered * scale, scale


def norm_back(normed, scale, d_normed):
    mean_d = jnp.mean(d_normed, axis=-1, keepdims=True)
    mean_dn = jnp.mean(d_normed * normed, axis=-1, keepdims=True)
    return scale * (d_normed - mean_d - normed * mean_dn)


def silu_back(pre, d_active):
    gate = lax.logistic(pre)
    return d_active * (gate * (1.0 + pre * (1.0 - gate)))


def find_places(row_total, node_count, some, senders, receivers, live, place, side, facts_out, counts):
    tiles = senders.shape[0]
    group = tiles * 128 // row_total
    first = lax.axis_index("row") * node_count
    lane = lax.broadcasted_iota(jnp.int32, (128, 128), 1)
    sub = lax.broadcasted_iota(jnp.int32, (128, 128), 0)
    before = (sub < lane).astype(BF16)
    owner_ids = lax.broadcasted_iota(jnp.int32, (row_total, 128), 0)
    carry = owner_ids[:, :1].astype(F32) * group if some[0] == 0 else counts[:, 0:1]
    for tile in some:
        send = senders[tile : tile + 1, :]
        recv = receivers[tile : tile + 1, :] - first
        owner = lax.div(send, node_count)
        local = send - owner * node_count
        mine = owner_ids == owner
        ranks = dot(mine.astype(BF16), before) + carry
        spot = jnp.sum(jnp.where(mine, ranks, 0.0), axis=0, keepdims=True)
        carry = carry + jnp.sum(mine.astype(F32), axis=1, keepdims=True)
        place[tile : tile + 1, :] = spot.astype(jnp.int32)
        alive = (lane[:1] + tile * 128 < live[0, 0]).astype(jnp.int32)
        facts = jnp.where(sub == 0, lax.div(local, 16), 0)
        facts = jnp.where(sub == 1, lax.rem(local, 16), facts)
        facts = jnp.where(sub == 2, lax.div(recv, 16), facts)
        facts = jnp.where(sub == 3, lax.rem(recv, 16), facts)
        facts = jnp.where(sub == 4, alive, facts).astype(F32)
        side[:, pl.ds(tile * 128, 128)] = facts[:16].astype(BF16)
        facts_out[pl.ds(tile * 128, 128), :] = facts.T.astype(BF16)
    counts[...] = jnp.broadcast_to(carry, counts.shape)


def picker(place, start, size):
    ids = lax.broadcasted_iota(jnp.int32, (size, 128), 0) + start
    return jnp.concatenate([(ids == place[tile : tile + 1, :]).astype(BF16) for tile in range(place.shape[0])], axis=1)


def one_hot_cols(ids, count):
    lanes = lax.broadcasted_iota(jnp.int32, (ids.shape[0], count), 1).astype(F32)
    return (ids == lanes).astype(BF16)


def one_hot_rows(ids, count):
    subs = lax.broadcasted_iota(jnp.int32, (count, ids.shape[1]), 0).astype(F32)
    return (ids == subs).astype(BF16)


def load_all(pairs, sems):
    copies = [pltpu.make_async_copy(src, dst, sems.at[i]) for i, (src, dst) in enumerate(pairs)]
    for copy in copies:
        copy.start()
    return copies


def forward_kernel(
    layer, levels, rows, first_layer, *refs
):
    (node, b1, b2, gain, shift, nb1, nb2, ngain, nshift, w1_all, w2_all, nw1_all, nw2_all, plain_all) = refs[:14]
    refs = refs[14:]
    if first_layer:
        senders, receivers, live = refs[:3]
        refs = refs[3:]
    else:
        place, rows_of, cols_all, edges_all, before_all = refs[:5]
        refs = refs[5:]
    sent_out, pre_out, normed_out, update_out, moved_out = refs[:5]
    refs = refs[5:]
    if first_layer:
        edges_out, place, rows_of, cols = refs[:4]
        refs = refs[4:]
    scale_out, block_out, node_out, recv_out, npre_out, nnormed_out, nscale_out, tally = refs[:8]
    (
        table, total, cast, near, far, w1, w2, nw1, nw2, plain, joined, ordered, out_buf, scale_buf,
        load_sem, out_sem, moved_sem, send_sem, recv_sem, near_send, near_recv,
    ) = refs[8:29]
    if first_layer:
        side, counts = refs[29:]
    else:
        cols, edges, before = refs[29:]
    g = Grid(levels, rows)
    h, width = node_out.shape
    if first_layer:
        node = node.at[pl.ds(pl.multiple_of(g.l * h, h), h)]
    count = plain.shape[0]
    group = count // rows
    node_count = h * levels
    pairs = ((plain_all, plain), (w1_all.at[layer], w1), (w2_all.at[layer], w2), (nw1_all.at[layer], nw1), (nw2_all.at[layer], nw2))
    if not first_layer:
        pairs += ((cols_all, cols), (edges_all, edges), (before_all, before))
    loads = load_all(pairs, load_sem)
    ag = Courier(g, table, h, 2, send_sem, recv_sem)
    ag.own()[...] = node[...].astype(BF16)
    tally[...] = jnp.zeros_like(tally)
    total[...] = jnp.zeros_like(total)
    g.greet()
    wide = lambda ref: ref[layer : layer + 1, :]
    outs = (sent_out, pre_out, normed_out, update_out) + ((edges_out,) if first_layer else ())

    def meanwhile(at):
        if first_layer:
            tiles = place.shape[0]
            some = range(at * tiles // 3, (at + 1) * tiles // 3)
            find_places(rows, node_count, some, senders, receivers, live, place, side, joined.at[:, pl.ds(width, 128)], counts)
        if at == 0:
            for copy in loads:
                copy.wait()

        def cast_rows(i, carry):
            part = pl.ds(pl.multiple_of(i * 2 * group, 2 * group), 2 * group)
            joined[part, 0:width] = plain[part, :].astype(BF16)
            return carry

        lax.fori_loop(at * rows // 6, (at + 1) * rows // 6, cast_rows, 0)

    def leave(n, part):
        slot = lax.rem(n, 2)
        copies = [pltpu.make_async_copy(out_buf.at[slot, i], ref.at[part], out_sem.at[slot, i]) for i, ref in enumerate(outs)]
        return copies + [pltpu.make_async_copy(scale_buf.at[slot], scale_out.at[part], out_sem.at[slot, 5])]

    def spot(z, x):
        pair = g.block(z, x, 0)
        first = pl.multiple_of(pair * group, 2 * group)
        return pair, first, pl.ds(first, 2 * group)

    def moved_copy(z, x):
        part = spot(z, x)[2]
        return pltpu.make_async_copy(ordered.at[part], moved_out.at[part], moved_sem.at[z * g.X + x])

    def prepare(z, x):
        pair, first, part = spot(z, x)
        pick = picker(place, first, 2 * group)
        moved = dot(pick, joined[...])
        ordered[part, :] = moved[:, :width].astype(BF16)
        moved_copy(z, x).start()
        if first_layer:
            digits = moved[:, width:]
            lanes = lax.broadcasted_iota(jnp.int32, digits.shape, 1)
            ids = digits[:, 0:1] * 16.0 + digits[:, 1:2]
            got = digits[:, 2:3] * 16.0 + digits[:, 3:4]
            cols[part, :] = jnp.where(lanes == 0, ids, jnp.where(lanes == 1, got, jnp.where(lanes == 2, digits[:, 4:5], 0.0)))
            for half in range(2):
                digits = dot_nt(side[...], pick[half * group : (half + 1) * group])
                rows_of[pair + half] = jnp.concatenate(
                    [digits[0:1] * 16.0 + digits[1:2], digits[2:3] * 16.0 + digits[3:4], digits[4:10]], axis=0
                )

    def work(z, x, n):
        def own():
            here = table[pl.ds(pl.multiple_of(g.row * node_count, 16), node_count), :]
            cast[...] = dot(here, w1[2 * width :, :]).astype(BF16)
            block_out[...] = here

        pl.when(n == 0)(own)
        pair, first, part = spot(z, x)

        def free():
            for copy in leave(n, part):
                copy.wait()

        pl.when(n >= 2)(free)
        slot = lax.rem(n, 2)
        low = ordered[part, :] if first_layer else edges[part, :]
        cols_here = cols[part, :]
        send_pick = one_hot_cols(cols_here[:, 0:1], node_count)
        recv_pick = one_hot_cols(cols_here[:, 1:2], node_count)
        start = pl.multiple_of(pair * node_count, 16)
        sent = jnp.concatenate(
            [
                dot(send_pick[:group], table[pl.ds(start, node_count), :]).astype(BF16),
                dot(send_pick[group:], table[pl.ds(start + node_count, node_count), :]).astype(BF16),
            ],
            axis=0,
        )
        out_buf[slot, 0] = sent
        pre = dot(low, w1[:width, :]) + dot(sent, w1[width : 2 * width, :]) + dot(recv_pick, cast[...]) + wide(b1)
        out_buf[slot, 1] = pre.astype(BF16)
        active = (pre * lax.logistic(pre)).astype(BF16)
        normed, scale = norm_parts(dot(active, w2[...]) + wide(b2))
        out_buf[slot, 2] = normed.astype(BF16)
        scale_buf[slot] = jnp.broadcast_to(scale, (2 * group, 128))
        update = (normed * wide(gain) + wide(shift)) * cols_here[:, 2:3]
        update_low = update.astype(BF16)
        edge = low.astype(F32) + update
        if first_layer:
            out_buf[slot, 3] = update_low
            out_buf[slot, 4] = edge.astype(BF16)
        else:
            out_buf[slot, 3] = (before[part, :].astype(F32) + update).astype(BF16)
        tally[8:16, :] += fold(edge * edge)
        tally[16:24, :] += fold(update * update)
        for half in range(2):
            pick = one_hot_rows(rows_of[pair + half][1:2, :], node_count)
            total[...] += dot(pick, update_low[half * group : (half + 1) * group])
        for copy in leave(n, part):
            copy.start()

    ag.run(FIRST_ORDER if first_layer else LAST_ORDER, meanwhile, prepare, work)
    copies = []
    for j in range(1, levels):
        l, l_dev = g.l_other(j)
        near[j - 1] = total[pl.ds(pl.multiple_of(l * h, h), h), :].astype(BF16)
        copy = pltpu.make_async_remote_copy(
            near.at[j - 1], far.at[levels - 1 - j], near_send.at[j - 1], near_recv.at[levels - 1 - j], device_id=l_dev, device_id_type=MESH
        )
        copy.start()
        copies.append(copy)
    received = total[pl.ds(pl.multiple_of(g.l * h, h), h), :]
    npre = dot(node[...].astype(BF16), nw1[:width, :]) + wide(nb1)
    for copy in copies:
        copy.wait()
    for j in range(1, levels):
        received = received + far[j - 1].astype(F32)
    received = received.astype(BF16)
    recv_out[...] = received
    npre = npre + dot(received, nw1[width:, :])
    npre_out[...] = npre
    nnormed, nscale = norm_parts(dot((npre * lax.logistic(npre)).astype(BF16), nw2[...]) + wide(nb2))
    nnormed_out[...] = nnormed
    nscale_out[...] = jnp.broadcast_to(nscale, (h, 128))
    change = nnormed * wide(ngain) + wide(nshift)
    new = node[...] + change
    node_out[...] = new
    tally[0:8, :] = fold(new * new)
    tally[24:32, :] = fold(change * change)
    for n in range(2):
        for copy in leave(n, pl.ds(0, 2 * group)):
            copy.wait()
    for n in range(4 * g.X):
        moved_copy(n // g.X, n % g.X).wait()
    ag.finish()


def forward_layer(layer, node, small, weights, plain, index, edges=None, before=None):
    levels, rows = lax.axis_size("lvl"), lax.axis_size("row")
    width = node.shape[1]
    h = node.shape[0] // (levels if layer == 0 else 1)
    count = plain.shape[0]
    group = count // rows
    vmem = pl.BlockSpec(memory_space=pltpu.VMEM)
    hbm = pl.BlockSpec(memory_space=pl.ANY)
    first_layer = layer == 0
    shape = jax.ShapeDtypeStruct
    wide = shape((count, width), BF16)
    ins = (node,) + small + weights + (plain,) + index
    in_specs = [vmem] * 9 + [hbm] * 5
    outs = [wide] * 5
    out_specs = [hbm] * 5
    scratch = []
    if first_layer:
        in_specs += [vmem, vmem, pl.BlockSpec(memory_space=pltpu.SMEM)]
        outs += [wide, shape(index[0].shape, jnp.int32), shape((rows, 8, group), F32), shape((count, 128), F32)]
        out_specs += [hbm, vmem, vmem, vmem]
        scratch = [pltpu.VMEM((16, count), BF16), pltpu.VMEM((rows, 128), F32)]
    else:
        ins += (edges, before)
        in_specs += [vmem, vmem, hbm, hbm, hbm]
        scratch = [pltpu.VMEM((count, 128), F32), pltpu.VMEM((count, width), BF16), pltpu.VMEM((count, width), BF16)]
    outs += [
        shape((count, 128), F32),
        shape((h * levels, width), BF16),
        shape((h, width), F32),
        shape((h, width), BF16),
        shape((h, width), F32),
        shape((h, width), F32),
        shape((h, 128), F32),
        shape((32, width), F32),
    ]
    out_specs += [hbm] + [vmem] * 7
    others = max(levels - 1, 1)
    return pl.pallas_call(
        functools.partial(forward_kernel, layer, levels, rows, first_layer),
        out_shape=outs,
        in_specs=in_specs,
        out_specs=out_specs,
        scratch_shapes=[
            pltpu.VMEM((rows * h * levels, width), BF16),
            pltpu.VMEM((h * levels, width), F32),
            pltpu.VMEM((h * levels, width), BF16),
            pltpu.VMEM((others, h, width), BF16),
            pltpu.VMEM((others, h, width), BF16),
        ]
        + [pltpu.VMEM(weight.shape[1:], BF16) for weight in weights]
        + [
            pltpu.VMEM((count, width), F32),
            pltpu.VMEM((count, width + (128 if first_layer else 0)), BF16),
            pltpu.VMEM((count, width), BF16),
            pltpu.VMEM((2, 5, 2 * group, width), BF16),
            pltpu.VMEM((2, 2 * group, 128), F32),
            pltpu.SemaphoreType.DMA((8,)),
            pltpu.SemaphoreType.DMA((2, 6)),
            pltpu.SemaphoreType.DMA((rows // 2,)),
            pltpu.SemaphoreType.DMA((Courier.sends(levels, rows, 2),)),
            pltpu.SemaphoreType.DMA((Courier.receives(levels, rows, 2),)),
            pltpu.SemaphoreType.DMA((others,)),
            pltpu.SemaphoreType.DMA((others,)),
        ]
        + scratch,
        compiler_params=pltpu.CompilerParams(collective_id=1 + layer, has_side_effects=True, vmem_limit_bytes=VMEM_BYTES),
        name=f"forward_{layer}",
    )(*ins)


def backward_kernel(
    layer, levels, rows, last_layer,
    d_node, block, recv, npre, nnormed, nscale, rows_of, gain, ngain, node, d_before, cols_all, scale_all, d_edges, pre, normed, edges, sent,
    w1_all, w2_all, nw1_all, nw2_all,
    d_node_out, d_edges_out, d_change_out, grads, tally, node_all,
    stage, inbox, bufs, d_recv, turned, own_sum, out_buf, cols, scale, w1, w2, nw1, nw2,
    load_sem, out_sem, send_sem, recv_sem, near_send, near_recv,
):
    g = Grid(levels, rows)
    h, width = d_node_out.shape
    if last_layer:
        d_node = d_node.at[pl.ds(pl.multiple_of(g.l * h, h), h)]
    count = pre.shape[0]
    group = count // rows
    node_count = h * levels
    loads = load_all(
        ((nw2_all.at[layer], nw2), (nw1_all.at[layer], nw1), (w1_all.at[layer], w1), (w2_all.at[layer], w2))
        + tuple((src, bufs.at[i]) for i, src in enumerate((d_edges, pre, normed, edges, sent)))
        + ((cols_all, cols), (scale_all, scale)),
        load_sem,
    )
    rs = Scatter(g, stage, inbox, h, send_sem, recv_sem)
    wide = lambda ref: ref[layer : layer + 1, :]
    mine = pl.ds(pl.multiple_of(g.l * h, h), h)
    own_sum[...] = jnp.zeros_like(own_sum)
    tally[...] = jnp.zeros_like(tally)
    for copy in loads[:2]:
        copy.wait()
    tally[48:56, :] = fold(d_node[...] * nnormed[...])
    tally[56:64, :] = fold(d_node[...])
    d_two = norm_back(nnormed[...], nscale[:, 0:1], d_node[...] * wide(ngain)).astype(BF16)
    tally[40:48, :] = fold(d_two.astype(F32))
    d_one = silu_back(npre[...], dot_nt(d_two, nw2[...])).astype(BF16)
    tally[32:40, :] = fold(d_one.astype(F32))
    d_recv[mine, :] = dot_nt(d_one, nw1[width:, :]).astype(BF16)
    g.greet()
    copies = []
    for j in range(1, levels):
        copy = pltpu.make_async_remote_copy(
            d_recv.at[mine], d_recv.at[mine], near_send.at[j - 1], near_recv.at[levels - 1 - j], device_id=g.l_other(j)[1], device_id_type=MESH
        )
        copy.start()
        copies.append(copy)
    d_node_out[...] = d_node[...] + dot_nt(d_one, nw1[:width, :])
    active = (npre[...] * lax.logistic(npre[...])).astype(BF16)
    grads[4 * width + width : 6 * width, :] = dot_tn(recv[...], d_one).astype(BF16)
    grads[4 * width : 5 * width, :] = dot_tn(block[mine, :], d_one).astype(BF16)
    grads[6 * width : 7 * width, :] = dot_tn(active, d_two).astype(BF16)
    if last_layer:
        node_all[mine, :] = node[...].astype(BF16)
    for copy in copies:
        copy.wait()
    copies = []
    for j in range(1, levels if last_layer else 1):
        copy = pltpu.make_async_remote_copy(
            node_all.at[mine],
            node_all.at[mine],
            near_send.at[levels + j - 2],
            near_recv.at[2 * levels - 2 - j],
            device_id=g.l_other(j)[1],
            device_id_type=MESH,
        )
        copy.start()
        copies.append(copy)
    for copy in loads[2:]:
        copy.wait()

    def work(z, x, i):
        pair = g.block(z, x, 0)
        start = pl.multiple_of(pair * group, 2 * group)
        place = pl.ds(start, 2 * group)
        if not last_layer:
            earlier = pltpu.make_async_copy(d_before.at[place], out_buf.at[lax.rem(i, 2), 0], out_sem.at[lax.rem(i, 2), 0])
            earlier.start()
        cols_here = cols[place, :]
        recv_pick = one_hot_cols(cols_here[:, 1:2], node_count)
        d_edge = bufs[0, place, :].astype(F32)
        d_update = (d_edge + dot(recv_pick, d_recv[...])) * cols_here[:, 2:3]
        norm_here = bufs[2, place, :].astype(F32)
        tally[16:24, :] += fold(d_update * norm_here)
        tally[24:32, :] += fold(d_update)
        d_two = norm_back(norm_here, scale[place, 0:1], d_update * wide(gain)).astype(BF16)
        tally[8:16, :] += fold(d_two.astype(F32))
        pre_here = bufs[1, place, :].astype(F32)
        gate = lax.logistic(pre_here)
        d_one = (dot_nt(d_two, w2[...]) * (gate * (1.0 + pre_here * (1.0 - gate)))).astype(BF16)
        tally[0:8, :] += fold(d_one.astype(F32))
        bufs[0, place, :] = d_one
        bufs[1, place, :] = (pre_here * gate).astype(BF16)
        bufs[2, place, :] = d_two
        d_here = dot_nt(d_one, w1[:width, :])
        slot = lax.rem(i, 2)
        used = [
            pltpu.make_async_copy(out_buf.at[slot, n], ref.at[place], out_sem.at[slot, n])
            for n, ref in enumerate((d_edges_out, d_change_out))
            if n or last_layer
        ]

        def free():
            for copy in used:
                copy.wait()

        pl.when(i >= 2)(free)
        if last_layer:
            out_buf[slot, 0] = (d_edge + d_here).astype(BF16)
            out_buf[slot, 1] = d_here.astype(BF16)
        else:
            earlier.wait()
            out_buf[slot, 1] = (out_buf[slot, 0].astype(F32) + d_here).astype(BF16)
        for copy in used:
            copy.start()
        d_sent = dot_nt(d_one, w1[width : 2 * width, :]).astype(BF16)
        for half in range(2):
            ids = rows_of[pair + half]
            part = slice(half * group, (half + 1) * group)
            own_sum[...] += dot(one_hot_rows(ids[1:2, :], node_count), d_one[part])
            spot = pl.ds(pl.multiple_of((pair + half) * node_count, 16), node_count)
            stage[spot, :] = dot(one_hot_rows(ids[0:1, :], node_count), d_sent[part]).astype(BF16)

        def close():
            low = own_sum[...].astype(BF16)
            spot = pl.ds(pl.multiple_of(g.row * node_count, 16), node_count)
            stage[spot, :] = (stage[spot, :].astype(F32) + dot_nt(low, w1[2 * width :, :])).astype(BF16)
            grads[2 * width : 3 * width, :] = dot_tn(block[...], low).astype(BF16)

        pl.when((z == g.z) & (x == g.x))(close)

    def extra(n):
        for i, (at, left, right) in enumerate(((0, 3, 0), (1, 4, 0), (3, 1, 2))):

            def grad(at=at, left=left, right=right):
                grads[at * width : (at + 1) * width, :] = dot_tn(bufs[left], bufs[right]).astype(BF16)

            pl.when(n == i)(grad)

    rs.run(TERMS_ORDER, work, extra)
    rs.last(turned)
    for copy in copies:
        copy.wait()
    d_node_out[...] += turned[...]
    for slot in range(2):
        for n, ref in enumerate((d_edges_out, d_change_out)):
            if n or last_layer:
                pltpu.make_async_copy(out_buf.at[slot, n], ref.at[pl.ds(0, 2 * group)], out_sem.at[slot, n]).wait()
    rs.finish()


def backward_layer(layer, last_layer, d_node, node_saved, cols, rows_of, scale, small, weights, d_edges, edge_saved, node, d_before):
    levels, rows = lax.axis_size("lvl"), lax.axis_size("row")
    width = d_node.shape[1]
    h = d_node.shape[0] // (levels if last_layer else 1)
    count = d_edges.shape[0]
    group = count // rows
    vmem = pl.BlockSpec(memory_space=pltpu.VMEM)
    hbm = pl.BlockSpec(memory_space=pl.ANY)
    shape = jax.ShapeDtypeStruct
    ins = (d_node,) + node_saved + (rows_of,) + small + (node, d_before, cols, scale, d_edges) + edge_saved + weights
    outs = (
        shape((h, width), F32),
        shape((count, width) if last_layer else (16, 128), BF16),
        shape((count, width), BF16),
        shape((7 * width, width), BF16),
        shape((64, width), F32),
        shape((h * levels, width) if last_layer else (16, 128), BF16),
    )
    others = max(levels - 1, 1)
    return pl.pallas_call(
        functools.partial(backward_kernel, layer, levels, rows, last_layer),
        out_shape=outs,
        in_specs=[vmem] * (len(ins) - 12) + [hbm] * 12,
        out_specs=(vmem, hbm, hbm, vmem, vmem, vmem),
        scratch_shapes=[
            pltpu.VMEM((rows * h * levels, width), BF16),
            pltpu.VMEM((Scatter.receives(levels, rows), h, width), BF16),
            pltpu.VMEM((5, count, width), BF16),
            pltpu.VMEM((h * levels, width), BF16),
            pltpu.VMEM((h, width), F32),
            pltpu.VMEM((h * levels, width), F32),
            pltpu.VMEM((2, 2, 2 * group, width), BF16),
            pltpu.VMEM((count, 128), F32),
            pltpu.VMEM((count, 128), F32),
        ]
        + [pltpu.VMEM(weight.shape[1:], BF16) for weight in weights]
        + [
            pltpu.SemaphoreType.DMA((11,)),
            pltpu.SemaphoreType.DMA((2, 2)),
            pltpu.SemaphoreType.DMA((Scatter.sends(levels, rows),)),
            pltpu.SemaphoreType.DMA((2 * Scatter.receives(levels, rows),)),
            pltpu.SemaphoreType.DMA((2 * others,)),
            pltpu.SemaphoreType.DMA((2 * others,)),
                ],
        compiler_params=pltpu.CompilerParams(collective_id=3 + layer, has_side_effects=True, vmem_limit_bytes=VMEM_BYTES),
        name=f"backward_{layer}",
    )(*ins)


def sum_cuts(h):
    return 3 if h % 48 == 0 else 1


def sum_kernel(levels, rows, h, count, *refs):
    d_node, place, sums, last_sums, tally, last_tally, update_all, d_change_all = refs[:8]
    terms = refs[8 : count + 8]
    (
        out, d_node_all, update_out, d_change_out, stage, inbox, total, update, d_change, back,
        scatter_send, scatter_recv, gather_send, gather_recv, load_sem, back_sem, near_send, near_recv,
    ) = refs[count + 8 :]
    g = Grid(levels, rows)
    mine = pl.ds(pl.multiple_of(g.l * d_node.shape[0], d_node.shape[0]), d_node.shape[0])
    d_node_all[mine, :] = d_node[...].astype(BF16)
    pairs = []
    at = 0
    for term in terms:
        pairs.append((term, stage.at[pl.ds(at, term.shape[0])]))
        at += term.shape[0]
    pairs += [(update_all, update), (d_change_all, d_change)]
    loads = load_all(pairs, load_sem)
    width = stage.shape[1]
    lanes = lax.broadcasted_iota(jnp.int32, (16, width), 1)
    subs = lax.broadcasted_iota(jnp.int32, (16, width), 0)
    squares = jnp.zeros((16, width), F32)
    for layer, ref in enumerate((tally, last_tally)):
        for i in range(4):
            part = jnp.sum(jnp.sum(ref[8 * i : 8 * i + 8, :], axis=0, keepdims=True), axis=1, keepdims=True)
            squares = jnp.where((subs == 0) & (lanes == 4 * layer + i), part, squares)
    few = [jnp.sum(ref[...].reshape(8, 8, width), axis=1) for ref in (sums, last_sums)]
    stage[at : at + 16, :] = jnp.concatenate(few, axis=0).astype(BF16)
    stage[at + 16 : at + 32, :] = squares.astype(BF16)
    if stage.shape[0] > at + 32:
        stage[at + 32 :, :] = jnp.zeros((stage.shape[0] - at - 32, width), BF16)
    g.greet()
    for copy in loads:
        copy.wait()
    copies = [
        pltpu.make_async_remote_copy(
            d_node_all.at[mine], d_node_all.at[mine], near_send.at[j - 1], near_recv.at[levels - 1 - j], device_id=g.l_other(j)[1], device_id_type=MESH
        )
        for j in range(1, levels)
    ]

    def exchange(at):
        for copy in copies if at == 0 else ():
            copy.start()

    tiles = place.shape[0]
    size = 256 if tiles % 2 == 0 else 128
    lane = lax.broadcasted_iota(jnp.int32, (128, 128), 1).astype(F32)

    def leave(i):
        here = pl.ds(pl.multiple_of(i * size, size), size)
        return [pltpu.make_async_copy(back.at[i, n], ref.at[here], back_sem.at[i, n]) for n, ref in enumerate((update_out, d_change_out))]

    def restore(i):
        pick = []
        for part in range(size // 128):
            spot = jnp.broadcast_to(place[pl.ds(i * (size // 128) + part, 1), :], (128, 128)).astype(F32).T
            pick.append(jnp.concatenate([(spot == lane + float(128 * j)).astype(BF16) for j in range(tiles)], axis=1))
        pick = jnp.concatenate(pick, axis=0)
        back[i, 0] = dot(pick, update[...]).astype(BF16)
        back[i, 1] = dot(pick, d_change[...]).astype(BF16)
        for copy in leave(i):
            copy.start()

    rs = Scatter(g, stage, inbox, h, scatter_send, scatter_recv)
    after = tiles * 128 // size

    def extra(n):
        pl.when(n < after)(lambda: restore(jnp.minimum(n, after - 1)))

    rs.run(SUM_ORDER, None, extra)

    def more(i, carry):
        restore(i)
        return carry

    if after > 10:
        lax.fori_loop(10, after, more, 0)
    rs.last(total)
    ag = Courier(g, out, h, sum_cuts(h), gather_send, gather_recv)
    ag.own()[...] = total[...].astype(BF16)
    ag.run(ORDER if ag.cuts == 3 else PLAIN_ORDER, exchange)
    for copy in copies:
        copy.wait()
    for i in range(after):
        for copy in leave(i):
            copy.wait()
    rs.finish()
    ag.finish()


def sum_pieces(d_node, place, small, update, d_change, terms, call):
    levels, rows = lax.axis_size("lvl"), lax.axis_size("row")
    width = terms[0].shape[1]
    used = sum(term.shape[0] for term in terms) + 32
    h = -(-used // (16 * levels * rows)) * 16
    count = h * levels * rows
    vmem = pl.BlockSpec(memory_space=pltpu.VMEM)
    hbm = pl.BlockSpec(memory_space=pl.ANY)
    shape = jax.ShapeDtypeStruct
    tiles = update.shape[0] // 128
    size = 256 if tiles % 2 == 0 else 128
    return pl.pallas_call(
        functools.partial(sum_kernel, levels, rows, h, len(terms)),
        out_shape=(
            shape((count, width), BF16),
            shape((d_node.shape[0] * levels, width), BF16),
            shape(update.shape, BF16),
            shape(update.shape, BF16),
        ),
        in_specs=[vmem] * 6 + [hbm] * (2 + len(terms)),
        out_specs=(vmem, vmem, hbm, hbm),
        scratch_shapes=[
            pltpu.VMEM((count, width), BF16),
            pltpu.VMEM((Scatter.receives(levels, rows), h, width), BF16),
            pltpu.VMEM((h, width), F32),
            pltpu.VMEM(update.shape, BF16),
            pltpu.VMEM(update.shape, BF16),
            pltpu.VMEM((tiles * 128 // size, 2, size, width), BF16),
            pltpu.SemaphoreType.DMA((Scatter.sends(levels, rows),)),
            pltpu.SemaphoreType.DMA((2 * Scatter.receives(levels, rows),)),
            pltpu.SemaphoreType.DMA((Courier.sends(levels, rows, sum_cuts(h)),)),
            pltpu.SemaphoreType.DMA((Courier.receives(levels, rows, sum_cuts(h)),)),
            pltpu.SemaphoreType.DMA((len(terms) + 2,)),
            pltpu.SemaphoreType.DMA((tiles * 128 // size, 2)),
            pltpu.SemaphoreType.DMA((max(levels - 1, 1),)),
            pltpu.SemaphoreType.DMA((max(levels - 1, 1),)),
        ],
        compiler_params=pltpu.CompilerParams(collective_id=call, has_side_effects=True, vmem_limit_bytes=VMEM_BYTES),
        name=f"sum_{call}",
    )(d_node, place, *small, update, d_change, *terms)


def finish_kernel(parts, smalls, update, d_change, all_sums, node, d_node, edges, cot, edge_out, cot_out, *refs):
    count = len(parts) + smalls
    wide_outs, small_outs = refs[: len(parts)], refs[len(parts) : count]
    rms_out, node_out, d_node_out, sums, rest, lows, ins, outs, wide, sums_sem, rest_sem, low_sem, in_sem, out_sem, wide_sem = refs[count:]
    size, width = ins.shape[2:]
    steps = edges.shape[0] // size
    targets = [(n, i) for n, part in enumerate(parts) for i in range(part)]
    big = sums.shape[1]
    loads = load_all([(all_sums.at[pl.ds(layer * big, big)], sums.at[layer]) for layer in range(2)], sums_sem)
    loads.append(pltpu.make_async_copy(all_sums.at[pl.ds(2 * big, rest.shape[0])], rest, rest_sem))
    loads[-1].start()

    def load(step):
        here = pl.ds(step * size, size)
        pairs = ((edges, ins.at[step, 0], in_sem.at[step, 0]), (cot, ins.at[step, 1], in_sem.at[step, 1]))
        pairs += ((update, lows.at[step, 0], low_sem.at[step, 0]), (d_change, lows.at[step, 1], low_sem.at[step, 1]))
        return [pltpu.make_async_copy(ref.at[here], to, sem) for ref, to, sem in pairs]

    def leave(step):
        here = pl.ds(step * size, size)
        return [pltpu.make_async_copy(outs.at[step, n], ref.at[here], out_sem.at[step, n]) for n, ref in enumerate((edge_out, cot_out))]

    def widen(at):
        n, i = targets[at % len(targets)]
        ref = wide_outs[n].at[at // len(targets), pl.ds(i * width, width)]
        return pltpu.make_async_copy(wide.at[at], ref, wide_sem.at[at])

    total = 2 * len(targets)
    done = 0
    for step in range(steps):
        for copy in load(step):
            copy.start()
    for step in range(steps):
        for copy in load(step):
            copy.wait()
        for n in range(2):
            outs[step, n] = ins[step, n] + lows[step, n].astype(F32)
        for copy in leave(step):
            copy.start()
        if step == 0:
            for copy in loads:
                copy.wait()
        while done < total * (step + 1) // steps:
            layer, at = done // len(targets), done % len(targets)
            wide[done] = sums[layer, at * width : (at + 1) * width, :].astype(F32)
            widen(done).start()
            done += 1
    few = rest[...].astype(F32)
    for n, out in enumerate(small_outs):
        for layer in range(2):
            out[layer : layer + 1, :] = few[layer * smalls + n : layer * smalls + n + 1]
    rms_out[...] = few[2 * smalls : 2 * smalls + 1]
    node_out[...] = node[...].astype(F32)
    d_node_out[...] = d_node[...].astype(F32)
    for step in range(steps):
        for copy in leave(step):
            copy.wait()
    for at in range(total):
        widen(at).wait()


def finish_all(update, d_change, all_sums, node, d_node, edges, cot, parts, smalls):
    count, width = edges.shape
    size = 512 if count % 512 == 0 else 128
    vmem = pl.BlockSpec(memory_space=pltpu.VMEM)
    hbm = pl.BlockSpec(memory_space=pl.ANY)
    shape = jax.ShapeDtypeStruct
    wide = (shape((count, width), F32),) * 2 + tuple(shape((2, part * width, width), F32) for part in parts)
    narrow = (shape((2, width), F32),) * smalls + (shape((1, width), F32), shape(node.shape, F32), shape(node.shape, F32))
    return pl.pallas_call(
        functools.partial(finish_kernel, parts, smalls),
        out_shape=wide + narrow,
        in_specs=[hbm] * 3 + [vmem] * 2 + [hbm] * 2,
        out_specs=(hbm,) * len(wide) + (vmem,) * len(narrow),
        scratch_shapes=[
            pltpu.VMEM((2, sum(parts) * width, width), BF16),
            pltpu.VMEM((32, width), BF16),
            pltpu.VMEM((count // size, 2, size, width), BF16),
            pltpu.VMEM((count // size, 2, size, width), F32),
            pltpu.VMEM((count // size, 2, size, width), F32),
            pltpu.VMEM((2 * sum(parts), width, width), F32),
            pltpu.SemaphoreType.DMA((2,)),
            pltpu.SemaphoreType.DMA,
            pltpu.SemaphoreType.DMA((count // size, 2)),
            pltpu.SemaphoreType.DMA((count // size, 2)),
            pltpu.SemaphoreType.DMA((count // size, 2)),
            pltpu.SemaphoreType.DMA((2 * sum(parts),)),
        ],
        compiler_params=pltpu.CompilerParams(vmem_limit_bytes=VMEM_BYTES),
        name="finish_all",
    )(update, d_change, all_sums, node, d_node, edges, cot)


def on_device(
    node_latent, edge_latent, senders, receivers, live_edges,
    edge_w1, edge_b1, edge_w2, edge_b2, edge_gain, edge_shift, node_w1, node_b1, node_w2, node_b2, node_gain, node_shift,
    node_cotangent, edge_cotangent,
):
    node_count, width = node_latent.shape
    edge_count = edge_latent.shape[0]
    layers = edge_w1.shape[0]
    row_total, level_total = lax.axis_size("row"), lax.axis_size("lvl")
    node = node_latent
    weights = (edge_w1, edge_w2, node_w1, node_w2)
    small = (edge_b1, edge_b2, edge_gain, edge_shift, node_b1, node_b2, node_gain, node_shift)
    tiles = edge_count // 128
    index = (senders.reshape(tiles, 128), receivers.reshape(tiles, 128), live_edges.reshape(1, 1))
    sent, pre, normed, update, edges, edges_next, place, rows_of, cols, scale, block, node, recv, npre, nnormed, nscale, tally = forward_layer(
        0, node, small, weights, edge_latent, index
    )
    first = ((block, recv, npre, nnormed, nscale), scale, (pre, normed, edges, sent))
    sent, pre, normed, update, d_edges, scale, block, node, recv, npre, nnormed, nscale, tally_last = forward_layer(
        1, node, small, weights, edge_cotangent, (place, rows_of, cols), edges_next, update
    )
    last = ((block, recv, npre, nnormed, nscale), scale, (pre, normed, edges_next, sent))
    d_node = node_cotangent
    gains = (edge_gain, node_gain)
    d_node, d_edges, d_change, last_grads, last_sums, node_all = backward_layer(
        1, True, d_node, last[0], cols, rows_of, last[1], gains, weights, d_edges, last[2], node, d_edges
    )
    d_node, _, d_change, first_grads, first_sums, _ = backward_layer(
        0, False, d_node, first[0], cols, rows_of, first[1], gains, weights, d_edges, first[2], node, d_change
    )
    flat, d_node_all, update, d_change = sum_pieces(
        d_node, place, (first_sums, last_sums, tally, tally_last), update, d_change, [first_grads, last_grads], 5
    )
    edge_out, edge_grad, w1, w2, nw1, nw2, b1, b2, gain, shift, nb1, nb2, ngain, nshift, squares, node, d_node = finish_all(
        update, d_change, flat, node_all, d_node_all, edge_latent, edge_cotangent, (3, 1, 2, 1), 8
    )
    node_entries = float(node_count * row_total * width)
    edge_entries = float(edge_count * row_total * level_total * width)
    entries = jnp.array([node_entries, edge_entries, edge_entries, node_entries], F32)
    rms = jnp.sqrt(squares[0, : 4 * layers].reshape(layers, 4) / entries[None, :])
    return node, edge_out, d_node, edge_grad, w1, b1, w2, b2, gain, shift, nw1, nb1, nw2, nb2, ngain, nshift, rms


def solution(mesh):
    rows, both, whole = P("row", None), P(("lvl", "row"), None), P()
    edge = P(("lvl", "row"))
    placed = (rows, both, edge, edge, edge) + (whole,) * 12 + (rows, both)
    outs = (rows, both, rows, both) + (whole,) * 13
    return jax.shard_map(on_device, mesh=mesh, in_specs=placed, out_specs=outs, check_vma=False)
```

```python
import functools

import jax
import jax.numpy as jnp
from jax import lax
from jax.experimental import pallas as pl
from jax.experimental.pallas import tpu as pltpu
from jax.sharding import PartitionSpec as P

MESH = pl.DeviceIdType.MESH
NORM_EPS = 1e-05
F32 = jnp.float32
BF16 = jnp.bfloat16
VMEM_BYTES = 61 * 2**20


FIRST_ORDER = (
    (
        1089728, 289296, 536069, 551556, 141360, 612561, 159764, 1528408, 356492, 400397,
        858841, 422440, 750249, 990892, 1707549, 1799737, 2097129,
    ),
    (
        1089728, 1392676, 131237, 197853, 1464864, 215760, 1448028, 272952, 399521, 881172,
        290876, 745128, 724581, 482457, 1774801, 1717985, 2097129,
    ),
)
LAST_ORDER = (
    (
        1089728, 526421, 84180, 1507921, 141360, 1530017, 159781, 1462872, 880781, 919081,
        330920, 854680, 745060, 480869, 466664, 1799737, 2097129,
    ),
    (
        1089728, 600797, 338944, 607233, 154201, 214620, 1378337, 920240, 815648, 988240,
        1575989, 1004689, 415277, 937573, 487633, 1734248, 2097133,
    ),
)
ORDER = (
    (
        67728, 295584, 137222, 165041, 594213, 203041, 216120, 630414, 724277, 691860,
        860188, 365736, 744729, 986937, 1022741, 2097070,
    ),
    (
        133632, 152228, 17702, 199298, 856077, 808974, 678584, 985110, 727841, 416061,
        942120, 693914, 563002, 286492, 397085, 2097042,
    ),
)
PLAIN_ORDER = (
    (
        524816, 133680, 204836, 857112, 923164, 2097084,
    ),
    (
        328704, 526372, 401420, 793128, 923164, 2097084,
    ),
)

TERMS_ORDER = (
    (
        246535, 84766, 213518, 51750, 36364, 21003, 153362, 722970, 4362, 527368,
        809258, 2097072,
    ),
    (
        115201, 197251, 362404, 149771, 493190, 2068, 463630, 33816, 431904, 563210,
        807980, 2097074,
    ),
)
SUM_ORDER = (
    (
        934663, 362370, 491653, 623118, 213428, 149012, 460196, 169728, 793232, 428296,
        891820, 921634, 808216, 2087219,
    ),
    (
        787329, 50308, 100229, 196638, 823824, 187277, 232210, 330808, 131382, 466086,
        167200, 562997, 807980, 2087475,
    ),
)


NEAREST = ((0, 1, 2, 3), (1, 0, 2, 3), (2, 3, 1, 0), (3, 2, 1, 0))


class Grid:
    def __init__(self, levels, rows):
        self.L, self.R = levels, rows
        self.Z = 4
        self.X = rows // (2 * self.Z)
        self.l = lax.axis_index("lvl")
        row = lax.axis_index("row")
        self.row = row
        self.core = lax.rem(row, 2)
        self.x = lax.rem(row // 2, self.X)
        self.z = row // (2 * self.X)
        self.up = self.z < self.Z - 1
        self.down = self.z > 0

    def block(self, z, x, core):
        return (z * self.X + x) * 2 + core

    def mate(self):
        return (self.l, self.block(self.z, self.x, 1 - self.core))

    def at_z(self, z):
        return (self.l, self.block(jnp.clip(z, 0, self.Z - 1), self.x, self.core))

    def x_other(self, i):
        x = lax.rem(self.x + i, self.X)
        return x, (self.l, self.block(self.z, x, self.core))

    def l_other(self, i):
        l = lax.rem(self.l + i, self.L)
        return l, (l, self.row)

    def nth(self, k, z=None):
        z_here = self.z if z is None else z
        order = NEAREST
        out = jnp.int32(0)
        for z in range(4):
            for j in range(4):
                if order[z][j]:
                    out = jnp.where((z_here == z) & (k == j), order[z][j], out)
        return out

    def local(self, zk, z=None):
        return (zk // 2) == lax.rem(self.z if z is None else z, 2)

    def corner_z(self, q):
        side = lax.rem(lax.rem(self.z, 2) + q // 2, 2)
        return side * 2 + lax.rem(q, 2)

    def pair_z(self):
        return self.z + 1 - 2 * lax.rem(self.z, 2)

    def greet(self):
        barrier = pltpu.get_barrier_semaphore()

        def hello(who):
            pl.semaphore_signal(barrier, inc=1, device_id=who, device_id_type=MESH)

        hello(self.mate())
        for i in range(1, self.X):
            hello(self.x_other(i)[1])
        for i in range(1, self.L):
            hello(self.l_other(i)[1])
        pl.when(self.up)(lambda: hello(self.at_z(self.z + 1)))
        pl.when(self.down)(lambda: hello(self.at_z(self.z - 1)))
        pl.semaphore_wait(barrier, self.X + self.L - 1 + self.up.astype(jnp.int32) + self.down.astype(jnp.int32))


def only(when, act):
    if when is None:
        act()
    else:
        pl.when(when)(act)


def cuts(h):
    first = -(-h // 32) * 16
    return ((0, first), (first, h - first)) if h > first else ((0, h),)


class Courier:
    def __init__(self, grid, table, h, cuts, send_sem, recv_sem):
        self.g, self.table, self.h = grid, table, h
        self.cuts = cuts
        self.size = h // self.cuts
        self.send_sem, self.recv_sem = send_sem, recv_sem
        self.drain = False

    @staticmethod
    def kinds(levels, rows):
        X, L = rows // 8, levels
        return (X + L + 1, (X - 1) * L, (L - 1) * X, 3 * (X - 1) * (L - 1))

    @staticmethod
    def sends(levels, rows, cuts):
        return 4 * sum(Courier.kinds(levels, rows)) * cuts

    @staticmethod
    def receives(levels, rows, cuts):
        return levels * rows * cuts

    def at(self, kind, zk, n, s):
        counts = self.kinds(self.g.L, self.g.R)
        return (4 * sum(counts[:kind]) + zk * counts[kind] + n) * self.cuts + s

    def slot(self, block, l, s=0, size=None):
        start = (block * self.g.L + l) * self.h + s * self.size
        return self.table.at[pl.ds(pl.multiple_of(start, 16), size or self.size)]

    def own(self):
        return self.slot(self.g.row, self.g.l, 0, self.h)

    def push(self, at, block, l, s, who, when=None):
        place = self.slot(block, l, s)
        copy = pltpu.make_async_remote_copy(
            place,
            place,
            self.send_sem.at[at],
            self.recv_sem.at[(block * self.g.L + l) * self.cuts + s],
            device_id=who,
            device_id_type=MESH,
        )
        only(when, copy.wait_send if self.drain else copy.start)

    def arrived(self, block, l, s):
        if self.drain:
            return
        place = self.slot(block, l, s)
        pltpu.make_async_remote_copy(
            place,
            place,
            self.send_sem.at[0],
            self.recv_sem.at[(block * self.g.L + l) * self.cuts + s],
            device_id=self.g.mate(),
            device_id_type=MESH,
        ).wait_recv()

    def near(self, zk):
        z = self.g.z
        return (zk == z) | ((z == 0) & (zk == 1)) | ((z == 3) & (zk == 2))

    def even(self, zk):
        return lax.rem(jnp.where(self.g.z < 2, zk, 3 - zk), 2) == 0

    def column(self, zk, s, own=False):
        g = self.g
        block = g.block(zk, g.x, g.core)
        if not own:
            self.arrived(block, g.l, s)
        self.push(self.at(0, zk, 0, s), block, g.l, s, g.at_z(g.z + 1), g.up & (zk <= g.z))
        self.push(self.at(0, zk, 1, s), block, g.l, s, g.at_z(g.z - 1), g.down & (zk >= g.z))
        for i in range(1, g.X):
            self.push(self.at(0, zk, 1 + i, s), block, g.l, s, g.x_other(i)[1])
        for j in range(1, g.L):
            self.push(self.at(0, zk, g.X + j, s), block, g.l, s, g.l_other(j)[1])
        self.push(self.at(0, zk, g.X + g.L, s), block, g.l, s, g.mate())

    def side_x(self, zk, s):
        g = self.g
        n = 0
        for i in range(1, g.X):
            block = g.block(zk, g.x_other(i)[0], g.core)
            self.arrived(block, g.l, s)
            for j in range(1, g.L):
                self.push(self.at(1, zk, n, s), block, g.l, s, g.l_other(j)[1], self.near(zk) & self.even(zk))
                n += 1
            self.push(self.at(1, zk, n, s), block, g.l, s, g.mate())
            n += 1

    def side_l(self, zk, s):
        g = self.g
        block = g.block(zk, g.x, g.core)
        n = 0
        for j in range(1, g.L):
            l = g.l_other(j)[0]
            self.arrived(block, l, s)
            for i in range(1, g.X):
                self.push(self.at(2, zk, n, s), block, l, s, g.x_other(i)[1], self.near(zk) & jnp.logical_not(self.even(zk)))
                n += 1
            self.push(self.at(2, zk, n, s), block, l, s, g.mate())
            n += 1

    def corner(self, zk, s):
        g = self.g
        n = 0
        for i in range(1, g.X):
            block = g.block(zk, g.x_other(i)[0], g.core)
            for j in range(1, g.L):
                l = g.l_other(j)[0]
                self.arrived(block, l, s)
                self.push(self.at(3, zk, n, s), block, l, s, g.at_z(g.z + 1), (zk <= 1) & (g.z >= zk) & g.up)
                self.push(self.at(3, zk, n + 1, s), block, l, s, g.at_z(g.z - 1), (zk >= 2) & (g.z <= zk) & g.down)
                self.push(self.at(3, zk, n + 2, s), block, l, s, g.mate())
                n += 3

    def mates(self, zk, x):
        def one(i, carry):
            self.arrived(self.g.block(zk, x, 1 - self.g.core), i // self.cuts, lax.rem(i, self.cuts))
            return carry

        lax.fori_loop(0, self.g.L * self.cuts, one, 0)

    def run(self, tables, meanwhile=None, prepare=None, work=None):
        g = self.g
        for s in range(self.cuts):
            self.column(g.z, s, own=True)
        low = g.z < 2
        first = (g.z == 0) | (g.z == 3)

        def one(m, done):
            word = jnp.int32(0)
            for at, (a, b) in enumerate(zip(*tables)):
                word = jnp.where(m // 3 == at, jnp.where(first, a, b), word)
            byte = lax.rem(m, 3)
            code = lax.rem(jnp.where(byte == 0, word, jnp.where(byte == 1, word // 128, word // 16384)), 128)
            zk = lax.rem(code // 4, 4)
            zk = jnp.where(low, zk, 3 - zk)
            s = lax.rem(code, 4)
            kind = code // 16
            pl.when(kind == 0)(lambda: self.column(zk, s))
            if g.X > 1:
                pl.when(kind == 1)(lambda: self.side_x(zk, s))
            if g.L > 1:
                pl.when(kind == 2)(lambda: self.side_l(zk, s))
            if g.X > 1 and g.L > 1:
                pl.when(kind == 3)(lambda: self.corner(zk, s))
            if meanwhile is not None:
                for at in range(3):
                    pl.when(code == 64 + at)(lambda at=at: meanwhile(at))
            count = jnp.int32(0)
            if work is not None:
                for off in range(g.X):
                    x = lax.rem(g.x + off, g.X)
                    hit = s == (0 if off == 0 else 1)
                    pl.when((kind == 5) & hit)(lambda x=x: prepare(zk, x))

                    def full(x=x, off=off):
                        self.mates(zk, x)
                        work(zk, x, done + max(off - 1, 0))

                    pl.when((kind == 6) & hit)(full)
                count = jnp.where(kind == 6, jnp.where(s == 0, 1, g.X - 1), 0)
            return done + count

        lax.fori_loop(0, 3 * len(tables[0]), one, jnp.int32(0))
        if work is None:

            def last(i, carry):
                self.mates(i // g.X, lax.rem(i, g.X))
                return carry

            lax.fori_loop(0, 4 * g.X, last, 0)

    def finish(self):
        self.drain = True

        def one(i, carry):
            zk, s = i // self.cuts, lax.rem(i, self.cuts)
            self.column(zk, s)
            self.side_x(zk, s)
            self.side_l(zk, s)
            self.corner(zk, s)
            return carry

        lax.fori_loop(0, 4 * self.cuts, one, 0)


class Scatter:
    def __init__(self, grid, stage, inbox, h, send_sem, recv_sem):
        self.g, self.stage, self.inbox, self.h = grid, stage, inbox, h
        self.cuts = cuts(h)
        self.send_sem, self.recv_sem = send_sem, recv_sem
        X, L = grid.X, grid.L
        at = 0
        self.base = {}
        for name, count in self.parts(X, L):
            self.base[name] = at
            at += count
        at = 0
        self.out = {}
        for name, count in self.out_parts(X, L):
            self.out[name] = at
            at += count
        self.drain = False

    @staticmethod
    def parts(X, L):
        side = (X - 1) * (L - 1)
        return (("mate", 4 * X * L), ("pair", 2 * side), ("l2", side), ("x2", side), ("xc", 4 * (X - 1)), ("lc", 4 * (L - 1)), ("z", 5))

    @staticmethod
    def out_parts(X, L):
        side = (X - 1) * (L - 1)
        return (("mate", 4 * X * L), ("corner", 8 * side), ("xc", 4 * (X - 1)), ("lc", 4 * (L - 1)), ("z", 4))

    @staticmethod
    def receives(levels, rows):
        return sum(count for _, count in Scatter.parts(rows // 8, levels))

    @staticmethod
    def sends(levels, rows):
        return 2 * sum(count for _, count in Scatter.out_parts(rows // 8, levels))

    def slot(self, block, l, s=None):
        start, size = (0, self.h) if s is None else self.cuts[s]
        return self.stage.at[pl.ds(pl.multiple_of((block * self.g.L + l) * self.h + start, 16), size)]

    def push(self, out, block, l, s, at, who, when=None):
        start, size = self.cuts[s]
        copy = pltpu.make_async_remote_copy(
            self.slot(block, l, s),
            self.inbox.at[at, pl.ds(start, size)],
            self.send_sem.at[2 * out + s],
            self.recv_sem.at[2 * at + s],
            device_id=who,
            device_id_type=MESH,
        )
        only(when, copy.wait_send if self.drain else copy.start)

    def arrived(self, at, s):
        start, size = self.cuts[s]
        place = self.inbox.at[at, pl.ds(start, size)]
        pltpu.make_async_remote_copy(
            place, place, self.send_sem.at[0], self.recv_sem.at[2 * at + s], device_id=self.g.mate(), device_id_type=MESH
        ).wait_recv()

    def total(self, block, l, s, ats):
        start, size = self.cuts[s]
        for at in ats:
            self.arrived(at, s)
        out = self.slot(block, l, s)[...].astype(F32)
        for at in ats:
            out = out + self.inbox[at, start : start + size].astype(F32)
        return out

    def add(self, block, l, s, ats, when=None):
        if self.drain:
            return

        def act():
            self.slot(block, l, s)[...] = self.total(block, l, s, ats).astype(BF16)

        only(when, act)

    def each(self):
        return range(len(self.cuts))

    def to_mate(self, z, x):
        g = self.g
        for l in range(g.L):
            at = (z * g.X + x) * g.L + l
            for s in self.each():
                self.push(self.out["mate"] + at, g.block(z, x, 1 - g.core), l, s, self.base["mate"] + at, g.mate())

    def from_mate(self, z, x):
        g = self.g
        for l in range(g.L):
            for s in self.each():
                self.add(g.block(z, x, g.core), l, s, [self.base["mate"] + (z * g.X + x) * g.L + l])

    def corner_far(self, z, i):
        g = self.g
        block = g.block(z, lax.rem(g.x + i, g.X), g.core)
        for j in range(1, g.L):
            l = g.l_other(j)[0]
            spot = (lax.rem(z, 2) * (g.X - 1) + i - 1) * (g.L - 1) + j - 1
            for s in self.each():
                self.push(self.out["corner"] + spot, block, l, s, self.base["pair"] + spot, g.at_z(g.pair_z()))

    def corner_near(self, z, i):
        g = self.g
        x, x_dev = g.x_other(i)
        block = g.block(z, x, g.core)
        even = self.even(z)
        side = (g.X - 1) * (g.L - 1)
        for j in range(1, g.L):
            l, l_dev = g.l_other(j)
            spot = (lax.rem(z, 2) * (g.X - 1) + i - 1) * (g.L - 1) + j - 1
            out = self.out["corner"] + 2 * side + spot
            for s in self.each():
                self.add(block, l, s, [self.base["pair"] + spot])
                self.push(out, block, l, s, self.base["l2"] + (i - 1) * (g.L - 1) + g.L - j - 1, l_dev, even)
                self.push(out, block, l, s, self.base["x2"] + (g.X - i - 1) * (g.L - 1) + j - 1, x_dev, jnp.logical_not(even))

    def side_x(self, zk, i, waits):
        g = self.g
        x, x_dev = g.x_other(i)
        block = g.block(zk, x, g.core)
        ats = [self.base["l2"] + (i - 1) * (g.L - 1) + j - 1 for j in range(1, g.L)]
        for s in self.each():
            if ats and waits:
                self.add(block, g.l, s, ats)
            self.push(self.out["xc"] + zk * (g.X - 1) + i - 1, block, g.l, s, self.base["xc"] + zk * (g.X - 1) + g.X - i - 1, x_dev)

    def side_l(self, zk, waits):
        g = self.g
        block = g.block(zk, g.x, g.core)
        for j in range(1, g.L):
            l, l_dev = g.l_other(j)
            ats = [self.base["x2"] + (i - 1) * (g.L - 1) + j - 1 for i in range(1, g.X)]
            for s in self.each():
                if waits:
                    self.add(block, l, s, ats)
                self.push(self.out["lc"] + zk * (g.L - 1) + j - 1, block, l, s, self.base["lc"] + zk * (g.L - 1) + g.L - j - 1, l_dev)

    def around(self, zk):
        g = self.g
        ats = [self.base["xc"] + zk * (g.X - 1) + i - 1 for i in range(1, g.X)]
        return ats + [self.base["lc"] + zk * (g.L - 1) + j - 1 for j in range(1, g.L)]

    def column(self, zk):
        g = self.g
        block = g.block(zk, g.x, g.core)
        behind = jnp.where(zk > g.z, g.down, g.up)
        near = jnp.abs(zk - g.z) == 1
        spot = jnp.where(near & (zk < g.z), 4, zk)
        for s in self.each():
            self.add(block, g.l, s, self.around(zk))
            self.add(block, g.l, s, [self.base["z"] + zk], behind)
            self.push(self.out["z"] + zk, block, g.l, s, self.base["z"] + spot, g.at_z(jnp.where(zk > g.z, g.z + 1, g.z - 1)))

    def last(self, out):
        g = self.g
        for s in self.each():
            start, size = self.cuts[s]
            out[start : start + size, :] = self.total(g.row, g.l, s, self.around(g.z))
            for at, there in ((self.base["z"] + g.z, g.down), (self.base["z"] + 4, g.up)):

                def take(at=at, s=s, start=start, size=size):
                    self.arrived(at, s)
                    out[start : start + size, :] += self.inbox[at, start : start + size].astype(F32)

                pl.when(there)(take)

    def even(self, zk):
        return lax.rem(jnp.where(self.g.z < 2, zk, 3 - zk), 2) == 0

    def decode(self, m):
        g = self.g
        first = (g.z == 0) | (g.z == 3)
        word = jnp.int32(0)
        for at, (a, b) in enumerate(zip(*self.tables)):
            word = jnp.where(m // 3 == at, jnp.where(first, a, b), word)
        byte = lax.rem(m, 3)
        code = lax.rem(jnp.where(byte == 0, word, jnp.where(byte == 1, word // 128, word // 16384)), 128)
        zk = lax.rem(code // 2, 4)
        return code, code // 8, jnp.where(g.z < 2, zk, 3 - zk), lax.rem(code, 2)

    def step(self, m, work=None, extra=None, done=0):
        g = self.g
        code, kind, zk, side = self.decode(m)
        for off in range(g.X):
            x = lax.rem(g.x + off, g.X)
            hit = side == (0 if off == 0 else 1)

            def make(x=x, off=off):
                if work is not None and not self.drain:
                    work(zk, x, done + max(off - 1, 0))
                self.to_mate(zk, x)

            pl.when((kind == 0) & hit)(make)
            if not self.drain:
                pl.when((kind == 1) & hit)(lambda x=x: self.from_mate(zk, x))
        near = g.local(zk)
        for i in range(1, g.X):
            if g.L > 1:
                pl.when((kind == 2) & near)(lambda i=i: self.corner_near(zk, i))
                pl.when((kind == 2) & jnp.logical_not(near))(lambda i=i: self.corner_far(zk, i))
            late = near & self.even(zk)
            pl.when((kind == 3) & late)(lambda i=i: self.side_x(zk, i, True))
            pl.when((kind == 3) & jnp.logical_not(late))(lambda i=i: self.side_x(zk, i, False))
        if g.L > 1:
            late = near & jnp.logical_not(self.even(zk))
            pl.when((kind == 4) & late)(lambda: self.side_l(zk, True))
            pl.when((kind == 4) & jnp.logical_not(late))(lambda: self.side_l(zk, False))
        pl.when(kind == 5)(lambda: self.column(zk))
        if extra is not None and not self.drain:
            pl.when(kind >= 6)(lambda: extra(code - 48))
        return jnp.where(kind == 0, jnp.where(side == 0, 1, g.X - 1), 0)

    def go(self, m, ahead, work=None, extra=None, done=0):
        count = self.step(m, work, extra, done)

        def wait():
            self.drain = True
            self.step(m - ahead)
            self.drain = False

        pl.when(m >= ahead)(wait)
        return count

    def run(self, tables, work=None, extra=None, beside=None, ahead=20):
        self.follow(tables, ahead)

        def one(m, done):
            count = self.go(m, self.ahead, work, extra, done)
            if beside is not None:
                beside(m)
            return done + count

        lax.fori_loop(0, self.steps, one, jnp.int32(0))

    def follow(self, tables, ahead):
        self.tables = tables
        self.steps = 3 * len(tables[0])
        self.ahead = min(ahead, self.steps)

    def finish(self):
        self.drain = True

        def one(m, carry):
            self.step(m)
            return carry

        lax.fori_loop(self.steps - self.ahead, self.steps, one, 0)


def dot(left, right):
    return jnp.dot(left, right, preferred_element_type=F32)


def dot_nt(left, right):
    return lax.dot_general(left, right, (((1,), (1,)), ((), ())), preferred_element_type=F32)


def dot_tn(left, right):
    return lax.dot_general(left, right, (((0,), (0,)), ((), ())), preferred_element_type=F32)


def fold(values):
    rows, width = values.shape
    return jnp.sum(values.reshape(rows // 8, 8, width), axis=0)


def norm_parts(values):
    average = jnp.mean(values, axis=-1, keepdims=True)
    centered = values - average
    scale = lax.rsqrt(jnp.mean(centered * centered, axis=-1, keepdims=True) + NORM_EPS)
    return centered * scale, scale


def norm_back(normed, scale, d_normed):
    mean_d = jnp.mean(d_normed, axis=-1, keepdims=True)
    mean_dn = jnp.mean(d_normed * normed, axis=-1, keepdims=True)
    return scale * (d_normed - mean_d - normed * mean_dn)


def silu_back(pre, d_active):
    gate = lax.logistic(pre)
    return d_active * (gate * (1.0 + pre * (1.0 - gate)))


def find_places(row_total, node_count, some, senders, receivers, live, place, side, facts_out, counts):
    tiles = senders.shape[0]
    group = tiles * 128 // row_total
    first = lax.axis_index("row") * node_count
    lane = lax.broadcasted_iota(jnp.int32, (128, 128), 1)
    sub = lax.broadcasted_iota(jnp.int32, (128, 128), 0)
    before = (sub < lane).astype(BF16)
    owner_ids = lax.broadcasted_iota(jnp.int32, (row_total, 128), 0)
    carry = owner_ids[:, :1].astype(F32) * group if some[0] == 0 else counts[:, 0:1]
    for tile in some:
        send = senders[tile : tile + 1, :]
        recv = receivers[tile : tile + 1, :] - first
        owner = lax.div(send, node_count)
        local = send - owner * node_count
        mine = owner_ids == owner
        ranks = dot(mine.astype(BF16), before) + carry
        spot = jnp.sum(jnp.where(mine, ranks, 0.0), axis=0, keepdims=True)
        carry = carry + jnp.sum(mine.astype(F32), axis=1, keepdims=True)
        place[tile : tile + 1, :] = spot.astype(jnp.int32)
        alive = (lane[:1] + tile * 128 < live[0, 0]).astype(jnp.int32)
        facts = jnp.where(sub == 0, lax.div(local, 16), 0)
        facts = jnp.where(sub == 1, lax.rem(local, 16), facts)
        facts = jnp.where(sub == 2, lax.div(recv, 16), facts)
        facts = jnp.where(sub == 3, lax.rem(recv, 16), facts)
        facts = jnp.where(sub == 4, alive, facts).astype(F32)
        side[:, pl.ds(tile * 128, 128)] = facts[:16].astype(BF16)
        facts_out[pl.ds(tile * 128, 128), :] = facts.T.astype(BF16)
    counts[...] = jnp.broadcast_to(carry, counts.shape)


def picker(place, start, size):
    ids = lax.broadcasted_iota(jnp.int32, (size, 128), 0) + start
    return jnp.concatenate([(ids == place[tile : tile + 1, :]).astype(BF16) for tile in range(place.shape[0])], axis=1)


def one_hot_cols(ids, count):
    lanes = lax.broadcasted_iota(jnp.int32, (ids.shape[0], count), 1).astype(F32)
    return (ids == lanes).astype(BF16)


def one_hot_rows(ids, count):
    subs = lax.broadcasted_iota(jnp.int32, (count, ids.shape[1]), 0).astype(F32)
    return (ids == subs).astype(BF16)


def load_all(pairs, sems):
    copies = [pltpu.make_async_copy(src, dst, sems.at[i]) for i, (src, dst) in enumerate(pairs)]
    for copy in copies:
        copy.start()
    return copies


def forward_kernel(
    layer, levels, rows, first_layer, *refs
):
    (node, b1, b2, gain, shift, nb1, nb2, ngain, nshift, w1_all, w2_all, nw1_all, nw2_all, plain_all) = refs[:14]
    refs = refs[14:]
    if first_layer:
        senders, receivers, live = refs[:3]
        refs = refs[3:]
    else:
        place, rows_of, cols_all, edges_all, before_all = refs[:5]
        refs = refs[5:]
    sent_out, pre_out, normed_out, update_out, moved_out = refs[:5]
    refs = refs[5:]
    if first_layer:
        edges_out, place, rows_of, cols = refs[:4]
        refs = refs[4:]
    scale_out, block_out, node_out, recv_out, npre_out, nnormed_out, nscale_out, tally = refs[:8]
    (
        table, total, cast, near, far, w1, w2, nw1, nw2, plain, joined, ordered, out_buf, scale_buf,
        load_sem, out_sem, moved_sem, send_sem, recv_sem, near_send, near_recv,
    ) = refs[8:29]
    if first_layer:
        side, counts = refs[29:]
    else:
        cols, edges, before = refs[29:]
    g = Grid(levels, rows)
    h, width = node_out.shape
    if first_layer:
        node = node.at[pl.ds(pl.multiple_of(g.l * h, h), h)]
    count = plain.shape[0]
    group = count // rows
    node_count = h * levels
    pairs = ((plain_all, plain), (w1_all.at[layer], w1), (w2_all.at[layer], w2), (nw1_all.at[layer], nw1), (nw2_all.at[layer], nw2))
    if not first_layer:
        pairs += ((cols_all, cols), (edges_all, edges), (before_all, before))
    loads = load_all(pairs, load_sem)
    ag = Courier(g, table, h, 2, send_sem, recv_sem)
    ag.own()[...] = node[...].astype(BF16)
    tally[...] = jnp.zeros_like(tally)
    total[...] = jnp.zeros_like(total)
    g.greet()
    wide = lambda ref: ref[layer : layer + 1, :]
    outs = (sent_out, pre_out, normed_out, update_out) + ((edges_out,) if first_layer else ())

    def meanwhile(at):
        if first_layer:
            tiles = place.shape[0]
            some = range(at * tiles // 3, (at + 1) * tiles // 3)
            find_places(rows, node_count, some, senders, receivers, live, place, side, joined.at[:, pl.ds(width, 128)], counts)
        if at == 0:
            for copy in loads:
                copy.wait()

        def cast_rows(i, carry):
            part = pl.ds(pl.multiple_of(i * 2 * group, 2 * group), 2 * group)
            joined[part, 0:width] = plain[part, :].astype(BF16)
            return carry

        lax.fori_loop(at * rows // 6, (at + 1) * rows // 6, cast_rows, 0)

    def leave(n, part):
        slot = lax.rem(n, 2)
        copies = [pltpu.make_async_copy(out_buf.at[slot, i], ref.at[part], out_sem.at[slot, i]) for i, ref in enumerate(outs)]
        return copies + [pltpu.make_async_copy(scale_buf.at[slot], scale_out.at[part], out_sem.at[slot, 5])]

    def spot(z, x):
        pair = g.block(z, x, 0)
        first = pl.multiple_of(pair * group, 2 * group)
        return pair, first, pl.ds(first, 2 * group)

    def moved_copy(z, x):
        part = spot(z, x)[2]
        return pltpu.make_async_copy(ordered.at[part], moved_out.at[part], moved_sem.at[z * g.X + x])

    def prepare(z, x):
        pair, first, part = spot(z, x)
        pick = picker(place, first, 2 * group)
        moved = dot(pick, joined[...])
        ordered[part, :] = moved[:, :width].astype(BF16)
        moved_copy(z, x).start()
        if first_layer:
            digits = moved[:, width:]
            lanes = lax.broadcasted_iota(jnp.int32, digits.shape, 1)
            ids = digits[:, 0:1] * 16.0 + digits[:, 1:2]
            got = digits[:, 2:3] * 16.0 + digits[:, 3:4]
            cols[part, :] = jnp.where(lanes == 0, ids, jnp.where(lanes == 1, got, jnp.where(lanes == 2, digits[:, 4:5], 0.0)))
            for half in range(2):
                digits = dot_nt(side[...], pick[half * group : (half + 1) * group])
                rows_of[pair + half] = jnp.concatenate(
                    [digits[0:1] * 16.0 + digits[1:2], digits[2:3] * 16.0 + digits[3:4], digits[4:10]], axis=0
                )

    def work(z, x, n):
        def own():
            here = table[pl.ds(pl.multiple_of(g.row * node_count, 16), node_count), :]
            cast[...] = dot(here, w1[2 * width :, :]).astype(BF16)
            block_out[...] = here

        pl.when(n == 0)(own)
        pair, first, part = spot(z, x)

        def free():
            for copy in leave(n, part):
                copy.wait()

        pl.when(n >= 2)(free)
        slot = lax.rem(n, 2)
        low = ordered[part, :] if first_layer else edges[part, :]
        cols_here = cols[part, :]
        send_pick = one_hot_cols(cols_here[:, 0:1], node_count)
        recv_pick = one_hot_cols(cols_here[:, 1:2], node_count)
        start = pl.multiple_of(pair * node_count, 16)
        sent = jnp.concatenate(
            [
                dot(send_pick[:group], table[pl.ds(start, node_count), :]).astype(BF16),
                dot(send_pick[group:], table[pl.ds(start + node_count, node_count), :]).astype(BF16),
            ],
            axis=0,
        )
        out_buf[slot, 0] = sent
        pre = dot(low, w1[:width, :]) + dot(sent, w1[width : 2 * width, :]) + dot(recv_pick, cast[...]) + wide(b1)
        out_buf[slot, 1] = pre.astype(BF16)
        active = (pre * lax.logistic(pre)).astype(BF16)
        normed, scale = norm_parts(dot(active, w2[...]) + wide(b2))
        out_buf[slot, 2] = normed.astype(BF16)
        scale_buf[slot] = jnp.broadcast_to(scale, (2 * group, 128))
        update = (normed * wide(gain) + wide(shift)) * cols_here[:, 2:3]
        update_low = update.astype(BF16)
        edge = low.astype(F32) + update
        if first_layer:
            out_buf[slot, 3] = update_low
            out_buf[slot, 4] = edge.astype(BF16)
        else:
            out_buf[slot, 3] = (before[part, :].astype(F32) + update).astype(BF16)
        tally[8:16, :] += fold(edge * edge)
        tally[16:24, :] += fold(update * update)
        for half in range(2):
            pick = one_hot_rows(rows_of[pair + half][1:2, :], node_count)
            total[...] += dot(pick, update_low[half * group : (half + 1) * group])
        for copy in leave(n, part):
            copy.start()

    ag.run(FIRST_ORDER if first_layer else LAST_ORDER, meanwhile, prepare, work)
    copies = []
    for j in range(1, levels):
        l, l_dev = g.l_other(j)
        near[j - 1] = total[pl.ds(pl.multiple_of(l * h, h), h), :].astype(BF16)
        copy = pltpu.make_async_remote_copy(
            near.at[j - 1], far.at[levels - 1 - j], near_send.at[j - 1], near_recv.at[levels - 1 - j], device_id=l_dev, device_id_type=MESH
        )
        copy.start()
        copies.append(copy)
    received = total[pl.ds(pl.multiple_of(g.l * h, h), h), :]
    npre = dot(node[...].astype(BF16), nw1[:width, :]) + wide(nb1)
    for copy in copies:
        copy.wait()
    for j in range(1, levels):
        received = received + far[j - 1].astype(F32)
    received = received.astype(BF16)
    recv_out[...] = received
    npre = npre + dot(received, nw1[width:, :])
    npre_out[...] = npre
    nnormed, nscale = norm_parts(dot((npre * lax.logistic(npre)).astype(BF16), nw2[...]) + wide(nb2))
    nnormed_out[...] = nnormed
    nscale_out[...] = jnp.broadcast_to(nscale, (h, 128))
    change = nnormed * wide(ngain) + wide(nshift)
    new = node[...] + change
    node_out[...] = new
    tally[0:8, :] = fold(new * new)
    tally[24:32, :] = fold(change * change)
    for n in range(2):
        for copy in leave(n, pl.ds(0, 2 * group)):
            copy.wait()
    for n in range(4 * g.X):
        moved_copy(n // g.X, n % g.X).wait()
    ag.finish()


def forward_layer(layer, node, small, weights, plain, index, edges=None, before=None):
    levels, rows = lax.axis_size("lvl"), lax.axis_size("row")
    width = node.shape[1]
    h = node.shape[0] // (levels if layer == 0 else 1)
    count = plain.shape[0]
    group = count // rows
    vmem = pl.BlockSpec(memory_space=pltpu.VMEM)
    hbm = pl.BlockSpec(memory_space=pl.ANY)
    first_layer = layer == 0
    shape = jax.ShapeDtypeStruct
    wide = shape((count, width), BF16)
    ins = (node,) + small + weights + (plain,) + index
    in_specs = [vmem] * 9 + [hbm] * 5
    outs = [wide] * 5
    out_specs = [hbm] * 5
    scratch = []
    if first_layer:
        in_specs += [vmem, vmem, pl.BlockSpec(memory_space=pltpu.SMEM)]
        outs += [wide, shape(index[0].shape, jnp.int32), shape((rows, 8, group), F32), shape((count, 128), F32)]
        out_specs += [hbm, vmem, vmem, vmem]
        scratch = [pltpu.VMEM((16, count), BF16), pltpu.VMEM((rows, 128), F32)]
    else:
        ins += (edges, before)
        in_specs += [vmem, vmem, hbm, hbm, hbm]
        scratch = [pltpu.VMEM((count, 128), F32), pltpu.VMEM((count, width), BF16), pltpu.VMEM((count, width), BF16)]
    outs += [
        shape((count, 128), F32),
        shape((h * levels, width), BF16),
        shape((h, width), F32),
        shape((h, width), BF16),
        shape((h, width), F32),
        shape((h, width), F32),
        shape((h, 128), F32),
        shape((32, width), F32),
    ]
    out_specs += [hbm] + [vmem] * 7
    others = max(levels - 1, 1)
    return pl.pallas_call(
        functools.partial(forward_kernel, layer, levels, rows, first_layer),
        out_shape=outs,
        in_specs=in_specs,
        out_specs=out_specs,
        scratch_shapes=[
            pltpu.VMEM((rows * h * levels, width), BF16),
            pltpu.VMEM((h * levels, width), F32),
            pltpu.VMEM((h * levels, width), BF16),
            pltpu.VMEM((others, h, width), BF16),
            pltpu.VMEM((others, h, width), BF16),
        ]
        + [pltpu.VMEM(weight.shape[1:], BF16) for weight in weights]
        + [
            pltpu.VMEM((count, width), F32),
            pltpu.VMEM((count, width + (128 if first_layer else 0)), BF16),
            pltpu.VMEM((count, width), BF16),
            pltpu.VMEM((2, 5, 2 * group, width), BF16),
            pltpu.VMEM((2, 2 * group, 128), F32),
            pltpu.SemaphoreType.DMA((8,)),
            pltpu.SemaphoreType.DMA((2, 6)),
            pltpu.SemaphoreType.DMA((rows // 2,)),
            pltpu.SemaphoreType.DMA((Courier.sends(levels, rows, 2),)),
            pltpu.SemaphoreType.DMA((Courier.receives(levels, rows, 2),)),
            pltpu.SemaphoreType.DMA((others,)),
            pltpu.SemaphoreType.DMA((others,)),
        ]
        + scratch,
        compiler_params=pltpu.CompilerParams(collective_id=1 + layer, has_side_effects=True, vmem_limit_bytes=VMEM_BYTES),
        name=f"forward_{layer}",
    )(*ins)


def backward_kernel(
    layer, levels, rows, last_layer,
    d_node, block, recv, npre, nnormed, nscale, rows_of, gain, ngain, node, d_before, cols_all, scale_all, d_edges, pre, normed, edges, sent,
    w1_all, w2_all, nw1_all, nw2_all,
    d_node_out, d_edges_out, d_change_out, grads, tally, node_all,
    stage, inbox, bufs, d_recv, turned, own_sum, out_buf, cols, scale, w1, w2, nw1, nw2,
    load_sem, out_sem, send_sem, recv_sem, near_send, near_recv,
):
    g = Grid(levels, rows)
    h, width = d_node_out.shape
    if last_layer:
        d_node = d_node.at[pl.ds(pl.multiple_of(g.l * h, h), h)]
    count = pre.shape[0]
    group = count // rows
    node_count = h * levels
    loads = load_all(
        ((nw2_all.at[layer], nw2), (nw1_all.at[layer], nw1), (w1_all.at[layer], w1), (w2_all.at[layer], w2))
        + tuple((src, bufs.at[i]) for i, src in enumerate((d_edges, pre, normed, edges, sent)))
        + ((cols_all, cols), (scale_all, scale)),
        load_sem,
    )
    rs = Scatter(g, stage, inbox, h, send_sem, recv_sem)
    wide = lambda ref: ref[layer : layer + 1, :]
    mine = pl.ds(pl.multiple_of(g.l * h, h), h)
    own_sum[...] = jnp.zeros_like(own_sum)
    tally[...] = jnp.zeros_like(tally)
    for copy in loads[:2]:
        copy.wait()
    tally[48:56, :] = fold(d_node[...] * nnormed[...])
    tally[56:64, :] = fold(d_node[...])
    d_two = norm_back(nnormed[...], nscale[:, 0:1], d_node[...] * wide(ngain)).astype(BF16)
    tally[40:48, :] = fold(d_two.astype(F32))
    d_one = silu_back(npre[...], dot_nt(d_two, nw2[...])).astype(BF16)
    tally[32:40, :] = fold(d_one.astype(F32))
    d_recv[mine, :] = dot_nt(d_one, nw1[width:, :]).astype(BF16)
    g.greet()
    copies = []
    for j in range(1, levels):
        copy = pltpu.make_async_remote_copy(
            d_recv.at[mine], d_recv.at[mine], near_send.at[j - 1], near_recv.at[levels - 1 - j], device_id=g.l_other(j)[1], device_id_type=MESH
        )
        copy.start()
        copies.append(copy)
    d_node_out[...] = d_node[...] + dot_nt(d_one, nw1[:width, :])
    active = (npre[...] * lax.logistic(npre[...])).astype(BF16)
    grads[4 * width + width : 6 * width, :] = dot_tn(recv[...], d_one).astype(BF16)
    grads[4 * width : 5 * width, :] = dot_tn(block[mine, :], d_one).astype(BF16)
    grads[6 * width : 7 * width, :] = dot_tn(active, d_two).astype(BF16)
    if last_layer:
        node_all[mine, :] = node[...].astype(BF16)
    for copy in copies:
        copy.wait()
    copies = []
    for j in range(1, levels if last_layer else 1):
        copy = pltpu.make_async_remote_copy(
            node_all.at[mine],
            node_all.at[mine],
            near_send.at[levels + j - 2],
            near_recv.at[2 * levels - 2 - j],
            device_id=g.l_other(j)[1],
            device_id_type=MESH,
        )
        copy.start()
        copies.append(copy)
    for copy in loads[2:]:
        copy.wait()

    def work(z, x, i):
        pair = g.block(z, x, 0)
        start = pl.multiple_of(pair * group, 2 * group)
        place = pl.ds(start, 2 * group)
        if not last_layer:
            earlier = pltpu.make_async_copy(d_before.at[place], out_buf.at[lax.rem(i, 2), 0], out_sem.at[lax.rem(i, 2), 0])
            earlier.start()
        cols_here = cols[place, :]
        recv_pick = one_hot_cols(cols_here[:, 1:2], node_count)
        d_edge = bufs[0, place, :].astype(F32)
        d_update = (d_edge + dot(recv_pick, d_recv[...])) * cols_here[:, 2:3]
        norm_here = bufs[2, place, :].astype(F32)
        tally[16:24, :] += fold(d_update * norm_here)
        tally[24:32, :] += fold(d_update)
        d_two = norm_back(norm_here, scale[place, 0:1], d_update * wide(gain)).astype(BF16)
        tally[8:16, :] += fold(d_two.astype(F32))
        pre_here = bufs[1, place, :].astype(F32)
        gate = lax.logistic(pre_here)
        d_one = (dot_nt(d_two, w2[...]) * (gate * (1.0 + pre_here * (1.0 - gate)))).astype(BF16)
        tally[0:8, :] += fold(d_one.astype(F32))
        bufs[0, place, :] = d_one
        bufs[1, place, :] = (pre_here * gate).astype(BF16)
        bufs[2, place, :] = d_two
        d_here = dot_nt(d_one, w1[:width, :])
        slot = lax.rem(i, 2)
        used = [
            pltpu.make_async_copy(out_buf.at[slot, n], ref.at[place], out_sem.at[slot, n])
            for n, ref in enumerate((d_edges_out, d_change_out))
            if n or last_layer
        ]

        def free():
            for copy in used:
                copy.wait()

        pl.when(i >= 2)(free)
        if last_layer:
            out_buf[slot, 0] = (d_edge + d_here).astype(BF16)
            out_buf[slot, 1] = d_here.astype(BF16)
        else:
            earlier.wait()
            out_buf[slot, 1] = (out_buf[slot, 0].astype(F32) + d_here).astype(BF16)
        for copy in used:
            copy.start()
        d_sent = dot_nt(d_one, w1[width : 2 * width, :]).astype(BF16)
        for half in range(2):
            ids = rows_of[pair + half]
            part = slice(half * group, (half + 1) * group)
            own_sum[...] += dot(one_hot_rows(ids[1:2, :], node_count), d_one[part])
            spot = pl.ds(pl.multiple_of((pair + half) * node_count, 16), node_count)
            stage[spot, :] = dot(one_hot_rows(ids[0:1, :], node_count), d_sent[part]).astype(BF16)

        def close():
            low = own_sum[...].astype(BF16)
            spot = pl.ds(pl.multiple_of(g.row * node_count, 16), node_count)
            stage[spot, :] = (stage[spot, :].astype(F32) + dot_nt(low, w1[2 * width :, :])).astype(BF16)
            grads[2 * width : 3 * width, :] = dot_tn(block[...], low).astype(BF16)

        pl.when((z == g.z) & (x == g.x))(close)

    def extra(n):
        for i, (at, left, right) in enumerate(((0, 3, 0), (1, 4, 0), (3, 1, 2))):

            def grad(at=at, left=left, right=right):
                grads[at * width : (at + 1) * width, :] = dot_tn(bufs[left], bufs[right]).astype(BF16)

            pl.when(n == i)(grad)

    rs.run(TERMS_ORDER, work, extra)
    rs.last(turned)
    for copy in copies:
        copy.wait()
    d_node_out[...] += turned[...]
    for slot in range(2):
        for n, ref in enumerate((d_edges_out, d_change_out)):
            if n or last_layer:
                pltpu.make_async_copy(out_buf.at[slot, n], ref.at[pl.ds(0, 2 * group)], out_sem.at[slot, n]).wait()
    rs.finish()


def backward_layer(layer, last_layer, d_node, node_saved, cols, rows_of, scale, small, weights, d_edges, edge_saved, node, d_before):
    levels, rows = lax.axis_size("lvl"), lax.axis_size("row")
    width = d_node.shape[1]
    h = d_node.shape[0] // (levels if last_layer else 1)
    count = d_edges.shape[0]
    group = count // rows
    vmem = pl.BlockSpec(memory_space=pltpu.VMEM)
    hbm = pl.BlockSpec(memory_space=pl.ANY)
    shape = jax.ShapeDtypeStruct
    ins = (d_node,) + node_saved + (rows_of,) + small + (node, d_before, cols, scale, d_edges) + edge_saved + weights
    outs = (
        shape((h, width), F32),
        shape((count, width) if last_layer else (16, 128), BF16),
        shape((count, width), BF16),
        shape((7 * width, width), BF16),
        shape((64, width), F32),
        shape((h * levels, width) if last_layer else (16, 128), BF16),
    )
    others = max(levels - 1, 1)
    return pl.pallas_call(
        functools.partial(backward_kernel, layer, levels, rows, last_layer),
        out_shape=outs,
        in_specs=[vmem] * (len(ins) - 12) + [hbm] * 12,
        out_specs=(vmem, hbm, hbm, vmem, vmem, vmem),
        scratch_shapes=[
            pltpu.VMEM((rows * h * levels, width), BF16),
            pltpu.VMEM((Scatter.receives(levels, rows), h, width), BF16),
            pltpu.VMEM((5, count, width), BF16),
            pltpu.VMEM((h * levels, width), BF16),
            pltpu.VMEM((h, width), F32),
            pltpu.VMEM((h * levels, width), F32),
            pltpu.VMEM((2, 2, 2 * group, width), BF16),
            pltpu.VMEM((count, 128), F32),
            pltpu.VMEM((count, 128), F32),
        ]
        + [pltpu.VMEM(weight.shape[1:], BF16) for weight in weights]
        + [
            pltpu.SemaphoreType.DMA((11,)),
            pltpu.SemaphoreType.DMA((2, 2)),
            pltpu.SemaphoreType.DMA((Scatter.sends(levels, rows),)),
            pltpu.SemaphoreType.DMA((2 * Scatter.receives(levels, rows),)),
            pltpu.SemaphoreType.DMA((2 * others,)),
            pltpu.SemaphoreType.DMA((2 * others,)),
                ],
        compiler_params=pltpu.CompilerParams(collective_id=3 + layer, has_side_effects=True, vmem_limit_bytes=VMEM_BYTES),
        name=f"backward_{layer}",
    )(*ins)


def sum_cuts(h):
    return 3 if h % 48 == 0 else 1


def sum_kernel(levels, rows, h, count, *refs):
    d_node, place, sums, last_sums, tally, last_tally, update_all, d_change_all = refs[:8]
    terms = refs[8 : count + 8]
    (
        out, d_node_all, update_out, d_change_out, stage, inbox, total, update, d_change, back,
        scatter_send, scatter_recv, gather_send, gather_recv, load_sem, back_sem, near_send, near_recv,
    ) = refs[count + 8 :]
    g = Grid(levels, rows)
    mine = pl.ds(pl.multiple_of(g.l * d_node.shape[0], d_node.shape[0]), d_node.shape[0])
    d_node_all[mine, :] = d_node[...].astype(BF16)
    pairs = []
    at = 0
    for term in terms:
        pairs.append((term, stage.at[pl.ds(at, term.shape[0])]))
        at += term.shape[0]
    pairs += [(update_all, update), (d_change_all, d_change)]
    loads = load_all(pairs, load_sem)
    width = stage.shape[1]
    lanes = lax.broadcasted_iota(jnp.int32, (16, width), 1)
    subs = lax.broadcasted_iota(jnp.int32, (16, width), 0)
    squares = jnp.zeros((16, width), F32)
    for layer, ref in enumerate((tally, last_tally)):
        for i in range(4):
            part = jnp.sum(jnp.sum(ref[8 * i : 8 * i + 8, :], axis=0, keepdims=True), axis=1, keepdims=True)
            squares = jnp.where((subs == 0) & (lanes == 4 * layer + i), part, squares)
    few = [jnp.sum(ref[...].reshape(8, 8, width), axis=1) for ref in (sums, last_sums)]
    stage[at : at + 16, :] = jnp.concatenate(few, axis=0).astype(BF16)
    stage[at + 16 : at + 32, :] = squares.astype(BF16)
    if stage.shape[0] > at + 32:
        stage[at + 32 :, :] = jnp.zeros((stage.shape[0] - at - 32, width), BF16)
    g.greet()
    for copy in loads:
        copy.wait()
    copies = [
        pltpu.make_async_remote_copy(
            d_node_all.at[mine], d_node_all.at[mine], near_send.at[j - 1], near_recv.at[levels - 1 - j], device_id=g.l_other(j)[1], device_id_type=MESH
        )
        for j in range(1, levels)
    ]

    def exchange(at):
        for copy in copies if at == 0 else ():
            copy.start()

    tiles = place.shape[0]
    size = 256 if tiles % 2 == 0 else 128
    lane = lax.broadcasted_iota(jnp.int32, (128, 128), 1).astype(F32)

    def leave(i):
        here = pl.ds(pl.multiple_of(i * size, size), size)
        return [pltpu.make_async_copy(back.at[i, n], ref.at[here], back_sem.at[i, n]) for n, ref in enumerate((update_out, d_change_out))]

    def restore(i):
        pick = []
        for part in range(size // 128):
            spot = jnp.broadcast_to(place[pl.ds(i * (size // 128) + part, 1), :], (128, 128)).astype(F32).T
            pick.append(jnp.concatenate([(spot == lane + float(128 * j)).astype(BF16) for j in range(tiles)], axis=1))
        pick = jnp.concatenate(pick, axis=0)
        back[i, 0] = dot(pick, update[...]).astype(BF16)
        back[i, 1] = dot(pick, d_change[...]).astype(BF16)
        for copy in leave(i):
            copy.start()

    rs = Scatter(g, stage, inbox, h, scatter_send, scatter_recv)
    after = tiles * 128 // size

    def extra(n):
        pl.when(n < after)(lambda: restore(jnp.minimum(n, after - 1)))

    rs.run(SUM_ORDER, None, extra)

    def more(i, carry):
        restore(i)
        return carry

    if after > 10:
        lax.fori_loop(10, after, more, 0)
    rs.last(total)
    ag = Courier(g, out, h, sum_cuts(h), gather_send, gather_recv)
    ag.own()[...] = total[...].astype(BF16)
    ag.run(ORDER if ag.cuts == 3 else PLAIN_ORDER, exchange)
    for copy in copies:
        copy.wait()
    for i in range(after):
        for copy in leave(i):
            copy.wait()
    rs.finish()
    ag.finish()


def sum_pieces(d_node, place, small, update, d_change, terms, call):
    levels, rows = lax.axis_size("lvl"), lax.axis_size("row")
    width = terms[0].shape[1]
    used = sum(term.shape[0] for term in terms) + 32
    h = -(-used // (16 * levels * rows)) * 16
    count = h * levels * rows
    vmem = pl.BlockSpec(memory_space=pltpu.VMEM)
    hbm = pl.BlockSpec(memory_space=pl.ANY)
    shape = jax.ShapeDtypeStruct
    tiles = update.shape[0] // 128
    size = 256 if tiles % 2 == 0 else 128
    return pl.pallas_call(
        functools.partial(sum_kernel, levels, rows, h, len(terms)),
        out_shape=(
            shape((count, width), BF16),
            shape((d_node.shape[0] * levels, width), BF16),
            shape(update.shape, BF16),
            shape(update.shape, BF16),
        ),
        in_specs=[vmem] * 6 + [hbm] * (2 + len(terms)),
        out_specs=(vmem, vmem, hbm, hbm),
        scratch_shapes=[
            pltpu.VMEM((count, width), BF16),
            pltpu.VMEM((Scatter.receives(levels, rows), h, width), BF16),
            pltpu.VMEM((h, width), F32),
            pltpu.VMEM(update.shape, BF16),
            pltpu.VMEM(update.shape, BF16),
            pltpu.VMEM((tiles * 128 // size, 2, size, width), BF16),
            pltpu.SemaphoreType.DMA((Scatter.sends(levels, rows),)),
            pltpu.SemaphoreType.DMA((2 * Scatter.receives(levels, rows),)),
            pltpu.SemaphoreType.DMA((Courier.sends(levels, rows, sum_cuts(h)),)),
            pltpu.SemaphoreType.DMA((Courier.receives(levels, rows, sum_cuts(h)),)),
            pltpu.SemaphoreType.DMA((len(terms) + 2,)),
            pltpu.SemaphoreType.DMA((tiles * 128 // size, 2)),
            pltpu.SemaphoreType.DMA((max(levels - 1, 1),)),
            pltpu.SemaphoreType.DMA((max(levels - 1, 1),)),
        ],
        compiler_params=pltpu.CompilerParams(collective_id=call, has_side_effects=True, vmem_limit_bytes=VMEM_BYTES),
        name=f"sum_{call}",
    )(d_node, place, *small, update, d_change, *terms)


def finish_kernel(parts, smalls, update, d_change, all_sums, node, d_node, edges, cot, edge_out, cot_out, *refs):
    count = len(parts) + smalls
    wide_outs, small_outs = refs[: len(parts)], refs[len(parts) : count]
    rms_out, node_out, d_node_out, sums, rest, lows, ins, outs, wide, sums_sem, rest_sem, low_sem, in_sem, out_sem, wide_sem = refs[count:]
    size, width = ins.shape[2:]
    steps = edges.shape[0] // size
    targets = [(n, i) for n, part in enumerate(parts) for i in range(part)]
    big = sums.shape[1]
    loads = load_all([(all_sums.at[pl.ds(layer * big, big)], sums.at[layer]) for layer in range(2)], sums_sem)
    loads.append(pltpu.make_async_copy(all_sums.at[pl.ds(2 * big, rest.shape[0])], rest, rest_sem))
    loads[-1].start()

    def load(step):
        here = pl.ds(step * size, size)
        pairs = ((edges, ins.at[step, 0], in_sem.at[step, 0]), (cot, ins.at[step, 1], in_sem.at[step, 1]))
        pairs += ((update, lows.at[step, 0], low_sem.at[step, 0]), (d_change, lows.at[step, 1], low_sem.at[step, 1]))
        return [pltpu.make_async_copy(ref.at[here], to, sem) for ref, to, sem in pairs]

    def leave(step):
        here = pl.ds(step * size, size)
        return [pltpu.make_async_copy(outs.at[step, n], ref.at[here], out_sem.at[step, n]) for n, ref in enumerate((edge_out, cot_out))]

    def widen(at):
        n, i = targets[at % len(targets)]
        ref = wide_outs[n].at[at // len(targets), pl.ds(i * width, width)]
        return pltpu.make_async_copy(wide.at[at], ref, wide_sem.at[at])

    total = 2 * len(targets)
    done = 0
    for step in range(steps):
        for copy in load(step):
            copy.start()
    for step in range(steps):
        for copy in load(step):
            copy.wait()
        for n in range(2):
            outs[step, n] = ins[step, n] + lows[step, n].astype(F32)
        for copy in leave(step):
            copy.start()
        if step == 0:
            for copy in loads:
                copy.wait()
        while done < total * (step + 1) // steps:
            layer, at = done // len(targets), done % len(targets)
            wide[done] = sums[layer, at * width : (at + 1) * width, :].astype(F32)
            widen(done).start()
            done += 1
    few = rest[...].astype(F32)
    for n, out in enumerate(small_outs):
        for layer in range(2):
            out[layer : layer + 1, :] = few[layer * smalls + n : layer * smalls + n + 1]
    rms_out[...] = few[2 * smalls : 2 * smalls + 1]
    node_out[...] = node[...].astype(F32)
    d_node_out[...] = d_node[...].astype(F32)
    for step in range(steps):
        for copy in leave(step):
            copy.wait()
    for at in range(total):
        widen(at).wait()


def finish_all(update, d_change, all_sums, node, d_node, edges, cot, parts, smalls):
    count, width = edges.shape
    size = 512 if count % 512 == 0 else 128
    vmem = pl.BlockSpec(memory_space=pltpu.VMEM)
    hbm = pl.BlockSpec(memory_space=pl.ANY)
    shape = jax.ShapeDtypeStruct
    wide = (shape((count, width), F32),) * 2 + tuple(shape((2, part * width, width), F32) for part in parts)
    narrow = (shape((2, width), F32),) * smalls + (shape((1, width), F32), shape(node.shape, F32), shape(node.shape, F32))
    return pl.pallas_call(
        functools.partial(finish_kernel, parts, smalls),
        out_shape=wide + narrow,
        in_specs=[hbm] * 3 + [vmem] * 2 + [hbm] * 2,
        out_specs=(hbm,) * len(wide) + (vmem,) * len(narrow),
        scratch_shapes=[
            pltpu.VMEM((2, sum(parts) * width, width), BF16),
            pltpu.VMEM((32, width), BF16),
            pltpu.VMEM((count // size, 2, size, width), BF16),
            pltpu.VMEM((count // size, 2, size, width), F32),
            pltpu.VMEM((count // size, 2, size, width), F32),
            pltpu.VMEM((2 * sum(parts), width, width), F32),
            pltpu.SemaphoreType.DMA((2,)),
            pltpu.SemaphoreType.DMA,
            pltpu.SemaphoreType.DMA((count // size, 2)),
            pltpu.SemaphoreType.DMA((count // size, 2)),
            pltpu.SemaphoreType.DMA((count // size, 2)),
            pltpu.SemaphoreType.DMA((2 * sum(parts),)),
        ],
        compiler_params=pltpu.CompilerParams(vmem_limit_bytes=VMEM_BYTES),
        name="finish_all",
    )(update, d_change, all_sums, node, d_node, edges, cot)


def on_device(
    node_latent, edge_latent, senders, receivers, live_edges,
    edge_w1, edge_b1, edge_w2, edge_b2, edge_gain, edge_shift, node_w1, node_b1, node_w2, node_b2, node_gain, node_shift,
    node_cotangent, edge_cotangent,
):
    node_count, width = node_latent.shape
    edge_count = edge_latent.shape[0]
    layers = edge_w1.shape[0]
    row_total, level_total = lax.axis_size("row"), lax.axis_size("lvl")
    node = node_latent
    weights = (edge_w1, edge_w2, node_w1, node_w2)
    small = (edge_b1, edge_b2, edge_gain, edge_shift, node_b1, node_b2, node_gain, node_shift)
    tiles = edge_count // 128
    index = (senders.reshape(tiles, 128), receivers.reshape(tiles, 128), live_edges.reshape(1, 1))
    sent, pre, normed, update, edges, edges_next, place, rows_of, cols, scale, block, node, recv, npre, nnormed, nscale, tally = forward_layer(
        0, node, small, weights, edge_latent, index
    )
    first = ((block, recv, npre, nnormed, nscale), scale, (pre, normed, edges, sent))
    sent, pre, normed, update, d_edges, scale, block, node, recv, npre, nnormed, nscale, tally_last = forward_layer(
        1, node, small, weights, edge_cotangent, (place, rows_of, cols), edges_next, update
    )
    last = ((block, recv, npre, nnormed, nscale), scale, (pre, normed, edges_next, sent))
    d_node = node_cotangent
    gains = (edge_gain, node_gain)
    d_node, d_edges, d_change, last_grads, last_sums, node_all = backward_layer(
        1, True, d_node, last[0], cols, rows_of, last[1], gains, weights, d_edges, last[2], node, d_edges
    )
    d_node, _, d_change, first_grads, first_sums, _ = backward_layer(
        0, False, d_node, first[0], cols, rows_of, first[1], gains, weights, d_edges, first[2], node, d_change
    )
    flat, d_node_all, update, d_change = sum_pieces(
        d_node, place, (first_sums, last_sums, tally, tally_last), update, d_change, [first_grads, last_grads], 5
    )
    edge_out, edge_grad, w1, w2, nw1, nw2, b1, b2, gain, shift, nb1, nb2, ngain, nshift, squares, node, d_node = finish_all(
        update, d_change, flat, node_all, d_node_all, edge_latent, edge_cotangent, (3, 1, 2, 1), 8
    )
    node_entries = float(node_count * row_total * width)
    edge_entries = float(edge_count * row_total * level_total * width)
    entries = jnp.array([node_entries, edge_entries, edge_entries, node_entries], F32)
    rms = jnp.sqrt(squares[0, : 4 * layers].reshape(layers, 4) / entries[None, :])
    return node, edge_out, d_node, edge_grad, w1, b1, w2, b2, gain, shift, nw1, nb1, nw2, nb2, ngain, nshift, rms


def solution(mesh):
    rows, both, whole = P("row", None), P(("lvl", "row"), None), P()
    edge = P(("lvl", "row"))
    placed = (rows, both, edge, edge, edge) + (whole,) * 12 + (rows, both)
    outs = (rows, both, rows, both) + (whole,) * 13
    return jax.shard_map(on_device, mesh=mesh, in_specs=placed, out_specs=outs, check_vma=False)
```

```python
import functools

import jax
import jax.numpy as jnp
from jax import lax
from jax.experimental import pallas as pl
from jax.experimental.pallas import tpu as pltpu
from jax.sharding import PartitionSpec as P

MESH = pl.DeviceIdType.MESH
NORM_EPS = 1e-05
F32 = jnp.float32
BF16 = jnp.bfloat16
VMEM_BYTES = 61 * 2**20


FIRST_ORDER = (
    (
        1089728, 289296, 536069, 551556, 141360, 612561, 159764, 1528408, 356492, 400397,
        858841, 422440, 750249, 990892, 1707549, 1799737, 2097129,
    ),
    (
        1089728, 1392676, 131237, 197853, 1464864, 215760, 1448028, 272952, 399521, 881172,
        290876, 745128, 724581, 482457, 1774801, 1717985, 2097129,
    ),
)
LAST_ORDER = (
    (
        1089728, 526421, 84180, 1507921, 141360, 1530017, 159781, 1462872, 880781, 919081,
        330920, 854680, 745060, 480869, 466664, 1799737, 2097129,
    ),
    (
        1089728, 600797, 338944, 607233, 154201, 214620, 1378337, 920240, 815648, 988240,
        1575989, 1004689, 415277, 937573, 487633, 1734248, 2097133,
    ),
)
ORDER = (
    (
        67728, 295584, 137222, 165041, 594213, 203041, 216120, 630414, 724277, 691860,
        860188, 365736, 744729, 986937, 1022741, 2097070,
    ),
    (
        133632, 152228, 17702, 199298, 856077, 808974, 678584, 985110, 727841, 416061,
        942120, 693914, 563002, 286492, 397085, 2097042,
    ),
)
PLAIN_ORDER = (
    (
        524816, 133680, 204836, 857112, 923164, 2097084,
    ),
    (
        328704, 526372, 401420, 793128, 923164, 2097084,
    ),
)

TERMS_ORDER = (
    (
        246535, 84766, 213518, 51750, 36364, 21003, 153362, 722970, 4362, 527368,
        809258, 2097072,
    ),
    (
        115201, 197251, 362404, 149771, 493190, 2068, 463630, 33816, 431904, 563210,
        807980, 2097074,
    ),
)
SUM_ORDER = (
    (
        934663, 362370, 491653, 623118, 213428, 149012, 460196, 169728, 793232, 428296,
        891820, 921634, 808216, 2087219,
    ),
    (
        787329, 50308, 100229, 196638, 823824, 187277, 232210, 330808, 131382, 466086,
        167200, 562997, 807980, 2087475,
    ),
)


NEAREST = ((0, 1, 2, 3), (1, 0, 2, 3), (2, 3, 1, 0), (3, 2, 1, 0))


class Grid:
    def __init__(self, levels, rows):
        self.L, self.R = levels, rows
        self.Z = 4
        self.X = rows // (2 * self.Z)
        self.l = lax.axis_index("lvl")
        row = lax.axis_index("row")
        self.row = row
        self.core = lax.rem(row, 2)
        self.x = lax.rem(row // 2, self.X)
        self.z = row // (2 * self.X)
        self.up = self.z < self.Z - 1
        self.down = self.z > 0

    def block(self, z, x, core):
        return (z * self.X + x) * 2 + core

    def mate(self):
        return (self.l, self.block(self.z, self.x, 1 - self.core))

    def at_z(self, z):
        return (self.l, self.block(jnp.clip(z, 0, self.Z - 1), self.x, self.core))

    def x_other(self, i):
        x = lax.rem(self.x + i, self.X)
        return x, (self.l, self.block(self.z, x, self.core))

    def l_other(self, i):
        l = lax.rem(self.l + i, self.L)
        return l, (l, self.row)

    def nth(self, k, z=None):
        z_here = self.z if z is None else z
        order = NEAREST
        out = jnp.int32(0)
        for z in range(4):
            for j in range(4):
                if order[z][j]:
                    out = jnp.where((z_here == z) & (k == j), order[z][j], out)
        return out

    def local(self, zk, z=None):
        return (zk // 2) == lax.rem(self.z if z is None else z, 2)

    def corner_z(self, q):
        side = lax.rem(lax.rem(self.z, 2) + q // 2, 2)
        return side * 2 + lax.rem(q, 2)

    def pair_z(self):
        return self.z + 1 - 2 * lax.rem(self.z, 2)

    def greet(self):
        barrier = pltpu.get_barrier_semaphore()

        def hello(who):
            pl.semaphore_signal(barrier, inc=1, device_id=who, device_id_type=MESH)

        hello(self.mate())
        for i in range(1, self.X):
            hello(self.x_other(i)[1])
        for i in range(1, self.L):
            hello(self.l_other(i)[1])
        pl.when(self.up)(lambda: hello(self.at_z(self.z + 1)))
        pl.when(self.down)(lambda: hello(self.at_z(self.z - 1)))
        pl.semaphore_wait(barrier, self.X + self.L - 1 + self.up.astype(jnp.int32) + self.down.astype(jnp.int32))


def only(when, act):
    if when is None:
        act()
    else:
        pl.when(when)(act)


def cuts(h):
    first = -(-h // 32) * 16
    return ((0, first), (first, h - first)) if h > first else ((0, h),)


class Courier:
    def __init__(self, grid, table, h, cuts, send_sem, recv_sem):
        self.g, self.table, self.h = grid, table, h
        self.cuts = cuts
        self.size = h // self.cuts
        self.send_sem, self.recv_sem = send_sem, recv_sem
        self.drain = False

    @staticmethod
    def kinds(levels, rows):
        X, L = rows // 8, levels
        return (X + L + 1, (X - 1) * L, (L - 1) * X, 3 * (X - 1) * (L - 1))

    @staticmethod
    def sends(levels, rows, cuts):
        return 4 * sum(Courier.kinds(levels, rows)) * cuts

    @staticmethod
    def receives(levels, rows, cuts):
        return levels * rows * cuts

    def at(self, kind, zk, n, s):
        counts = self.kinds(self.g.L, self.g.R)
        return (4 * sum(counts[:kind]) + zk * counts[kind] + n) * self.cuts + s

    def slot(self, block, l, s=0, size=None):
        start = (block * self.g.L + l) * self.h + s * self.size
        return self.table.at[pl.ds(pl.multiple_of(start, 16), size or self.size)]

    def own(self):
        return self.slot(self.g.row, self.g.l, 0, self.h)

    def push(self, at, block, l, s, who, when=None):
        place = self.slot(block, l, s)
        copy = pltpu.make_async_remote_copy(
            place,
            place,
            self.send_sem.at[at],
            self.recv_sem.at[(block * self.g.L + l) * self.cuts + s],
            device_id=who,
            device_id_type=MESH,
        )
        only(when, copy.wait_send if self.drain else copy.start)

    def arrived(self, block, l, s):
        if self.drain:
            return
        place = self.slot(block, l, s)
        pltpu.make_async_remote_copy(
            place,
            place,
            self.send_sem.at[0],
            self.recv_sem.at[(block * self.g.L + l) * self.cuts + s],
            device_id=self.g.mate(),
            device_id_type=MESH,
        ).wait_recv()

    def near(self, zk):
        z = self.g.z
        return (zk == z) | ((z == 0) & (zk == 1)) | ((z == 3) & (zk == 2))

    def even(self, zk):
        return lax.rem(jnp.where(self.g.z < 2, zk, 3 - zk), 2) == 0

    def column(self, zk, s, own=False):
        g = self.g
        block = g.block(zk, g.x, g.core)
        if not own:
            self.arrived(block, g.l, s)
        self.push(self.at(0, zk, 0, s), block, g.l, s, g.at_z(g.z + 1), g.up & (zk <= g.z))
        self.push(self.at(0, zk, 1, s), block, g.l, s, g.at_z(g.z - 1), g.down & (zk >= g.z))
        for i in range(1, g.X):
            self.push(self.at(0, zk, 1 + i, s), block, g.l, s, g.x_other(i)[1])
        for j in range(1, g.L):
            self.push(self.at(0, zk, g.X + j, s), block, g.l, s, g.l_other(j)[1])
        self.push(self.at(0, zk, g.X + g.L, s), block, g.l, s, g.mate())

    def side_x(self, zk, s):
        g = self.g
        n = 0
        for i in range(1, g.X):
            block = g.block(zk, g.x_other(i)[0], g.core)
            self.arrived(block, g.l, s)
            for j in range(1, g.L):
                self.push(self.at(1, zk, n, s), block, g.l, s, g.l_other(j)[1], self.near(zk) & self.even(zk))
                n += 1
            self.push(self.at(1, zk, n, s), block, g.l, s, g.mate())
            n += 1

    def side_l(self, zk, s):
        g = self.g
        block = g.block(zk, g.x, g.core)
        n = 0
        for j in range(1, g.L):
            l = g.l_other(j)[0]
            self.arrived(block, l, s)
            for i in range(1, g.X):
                self.push(self.at(2, zk, n, s), block, l, s, g.x_other(i)[1], self.near(zk) & jnp.logical_not(self.even(zk)))
                n += 1
            self.push(self.at(2, zk, n, s), block, l, s, g.mate())
            n += 1

    def corner(self, zk, s):
        g = self.g
        n = 0
        for i in range(1, g.X):
            block = g.block(zk, g.x_other(i)[0], g.core)
            for j in range(1, g.L):
                l = g.l_other(j)[0]
                self.arrived(block, l, s)
                self.push(self.at(3, zk, n, s), block, l, s, g.at_z(g.z + 1), (zk <= 1) & (g.z >= zk) & g.up)
                self.push(self.at(3, zk, n + 1, s), block, l, s, g.at_z(g.z - 1), (zk >= 2) & (g.z <= zk) & g.down)
                self.push(self.at(3, zk, n + 2, s), block, l, s, g.mate())
                n += 3

    def mates(self, zk, x):
        def one(i, carry):
            self.arrived(self.g.block(zk, x, 1 - self.g.core), i // self.cuts, lax.rem(i, self.cuts))
            return carry

        lax.fori_loop(0, self.g.L * self.cuts, one, 0)

    def run(self, tables, meanwhile=None, prepare=None, work=None):
        g = self.g
        for s in range(self.cuts):
            self.column(g.z, s, own=True)
        low = g.z < 2
        first = (g.z == 0) | (g.z == 3)

        def one(m, done):
            word = jnp.int32(0)
            for at, (a, b) in enumerate(zip(*tables)):
                word = jnp.where(m // 3 == at, jnp.where(first, a, b), word)
            byte = lax.rem(m, 3)
            code = lax.rem(jnp.where(byte == 0, word, jnp.where(byte == 1, word // 128, word // 16384)), 128)
            zk = lax.rem(code // 4, 4)
            zk = jnp.where(low, zk, 3 - zk)
            s = lax.rem(code, 4)
            kind = code // 16
            pl.when(kind == 0)(lambda: self.column(zk, s))
            if g.X > 1:
                pl.when(kind == 1)(lambda: self.side_x(zk, s))
            if g.L > 1:
                pl.when(kind == 2)(lambda: self.side_l(zk, s))
            if g.X > 1 and g.L > 1:
                pl.when(kind == 3)(lambda: self.corner(zk, s))
            if meanwhile is not None:
                for at in range(3):
                    pl.when(code == 64 + at)(lambda at=at: meanwhile(at))
            count = jnp.int32(0)
            if work is not None:
                for off in range(g.X):
                    x = lax.rem(g.x + off, g.X)
                    hit = s == (0 if off == 0 else 1)
                    pl.when((kind == 5) & hit)(lambda x=x: prepare(zk, x))

                    def full(x=x, off=off):
                        self.mates(zk, x)
                        work(zk, x, done + max(off - 1, 0))

                    pl.when((kind == 6) & hit)(full)
                count = jnp.where(kind == 6, jnp.where(s == 0, 1, g.X - 1), 0)
            return done + count

        lax.fori_loop(0, 3 * len(tables[0]), one, jnp.int32(0))
        if work is None:

            def last(i, carry):
                self.mates(i // g.X, lax.rem(i, g.X))
                return carry

            lax.fori_loop(0, 4 * g.X, last, 0)

    def finish(self):
        self.drain = True

        def one(i, carry):
            zk, s = i // self.cuts, lax.rem(i, self.cuts)
            self.column(zk, s)
            self.side_x(zk, s)
            self.side_l(zk, s)
            self.corner(zk, s)
            return carry

        lax.fori_loop(0, 4 * self.cuts, one, 0)


class Scatter:
    def __init__(self, grid, stage, inbox, h, send_sem, recv_sem):
        self.g, self.stage, self.inbox, self.h = grid, stage, inbox, h
        self.cuts = cuts(h)
        self.send_sem, self.recv_sem = send_sem, recv_sem
        X, L = grid.X, grid.L
        at = 0
        self.base = {}
        for name, count in self.parts(X, L):
            self.base[name] = at
            at += count
        at = 0
        self.out = {}
        for name, count in self.out_parts(X, L):
            self.out[name] = at
            at += count
        self.drain = False

    @staticmethod
    def parts(X, L):
        side = (X - 1) * (L - 1)
        return (("mate", 4 * X * L), ("pair", 2 * side), ("l2", side), ("x2", side), ("xc", 4 * (X - 1)), ("lc", 4 * (L - 1)), ("z", 5))

    @staticmethod
    def out_parts(X, L):
        side = (X - 1) * (L - 1)
        return (("mate", 4 * X * L), ("corner", 8 * side), ("xc", 4 * (X - 1)), ("lc", 4 * (L - 1)), ("z", 4))

    @staticmethod
    def receives(levels, rows):
        return sum(count for _, count in Scatter.parts(rows // 8, levels))

    @staticmethod
    def sends(levels, rows):
        return 2 * sum(count for _, count in Scatter.out_parts(rows // 8, levels))

    def slot(self, block, l, s=None):
        start, size = (0, self.h) if s is None else self.cuts[s]
        return self.stage.at[pl.ds(pl.multiple_of((block * self.g.L + l) * self.h + start, 16), size)]

    def push(self, out, block, l, s, at, who, when=None):
        start, size = self.cuts[s]
        copy = pltpu.make_async_remote_copy(
            self.slot(block, l, s),
            self.inbox.at[at, pl.ds(start, size)],
            self.send_sem.at[2 * out + s],
            self.recv_sem.at[2 * at + s],
            device_id=who,
            device_id_type=MESH,
        )
        only(when, copy.wait_send if self.drain else copy.start)

    def arrived(self, at, s):
        start, size = self.cuts[s]
        place = self.inbox.at[at, pl.ds(start, size)]
        pltpu.make_async_remote_copy(
            place, place, self.send_sem.at[0], self.recv_sem.at[2 * at + s], device_id=self.g.mate(), device_id_type=MESH
        ).wait_recv()

    def total(self, block, l, s, ats):
        start, size = self.cuts[s]
        for at in ats:
            self.arrived(at, s)
        out = self.slot(block, l, s)[...].astype(F32)
        for at in ats:
            out = out + self.inbox[at, start : start + size].astype(F32)
        return out

    def add(self, block, l, s, ats, when=None):
        if self.drain:
            return

        def act():
            self.slot(block, l, s)[...] = self.total(block, l, s, ats).astype(BF16)

        only(when, act)

    def each(self):
        return range(len(self.cuts))

    def to_mate(self, z, x):
        g = self.g
        for l in range(g.L):
            at = (z * g.X + x) * g.L + l
            for s in self.each():
                self.push(self.out["mate"] + at, g.block(z, x, 1 - g.core), l, s, self.base["mate"] + at, g.mate())

    def from_mate(self, z, x):
        g = self.g
        for l in range(g.L):
            for s in self.each():
                self.add(g.block(z, x, g.core), l, s, [self.base["mate"] + (z * g.X + x) * g.L + l])

    def corner_far(self, z, i):
        g = self.g
        block = g.block(z, lax.rem(g.x + i, g.X), g.core)
        for j in range(1, g.L):
            l = g.l_other(j)[0]
            spot = (lax.rem(z, 2) * (g.X - 1) + i - 1) * (g.L - 1) + j - 1
            for s in self.each():
                self.push(self.out["corner"] + spot, block, l, s, self.base["pair"] + spot, g.at_z(g.pair_z()))

    def corner_near(self, z, i):
        g = self.g
        x, x_dev = g.x_other(i)
        block = g.block(z, x, g.core)
        even = self.even(z)
        side = (g.X - 1) * (g.L - 1)
        for j in range(1, g.L):
            l, l_dev = g.l_other(j)
            spot = (lax.rem(z, 2) * (g.X - 1) + i - 1) * (g.L - 1) + j - 1
            out = self.out["corner"] + 2 * side + spot
            for s in self.each():
                self.add(block, l, s, [self.base["pair"] + spot])
                self.push(out, block, l, s, self.base["l2"] + (i - 1) * (g.L - 1) + g.L - j - 1, l_dev, even)
                self.push(out, block, l, s, self.base["x2"] + (g.X - i - 1) * (g.L - 1) + j - 1, x_dev, jnp.logical_not(even))

    def side_x(self, zk, i, waits):
        g = self.g
        x, x_dev = g.x_other(i)
        block = g.block(zk, x, g.core)
        ats = [self.base["l2"] + (i - 1) * (g.L - 1) + j - 1 for j in range(1, g.L)]
        for s in self.each():
            if ats and waits:
                self.add(block, g.l, s, ats)
            self.push(self.out["xc"] + zk * (g.X - 1) + i - 1, block, g.l, s, self.base["xc"] + zk * (g.X - 1) + g.X - i - 1, x_dev)

    def side_l(self, zk, waits):
        g = self.g
        block = g.block(zk, g.x, g.core)
        for j in range(1, g.L):
            l, l_dev = g.l_other(j)
            ats = [self.base["x2"] + (i - 1) * (g.L - 1) + j - 1 for i in range(1, g.X)]
            for s in self.each():
                if waits:
                    self.add(block, l, s, ats)
                self.push(self.out["lc"] + zk * (g.L - 1) + j - 1, block, l, s, self.base["lc"] + zk * (g.L - 1) + g.L - j - 1, l_dev)

    def around(self, zk):
        g = self.g
        ats = [self.base["xc"] + zk * (g.X - 1) + i - 1 for i in range(1, g.X)]
        return ats + [self.base["lc"] + zk * (g.L - 1) + j - 1 for j in range(1, g.L)]

    def column(self, zk):
        g = self.g
        block = g.block(zk, g.x, g.core)
        behind = jnp.where(zk > g.z, g.down, g.up)
        near = jnp.abs(zk - g.z) == 1
        spot = jnp.where(near & (zk < g.z), 4, zk)
        for s in self.each():
            self.add(block, g.l, s, self.around(zk))
            self.add(block, g.l, s, [self.base["z"] + zk], behind)
            self.push(self.out["z"] + zk, block, g.l, s, self.base["z"] + spot, g.at_z(jnp.where(zk > g.z, g.z + 1, g.z - 1)))

    def last(self, out):
        g = self.g
        for s in self.each():
            start, size = self.cuts[s]
            out[start : start + size, :] = self.total(g.row, g.l, s, self.around(g.z))
            for at, there in ((self.base["z"] + g.z, g.down), (self.base["z"] + 4, g.up)):

                def take(at=at, s=s, start=start, size=size):
                    self.arrived(at, s)
                    out[start : start + size, :] += self.inbox[at, start : start + size].astype(F32)

                pl.when(there)(take)

    def even(self, zk):
        return lax.rem(jnp.where(self.g.z < 2, zk, 3 - zk), 2) == 0

    def decode(self, m):
        g = self.g
        first = (g.z == 0) | (g.z == 3)
        word = jnp.int32(0)
        for at, (a, b) in enumerate(zip(*self.tables)):
            word = jnp.where(m // 3 == at, jnp.where(first, a, b), word)
        byte = lax.rem(m, 3)
        code = lax.rem(jnp.where(byte == 0, word, jnp.where(byte == 1, word // 128, word // 16384)), 128)
        zk = lax.rem(code // 2, 4)
        return code, code // 8, jnp.where(g.z < 2, zk, 3 - zk), lax.rem(code, 2)

    def step(self, m, work=None, extra=None, done=0):
        g = self.g
        code, kind, zk, side = self.decode(m)
        for off in range(g.X):
            x = lax.rem(g.x + off, g.X)
            hit = side == (0 if off == 0 else 1)

            def make(x=x, off=off):
                if work is not None and not self.drain:
                    work(zk, x, done + max(off - 1, 0))
                self.to_mate(zk, x)

            pl.when((kind == 0) & hit)(make)
            if not self.drain:
                pl.when((kind == 1) & hit)(lambda x=x: self.from_mate(zk, x))
        near = g.local(zk)
        for i in range(1, g.X):
            if g.L > 1:
                pl.when((kind == 2) & near)(lambda i=i: self.corner_near(zk, i))
                pl.when((kind == 2) & jnp.logical_not(near))(lambda i=i: self.corner_far(zk, i))
            late = near & self.even(zk)
            pl.when((kind == 3) & late)(lambda i=i: self.side_x(zk, i, True))
            pl.when((kind == 3) & jnp.logical_not(late))(lambda i=i: self.side_x(zk, i, False))
        if g.L > 1:
            late = near & jnp.logical_not(self.even(zk))
            pl.when((kind == 4) & late)(lambda: self.side_l(zk, True))
            pl.when((kind == 4) & jnp.logical_not(late))(lambda: self.side_l(zk, False))
        pl.when(kind == 5)(lambda: self.column(zk))
        if extra is not None and not self.drain:
            pl.when(kind >= 6)(lambda: extra(code - 48))
        return jnp.where(kind == 0, jnp.where(side == 0, 1, g.X - 1), 0)

    def go(self, m, ahead, work=None, extra=None, done=0):
        count = self.step(m, work, extra, done)

        def wait():
            self.drain = True
            self.step(m - ahead)
            self.drain = False

        pl.when(m >= ahead)(wait)
        return count

    def run(self, tables, work=None, extra=None, beside=None, ahead=20):
        self.follow(tables, ahead)

        def one(m, done):
            count = self.go(m, self.ahead, work, extra, done)
            if beside is not None:
                beside(m)
            return done + count

        lax.fori_loop(0, self.steps, one, jnp.int32(0))

    def follow(self, tables, ahead):
        self.tables = tables
        self.steps = 3 * len(tables[0])
        self.ahead = min(ahead, self.steps)

    def finish(self):
        self.drain = True

        def one(m, carry):
            self.step(m)
            return carry

        lax.fori_loop(self.steps - self.ahead, self.steps, one, 0)


def dot(left, right):
    return jnp.dot(left, right, preferred_element_type=F32)


def dot_nt(left, right):
    return lax.dot_general(left, right, (((1,), (1,)), ((), ())), preferred_element_type=F32)


def dot_tn(left, right):
    return lax.dot_general(left, right, (((0,), (0,)), ((), ())), preferred_element_type=F32)


def fold(values):
    rows, width = values.shape
    return jnp.sum(values.reshape(rows // 8, 8, width), axis=0)


def norm_parts(values):
    average = jnp.mean(values, axis=-1, keepdims=True)
    centered = values - average
    scale = lax.rsqrt(jnp.mean(centered * centered, axis=-1, keepdims=True) + NORM_EPS)
    return centered * scale, scale


def norm_back(normed, scale, d_normed):
    mean_d = jnp.mean(d_normed, axis=-1, keepdims=True)
    mean_dn = jnp.mean(d_normed * normed, axis=-1, keepdims=True)
    return scale * (d_normed - mean_d - normed * mean_dn)


def silu_back(pre, d_active):
    gate = lax.logistic(pre)
    return d_active * (gate * (1.0 + pre * (1.0 - gate)))


def find_places(row_total, node_count, some, senders, receivers, live, place, side, facts_out, counts):
    tiles = senders.shape[0]
    group = tiles * 128 // row_total
    first = lax.axis_index("row") * node_count
    lane = lax.broadcasted_iota(jnp.int32, (128, 128), 1)
    sub = lax.broadcasted_iota(jnp.int32, (128, 128), 0)
    before = (sub < lane).astype(BF16)
    owner_ids = lax.broadcasted_iota(jnp.int32, (row_total, 128), 0)
    carry = owner_ids[:, :1].astype(F32) * group if some[0] == 0 else counts[:, 0:1]
    for tile in some:
        send = senders[tile : tile + 1, :]
        recv = receivers[tile : tile + 1, :] - first
        owner = lax.div(send, node_count)
        local = send - owner * node_count
        mine = owner_ids == owner
        ranks = dot(mine.astype(BF16), before) + carry
        spot = jnp.sum(jnp.where(mine, ranks, 0.0), axis=0, keepdims=True)
        carry = carry + jnp.sum(mine.astype(F32), axis=1, keepdims=True)
        place[tile : tile + 1, :] = spot.astype(jnp.int32)
        alive = (lane[:1] + tile * 128 < live[0, 0]).astype(jnp.int32)
        facts = jnp.where(sub == 0, lax.div(local, 16), 0)
        facts = jnp.where(sub == 1, lax.rem(local, 16), facts)
        facts = jnp.where(sub == 2, lax.div(recv, 16), facts)
        facts = jnp.where(sub == 3, lax.rem(recv, 16), facts)
        facts = jnp.where(sub == 4, alive, facts).astype(F32)
        side[:, pl.ds(tile * 128, 128)] = facts[:16].astype(BF16)
        facts_out[pl.ds(tile * 128, 128), :] = facts.T.astype(BF16)
    counts[...] = jnp.broadcast_to(carry, counts.shape)


def picker(place, start, size):
    ids = lax.broadcasted_iota(jnp.int32, (size, 128), 0) + start
    return jnp.concatenate([(ids == place[tile : tile + 1, :]).astype(BF16) for tile in range(place.shape[0])], axis=1)


def one_hot_cols(ids, count):
    lanes = lax.broadcasted_iota(jnp.int32, (ids.shape[0], count), 1).astype(F32)
    return (ids == lanes).astype(BF16)


def one_hot_rows(ids, count):
    subs = lax.broadcasted_iota(jnp.int32, (count, ids.shape[1]), 0).astype(F32)
    return (ids == subs).astype(BF16)


def load_all(pairs, sems):
    copies = [pltpu.make_async_copy(src, dst, sems.at[i]) for i, (src, dst) in enumerate(pairs)]
    for copy in copies:
        copy.start()
    return copies


def forward_kernel(
    layer, levels, rows, first_layer, *refs
):
    (node, b1, b2, gain, shift, nb1, nb2, ngain, nshift, w1_all, w2_all, nw1_all, nw2_all, plain_all) = refs[:14]
    refs = refs[14:]
    if first_layer:
        senders, receivers, live = refs[:3]
        refs = refs[3:]
    else:
        place, rows_of, cols_all, edges_all, before_all = refs[:5]
        refs = refs[5:]
    sent_out, pre_out, normed_out, update_out, moved_out = refs[:5]
    refs = refs[5:]
    if first_layer:
        edges_out, place, rows_of, cols = refs[:4]
        refs = refs[4:]
    scale_out, block_out, node_out, recv_out, npre_out, nnormed_out, nscale_out, tally = refs[:8]
    (
        table, total, cast, near, far, w1, w2, nw1, nw2, plain, joined, ordered, out_buf, scale_buf,
        load_sem, out_sem, moved_sem, send_sem, recv_sem, near_send, near_recv,
    ) = refs[8:29]
    if first_layer:
        side, counts = refs[29:]
    else:
        cols, edges, before = refs[29:]
    g = Grid(levels, rows)
    h, width = node_out.shape
    if first_layer:
        node = node.at[pl.ds(pl.multiple_of(g.l * h, h), h)]
    count = plain.shape[0]
    group = count // rows
    node_count = h * levels
    pairs = ((plain_all, plain), (w1_all.at[layer], w1), (w2_all.at[layer], w2), (nw1_all.at[layer], nw1), (nw2_all.at[layer], nw2))
    if not first_layer:
        pairs += ((cols_all, cols), (edges_all, edges), (before_all, before))
    loads = load_all(pairs, load_sem)
    ag = Courier(g, table, h, 2, send_sem, recv_sem)
    ag.own()[...] = node[...].astype(BF16)
    tally[...] = jnp.zeros_like(tally)
    total[...] = jnp.zeros_like(total)
    g.greet()
    wide = lambda ref: ref[layer : layer + 1, :]
    outs = (sent_out, pre_out, normed_out, update_out) + ((edges_out,) if first_layer else ())

    def meanwhile(at):
        if first_layer:
            tiles = place.shape[0]
            some = range(at * tiles // 3, (at + 1) * tiles // 3)
            find_places(rows, node_count, some, senders, receivers, live, place, side, joined.at[:, pl.ds(width, 128)], counts)
        if at == 0:
            for copy in loads:
                copy.wait()

        def cast_rows(i, carry):
            part = pl.ds(pl.multiple_of(i * 2 * group, 2 * group), 2 * group)
            joined[part, 0:width] = plain[part, :].astype(BF16)
            return carry

        lax.fori_loop(at * rows // 6, (at + 1) * rows // 6, cast_rows, 0)

    def leave(n, part):
        slot = lax.rem(n, 2)
        copies = [pltpu.make_async_copy(out_buf.at[slot, i], ref.at[part], out_sem.at[slot, i]) for i, ref in enumerate(outs)]
        return copies + [pltpu.make_async_copy(scale_buf.at[slot], scale_out.at[part], out_sem.at[slot, 5])]

    def spot(z, x):
        pair = g.block(z, x, 0)
        first = pl.multiple_of(pair * group, 2 * group)
        return pair, first, pl.ds(first, 2 * group)

    def moved_copy(z, x):
        part = spot(z, x)[2]
        return pltpu.make_async_copy(ordered.at[part], moved_out.at[part], moved_sem.at[z * g.X + x])

    def prepare(z, x):
        pair, first, part = spot(z, x)
        pick = picker(place, first, 2 * group)
        moved = dot(pick, joined[...])
        ordered[part, :] = moved[:, :width].astype(BF16)
        moved_copy(z, x).start()
        if first_layer:
            digits = moved[:, width:]
            lanes = lax.broadcasted_iota(jnp.int32, digits.shape, 1)
            ids = digits[:, 0:1] * 16.0 + digits[:, 1:2]
            got = digits[:, 2:3] * 16.0 + digits[:, 3:4]
            cols[part, :] = jnp.where(lanes == 0, ids, jnp.where(lanes == 1, got, jnp.where(lanes == 2, digits[:, 4:5], 0.0)))
            for half in range(2):
                digits = dot_nt(side[...], pick[half * group : (half + 1) * group])
                rows_of[pair + half] = jnp.concatenate(
                    [digits[0:1] * 16.0 + digits[1:2], digits[2:3] * 16.0 + digits[3:4], digits[4:10]], axis=0
                )

    def work(z, x, n):
        def own():
            here = table[pl.ds(pl.multiple_of(g.row * node_count, 16), node_count), :]
            cast[...] = dot(here, w1[2 * width :, :]).astype(BF16)
            block_out[...] = here

        pl.when(n == 0)(own)
        pair, first, part = spot(z, x)

        def free():
            for copy in leave(n, part):
                copy.wait()

        pl.when(n >= 2)(free)
        slot = lax.rem(n, 2)
        low = ordered[part, :] if first_layer else edges[part, :]
        cols_here = cols[part, :]
        send_pick = one_hot_cols(cols_here[:, 0:1], node_count)
        recv_pick = one_hot_cols(cols_here[:, 1:2], node_count)
        start = pl.multiple_of(pair * node_count, 16)
        sent = jnp.concatenate(
            [
                dot(send_pick[:group], table[pl.ds(start, node_count), :]).astype(BF16),
                dot(send_pick[group:], table[pl.ds(start + node_count, node_count), :]).astype(BF16),
            ],
            axis=0,
        )
        out_buf[slot, 0] = sent
        pre = dot(low, w1[:width, :]) + dot(sent, w1[width : 2 * width, :]) + dot(recv_pick, cast[...]) + wide(b1)
        out_buf[slot, 1] = pre.astype(BF16)
        active = (pre * lax.logistic(pre)).astype(BF16)
        normed, scale = norm_parts(dot(active, w2[...]) + wide(b2))
        out_buf[slot, 2] = normed.astype(BF16)
        scale_buf[slot] = jnp.broadcast_to(scale, (2 * group, 128))
        update = (normed * wide(gain) + wide(shift)) * cols_here[:, 2:3]
        update_low = update.astype(BF16)
        edge = low.astype(F32) + update
        if first_layer:
            out_buf[slot, 3] = update_low
            out_buf[slot, 4] = edge.astype(BF16)
        else:
            out_buf[slot, 3] = (before[part, :].astype(F32) + update).astype(BF16)
        tally[8:16, :] += fold(edge * edge)
        tally[16:24, :] += fold(update * update)
        for half in range(2):
            pick = one_hot_rows(rows_of[pair + half][1:2, :], node_count)
            total[...] += dot(pick, update_low[half * group : (half + 1) * group])
        for copy in leave(n, part):
            copy.start()

    ag.run(FIRST_ORDER if first_layer else LAST_ORDER, meanwhile, prepare, work)
    half = h // 2
    copies = [[], []]
    for part in range(2):
        here = slice(part * half, (part + 1) * half)
        for j in range(1, levels):
            l, l_dev = g.l_other(j)
            near[j - 1, here, :] = total[pl.ds(pl.multiple_of(l * h + part * half, half), half), :].astype(BF16)
            copy = pltpu.make_async_remote_copy(
                near.at[j - 1, pl.ds(part * half, half)],
                far.at[levels - 1 - j, pl.ds(part * half, half)],
                near_send.at[2 * (j - 1) + part],
                near_recv.at[2 * (levels - 1 - j) + part],
                device_id=l_dev,
                device_id_type=MESH,
            )
            copy.start()
            copies[part].append(copy)
    npre_out[...] = dot(node[...].astype(BF16), nw1[:width, :]) + wide(nb1)
    for part in range(2):
        here = slice(part * half, (part + 1) * half)
        received = total[pl.ds(pl.multiple_of(g.l * h + part * half, half), half), :]
        for copy in copies[part]:
            copy.wait()
        for j in range(1, levels):
            received = received + far[j - 1, here, :].astype(F32)
        received = received.astype(BF16)
        recv_out[here, :] = received
        npre = npre_out[here, :] + dot(received, nw1[width:, :])
        npre_out[here, :] = npre
        nnormed, nscale = norm_parts(dot((npre * lax.logistic(npre)).astype(BF16), nw2[...]) + wide(nb2))
        nnormed_out[here, :] = nnormed
        nscale_out[here, :] = jnp.broadcast_to(nscale, (half, 128))
        change = nnormed * wide(ngain) + wide(nshift)
        new = node[here, :] + change
        node_out[here, :] = new
        tally[0:8, :] += fold(new * new)
        tally[24:32, :] += fold(change * change)
    for n in range(2):
        for copy in leave(n, pl.ds(0, 2 * group)):
            copy.wait()
    for n in range(4 * g.X):
        moved_copy(n // g.X, n % g.X).wait()
    ag.finish()


def forward_layer(layer, node, small, weights, plain, index, edges=None, before=None):
    levels, rows = lax.axis_size("lvl"), lax.axis_size("row")
    width = node.shape[1]
    h = node.shape[0] // (levels if layer == 0 else 1)
    count = plain.shape[0]
    group = count // rows
    vmem = pl.BlockSpec(memory_space=pltpu.VMEM)
    hbm = pl.BlockSpec(memory_space=pl.ANY)
    first_layer = layer == 0
    shape = jax.ShapeDtypeStruct
    wide = shape((count, width), BF16)
    ins = (node,) + small + weights + (plain,) + index
    in_specs = [vmem] * 9 + [hbm] * 5
    outs = [wide] * 5
    out_specs = [hbm] * 5
    scratch = []
    if first_layer:
        in_specs += [vmem, vmem, pl.BlockSpec(memory_space=pltpu.SMEM)]
        outs += [wide, shape(index[0].shape, jnp.int32), shape((rows, 8, group), F32), shape((count, 128), F32)]
        out_specs += [hbm, vmem, vmem, vmem]
        scratch = [pltpu.VMEM((16, count), BF16), pltpu.VMEM((rows, 128), F32)]
    else:
        ins += (edges, before)
        in_specs += [vmem, vmem, hbm, hbm, hbm]
        scratch = [pltpu.VMEM((count, 128), F32), pltpu.VMEM((count, width), BF16), pltpu.VMEM((count, width), BF16)]
    outs += [
        shape((count, 128), F32),
        shape((h * levels, width), BF16),
        shape((h, width), F32),
        shape((h, width), BF16),
        shape((h, width), F32),
        shape((h, width), F32),
        shape((h, 128), F32),
        shape((32, width), F32),
    ]
    out_specs += [hbm] + [vmem] * 7
    others = max(levels - 1, 1)
    return pl.pallas_call(
        functools.partial(forward_kernel, layer, levels, rows, first_layer),
        out_shape=outs,
        in_specs=in_specs,
        out_specs=out_specs,
        scratch_shapes=[
            pltpu.VMEM((rows * h * levels, width), BF16),
            pltpu.VMEM((h * levels, width), F32),
            pltpu.VMEM((h * levels, width), BF16),
            pltpu.VMEM((others, h, width), BF16),
            pltpu.VMEM((others, h, width), BF16),
        ]
        + [pltpu.VMEM(weight.shape[1:], BF16) for weight in weights]
        + [
            pltpu.VMEM((count, width), F32),
            pltpu.VMEM((count, width + (128 if first_layer else 0)), BF16),
            pltpu.VMEM((count, width), BF16),
            pltpu.VMEM((2, 5, 2 * group, width), BF16),
            pltpu.VMEM((2, 2 * group, 128), F32),
            pltpu.SemaphoreType.DMA((8,)),
            pltpu.SemaphoreType.DMA((2, 6)),
            pltpu.SemaphoreType.DMA((rows // 2,)),
            pltpu.SemaphoreType.DMA((Courier.sends(levels, rows, 2),)),
            pltpu.SemaphoreType.DMA((Courier.receives(levels, rows, 2),)),
            pltpu.SemaphoreType.DMA((2 * others,)),
            pltpu.SemaphoreType.DMA((2 * others,)),
        ]
        + scratch,
        compiler_params=pltpu.CompilerParams(collective_id=1 + layer, has_side_effects=True, vmem_limit_bytes=VMEM_BYTES),
        name=f"forward_{layer}",
    )(*ins)


def backward_kernel(
    layer, levels, rows, last_layer,
    d_node, block, recv, npre, nnormed, nscale, rows_of, gain, ngain, node, d_before, cols_all, scale_all, d_edges, pre, normed, edges, sent,
    w1_all, w2_all, nw1_all, nw2_all,
    d_node_out, d_edges_out, d_change_out, grads, tally, node_all,
    stage, inbox, bufs, d_recv, turned, own_sum, out_buf, cols, scale, w1, w2, nw1, nw2,
    load_sem, out_sem, send_sem, recv_sem, near_send, near_recv,
):
    g = Grid(levels, rows)
    h, width = d_node_out.shape
    if last_layer:
        d_node = d_node.at[pl.ds(pl.multiple_of(g.l * h, h), h)]
    count = pre.shape[0]
    group = count // rows
    node_count = h * levels
    loads = load_all(
        ((nw2_all.at[layer], nw2), (nw1_all.at[layer], nw1), (w1_all.at[layer], w1), (w2_all.at[layer], w2))
        + tuple((src, bufs.at[i]) for i, src in enumerate((d_edges, pre, normed, edges, sent)))
        + ((cols_all, cols), (scale_all, scale)),
        load_sem,
    )
    rs = Scatter(g, stage, inbox, h, send_sem, recv_sem)
    wide = lambda ref: ref[layer : layer + 1, :]
    mine = pl.ds(pl.multiple_of(g.l * h, h), h)
    own_sum[...] = jnp.zeros_like(own_sum)
    tally[...] = jnp.zeros_like(tally)
    for copy in loads[:2]:
        copy.wait()
    tally[48:56, :] = fold(d_node[...] * nnormed[...])
    tally[56:64, :] = fold(d_node[...])
    d_two = norm_back(nnormed[...], nscale[:, 0:1], d_node[...] * wide(ngain)).astype(BF16)
    tally[40:48, :] = fold(d_two.astype(F32))
    d_one = silu_back(npre[...], dot_nt(d_two, nw2[...])).astype(BF16)
    tally[32:40, :] = fold(d_one.astype(F32))
    d_recv[mine, :] = dot_nt(d_one, nw1[width:, :]).astype(BF16)
    g.greet()
    copies = []
    for j in range(1, levels):
        copy = pltpu.make_async_remote_copy(
            d_recv.at[mine], d_recv.at[mine], near_send.at[j - 1], near_recv.at[levels - 1 - j], device_id=g.l_other(j)[1], device_id_type=MESH
        )
        copy.start()
        copies.append(copy)
    d_node_out[...] = d_node[...] + dot_nt(d_one, nw1[:width, :])
    active = (npre[...] * lax.logistic(npre[...])).astype(BF16)
    grads[4 * width + width : 6 * width, :] = dot_tn(recv[...], d_one).astype(BF16)
    grads[4 * width : 5 * width, :] = dot_tn(block[mine, :], d_one).astype(BF16)
    grads[6 * width : 7 * width, :] = dot_tn(active, d_two).astype(BF16)
    if last_layer:
        node_all[mine, :] = node[...].astype(BF16)
    for copy in copies:
        copy.wait()
    copies = []
    for j in range(1, levels if last_layer else 1):
        copy = pltpu.make_async_remote_copy(
            node_all.at[mine],
            node_all.at[mine],
            near_send.at[levels + j - 2],
            near_recv.at[2 * levels - 2 - j],
            device_id=g.l_other(j)[1],
            device_id_type=MESH,
        )
        copy.start()
        copies.append(copy)
    for copy in loads[2:]:
        copy.wait()

    def work(z, x, i):
        pair = g.block(z, x, 0)
        start = pl.multiple_of(pair * group, 2 * group)
        place = pl.ds(start, 2 * group)
        if not last_layer:
            earlier = pltpu.make_async_copy(d_before.at[place], out_buf.at[lax.rem(i, 2), 0], out_sem.at[lax.rem(i, 2), 0])
            earlier.start()
        cols_here = cols[place, :]
        recv_pick = one_hot_cols(cols_here[:, 1:2], node_count)
        d_edge = bufs[0, place, :].astype(F32)
        d_update = (d_edge + dot(recv_pick, d_recv[...])) * cols_here[:, 2:3]
        norm_here = bufs[2, place, :].astype(F32)
        tally[16:24, :] += fold(d_update * norm_here)
        tally[24:32, :] += fold(d_update)
        d_two = norm_back(norm_here, scale[place, 0:1], d_update * wide(gain)).astype(BF16)
        tally[8:16, :] += fold(d_two.astype(F32))
        pre_here = bufs[1, place, :].astype(F32)
        gate = lax.logistic(pre_here)
        d_one = (dot_nt(d_two, w2[...]) * (gate * (1.0 + pre_here * (1.0 - gate)))).astype(BF16)
        tally[0:8, :] += fold(d_one.astype(F32))
        bufs[0, place, :] = d_one
        bufs[1, place, :] = (pre_here * gate).astype(BF16)
        bufs[2, place, :] = d_two
        d_here = dot_nt(d_one, w1[:width, :])
        slot = lax.rem(i, 2)
        used = [
            pltpu.make_async_copy(out_buf.at[slot, n], ref.at[place], out_sem.at[slot, n])
            for n, ref in enumerate((d_edges_out, d_change_out))
            if n or last_layer
        ]

        def free():
            for copy in used:
                copy.wait()

        pl.when(i >= 2)(free)
        if last_layer:
            out_buf[slot, 0] = (d_edge + d_here).astype(BF16)
            out_buf[slot, 1] = d_here.astype(BF16)
        else:
            earlier.wait()
            out_buf[slot, 1] = (out_buf[slot, 0].astype(F32) + d_here).astype(BF16)
        for copy in used:
            copy.start()
        d_sent = dot_nt(d_one, w1[width : 2 * width, :]).astype(BF16)
        for half in range(2):
            ids = rows_of[pair + half]
            part = slice(half * group, (half + 1) * group)
            own_sum[...] += dot(one_hot_rows(ids[1:2, :], node_count), d_one[part])
            spot = pl.ds(pl.multiple_of((pair + half) * node_count, 16), node_count)
            stage[spot, :] = dot(one_hot_rows(ids[0:1, :], node_count), d_sent[part]).astype(BF16)

        def close():
            low = own_sum[...].astype(BF16)
            spot = pl.ds(pl.multiple_of(g.row * node_count, 16), node_count)
            stage[spot, :] = (stage[spot, :].astype(F32) + dot_nt(low, w1[2 * width :, :])).astype(BF16)
            grads[2 * width : 3 * width, :] = dot_tn(block[...], low).astype(BF16)

        pl.when((z == g.z) & (x == g.x))(close)

    def extra(n):
        for i, (at, left, right) in enumerate(((0, 3, 0), (1, 4, 0), (3, 1, 2))):

            def grad(at=at, left=left, right=right):
                grads[at * width : (at + 1) * width, :] = dot_tn(bufs[left], bufs[right]).astype(BF16)

            pl.when(n == i)(grad)

    rs.run(TERMS_ORDER, work, extra)
    rs.last(turned)
    for copy in copies:
        copy.wait()
    d_node_out[...] += turned[...]
    for slot in range(2):
        for n, ref in enumerate((d_edges_out, d_change_out)):
            if n or last_layer:
                pltpu.make_async_copy(out_buf.at[slot, n], ref.at[pl.ds(0, 2 * group)], out_sem.at[slot, n]).wait()
    rs.finish()


def backward_layer(layer, last_layer, d_node, node_saved, cols, rows_of, scale, small, weights, d_edges, edge_saved, node, d_before):
    levels, rows = lax.axis_size("lvl"), lax.axis_size("row")
    width = d_node.shape[1]
    h = d_node.shape[0] // (levels if last_layer else 1)
    count = d_edges.shape[0]
    group = count // rows
    vmem = pl.BlockSpec(memory_space=pltpu.VMEM)
    hbm = pl.BlockSpec(memory_space=pl.ANY)
    shape = jax.ShapeDtypeStruct
    ins = (d_node,) + node_saved + (rows_of,) + small + (node, d_before, cols, scale, d_edges) + edge_saved + weights
    outs = (
        shape((h, width), F32),
        shape((count, width) if last_layer else (16, 128), BF16),
        shape((count, width), BF16),
        shape((7 * width, width), BF16),
        shape((64, width), F32),
        shape((h * levels, width) if last_layer else (16, 128), BF16),
    )
    others = max(levels - 1, 1)
    return pl.pallas_call(
        functools.partial(backward_kernel, layer, levels, rows, last_layer),
        out_shape=outs,
        in_specs=[vmem] * (len(ins) - 12) + [hbm] * 12,
        out_specs=(vmem, hbm, hbm, vmem, vmem, vmem),
        scratch_shapes=[
            pltpu.VMEM((rows * h * levels, width), BF16),
            pltpu.VMEM((Scatter.receives(levels, rows), h, width), BF16),
            pltpu.VMEM((5, count, width), BF16),
            pltpu.VMEM((h * levels, width), BF16),
            pltpu.VMEM((h, width), F32),
            pltpu.VMEM((h * levels, width), F32),
            pltpu.VMEM((2, 2, 2 * group, width), BF16),
            pltpu.VMEM((count, 128), F32),
            pltpu.VMEM((count, 128), F32),
        ]
        + [pltpu.VMEM(weight.shape[1:], BF16) for weight in weights]
        + [
            pltpu.SemaphoreType.DMA((11,)),
            pltpu.SemaphoreType.DMA((2, 2)),
            pltpu.SemaphoreType.DMA((Scatter.sends(levels, rows),)),
            pltpu.SemaphoreType.DMA((2 * Scatter.receives(levels, rows),)),
            pltpu.SemaphoreType.DMA((2 * others,)),
            pltpu.SemaphoreType.DMA((2 * others,)),
                ],
        compiler_params=pltpu.CompilerParams(collective_id=3 + layer, has_side_effects=True, vmem_limit_bytes=VMEM_BYTES),
        name=f"backward_{layer}",
    )(*ins)


def sum_cuts(h):
    return 3 if h % 48 == 0 else 1


def sum_kernel(levels, rows, h, count, *refs):
    d_node, place, sums, last_sums, tally, last_tally, update_all, d_change_all = refs[:8]
    terms = refs[8 : count + 8]
    (
        out, d_node_all, update_out, d_change_out, stage, inbox, total, update, d_change, back,
        scatter_send, scatter_recv, gather_send, gather_recv, load_sem, back_sem, near_send, near_recv,
    ) = refs[count + 8 :]
    g = Grid(levels, rows)
    mine = pl.ds(pl.multiple_of(g.l * d_node.shape[0], d_node.shape[0]), d_node.shape[0])
    d_node_all[mine, :] = d_node[...].astype(BF16)
    pairs = []
    at = 0
    for term in terms:
        pairs.append((term, stage.at[pl.ds(at, term.shape[0])]))
        at += term.shape[0]
    pairs += [(update_all, update), (d_change_all, d_change)]
    loads = load_all(pairs, load_sem)
    width = stage.shape[1]
    lanes = lax.broadcasted_iota(jnp.int32, (16, width), 1)
    subs = lax.broadcasted_iota(jnp.int32, (16, width), 0)
    squares = jnp.zeros((16, width), F32)
    for layer, ref in enumerate((tally, last_tally)):
        for i in range(4):
            part = jnp.sum(jnp.sum(ref[8 * i : 8 * i + 8, :], axis=0, keepdims=True), axis=1, keepdims=True)
            squares = jnp.where((subs == 0) & (lanes == 4 * layer + i), part, squares)
    few = [jnp.sum(ref[...].reshape(8, 8, width), axis=1) for ref in (sums, last_sums)]
    stage[at : at + 16, :] = jnp.concatenate(few, axis=0).astype(BF16)
    stage[at + 16 : at + 32, :] = squares.astype(BF16)
    if stage.shape[0] > at + 32:
        stage[at + 32 :, :] = jnp.zeros((stage.shape[0] - at - 32, width), BF16)
    g.greet()
    for copy in loads:
        copy.wait()
    copies = [
        pltpu.make_async_remote_copy(
            d_node_all.at[mine], d_node_all.at[mine], near_send.at[j - 1], near_recv.at[levels - 1 - j], device_id=g.l_other(j)[1], device_id_type=MESH
        )
        for j in range(1, levels)
    ]

    def exchange(at):
        for copy in copies if at == 0 else ():
            copy.start()

    tiles = place.shape[0]
    size = 256 if tiles % 2 == 0 else 128
    lane = lax.broadcasted_iota(jnp.int32, (128, 128), 1).astype(F32)

    def leave(i):
        here = pl.ds(pl.multiple_of(i * size, size), size)
        return [pltpu.make_async_copy(back.at[i, n], ref.at[here], back_sem.at[i, n]) for n, ref in enumerate((update_out, d_change_out))]

    def restore(i):
        pick = []
        for part in range(size // 128):
            spot = jnp.broadcast_to(place[pl.ds(i * (size // 128) + part, 1), :], (128, 128)).astype(F32).T
            pick.append(jnp.concatenate([(spot == lane + float(128 * j)).astype(BF16) for j in range(tiles)], axis=1))
        pick = jnp.concatenate(pick, axis=0)
        back[i, 0] = dot(pick, update[...]).astype(BF16)
        back[i, 1] = dot(pick, d_change[...]).astype(BF16)
        for copy in leave(i):
            copy.start()

    rs = Scatter(g, stage, inbox, h, scatter_send, scatter_recv)
    after = tiles * 128 // size

    def extra(n):
        pl.when(n < after)(lambda: restore(jnp.minimum(n, after - 1)))

    rs.run(SUM_ORDER, None, extra)

    def more(i, carry):
        restore(i)
        return carry

    if after > 10:
        lax.fori_loop(10, after, more, 0)
    rs.last(total)
    ag = Courier(g, out, h, sum_cuts(h), gather_send, gather_recv)
    ag.own()[...] = total[...].astype(BF16)
    ag.run(ORDER if ag.cuts == 3 else PLAIN_ORDER, exchange)
    for copy in copies:
        copy.wait()
    for i in range(after):
        for copy in leave(i):
            copy.wait()
    rs.finish()
    ag.finish()


def sum_pieces(d_node, place, small, update, d_change, terms, call):
    levels, rows = lax.axis_size("lvl"), lax.axis_size("row")
    width = terms[0].shape[1]
    used = sum(term.shape[0] for term in terms) + 32
    h = -(-used // (16 * levels * rows)) * 16
    count = h * levels * rows
    vmem = pl.BlockSpec(memory_space=pltpu.VMEM)
    hbm = pl.BlockSpec(memory_space=pl.ANY)
    shape = jax.ShapeDtypeStruct
    tiles = update.shape[0] // 128
    size = 256 if tiles % 2 == 0 else 128
    return pl.pallas_call(
        functools.partial(sum_kernel, levels, rows, h, len(terms)),
        out_shape=(
            shape((count, width), BF16),
            shape((d_node.shape[0] * levels, width), BF16),
            shape(update.shape, BF16),
            shape(update.shape, BF16),
        ),
        in_specs=[vmem] * 6 + [hbm] * (2 + len(terms)),
        out_specs=(vmem, vmem, hbm, hbm),
        scratch_shapes=[
            pltpu.VMEM((count, width), BF16),
            pltpu.VMEM((Scatter.receives(levels, rows), h, width), BF16),
            pltpu.VMEM((h, width), F32),
            pltpu.VMEM(update.shape, BF16),
            pltpu.VMEM(update.shape, BF16),
            pltpu.VMEM((tiles * 128 // size, 2, size, width), BF16),
            pltpu.SemaphoreType.DMA((Scatter.sends(levels, rows),)),
            pltpu.SemaphoreType.DMA((2 * Scatter.receives(levels, rows),)),
            pltpu.SemaphoreType.DMA((Courier.sends(levels, rows, sum_cuts(h)),)),
            pltpu.SemaphoreType.DMA((Courier.receives(levels, rows, sum_cuts(h)),)),
            pltpu.SemaphoreType.DMA((len(terms) + 2,)),
            pltpu.SemaphoreType.DMA((tiles * 128 // size, 2)),
            pltpu.SemaphoreType.DMA((max(levels - 1, 1),)),
            pltpu.SemaphoreType.DMA((max(levels - 1, 1),)),
        ],
        compiler_params=pltpu.CompilerParams(collective_id=call, has_side_effects=True, vmem_limit_bytes=VMEM_BYTES),
        name=f"sum_{call}",
    )(d_node, place, *small, update, d_change, *terms)


def finish_kernel(parts, smalls, update, d_change, all_sums, node, d_node, edges, cot, edge_out, cot_out, *refs):
    count = len(parts) + smalls
    wide_outs, small_outs = refs[: len(parts)], refs[len(parts) : count]
    rms_out, node_out, d_node_out, sums, rest, lows, ins, outs, wide, sums_sem, rest_sem, low_sem, in_sem, out_sem, wide_sem = refs[count:]
    size, width = ins.shape[2:]
    steps = edges.shape[0] // size
    targets = [(n, i) for n, part in enumerate(parts) for i in range(part)]
    big = sums.shape[1]
    loads = load_all([(all_sums.at[pl.ds(layer * big, big)], sums.at[layer]) for layer in range(2)], sums_sem)
    loads.append(pltpu.make_async_copy(all_sums.at[pl.ds(2 * big, rest.shape[0])], rest, rest_sem))
    loads[-1].start()

    def load(step):
        here = pl.ds(step * size, size)
        pairs = ((edges, ins.at[step, 0], in_sem.at[step, 0]), (cot, ins.at[step, 1], in_sem.at[step, 1]))
        pairs += ((update, lows.at[step, 0], low_sem.at[step, 0]), (d_change, lows.at[step, 1], low_sem.at[step, 1]))
        return [pltpu.make_async_copy(ref.at[here], to, sem) for ref, to, sem in pairs]

    def leave(step):
        here = pl.ds(step * size, size)
        return [pltpu.make_async_copy(outs.at[step, n], ref.at[here], out_sem.at[step, n]) for n, ref in enumerate((edge_out, cot_out))]

    def widen(at):
        n, i = targets[at % len(targets)]
        ref = wide_outs[n].at[at // len(targets), pl.ds(i * width, width)]
        return pltpu.make_async_copy(wide.at[at], ref, wide_sem.at[at])

    total = 2 * len(targets)
    done = 0
    for step in range(steps):
        for copy in load(step):
            copy.start()
    for step in range(steps):
        for copy in load(step):
            copy.wait()
        for n in range(2):
            outs[step, n] = ins[step, n] + lows[step, n].astype(F32)
        for copy in leave(step):
            copy.start()
        if step == 0:
            for copy in loads:
                copy.wait()
        while done < total * (step + 1) // steps:
            layer, at = done // len(targets), done % len(targets)
            wide[done] = sums[layer, at * width : (at + 1) * width, :].astype(F32)
            widen(done).start()
            done += 1
    few = rest[...].astype(F32)
    for n, out in enumerate(small_outs):
        for layer in range(2):
            out[layer : layer + 1, :] = few[layer * smalls + n : layer * smalls + n + 1]
    rms_out[...] = few[2 * smalls : 2 * smalls + 1]
    node_out[...] = node[...].astype(F32)
    d_node_out[...] = d_node[...].astype(F32)
    for step in range(steps):
        for copy in leave(step):
            copy.wait()
    for at in range(total):
        widen(at).wait()


def finish_all(update, d_change, all_sums, node, d_node, edges, cot, parts, smalls):
    count, width = edges.shape
    size = 512 if count % 512 == 0 else 128
    vmem = pl.BlockSpec(memory_space=pltpu.VMEM)
    hbm = pl.BlockSpec(memory_space=pl.ANY)
    shape = jax.ShapeDtypeStruct
    wide = (shape((count, width), F32),) * 2 + tuple(shape((2, part * width, width), F32) for part in parts)
    narrow = (shape((2, width), F32),) * smalls + (shape((1, width), F32), shape(node.shape, F32), shape(node.shape, F32))
    return pl.pallas_call(
        functools.partial(finish_kernel, parts, smalls),
        out_shape=wide + narrow,
        in_specs=[hbm] * 3 + [vmem] * 2 + [hbm] * 2,
        out_specs=(hbm,) * len(wide) + (vmem,) * len(narrow),
        scratch_shapes=[
            pltpu.VMEM((2, sum(parts) * width, width), BF16),
            pltpu.VMEM((32, width), BF16),
            pltpu.VMEM((count // size, 2, size, width), BF16),
            pltpu.VMEM((count // size, 2, size, width), F32),
            pltpu.VMEM((count // size, 2, size, width), F32),
            pltpu.VMEM((2 * sum(parts), width, width), F32),
            pltpu.SemaphoreType.DMA((2,)),
            pltpu.SemaphoreType.DMA,
            pltpu.SemaphoreType.DMA((count // size, 2)),
            pltpu.SemaphoreType.DMA((count // size, 2)),
            pltpu.SemaphoreType.DMA((count // size, 2)),
            pltpu.SemaphoreType.DMA((2 * sum(parts),)),
        ],
        compiler_params=pltpu.CompilerParams(vmem_limit_bytes=VMEM_BYTES),
        name="finish_all",
    )(update, d_change, all_sums, node, d_node, edges, cot)


def on_device(
    node_latent, edge_latent, senders, receivers, live_edges,
    edge_w1, edge_b1, edge_w2, edge_b2, edge_gain, edge_shift, node_w1, node_b1, node_w2, node_b2, node_gain, node_shift,
    node_cotangent, edge_cotangent,
):
    node_count, width = node_latent.shape
    edge_count = edge_latent.shape[0]
    layers = edge_w1.shape[0]
    row_total, level_total = lax.axis_size("row"), lax.axis_size("lvl")
    node = node_latent
    weights = (edge_w1, edge_w2, node_w1, node_w2)
    small = (edge_b1, edge_b2, edge_gain, edge_shift, node_b1, node_b2, node_gain, node_shift)
    tiles = edge_count // 128
    index = (senders.reshape(tiles, 128), receivers.reshape(tiles, 128), live_edges.reshape(1, 1))
    sent, pre, normed, update, edges, edges_next, place, rows_of, cols, scale, block, node, recv, npre, nnormed, nscale, tally = forward_layer(
        0, node, small, weights, edge_latent, index
    )
    first = ((block, recv, npre, nnormed, nscale), scale, (pre, normed, edges, sent))
    sent, pre, normed, update, d_edges, scale, block, node, recv, npre, nnormed, nscale, tally_last = forward_layer(
        1, node, small, weights, edge_cotangent, (place, rows_of, cols), edges_next, update
    )
    last = ((block, recv, npre, nnormed, nscale), scale, (pre, normed, edges_next, sent))
    d_node = node_cotangent
    gains = (edge_gain, node_gain)
    d_node, d_edges, d_change, last_grads, last_sums, node_all = backward_layer(
        1, True, d_node, last[0], cols, rows_of, last[1], gains, weights, d_edges, last[2], node, d_edges
    )
    d_node, _, d_change, first_grads, first_sums, _ = backward_layer(
        0, False, d_node, first[0], cols, rows_of, first[1], gains, weights, d_edges, first[2], node, d_change
    )
    flat, d_node_all, update, d_change = sum_pieces(
        d_node, place, (first_sums, last_sums, tally, tally_last), update, d_change, [first_grads, last_grads], 5
    )
    edge_out, edge_grad, w1, w2, nw1, nw2, b1, b2, gain, shift, nb1, nb2, ngain, nshift, squares, node, d_node = finish_all(
        update, d_change, flat, node_all, d_node_all, edge_latent, edge_cotangent, (3, 1, 2, 1), 8
    )
    node_entries = float(node_count * row_total * width)
    edge_entries = float(edge_count * row_total * level_total * width)
    entries = jnp.array([node_entries, edge_entries, edge_entries, node_entries], F32)
    rms = jnp.sqrt(squares[0, : 4 * layers].reshape(layers, 4) / entries[None, :])
    return node, edge_out, d_node, edge_grad, w1, b1, w2, b2, gain, shift, nw1, nb1, nw2, nb2, ngain, nshift, rms


def solution(mesh):
    rows, both, whole = P("row", None), P(("lvl", "row"), None), P()
    edge = P(("lvl", "row"))
    placed = (rows, both, edge, edge, edge) + (whole,) * 12 + (rows, both)
    outs = (rows, both, rows, both) + (whole,) * 13
    return jax.shard_map(on_device, mesh=mesh, in_specs=placed, out_specs=outs, check_vma=False)
```
